32 devices in a mesh: scan: 2 (over x), slab: 16 (over z, y, core).
Axes of the slice: x: 2, y: 2, z: 4, core: 2. Of those that a mesh axis runs over, the one named last changes fastest.
Arguments:
- volume: float32 [64, 64, 1024], P(('scan', 'slab')), parts along dimension 0, may hold values from 0.3 to 3
- measured: float32 [96, 8, 1024], P(('scan', 'slab')), parts along dimension 0, may hold values from 0.3 to 3
- view_angle: int32 [16], P('scan'), parts along dimension 0, may hold values from 0 to 179
- view_lift: int32 [16], P('scan'), parts along dimension 0, may hold values from -6 to 6, as said below
- subset: int32 [8], P('scan'), parts along dimension 0, may hold values from 0 to 7, as said below
Outputs:
- residual: float32 [96, 8, 1024], P(('scan', 'slab')), parts along dimension 0
- updated: float32 [64, 64, 1024], P(('scan', 'slab')), parts along dimension 0
The draws below stay inside these ranges and needn't reach their ends.
There are 2 independent parts, one for each index of `scan`. The reference program is written for one: setup_inputs(seed, part) draws one part's arguments, and reference() takes and returns one part's arrays. A program takes and returns all parts, laid end to end along the dimension named above; each array names one. Nothing has to cross between parts.
Inputs may be any that keep to these rules, and one draw needn't show every extreme that they name: `view_lift`: in every scan some view has shift 6 and another has shift -6. `subset`: 4 different view numbers.
All inputs are finite; a program needn't handle non-finite values.
Results may differ from the reference program's by a relative error of at most 0.0003.
Values sent between devices are 32-bit elements; how exact they have to be, the bound alone decides.
No kernel may reach another device: no remote copies, remote signals or barrier semaphores. Data moves between devices by JAX's collectives and lax.ppermute only.
A program may use at most 64 MiB of HBM per device.

```python
import math
import jax
import jax.numpy as jnp
from jax import lax

NX = 1024
NCOL = 1024
NY = 64
VIEWS = 8
SUBS = 4
ANGLES = 180
NZ = 32
NROW = 48
LIFT = 6


def draw_view_lift(key, part):
    key = jax.random.fold_in(key, 11)
    key_values, key_shuffle = jax.random.split(key)
    values = jax.random.randint(key_values, (VIEWS,), -LIFT, LIFT + 1, dtype=jnp.int32)
    shuffle = jax.random.permutation(key_shuffle, VIEWS)
    values = values.at[shuffle[0]].set(LIFT)
    return values.at[shuffle[1]].set(-LIFT)


def draw_subset(key, part):
    key = jax.random.fold_in(key, 23)
    key_inner, key_shuffle = jax.random.split(key)
    inner = jax.random.permutation(key_inner, VIEWS - 2)[:SUBS - 2].astype(jnp.int32) + 1
    listed = jnp.concatenate([jnp.array([0, VIEWS - 1], dtype=jnp.int32), inner])
    return listed[jax.random.permutation(key_shuffle, SUBS)]


def touch_ends(result, stream_key, least, top_value):
    longest = result.shape.index(max(result.shape))
    spots = []
    for shift in (0, 1):
        where = [jax.random.randint(jax.random.fold_in(stream_key, axis), (), 0, length) for axis, length in enumerate(result.shape)]
        where[longest] = (where[longest] + shift) % result.shape[longest]
        spots.append(tuple(where))
    return result.at[spots[0]].set(least).at[spots[1]].set(top_value)


def block_scale(key, extent, shards, least, top_value):
    def one(dim, parts):
        steps = jax.random.uniform(jax.random.fold_in(jax.random.fold_in(key, 6), dim), (parts,), jnp.float32, least / len(shards), top_value / len(shards))
        return jnp.repeat(jnp.exp(steps), extent[dim] // parts).reshape((-1,) + (1,) * (len(extent) - dim - 1))

    loudness = one(*shards[0])
    for cut in shards[1:]:
        loudness = loudness * one(*cut)
    return loudness


def setup_inputs(seed: int = 0, part: int = 0) -> dict:
    keys = jax.random.split(jax.random.key(seed), 6)
    own_keys = jax.random.split(jax.random.fold_in(keys[5], part), 6)
    return {
        "volume": jnp.clip(jnp.exp(math.log(3.0) - 2.3025851 * jax.random.uniform(own_keys[0], (NZ, NY, NX), jnp.float32) ** block_scale(own_keys[0], (NZ, NY, NX), ((0, 16),), -0.2, 0.2)), 0.3, 3.0),
        "measured": jnp.clip(jnp.exp(math.log(3.0) - 2.3025851 * jax.random.uniform(own_keys[1], (NROW, VIEWS, NCOL), jnp.float32) ** block_scale(own_keys[1], (NROW, VIEWS, NCOL), ((0, 16),), -0.2, 0.2)), 0.3, 3.0),
        "view_angle": touch_ends(jax.random.randint(own_keys[2], (VIEWS,), 0, ANGLES), jax.random.fold_in(own_keys[2], 1), 0, ANGLES - 1).astype(jnp.int32),
        "view_lift": draw_view_lift(jax.random.fold_in(jax.random.fold_in(keys[5], part), 71), part),
        "subset": draw_subset(jax.random.fold_in(jax.random.fold_in(keys[5], part), 71), part),
    }


PITCH = 0.9
MAG_BASE = 1.5
ECCENTRIC = 0.12
LEN_FLOOR = 0.25


def view_geometry(angle_index, height):
    radians = (angle_index.astype(jnp.float32) + 0.5) * (0.5 * math.pi / ANGLES) - 0.25 * math.pi
    cosine = jnp.cos(radians)
    tangent = jnp.tan(radians)
    magnify = MAG_BASE / (1.0 - ECCENTRIC * jnp.sin(2.0 * radians + 1.0))
    return cosine, tangent, magnify, height.astype(jnp.float32)


def cone_weights(row_index, slice_index, magnify, height, rows_total, slices_total):
    sample = (row_index[None, :] + 0.5 - rows_total / 2 - height[:, None]) / magnify[:, None] + slices_total / 2 - 0.5
    return jnp.maximum(0.0, 1.0 - jnp.abs(sample[:, :, None] - slice_index[None, None, :]))


def column_weights(cosine, column_count, cell_count):
    center = (jnp.arange(column_count, dtype=jnp.float32) + 0.5 - column_count / 2) * (PITCH * cell_count / column_count) / cosine + cell_count / 2 - 0.5
    position = jnp.arange(cell_count, dtype=jnp.float32)
    return jnp.maximum(0.0, 1.0 - jnp.abs(position[None, :] - center[:, None]))


def shear_forward(field, tangent):
    row_count, cell_count = field.shape[-2], field.shape[-1]
    offset = (jnp.arange(row_count, dtype=jnp.float32) + 0.5 - row_count / 2) * tangent
    step_whole = jnp.floor(offset)
    fraction = offset - step_whole
    margin = row_count // 2 + 2
    padded = jnp.pad(field, [(0, 0)] * (field.ndim - 1) + [(margin, margin)])
    lookup = jnp.arange(cell_count, dtype=jnp.int32)[None, :] + step_whole.astype(jnp.int32)[:, None] + margin
    lookup = jnp.broadcast_to(lookup, field.shape)
    lower_tap = jnp.take_along_axis(padded, lookup, axis=-1)
    upper_tap = jnp.take_along_axis(padded, lookup + 1, axis=-1)
    return (1.0 - fraction)[:, None] * lower_tap + fraction[:, None] * upper_tap


def shear_adjoint(profile, tangent, row_count):
    cell_count = profile.shape[-1]
    offset = (jnp.arange(row_count, dtype=jnp.float32) + 0.5 - row_count / 2) * tangent
    step_whole = jnp.floor(offset)
    fraction = offset - step_whole
    margin = row_count // 2 + 2
    padded = jnp.pad(profile, [(0, 0)] * (profile.ndim - 1) + [(margin, margin)])
    lookup = jnp.arange(cell_count, dtype=jnp.int32)[None, :] - step_whole.astype(jnp.int32)[:, None] + margin
    lower_tap = jnp.take(padded, lookup, axis=-1)
    upper_tap = jnp.take(padded, lookup - 1, axis=-1)
    return (1.0 - fraction)[:, None] * lower_tap + fraction[:, None] * upper_tap


def reference(volume, measured, view_angle, view_lift, subset):
    highest = lax.Precision.HIGHEST
    cosine, tangent, magnify, height = view_geometry(view_angle, view_lift)
    all_rows = jnp.arange(NROW, dtype=jnp.float32)
    all_slices = jnp.arange(NZ, dtype=jnp.float32)
    cone_map = cone_weights(all_rows, all_slices, magnify, height, NROW, NZ)
    unit_field = jnp.ones((NY, NX), jnp.float32)

    def one_view(packed):
        cosine_one, tangent_one, cone_one = packed
        factor = 1.0 / (NY * cosine_one)
        collapsed = jnp.sum(shear_forward(volume, tangent_one), axis=1) * factor
        column_map = column_weights(cosine_one, NCOL, NX)
        profile = jnp.dot(collapsed, column_map.T, precision=highest)
        detector_image = jnp.dot(cone_one, profile, precision=highest)
        coverage_in = jnp.sum(shear_forward(unit_field, tangent_one), axis=0) * factor
        coverage = jnp.dot(column_map, coverage_in, precision=highest)
        length = jnp.sum(cone_one, axis=1)[:, None] * coverage[None, :]
        return detector_image, length

    images, lengths = lax.map(one_view, (cosine, tangent, cone_map))
    projection = jnp.transpose(images, (1, 0, 2))
    ray_length = jnp.transpose(lengths, (1, 0, 2))
    residual = (measured - projection) / jnp.maximum(ray_length, LEN_FLOOR)

    accumulated = jnp.zeros((NZ, NY, NX), jnp.float32)
    weight = jnp.zeros((NZ, NY, NX), jnp.float32)
    for member in range(SUBS):
        chosen_view = subset[member]
        cosine_one = cosine[chosen_view]
        tangent_one = tangent[chosen_view]
        cone_one = cone_map[chosen_view]
        factor = 1.0 / (NY * cosine_one)
        column_map = column_weights(cosine_one, NCOL, NX)
        spread = jnp.dot(cone_one.T, residual[:, chosen_view, :], precision=highest)
        profile = jnp.dot(spread, column_map, precision=highest) * factor
        accumulated = accumulated + shear_adjoint(profile, tangent_one, NY)
        edge_line = jnp.sum(column_map, axis=0) * factor
        weight = weight + jnp.sum(cone_one, axis=0)[:, None, None] * shear_adjoint(edge_line, tangent_one, NY)[None]
    updated = volume + accumulated / jnp.maximum(weight, LEN_FLOOR * SUBS / NY)
    return residual, updated
```

```python
import functools
import math

import jax
import jax.numpy as jnp
import numpy as np
from jax import lax
from jax.experimental import pallas as pl
from jax.experimental.pallas import tpu as pltpu
from jax.sharding import PartitionSpec as P

ANGLES = 180
LIFT = 6
PITCH = 0.9
MAG_BASE = 1.5
ECCENTRIC = 0.12
LEN_FLOOR = 0.25
LANES = 128
SUBLANES = 8
F32 = jnp.float32


def angle_table():
    radians = (np.arange(ANGLES) + 0.5) * (0.5 * math.pi / ANGLES) - 0.25 * math.pi
    magnify = MAG_BASE / (1.0 - ECCENTRIC * np.sin(2.0 * radians + 1.0))
    return np.cos(radians), magnify


def slab_reach(slab_count, slab_depth, row_share):
    _, magnify = angle_table()
    total_rows, total_slices = row_share * slab_count, slab_depth * slab_count
    rows = np.arange(total_rows)
    reach = 0
    for lift in range(-LIFT, LIFT + 1):
        sample = (rows[None] + 0.5 - total_rows / 2 - lift) / magnify[:, None] + total_slices / 2 - 0.5
        for tap in (np.floor(sample - 1e-3), np.floor(sample + 1e-3) + 1):
            inside = (tap >= 0) & (tap < total_slices)
            distance = np.abs(tap // slab_depth - rows[None] // row_share)
            reach = max(reach, int(distance[inside].max()))
    return reach


def lane_index():
    return lax.broadcasted_iota(jnp.int32, (SUBLANES, LANES), 1)


def sublane_index():
    return lax.broadcasted_iota(jnp.int32, (SUBLANES, LANES), 0)


def angle_facts(index):
    x = (index.astype(F32) + 0.5) * (0.5 * math.pi / ANGLES) - 0.25 * math.pi
    s = x * x
    sine = x * (1.0 + s * (-1 / 6 + s * (1 / 120 + s * (-1 / 5040 + s * (1 / 362880)))))
    cosine = 1.0 + s * (-1 / 2 + s * (1 / 24 + s * (-1 / 720 + s * (1 / 40320 + s * (-1 / 3628800)))))
    double = 2.0 * sine * cosine * math.cos(1.0) + (1.0 - 2.0 * sine * sine) * math.sin(1.0)
    return cosine, sine / cosine, (1.0 - ECCENTRIC * double) * (1.0 / MAG_BASE)


def spread_scalars(read, count, place):
    out = jnp.full((SUBLANES, LANES), read(0), jnp.int32)
    for item in range(1, count):
        out = jnp.where(place == item, read(item), out)
    return out


def pick(tile, index):
    return jnp.take_along_axis(tile, index, axis=1, mode="promise_in_bounds")


def next_lane(tile, following):
    lane = lane_index()
    return jnp.where(lane < LANES - 1, pltpu.roll(tile, LANES - 1, 1), pltpu.roll(following, LANES - 1, 1))


def rows_summed(parts):
    sub = sublane_index()
    step = SUBLANES // 2
    while step:
        low = jnp.bitwise_and(sub, step) == 0
        half = len(parts) // 2
        parts = [
            jnp.where(low, a, pltpu.roll(b, step, 0)) + jnp.where(low, pltpu.roll(a, SUBLANES - step, 0), b)
            for a, b in zip(parts[:half], parts[half:])
        ]
        step //= 2
    return parts[0]


def tile_of(ref, lead, tile):
    return ref[lead + (slice(None), slice(tile * LANES, (tile + 1) * LANES))]


def column_center(column, cosine, column_count, cell_count):
    return (column + 0.5 - column_count / 2) * (PITCH * cell_count / column_count) / cosine + (
        cell_count / 2 - 0.5
    )


def shear_steps(group, row_count, tangent):
    row = (sublane_index() + group * SUBLANES).astype(F32)
    offset = (row + 0.5 - row_count / 2) * tangent
    whole = jnp.floor(offset)
    return whole.astype(jnp.int32), offset - whole


def project_kernel(
    angle_ref, subset_ref, volume_ref, measured_ref, block_ref, cover_ref, part_sum_ref, part_up_ref, cell_ref, slope_ref
):
    slab_depth, row_count, cell_count = volume_ref.shape
    row_share, view_count, column_count = measured_ref.shape
    subset_count = subset_ref.shape[0]
    half = row_count // 2
    tiles = cell_count // LANES
    groups = row_count // SUBLANES
    lane, sub = lane_index(), sublane_index()
    zero = jnp.zeros((SUBLANES, LANES), F32)
    width = column_count // 2

    for row in range(row_share):
        for member in range(subset_count):
            view = subset_ref[member]
            for side in range(2):
                block_ref[2 * slab_depth + row, side * subset_count + member : side * subset_count + member + 1, :] = (
                    measured_ref[row, pl.ds(view, 1), side * width : (side + 1) * width]
                )

    def one_view(view, carry):
        _, tangent, _ = angle_facts(jnp.full((SUBLANES, LANES), angle_ref[view], jnp.int32))
        first_sum, first_up, last_sum, last_up, all_up = zero, zero, zero, zero, zero
        for group in range(groups):
            whole, fraction = shear_steps(group, row_count, tangent)
            near = lane + (whole + half) < LANES
            first_sum += jnp.where(near, 0.0, 1.0)
            first_up += jnp.where(near, 0.0, fraction)
            last_sum += jnp.where(near, 1.0, 0.0)
            last_up += jnp.where(near, fraction, 0.0)
            all_up += fraction
        for tile, pair in ((0, (first_sum, first_up)), (tiles, (last_sum, last_up)), (1, (zero, all_up))):
            cut = slice(tile * LANES, (tile + 1) * LANES)
            part_sum_ref[slab_depth, view, :, cut], part_up_ref[slab_depth, view, :, cut] = pair
        for depth in range(slab_depth):
            sums, ups = [zero] * (tiles + 1), [zero] * (tiles + 1)
            for group in range(groups):
                whole, fraction = shear_steps(group, row_count, tangent)
                place = lane + (whole + half)
                index = jnp.bitwise_and(place, LANES - 1)
                near = place < LANES
                before = zero
                for tile in range(tiles + 1):
                    after = zero
                    if tile < tiles:
                        cells = volume_ref[
                            depth, group * SUBLANES : (group + 1) * SUBLANES, tile * LANES : (tile + 1) * LANES
                        ]
                        after = pick(cells, index)
                    moved = jnp.where(near, before, after)
                    sums[tile] = sums[tile] + moved
                    ups[tile] = ups[tile] + fraction * moved
                    before = after
            for tile in range(tiles + 1):
                cut = slice(tile * LANES, (tile + 1) * LANES)
                part_sum_ref[depth, view, :, cut] = sums[tile]
                part_up_ref[depth, view, :, cut] = ups[tile]
        return carry

    lax.fori_loop(0, view_count, one_view, 0)

    shift = LANES - half
    for depth in range(slab_depth + 1):
        collapsed = []
        held = lambda ref, tile: rows_summed([tile_of(ref, (depth, view), tile) for view in range(view_count)])
        if depth < slab_depth:
            sums = [held(part_sum_ref, tile) for tile in range(tiles + 1)]
            ups = [held(part_up_ref, tile) for tile in range(tiles + 1)]
        else:
            sums = [held(part_sum_ref, 0)] + [zero + float(row_count)] * (tiles - 1) + [held(part_sum_ref, tiles)]
            ups = [held(part_up_ref, 0)] + [held(part_up_ref, 1)] * (tiles - 1) + [held(part_up_ref, tiles)]
        ups.append(zero)
        for tile in range(tiles + 1):
            cells = sums[tile] - ups[tile] + next_lane(ups[tile], ups[tile + 1])
            cell = lane + (tile * LANES - shift)
            if tile in (0, tiles):
                cells = jnp.where((cell >= 0) & (cell < cell_count), cells, 0.0)
            collapsed.append(cells)
        collapsed.append(zero)
        for tile in range(tiles + 1):
            cut = slice(tile * LANES, (tile + 1) * LANES)
            cell_ref[depth, :, cut] = collapsed[tile]
            slope_ref[depth, :, cut] = next_lane(collapsed[tile], collapsed[tile + 1]) - collapsed[tile]

    cosine, _, _ = angle_facts(spread_scalars(lambda v: angle_ref[v], view_count, sub))
    factor = 1.0 / (row_count * cosine)
    least = angle_table()[0].min()
    for tile in range(column_count // LANES):
        column = (lane + tile * LANES).astype(F32)
        center = column_center(column, cosine, column_count, cell_count)
        whole = jnp.floor(center)
        fraction = center - whole
        place = jnp.clip(whole.astype(jnp.int32) + shift, shift - 2, shift + cell_count)
        block, index = jnp.right_shift(place, 7), jnp.bitwise_and(place, LANES - 1)
        ends = [column_center(tile * LANES + e, c, column_count, cell_count) for e in (0, LANES - 1) for c in (1.0, least)]
        low = min(max(math.floor(min(ends) - 1e-2) + shift, shift - 2), shift + cell_count) // LANES
        high = min(max(math.floor(max(ends) + 1e-2) + shift, shift - 2), shift + cell_count) // LANES
        for depth in range(slab_depth + 1):
            cells, slope = zero, zero
            for source in range(low, high + 1):
                here = block == source
                cells = jnp.where(here, pick(tile_of(cell_ref, (depth,), source), index), cells)
                slope = jnp.where(here, pick(tile_of(slope_ref, (depth,), source), index), slope)
            profile = (cells + fraction * slope) * factor
            if depth == slab_depth:
                cover_ref[:, tile * LANES : (tile + 1) * LANES] = profile
            else:
                side, inner = divmod(tile * LANES, width)
                block_ref[depth * 2 + side, :, inner : inner + LANES] = profile


def update_kernel(
    slab_count,
    reach,
    angle_ref,
    lift_ref,
    subset_ref,
    volume_ref,
    measured_ref,
    cover_ref,
    *refs,
):
    blocks = refs[: 2 * reach + 1]
    residual_ref, updated_ref, profile_ref, cover_sub_ref, spread_ref, cell_ref, slope_ref, edge_ref, bend_ref = refs[
        2 * reach + 1 :
    ]
    slab_depth, row_count, cell_count = volume_ref.shape
    row_share, view_count, column_count = measured_ref.shape
    subset_count = subset_ref.shape[0]
    total_rows, total_slices = row_share * slab_count, slab_depth * slab_count
    half = row_count // 2
    tiles, columns = cell_count // LANES, column_count // LANES
    width = column_count // 2
    lane, sub = lane_index(), sublane_index()
    zero = jnp.zeros((SUBLANES, LANES), F32)
    slab = lax.axis_index("slab")
    odd = lax.rem(slab, 2)
    toward = 2 * odd - 1
    origin = [slab] + [slab + toward * j for j in range(1, reach + 1)]
    origin += [slab - toward * j for j in range(1, reach + 1)]

    def cone(rows, lifts, flat):
        return (rows + 0.5 - total_rows / 2 - lifts) * flat + (total_slices / 2 - 0.5)

    def cone_total(sample):
        whole = jnp.floor(sample)
        fraction = sample - whole
        low = jnp.where((whole >= 0) & (whole < total_slices), 1.0 - fraction, 0.0)
        return low + jnp.where((whole >= -1) & (whole < total_slices - 1), fraction, 0.0)

    def column_of(tile, at):
        return jnp.broadcast_to(tile[:, at : at + 1], (SUBLANES, LANES))

    _, _, flat = angle_facts(spread_scalars(lambda v: angle_ref[v], view_count, sub))
    lifts = spread_scalars(lambda v: lift_ref[v], view_count, sub).astype(F32)
    source = jnp.right_shift(lane, slab_depth.bit_length() - 1) if slab_depth & (slab_depth - 1) == 0 else lane // slab_depth
    slices = spread_scalars(lambda b: origin[b], len(blocks), source) * slab_depth + (lane - source * slab_depth)
    slices = slices.astype(F32)
    for row in range(row_share):
        sample = cone((slab * row_share + row).astype(F32), lifts, flat)
        weights = jnp.maximum(0.0, 1.0 - jnp.abs(sample - slices))
        total = cone_total(sample)
        image = [zero] * columns
        for place, block in enumerate(blocks):
            for depth in range(slab_depth):
                weight = column_of(weights, place * slab_depth + depth)
                for tile in range(columns):
                    side, inner = divmod(tile * LANES, width)
                    image[tile] = image[tile] + weight * block[depth * 2 + side, :, inner : inner + LANES]
        for tile in range(columns):
            cut = slice(tile * LANES, (tile + 1) * LANES)
            length = total * cover_ref[:, cut]
            residual_ref[row, :, cut] = (measured_ref[row, :, cut] - image[tile]) / jnp.maximum(length, LEN_FLOOR)

    member_of = jnp.bitwise_and(sub, subset_count - 1)
    cosine, _, flat = angle_facts(spread_scalars(lambda k: angle_ref[subset_ref[k]], subset_count, member_of))
    lifts = spread_scalars(lambda k: lift_ref[subset_ref[k]], subset_count, member_of).astype(F32)
    factor = 1.0 / (row_count * cosine)
    for member in range(subset_count):
        view = pl.ds(subset_ref[member], 1)
        for side in range(2):
            at = slice(side * subset_count + member, side * subset_count + member + 1)
            cover_sub_ref[at, :] = cover_ref[view, side * width : (side + 1) * width]
            near = blocks[1][(slab_depth - 1) * 2 + side, view, :], blocks[1][side, view, :]
            mate = blocks[1 + reach][(slab_depth - 1) * 2 + side, view, :], blocks[1 + reach][side, view, :]
            profile_ref[0, at, :] = jnp.where(odd == 0, near[0], mate[0])
            for depth in range(slab_depth):
                profile_ref[1 + depth, at, :] = blocks[0][depth * 2 + side, view, :]
            profile_ref[1 + slab_depth, at, :] = jnp.where(odd == 0, mate[1], near[1])

    rows_here = row_share * len(blocks)
    source = sum(jnp.where(lane >= row_share * b, 1, 0) for b in range(1, len(blocks)))
    rows = spread_scalars(lambda b: origin[b], len(blocks), source) * row_share + (lane - source * row_share)
    real = (rows >= 0) & (rows < total_rows) & (lane < rows_here)
    sample = cone(rows.astype(F32), lifts, flat)
    total = cone_total(sample)
    weights = [
        jnp.where(real, jnp.maximum(0.0, 1.0 - jnp.abs(sample - (slab * slab_depth + z).astype(F32))), 0.0)
        for z in range(-1, slab_depth + 1)
    ]
    inner_tiles = width // LANES
    spread = [[zero] * inner_tiles for _ in range(slab_depth)]
    for place in range(rows_here):
        weight = [column_of(w, place) for w in weights]
        length = column_of(total, place)
        block, row = blocks[place // row_share], place % row_share
        for tile in range(inner_tiles):
            cut = slice(tile * LANES, (tile + 1) * LANES)
            image = weight[0] * profile_ref[0, :, cut]
            for z in range(1, slab_depth + 2):
                image = image + weight[z] * profile_ref[z, :, cut]
            rest = (block[2 * slab_depth + row, :, cut] - image) / jnp.maximum(
                length * cover_sub_ref[:, cut], LEN_FLOOR
            )
            for depth in range(slab_depth):
                spread[depth][tile] = spread[depth][tile] + weight[1 + depth] * rest
    for depth in range(slab_depth):
        for tile in range(inner_tiles):
            for side in range(2):
                spread_ref[
                    depth * subset_count : (depth + 1) * subset_count,
                    side * width + tile * LANES : side * width + (tile + 1) * LANES,
                ] = spread[depth][tile][side * subset_count : (side + 1) * subset_count]

    least = angle_table()[0].min()
    spacing = PITCH * cell_count / column_count
    shifted, edges = [], []
    for tile in range(tiles + 1):
        cell = (lane + (tile * LANES - half)).astype(F32)
        inside = (cell >= 0) & (cell < cell_count)
        first = jnp.floor((cell - (cell_count / 2 + 0.5)) * cosine * (1.0 / spacing) + (column_count / 2 - 0.5 - 1e-3)) + 1.0
        ends = [
            (tile * LANES - half + e - cell_count / 2 - 0.5) * c / spacing + column_count / 2 + 0.5
            for e in (0, LANES - 1)
            for c in (1.0, least)
        ]
        value, edge = zero, zero
        for tap in range(3):
            column = first + tap
            weight = jnp.maximum(0.0, 1.0 - jnp.abs(cell - column_center(column, cosine, column_count, cell_count)))
            weight = jnp.where(inside & (column >= 0) & (column < column_count), weight, 0.0)
            place = jnp.clip(column.astype(jnp.int32), 0, column_count - 1)
            block, index = jnp.right_shift(place, 7), jnp.bitwise_and(place, LANES - 1)
            low = min(max(math.floor(min(ends) + tap - 0.6), 0), column_count - 1) // LANES
            high = min(max(math.ceil(max(ends) + tap + 0.6), 0), column_count - 1) // LANES
            found = zero
            for at in range(low, high + 1):
                found = jnp.where(block == at, pick(tile_of(spread_ref, (), at), index), found)
            value = value + weight * found
            edge = edge + weight
        shifted.append(value * factor)
        edges.append(edge * factor)
    shifted.append(zero)
    edges.append(zero)
    for tile in range(tiles + 1):
        cut = slice(tile * LANES, (tile + 1) * LANES)
        cell_ref[:, cut] = shifted[tile]
        slope_ref[:, cut] = next_lane(shifted[tile], shifted[tile + 1]) - shifted[tile]
        edge_ref[:, cut] = edges[tile]
        bend_ref[:, cut] = next_lane(edges[tile], edges[tile + 1]) - edges[tile]

    slice_total = [jnp.sum(weights[1 + depth], axis=1, keepdims=True) for depth in range(slab_depth)]
    slice_total = [
        [jnp.broadcast_to(t[k : k + 1], (SUBLANES, LANES)) for k in range(subset_count)] for t in slice_total
    ]
    tangents = [
        angle_facts(jnp.full((SUBLANES, LANES), angle_ref[subset_ref[k]], jnp.int32))[1] for k in range(subset_count)
    ]

    def one_group(group, carry):
        band = pl.ds(pl.multiple_of(group * SUBLANES, SUBLANES), SUBLANES)
        steps = []
        for member in range(subset_count):
            whole, fraction = shear_steps(group, row_count, tangents[member])
            place = lane + (half - 1 - whole)
            steps.append((jnp.bitwise_and(place, LANES - 1), place < LANES, 1.0 - fraction))

        def sheared(base_ref, bend, row, member):
            index, near, share = steps[member]
            before = None
            out = []
            for tile in range(tiles + 1):
                cut = slice(tile * LANES, (tile + 1) * LANES)
                low = pick(jnp.broadcast_to(base_ref[row : row + 1, cut], (SUBLANES, LANES)), index)
                rise = pick(jnp.broadcast_to(bend[row : row + 1, cut], (SUBLANES, LANES)), index)
                after = low + share * rise
                if tile:
                    out.append(jnp.where(near, before, after))
                before = after
            return out

        weight = [[zero] * tiles for _ in range(slab_depth)]
        for member in range(subset_count):
            line = sheared(edge_ref, bend_ref, member, member)
            for depth in range(slab_depth):
                for tile in range(tiles):
                    weight[depth][tile] = weight[depth][tile] + slice_total[depth][member] * line[tile]
        for depth in range(slab_depth):
            for tile in range(tiles):
                updated_ref[depth, band, tile * LANES : (tile + 1) * LANES] = jnp.maximum(
                    weight[depth][tile], LEN_FLOOR * subset_count / row_count
                )
        for depth in range(slab_depth):
            back = [zero] * tiles
            for member in range(subset_count):
                line = sheared(cell_ref, slope_ref, depth * subset_count + member, member)
                back = [b + a for b, a in zip(back, line)]
            for tile in range(tiles):
                cut = slice(tile * LANES, (tile + 1) * LANES)
                updated_ref[depth, band, cut] = volume_ref[depth, band, cut] + back[tile] / updated_ref[depth, band, cut]
        return carry

    lax.fori_loop(0, row_count // SUBLANES, one_group, 0)


def swapped(block):
    return lax.ppermute(block, "slab", [(i, i ^ 1) for i in range(lax.axis_size("slab"))])


def from_side(block, distance):
    slabs = range(lax.axis_size("slab"))
    below = [(i - distance, i) for i in slabs if i % 2 == 0 and i - distance in slabs]
    above = [(i + distance, i) for i in slabs if i % 2 == 1 and i + distance in slabs]
    return lax.ppermute(block, "slab", below + above)


def per_device(volume, measured, view_angle, view_lift, subset):
    slab_count = lax.axis_size("slab")
    slab_depth, row_count, cell_count = volume.shape
    row_share, view_count, column_count = measured.shape
    subset_count = subset.shape[0]
    tiles = cell_count // LANES
    reach = slab_reach(slab_count, slab_depth, row_share)
    smem, vmem = pl.BlockSpec(memory_space=pltpu.SMEM), pl.BlockSpec(memory_space=pltpu.VMEM)
    wide = (tiles + 1) * LANES
    block_shape = (2 * slab_depth + row_share, SUBLANES, column_count // 2)
    own, cover = pl.pallas_call(
        project_kernel,
        out_shape=(
            jax.ShapeDtypeStruct(block_shape, F32),
            jax.ShapeDtypeStruct((view_count, column_count), F32),
        ),
        in_specs=[smem, smem, vmem, vmem],
        out_specs=(vmem, vmem),
        scratch_shapes=[pltpu.VMEM((slab_depth + 1, view_count, SUBLANES, wide), F32)] * 2
        + [pltpu.VMEM((slab_depth + 1, SUBLANES, wide), F32)] * 2,
        name="project",
    )(view_angle, subset, volume, measured)
    near = [from_side(own, j) for j in range(1, reach + 1)]
    mate = swapped(own)
    far = [mate] + [swapped(b) for b in near[:-1]]
    return pl.pallas_call(
        functools.partial(update_kernel, slab_count, reach),
        out_shape=(
            jax.ShapeDtypeStruct(measured.shape, F32),
            jax.ShapeDtypeStruct(volume.shape, F32),
        ),
        in_specs=[smem] * 3 + [vmem] * (3 + 1 + 2 * reach),
        out_specs=(vmem, vmem),
        scratch_shapes=[
            pltpu.VMEM((slab_depth + 2, SUBLANES, column_count // 2), F32),
            pltpu.VMEM((SUBLANES, column_count // 2), F32),
            pltpu.VMEM((SUBLANES, column_count), F32),
        ]
        + [pltpu.VMEM((SUBLANES, wide), F32)] * 4,
        name="update",
    )(view_angle, view_lift, subset, volume, measured, cover, own, *near, *far)


def solution(mesh):
    in_specs = (
        P(("scan", "slab"), None, None),
        P(("scan", "slab"), None, None),
        P("scan"),
        P("scan"),
        P("scan"),
    )
    out_specs = (P(("scan", "slab"), None, None), P(("scan", "slab"), None, None))
    return jax.shard_map(
        per_device, mesh=mesh, in_specs=in_specs, out_specs=out_specs, check_vma=False
    )
```

```python
import functools
import math

import jax
import jax.numpy as jnp
import numpy as np
from jax import lax
from jax.experimental import pallas as pl
from jax.experimental.pallas import tpu as pltpu
from jax.sharding import PartitionSpec as P

ANGLES = 180
LIFT = 6
PITCH = 0.9
MAG_BASE = 1.5
ECCENTRIC = 0.12
LEN_FLOOR = 0.25
LANES = 128
SUBLANES = 8
F32 = jnp.float32


def angle_table():
    radians = (np.arange(ANGLES) + 0.5) * (0.5 * math.pi / ANGLES) - 0.25 * math.pi
    magnify = MAG_BASE / (1.0 - ECCENTRIC * np.sin(2.0 * radians + 1.0))
    return np.cos(radians), magnify


def slab_reach(slab_count, slab_depth, row_share):
    _, magnify = angle_table()
    total_rows, total_slices = row_share * slab_count, slab_depth * slab_count
    rows = np.arange(total_rows)
    reach = 0
    for lift in range(-LIFT, LIFT + 1):
        sample = (rows[None] + 0.5 - total_rows / 2 - lift) / magnify[:, None] + total_slices / 2 - 0.5
        for tap in (np.floor(sample - 1e-3), np.floor(sample + 1e-3) + 1):
            inside = (tap >= 0) & (tap < total_slices)
            distance = np.abs(tap // slab_depth - rows[None] // row_share)
            reach = max(reach, int(distance[inside].max()))
    return reach


def lane_index():
    return lax.broadcasted_iota(jnp.int32, (SUBLANES, LANES), 1)


def sublane_index():
    return lax.broadcasted_iota(jnp.int32, (SUBLANES, LANES), 0)


def angle_facts(index):
    x = (index.astype(F32) + 0.5) * (0.5 * math.pi / ANGLES) - 0.25 * math.pi
    s = x * x
    sine = x * (1.0 + s * (-1 / 6 + s * (1 / 120 + s * (-1 / 5040 + s * (1 / 362880)))))
    cosine = 1.0 + s * (-1 / 2 + s * (1 / 24 + s * (-1 / 720 + s * (1 / 40320 + s * (-1 / 3628800)))))
    double = 2.0 * sine * cosine * math.cos(1.0) + (1.0 - 2.0 * sine * sine) * math.sin(1.0)
    return cosine, sine / cosine, (1.0 - ECCENTRIC * double) * (1.0 / MAG_BASE)


def spread_scalars(read, count, place):
    out = jnp.full((SUBLANES, LANES), read(0), jnp.int32)
    for item in range(1, count):
        out = jnp.where(place == item, read(item), out)
    return out


def pick(tile, index):
    return jnp.take_along_axis(tile, index, axis=1, mode="promise_in_bounds")


def next_lane(tile, following):
    lane = lane_index()
    return jnp.where(lane < LANES - 1, pltpu.roll(tile, LANES - 1, 1), pltpu.roll(following, LANES - 1, 1))


def rows_summed(parts):
    sub = sublane_index()
    step = SUBLANES // 2
    while step:
        low = jnp.bitwise_and(sub, step) == 0
        half = len(parts) // 2
        parts = [
            jnp.where(low, a, pltpu.roll(b, step, 0)) + jnp.where(low, pltpu.roll(a, SUBLANES - step, 0), b)
            for a, b in zip(parts[:half], parts[half:])
        ]
        step //= 2
    return parts[0]


def tile_of(ref, lead, tile):
    return ref[lead + (slice(None), slice(tile * LANES, (tile + 1) * LANES))]


def column_center(column, cosine, column_count, cell_count):
    return (column + 0.5 - column_count / 2) * (PITCH * cell_count / column_count) / cosine + (
        cell_count / 2 - 0.5
    )


def shear_steps(group, row_count, tangent):
    row = (sublane_index() + group * SUBLANES).astype(F32)
    offset = (row + 0.5 - row_count / 2) * tangent
    whole = jnp.floor(offset)
    return whole.astype(jnp.int32), offset - whole


def project_kernel(
    angle_ref, subset_ref, volume_ref, measured_ref, block_ref, cover_ref, part_sum_ref, part_up_ref, cell_ref, slope_ref
):
    slab_depth, row_count, cell_count = volume_ref.shape
    row_share, view_count, column_count = measured_ref.shape
    subset_count = subset_ref.shape[0]
    half = row_count // 2
    tiles = cell_count // LANES
    groups = row_count // SUBLANES
    lane, sub = lane_index(), sublane_index()
    zero = jnp.zeros((SUBLANES, LANES), F32)
    width = column_count // 2

    for row in range(row_share):
        for member in range(subset_count):
            view = subset_ref[member]
            for side in range(2):
                block_ref[2 * slab_depth + row, side * subset_count + member : side * subset_count + member + 1, :] = (
                    measured_ref[row, pl.ds(view, 1), side * width : (side + 1) * width]
                )

    def one_view(view, carry):
        _, tangent, _ = angle_facts(jnp.full((SUBLANES, LANES), angle_ref[view], jnp.int32))
        first_sum, first_up, last_sum, last_up, all_up = zero, zero, zero, zero, zero
        for group in range(groups):
            whole, fraction = shear_steps(group, row_count, tangent)
            near = lane + (whole + half) < LANES
            first_sum += jnp.where(near, 0.0, 1.0)
            first_up += jnp.where(near, 0.0, fraction)
            last_sum += jnp.where(near, 1.0, 0.0)
            last_up += jnp.where(near, fraction, 0.0)
            all_up += fraction
        for tile, pair in ((0, (first_sum, first_up)), (tiles, (last_sum, last_up)), (1, (zero, all_up))):
            cut = slice(tile * LANES, (tile + 1) * LANES)
            part_sum_ref[slab_depth, view, :, cut], part_up_ref[slab_depth, view, :, cut] = pair
        for depth in range(slab_depth):
            sums, ups = [zero] * (tiles + 1), [zero] * (tiles + 1)
            for group in range(groups):
                whole, fraction = shear_steps(group, row_count, tangent)
                place = lane + (whole + half)
                index = jnp.bitwise_and(place, LANES - 1)
                near = place < LANES
                before = zero
                for tile in range(tiles + 1):
                    after = zero
                    if tile < tiles:
                        cells = volume_ref[
                            depth, group * SUBLANES : (group + 1) * SUBLANES, tile * LANES : (tile + 1) * LANES
                        ]
                        after = pick(cells, index)
                    moved = jnp.where(near, before, after)
                    sums[tile] = sums[tile] + moved
                    ups[tile] = ups[tile] + fraction * moved
                    before = after
            for tile in range(tiles + 1):
                cut = slice(tile * LANES, (tile + 1) * LANES)
                part_sum_ref[depth, view, :, cut] = sums[tile]
                part_up_ref[depth, view, :, cut] = ups[tile]
        return carry

    lax.fori_loop(0, view_count, one_view, 0)

    shift = LANES - half
    for depth in range(slab_depth + 1):
        collapsed = []
        held = lambda ref, tile: rows_summed([tile_of(ref, (depth, view), tile) for view in range(view_count)])
        if depth < slab_depth:
            sums = [held(part_sum_ref, tile) for tile in range(tiles + 1)]
            ups = [held(part_up_ref, tile) for tile in range(tiles + 1)]
        else:
            sums = [held(part_sum_ref, 0)] + [zero + float(row_count)] * (tiles - 1) + [held(part_sum_ref, tiles)]
            ups = [held(part_up_ref, 0)] + [held(part_up_ref, 1)] * (tiles - 1) + [held(part_up_ref, tiles)]
        ups.append(zero)
        for tile in range(tiles + 1):
            cells = sums[tile] - ups[tile] + next_lane(ups[tile], ups[tile + 1])
            cell = lane + (tile * LANES - shift)
            if tile in (0, tiles):
                cells = jnp.where((cell >= 0) & (cell < cell_count), cells, 0.0)
            collapsed.append(cells)
        collapsed.append(zero)
        for tile in range(tiles + 1):
            cut = slice(tile * LANES, (tile + 1) * LANES)
            cell_ref[depth, :, cut] = collapsed[tile]
            slope_ref[depth, :, cut] = next_lane(collapsed[tile], collapsed[tile + 1]) - collapsed[tile]

    cosine, _, _ = angle_facts(spread_scalars(lambda v: angle_ref[v], view_count, sub))
    factor = 1.0 / (row_count * cosine)
    least = angle_table()[0].min()
    for tile in range(column_count // LANES):
        column = (lane + tile * LANES).astype(F32)
        center = column_center(column, cosine, column_count, cell_count)
        whole = jnp.floor(center)
        fraction = center - whole
        place = jnp.clip(whole.astype(jnp.int32) + shift, shift - 2, shift + cell_count)
        block, index = jnp.right_shift(place, 7), jnp.bitwise_and(place, LANES - 1)
        ends = [column_center(tile * LANES + e, c, column_count, cell_count) for e in (0, LANES - 1) for c in (1.0, least)]
        low = min(max(math.floor(min(ends) - 1e-2) + shift, shift - 2), shift + cell_count) // LANES
        high = min(max(math.floor(max(ends) + 1e-2) + shift, shift - 2), shift + cell_count) // LANES
        for depth in range(slab_depth + 1):
            cells, slope = zero, zero
            for source in range(low, high + 1):
                here = block == source
                cells = jnp.where(here, pick(tile_of(cell_ref, (depth,), source), index), cells)
                slope = jnp.where(here, pick(tile_of(slope_ref, (depth,), source), index), slope)
            profile = (cells + fraction * slope) * factor
            if depth == slab_depth:
                cover_ref[:, tile * LANES : (tile + 1) * LANES] = profile
            else:
                side, inner = divmod(tile * LANES, width)
                block_ref[depth * 2 + side, :, inner : inner + LANES] = profile


def update_kernel(
    slab_count,
    reach,
    angle_ref,
    lift_ref,
    subset_ref,
    volume_ref,
    measured_ref,
    cover_ref,
    *refs,
):
    blocks = refs[: 2 * reach + 1]
    residual_ref, updated_ref, profile_ref, cover_sub_ref, spread_ref, cell_ref, slope_ref, edge_ref, bend_ref = refs[
        2 * reach + 1 :
    ]
    slab_depth, row_count, cell_count = volume_ref.shape
    row_share, view_count, column_count = measured_ref.shape
    subset_count = subset_ref.shape[0]
    total_rows, total_slices = row_share * slab_count, slab_depth * slab_count
    half = row_count // 2
    tiles, columns = cell_count // LANES, column_count // LANES
    width = column_count // 2
    lane, sub = lane_index(), sublane_index()
    zero = jnp.zeros((SUBLANES, LANES), F32)
    slab = lax.axis_index("slab")
    odd = lax.rem(slab, 2)
    toward = 2 * odd - 1
    origin = [slab] + [slab + toward * j for j in range(1, reach + 1)]
    origin += [slab - toward * j for j in range(1, reach + 1)]

    def cone(rows, lifts, flat):
        return (rows + 0.5 - total_rows / 2 - lifts) * flat + (total_slices / 2 - 0.5)

    def cone_total(sample):
        whole = jnp.floor(sample)
        fraction = sample - whole
        low = jnp.where((whole >= 0) & (whole < total_slices), 1.0 - fraction, 0.0)
        return low + jnp.where((whole >= -1) & (whole < total_slices - 1), fraction, 0.0)

    def column_of(tile, at):
        return jnp.broadcast_to(tile[:, at : at + 1], (SUBLANES, LANES))

    _, _, flat = angle_facts(spread_scalars(lambda v: angle_ref[v], view_count, sub))
    lifts = spread_scalars(lambda v: lift_ref[v], view_count, sub).astype(F32)
    source = jnp.right_shift(lane, slab_depth.bit_length() - 1) if slab_depth & (slab_depth - 1) == 0 else lane // slab_depth
    slices = spread_scalars(lambda b: origin[b], len(blocks), source) * slab_depth + (lane - source * slab_depth)
    held = (slices >= 0) & (slices < total_slices)
    slices = slices.astype(F32)
    for row in range(row_share):
        sample = cone((slab * row_share + row).astype(F32), lifts, flat)
        weights = jnp.where(held, jnp.maximum(0.0, 1.0 - jnp.abs(sample - slices)), 0.0)
        total = cone_total(sample)
        image = [zero] * columns
        for place, block in enumerate(blocks):
            for depth in range(slab_depth):
                weight = column_of(weights, place * slab_depth + depth)
                for tile in range(columns):
                    side, inner = divmod(tile * LANES, width)
                    image[tile] = image[tile] + weight * block[depth * 2 + side, :, inner : inner + LANES]
        for tile in range(columns):
            cut = slice(tile * LANES, (tile + 1) * LANES)
            length = total * cover_ref[:, cut]
            residual_ref[row, :, cut] = (measured_ref[row, :, cut] - image[tile]) / jnp.maximum(length, LEN_FLOOR)

    member_of = jnp.bitwise_and(sub, subset_count - 1)
    cosine, _, flat = angle_facts(spread_scalars(lambda k: angle_ref[subset_ref[k]], subset_count, member_of))
    lifts = spread_scalars(lambda k: lift_ref[subset_ref[k]], subset_count, member_of).astype(F32)
    factor = 1.0 / (row_count * cosine)
    for member in range(subset_count):
        view = pl.ds(subset_ref[member], 1)
        for side in range(2):
            at = slice(side * subset_count + member, side * subset_count + member + 1)
            cover_sub_ref[at, :] = cover_ref[view, side * width : (side + 1) * width]
            near = blocks[1][(slab_depth - 1) * 2 + side, view, :], blocks[1][side, view, :]
            mate = blocks[1 + reach][(slab_depth - 1) * 2 + side, view, :], blocks[1 + reach][side, view, :]
            profile_ref[0, at, :] = jnp.where(odd == 0, near[0], mate[0])
            for depth in range(slab_depth):
                profile_ref[1 + depth, at, :] = blocks[0][depth * 2 + side, view, :]
            profile_ref[1 + slab_depth, at, :] = jnp.where(odd == 0, mate[1], near[1])

    rows_here = row_share * len(blocks)
    source = sum(jnp.where(lane >= row_share * b, 1, 0) for b in range(1, len(blocks)))
    rows = spread_scalars(lambda b: origin[b], len(blocks), source) * row_share + (lane - source * row_share)
    real = (rows >= 0) & (rows < total_rows) & (lane < rows_here)
    sample = cone(rows.astype(F32), lifts, flat)
    total = cone_total(sample)
    weights = []
    for z in range(-1, slab_depth + 1):
        at = slab * slab_depth + z
        use = real & (at >= 0) & (at < total_slices)
        weights.append(jnp.where(use, jnp.maximum(0.0, 1.0 - jnp.abs(sample - at.astype(F32))), 0.0))
    inner_tiles = width // LANES
    spread = [[zero] * inner_tiles for _ in range(slab_depth)]
    for place in range(rows_here):
        weight = [column_of(w, place) for w in weights]
        length = column_of(total, place)
        block, row = blocks[place // row_share], place % row_share
        for tile in range(inner_tiles):
            cut = slice(tile * LANES, (tile + 1) * LANES)
            image = weight[0] * profile_ref[0, :, cut]
            for z in range(1, slab_depth + 2):
                image = image + weight[z] * profile_ref[z, :, cut]
            rest = (block[2 * slab_depth + row, :, cut] - image) / jnp.maximum(
                length * cover_sub_ref[:, cut], LEN_FLOOR
            )
            for depth in range(slab_depth):
                spread[depth][tile] = spread[depth][tile] + weight[1 + depth] * rest
    for depth in range(slab_depth):
        for tile in range(inner_tiles):
            for side in range(2):
                spread_ref[
                    depth * subset_count : (depth + 1) * subset_count,
                    side * width + tile * LANES : side * width + (tile + 1) * LANES,
                ] = spread[depth][tile][side * subset_count : (side + 1) * subset_count]

    least = angle_table()[0].min()
    spacing = PITCH * cell_count / column_count
    shifted, edges = [], []
    for tile in range(tiles + 1):
        cell = (lane + (tile * LANES - half)).astype(F32)
        inside = (cell >= 0) & (cell < cell_count)
        first = jnp.floor((cell - (cell_count / 2 + 0.5)) * cosine * (1.0 / spacing) + (column_count / 2 - 0.5 - 1e-3)) + 1.0
        ends = [
            (tile * LANES - half + e - cell_count / 2 - 0.5) * c / spacing + column_count / 2 + 0.5
            for e in (0, LANES - 1)
            for c in (1.0, least)
        ]
        value, edge = zero, zero
        for tap in range(3):
            column = first + tap
            weight = jnp.maximum(0.0, 1.0 - jnp.abs(cell - column_center(column, cosine, column_count, cell_count)))
            weight = jnp.where(inside & (column >= 0) & (column < column_count), weight, 0.0)
            place = jnp.clip(column.astype(jnp.int32), 0, column_count - 1)
            block, index = jnp.right_shift(place, 7), jnp.bitwise_and(place, LANES - 1)
            low = min(max(math.floor(min(ends) + tap - 0.6), 0), column_count - 1) // LANES
            high = min(max(math.ceil(max(ends) + tap + 0.6), 0), column_count - 1) // LANES
            found = zero
            for at in range(low, high + 1):
                found = jnp.where(block == at, pick(tile_of(spread_ref, (), at), index), found)
            value = value + weight * found
            edge = edge + weight
        shifted.append(value * factor)
        edges.append(edge * factor)
    shifted.append(zero)
    edges.append(zero)
    for tile in range(tiles + 1):
        cut = slice(tile * LANES, (tile + 1) * LANES)
        cell_ref[:, cut] = shifted[tile]
        slope_ref[:, cut] = next_lane(shifted[tile], shifted[tile + 1]) - shifted[tile]
        edge_ref[:, cut] = edges[tile]
        bend_ref[:, cut] = next_lane(edges[tile], edges[tile + 1]) - edges[tile]

    slice_total = [jnp.sum(weights[1 + depth], axis=1, keepdims=True) for depth in range(slab_depth)]
    slice_total = [
        [jnp.broadcast_to(t[k : k + 1], (SUBLANES, LANES)) for k in range(subset_count)] for t in slice_total
    ]
    tangents = [
        angle_facts(jnp.full((SUBLANES, LANES), angle_ref[subset_ref[k]], jnp.int32))[1] for k in range(subset_count)
    ]

    def one_group(group, carry):
        band = pl.ds(pl.multiple_of(group * SUBLANES, SUBLANES), SUBLANES)
        steps = []
        for member in range(subset_count):
            whole, fraction = shear_steps(group, row_count, tangents[member])
            place = lane + (half - 1 - whole)
            steps.append((jnp.bitwise_and(place, LANES - 1), place < LANES, 1.0 - fraction))

        def sheared(base_ref, bend, row, member):
            index, near, share = steps[member]
            before = None
            out = []
            for tile in range(tiles + 1):
                cut = slice(tile * LANES, (tile + 1) * LANES)
                low = pick(jnp.broadcast_to(base_ref[row : row + 1, cut], (SUBLANES, LANES)), index)
                rise = pick(jnp.broadcast_to(bend[row : row + 1, cut], (SUBLANES, LANES)), index)
                after = low + share * rise
                if tile:
                    out.append(jnp.where(near, before, after))
                before = after
            return out

        weight = [[zero] * tiles for _ in range(slab_depth)]
        for member in range(subset_count):
            line = sheared(edge_ref, bend_ref, member, member)
            for depth in range(slab_depth):
                for tile in range(tiles):
                    weight[depth][tile] = weight[depth][tile] + slice_total[depth][member] * line[tile]
        for depth in range(slab_depth):
            for tile in range(tiles):
                updated_ref[depth, band, tile * LANES : (tile + 1) * LANES] = jnp.maximum(
                    weight[depth][tile], LEN_FLOOR * subset_count / row_count
                )
        for depth in range(slab_depth):
            back = [zero] * tiles
            for member in range(subset_count):
                line = sheared(cell_ref, slope_ref, depth * subset_count + member, member)
                back = [b + a for b, a in zip(back, line)]
            for tile in range(tiles):
                cut = slice(tile * LANES, (tile + 1) * LANES)
                updated_ref[depth, band, cut] = volume_ref[depth, band, cut] + back[tile] / updated_ref[depth, band, cut]
        return carry

    lax.fori_loop(0, row_count // SUBLANES, one_group, 0)


def swapped(block):
    return lax.ppermute(block, "slab", [(i, i ^ 1) for i in range(lax.axis_size("slab"))])


def from_side(block, distance):
    slabs = range(lax.axis_size("slab"))
    pairs = [(i - distance, i) for i in slabs if i % 2 == 0 and i - distance in slabs]
    pairs += [(i + distance, i) for i in slabs if i % 2 == 1 and i + distance in slabs]
    idle = [i for i in slabs if i not in [p[0] for p in pairs]]
    unmet = [i for i in slabs if i not in [p[1] for p in pairs]]
    both = [i for i in idle if i in unmet]
    pairs += [(i, i) for i in both]
    pairs += list(zip([i for i in idle if i not in both], [i for i in unmet if i not in both]))
    return lax.ppermute(block, "slab", pairs)


def per_device(volume, measured, view_angle, view_lift, subset):
    slab_count = lax.axis_size("slab")
    slab_depth, row_count, cell_count = volume.shape
    row_share, view_count, column_count = measured.shape
    subset_count = subset.shape[0]
    tiles = cell_count // LANES
    reach = slab_reach(slab_count, slab_depth, row_share)
    smem, vmem = pl.BlockSpec(memory_space=pltpu.SMEM), pl.BlockSpec(memory_space=pltpu.VMEM)
    wide = (tiles + 1) * LANES
    block_shape = (2 * slab_depth + row_share, SUBLANES, column_count // 2)
    own, cover = pl.pallas_call(
        project_kernel,
        out_shape=(
            pltpu.VMEM(block_shape, F32),
            pltpu.VMEM((view_count, column_count), F32),
        ),
        in_specs=[smem, smem, vmem, vmem],
        out_specs=(vmem, vmem),
        scratch_shapes=[pltpu.VMEM((slab_depth + 1, view_count, SUBLANES, wide), F32)] * 2
        + [pltpu.VMEM((slab_depth + 1, SUBLANES, wide), F32)] * 2,
        name="project",
    )(view_angle, subset, volume, measured)
    near = [from_side(own, j) for j in range(1, reach + 1)]
    mate = swapped(own)
    far = [mate] + [swapped(b) for b in near[:-1]]
    here = lambda x: pltpu.with_memory_space_constraint(x, pltpu.VMEM)
    return pl.pallas_call(
        functools.partial(update_kernel, slab_count, reach),
        out_shape=(
            jax.ShapeDtypeStruct(measured.shape, F32),
            jax.ShapeDtypeStruct(volume.shape, F32),
        ),
        in_specs=[smem] * 3 + [vmem] * (3 + 1 + 2 * reach),
        out_specs=(vmem, vmem),
        scratch_shapes=[
            pltpu.VMEM((slab_depth + 2, SUBLANES, column_count // 2), F32),
            pltpu.VMEM((SUBLANES, column_count // 2), F32),
            pltpu.VMEM((SUBLANES, column_count), F32),
        ]
        + [pltpu.VMEM((SUBLANES, wide), F32)] * 4,
        name="update",
    )(view_angle, view_lift, subset, volume, measured, here(cover), *map(here, (own, *near, *far)))


def solution(mesh):
    in_specs = (
        P(("scan", "slab"), None, None),
        P(("scan", "slab"), None, None),
        P("scan"),
        P("scan"),
        P("scan"),
    )
    out_specs = (P(("scan", "slab"), None, None), P(("scan", "slab"), None, None))
    return jax.shard_map(
        per_device, mesh=mesh, in_specs=in_specs, out_specs=out_specs, check_vma=False
    )
```

```python
import functools
import math

import jax
import jax.numpy as jnp
import numpy as np
from jax import lax
from jax.experimental import pallas as pl
from jax.experimental.pallas import tpu as pltpu
from jax.sharding import PartitionSpec as P

ANGLES = 180
LIFT = 6
PITCH = 0.9
MAG_BASE = 1.5
ECCENTRIC = 0.12
LEN_FLOOR = 0.25
LANES = 128
SUBLANES = 8
F32 = jnp.float32


def angle_table():
    radians = (np.arange(ANGLES) + 0.5) * (0.5 * math.pi / ANGLES) - 0.25 * math.pi
    magnify = MAG_BASE / (1.0 - ECCENTRIC * np.sin(2.0 * radians + 1.0))
    return np.cos(radians), magnify


def slab_reach(slab_count, slab_depth, row_share):
    _, magnify = angle_table()
    total_rows, total_slices = row_share * slab_count, slab_depth * slab_count
    rows = np.arange(total_rows)
    reach = 0
    for lift in range(-LIFT, LIFT + 1):
        sample = (rows[None] + 0.5 - total_rows / 2 - lift) / magnify[:, None] + total_slices / 2 - 0.5
        for tap in (np.floor(sample - 1e-3), np.floor(sample + 1e-3) + 1):
            inside = (tap >= 0) & (tap < total_slices)
            distance = np.abs(tap // slab_depth - rows[None] // row_share)
            reach = max(reach, int(distance[inside].max()))
    return reach


def lane_index():
    return lax.broadcasted_iota(jnp.int32, (SUBLANES, LANES), 1)


def sublane_index():
    return lax.broadcasted_iota(jnp.int32, (SUBLANES, LANES), 0)


def angle_facts(index):
    x = (index.astype(F32) + 0.5) * (0.5 * math.pi / ANGLES) - 0.25 * math.pi
    s = x * x
    sine = x * (1.0 + s * (-1 / 6 + s * (1 / 120 + s * (-1 / 5040 + s * (1 / 362880)))))
    cosine = 1.0 + s * (-1 / 2 + s * (1 / 24 + s * (-1 / 720 + s * (1 / 40320 + s * (-1 / 3628800)))))
    double = 2.0 * sine * cosine * math.cos(1.0) + (1.0 - 2.0 * sine * sine) * math.sin(1.0)
    return cosine, sine / cosine, (1.0 - ECCENTRIC * double) * (1.0 / MAG_BASE)


def spread_scalars(read, count, place):
    out = jnp.full((SUBLANES, LANES), read(0), jnp.int32)
    for item in range(1, count):
        out = jnp.where(place == item, read(item), out)
    return out


def pick(tile, index):
    return jnp.take_along_axis(tile, index, axis=1, mode="promise_in_bounds")


def next_lane(tile, following):
    lane = lane_index()
    return jnp.where(lane < LANES - 1, pltpu.roll(tile, LANES - 1, 1), pltpu.roll(following, LANES - 1, 1))


def rows_summed(parts):
    sub = sublane_index()
    step = SUBLANES // 2
    while step:
        low = jnp.bitwise_and(sub, step) == 0
        half = len(parts) // 2
        parts = [
            jnp.where(low, a, pltpu.roll(b, step, 0)) + jnp.where(low, pltpu.roll(a, SUBLANES - step, 0), b)
            for a, b in zip(parts[:half], parts[half:])
        ]
        step //= 2
    return parts[0]


def tile_of(ref, lead, tile):
    return ref[lead + (slice(None), slice(tile * LANES, (tile + 1) * LANES))]


def column_center(column, cosine, column_count, cell_count):
    return (column + 0.5 - column_count / 2) * (PITCH * cell_count / column_count) / cosine + (
        cell_count / 2 - 0.5
    )


def shear_steps(group, row_count, tangent):
    row = (sublane_index() + group * SUBLANES).astype(F32)
    offset = (row + 0.5 - row_count / 2) * tangent
    whole = jnp.floor(offset)
    return whole.astype(jnp.int32), offset - whole


def project_kernel(
    angle_ref, subset_ref, volume_ref, measured_ref, block_ref, cover_ref, part_sum_ref, part_up_ref, cell_ref, slope_ref
):
    slab_depth, row_count, cell_count = volume_ref.shape
    row_share, view_count, column_count = measured_ref.shape
    subset_count = subset_ref.shape[0]
    half = row_count // 2
    tiles = cell_count // LANES
    groups = row_count // SUBLANES
    lane, sub = lane_index(), sublane_index()
    zero = jnp.zeros((SUBLANES, LANES), F32)
    width = column_count // 2

    for row in range(row_share):
        for member in range(subset_count):
            view = subset_ref[member]
            for side in range(2):
                block_ref[2 * slab_depth + row, side * subset_count + member : side * subset_count + member + 1, :] = (
                    measured_ref[row, pl.ds(view, 1), side * width : (side + 1) * width]
                )

    def one_view(view, carry):
        _, tangent, _ = angle_facts(jnp.full((SUBLANES, LANES), angle_ref[view], jnp.int32))
        first_sum, first_up, last_sum, last_up, all_up = zero, zero, zero, zero, zero
        for group in range(groups):
            whole, fraction = shear_steps(group, row_count, tangent)
            near = lane + (whole + half) < LANES
            first_sum += jnp.where(near, 0.0, 1.0)
            first_up += jnp.where(near, 0.0, fraction)
            last_sum += jnp.where(near, 1.0, 0.0)
            last_up += jnp.where(near, fraction, 0.0)
            all_up += fraction
        for tile, pair in ((0, (first_sum, first_up)), (tiles, (last_sum, last_up)), (1, (zero, all_up))):
            cut = slice(tile * LANES, (tile + 1) * LANES)
            part_sum_ref[slab_depth, view, :, cut], part_up_ref[slab_depth, view, :, cut] = pair
        for depth in range(slab_depth):
            sums, ups = [zero] * (tiles + 1), [zero] * (tiles + 1)
            for group in range(groups):
                whole, fraction = shear_steps(group, row_count, tangent)
                place = lane + (whole + half)
                index = jnp.bitwise_and(place, LANES - 1)
                near = place < LANES
                before = zero
                for tile in range(tiles + 1):
                    after = zero
                    if tile < tiles:
                        cells = volume_ref[
                            depth, group * SUBLANES : (group + 1) * SUBLANES, tile * LANES : (tile + 1) * LANES
                        ]
                        after = pick(cells, index)
                    moved = jnp.where(near, before, after)
                    sums[tile] = sums[tile] + moved
                    ups[tile] = ups[tile] + fraction * moved
                    before = after
            for tile in range(tiles + 1):
                cut = slice(tile * LANES, (tile + 1) * LANES)
                part_sum_ref[depth, view, :, cut] = sums[tile]
                part_up_ref[depth, view, :, cut] = ups[tile]
        return carry

    lax.fori_loop(0, view_count, one_view, 0)

    shift = LANES - half
    for depth in range(slab_depth + 1):
        collapsed = []
        held = lambda ref, tile: rows_summed([tile_of(ref, (depth, view), tile) for view in range(view_count)])
        if depth < slab_depth:
            sums = [held(part_sum_ref, tile) for tile in range(tiles + 1)]
            ups = [held(part_up_ref, tile) for tile in range(tiles + 1)]
        else:
            sums = [held(part_sum_ref, 0)] + [zero + float(row_count)] * (tiles - 1) + [held(part_sum_ref, tiles)]
            ups = [held(part_up_ref, 0)] + [held(part_up_ref, 1)] * (tiles - 1) + [held(part_up_ref, tiles)]
        ups.append(zero)
        for tile in range(tiles + 1):
            cells = sums[tile] - ups[tile] + next_lane(ups[tile], ups[tile + 1])
            cell = lane + (tile * LANES - shift)
            if tile in (0, tiles):
                cells = jnp.where((cell >= 0) & (cell < cell_count), cells, 0.0)
            collapsed.append(cells)
        collapsed.append(zero)
        for tile in range(tiles + 1):
            cut = slice(tile * LANES, (tile + 1) * LANES)
            cell_ref[depth, :, cut] = collapsed[tile]
            slope_ref[depth, :, cut] = next_lane(collapsed[tile], collapsed[tile + 1]) - collapsed[tile]

    cosine, _, _ = angle_facts(spread_scalars(lambda v: angle_ref[v], view_count, sub))
    factor = 1.0 / (row_count * cosine)
    least = angle_table()[0].min()
    for tile in range(column_count // LANES):
        column = (lane + tile * LANES).astype(F32)
        center = column_center(column, cosine, column_count, cell_count)
        whole = jnp.floor(center)
        fraction = center - whole
        place = jnp.clip(whole.astype(jnp.int32) + shift, shift - 2, shift + cell_count)
        block, index = jnp.right_shift(place, 7), jnp.bitwise_and(place, LANES - 1)
        ends = [column_center(tile * LANES + e, c, column_count, cell_count) for e in (0, LANES - 1) for c in (1.0, least)]
        low = min(max(math.floor(min(ends) - 1e-2) + shift, shift - 2), shift + cell_count) // LANES
        high = min(max(math.floor(max(ends) + 1e-2) + shift, shift - 2), shift + cell_count) // LANES
        for depth in range(slab_depth + 1):
            cells, slope = zero, zero
            for source in range(low, high + 1):
                here = block == source
                cells = jnp.where(here, pick(tile_of(cell_ref, (depth,), source), index), cells)
                slope = jnp.where(here, pick(tile_of(slope_ref, (depth,), source), index), slope)
            profile = (cells + fraction * slope) * factor
            if depth == slab_depth:
                cover_ref[:, tile * LANES : (tile + 1) * LANES] = profile
            else:
                side, inner = divmod(tile * LANES, width)
                block_ref[depth * 2 + side, :, inner : inner + LANES] = profile


def update_kernel(
    slab_count,
    order,
    angle_ref,
    lift_ref,
    subset_ref,
    volume_ref,
    measured_ref,
    cover_ref,
    *refs,
):
    blocks = refs[: len(order)]
    residual_ref, updated_ref, profile_ref, cover_sub_ref, spread_ref, cell_ref, slope_ref, edge_ref, bend_ref = refs[
        len(order) :
    ]
    slab_depth, row_count, cell_count = volume_ref.shape
    row_share, view_count, column_count = measured_ref.shape
    subset_count = subset_ref.shape[0]
    total_rows, total_slices = row_share * slab_count, slab_depth * slab_count
    half = row_count // 2
    tiles, columns = cell_count // LANES, column_count // LANES
    width = column_count // 2
    lane, sub = lane_index(), sublane_index()
    zero = jnp.zeros((SUBLANES, LANES), F32)
    slab = lax.axis_index("slab")
    odd = lax.rem(slab, 2)
    origin = [slab + (1 - 2 * odd) * away for away in order]
    mate_block, other_block = (blocks[order.index(away)] for away in (1, -1))

    def cone(rows, lifts, flat):
        return (rows + 0.5 - total_rows / 2 - lifts) * flat + (total_slices / 2 - 0.5)

    def cone_total(sample):
        whole = jnp.floor(sample)
        fraction = sample - whole
        low = jnp.where((whole >= 0) & (whole < total_slices), 1.0 - fraction, 0.0)
        return low + jnp.where((whole >= -1) & (whole < total_slices - 1), fraction, 0.0)

    def column_of(tile, at):
        return jnp.broadcast_to(tile[:, at : at + 1], (SUBLANES, LANES))

    _, _, flat = angle_facts(spread_scalars(lambda v: angle_ref[v], view_count, sub))
    lifts = spread_scalars(lambda v: lift_ref[v], view_count, sub).astype(F32)
    source = jnp.right_shift(lane, slab_depth.bit_length() - 1) if slab_depth & (slab_depth - 1) == 0 else lane // slab_depth
    slices = spread_scalars(lambda b: origin[b], len(blocks), source) * slab_depth + (lane - source * slab_depth)
    held = (slices >= 0) & (slices < total_slices)
    slices = slices.astype(F32)
    for row in range(row_share):
        sample = cone((slab * row_share + row).astype(F32), lifts, flat)
        weights = jnp.where(held, jnp.maximum(0.0, 1.0 - jnp.abs(sample - slices)), 0.0)
        total = cone_total(sample)
        image = [zero] * columns
        for place, block in enumerate(blocks):
            for depth in range(slab_depth):
                weight = column_of(weights, place * slab_depth + depth)
                for tile in range(columns):
                    side, inner = divmod(tile * LANES, width)
                    image[tile] = image[tile] + weight * block[depth * 2 + side, :, inner : inner + LANES]
        for tile in range(columns):
            cut = slice(tile * LANES, (tile + 1) * LANES)
            length = total * cover_ref[:, cut]
            residual_ref[row, :, cut] = (measured_ref[row, :, cut] - image[tile]) / jnp.maximum(length, LEN_FLOOR)

    member_of = jnp.bitwise_and(sub, subset_count - 1)
    cosine, _, flat = angle_facts(spread_scalars(lambda k: angle_ref[subset_ref[k]], subset_count, member_of))
    lifts = spread_scalars(lambda k: lift_ref[subset_ref[k]], subset_count, member_of).astype(F32)
    factor = 1.0 / (row_count * cosine)
    for member in range(subset_count):
        view = pl.ds(subset_ref[member], 1)
        for side in range(2):
            at = slice(side * subset_count + member, side * subset_count + member + 1)
            cover_sub_ref[at, :] = cover_ref[view, side * width : (side + 1) * width]
            other = other_block[(slab_depth - 1) * 2 + side, view, :], other_block[side, view, :]
            mate = mate_block[(slab_depth - 1) * 2 + side, view, :], mate_block[side, view, :]
            profile_ref[0, at, :] = jnp.where(odd == 0, other[0], mate[0])
            for depth in range(slab_depth):
                profile_ref[1 + depth, at, :] = blocks[0][depth * 2 + side, view, :]
            profile_ref[1 + slab_depth, at, :] = jnp.where(odd == 0, mate[1], other[1])

    rows_here = row_share * len(blocks)
    source = sum(jnp.where(lane >= row_share * b, 1, 0) for b in range(1, len(blocks)))
    rows = spread_scalars(lambda b: origin[b], len(blocks), source) * row_share + (lane - source * row_share)
    real = (rows >= 0) & (rows < total_rows) & (lane < rows_here)
    sample = cone(rows.astype(F32), lifts, flat)
    total = cone_total(sample)
    weights = []
    for z in range(-1, slab_depth + 1):
        at = slab * slab_depth + z
        use = real & (at >= 0) & (at < total_slices)
        weights.append(jnp.where(use, jnp.maximum(0.0, 1.0 - jnp.abs(sample - at.astype(F32))), 0.0))
    inner_tiles = width // LANES
    spread = [[zero] * inner_tiles for _ in range(slab_depth)]
    for place in range(rows_here):
        weight = [column_of(w, place) for w in weights]
        length = column_of(total, place)
        block, row = blocks[place // row_share], place % row_share
        for tile in range(inner_tiles):
            cut = slice(tile * LANES, (tile + 1) * LANES)
            image = weight[0] * profile_ref[0, :, cut]
            for z in range(1, slab_depth + 2):
                image = image + weight[z] * profile_ref[z, :, cut]
            rest = (block[2 * slab_depth + row, :, cut] - image) / jnp.maximum(
                length * cover_sub_ref[:, cut], LEN_FLOOR
            )
            for depth in range(slab_depth):
                spread[depth][tile] = spread[depth][tile] + weight[1 + depth] * rest
    for depth in range(slab_depth):
        for tile in range(inner_tiles):
            for side in range(2):
                spread_ref[
                    depth * subset_count : (depth + 1) * subset_count,
                    side * width + tile * LANES : side * width + (tile + 1) * LANES,
                ] = spread[depth][tile][side * subset_count : (side + 1) * subset_count]

    least = angle_table()[0].min()
    spacing = PITCH * cell_count / column_count
    shifted, edges = [], []
    for tile in range(tiles + 1):
        cell = (lane + (tile * LANES - half)).astype(F32)
        inside = (cell >= 0) & (cell < cell_count)
        first = jnp.floor((cell - (cell_count / 2 + 0.5)) * cosine * (1.0 / spacing) + (column_count / 2 - 0.5 - 1e-3)) + 1.0
        ends = [
            (tile * LANES - half + e - cell_count / 2 - 0.5) * c / spacing + column_count / 2 + 0.5
            for e in (0, LANES - 1)
            for c in (1.0, least)
        ]
        value, edge = zero, zero
        for tap in range(3):
            column = first + tap
            weight = jnp.maximum(0.0, 1.0 - jnp.abs(cell - column_center(column, cosine, column_count, cell_count)))
            weight = jnp.where(inside & (column >= 0) & (column < column_count), weight, 0.0)
            place = jnp.clip(column.astype(jnp.int32), 0, column_count - 1)
            block, index = jnp.right_shift(place, 7), jnp.bitwise_and(place, LANES - 1)
            low = min(max(math.floor(min(ends) + tap - 0.6), 0), column_count - 1) // LANES
            high = min(max(math.ceil(max(ends) + tap + 0.6), 0), column_count - 1) // LANES
            found = zero
            for at in range(low, high + 1):
                found = jnp.where(block == at, pick(tile_of(spread_ref, (), at), index), found)
            value = value + weight * found
            edge = edge + weight
        shifted.append(value * factor)
        edges.append(edge * factor)
    shifted.append(zero)
    edges.append(zero)
    for tile in range(tiles + 1):
        cut = slice(tile * LANES, (tile + 1) * LANES)
        cell_ref[:, cut] = shifted[tile]
        slope_ref[:, cut] = next_lane(shifted[tile], shifted[tile + 1]) - shifted[tile]
        edge_ref[:, cut] = edges[tile]
        bend_ref[:, cut] = next_lane(edges[tile], edges[tile + 1]) - edges[tile]

    slice_total = [jnp.sum(weights[1 + depth], axis=1, keepdims=True) for depth in range(slab_depth)]
    slice_total = [
        [jnp.broadcast_to(t[k : k + 1], (SUBLANES, LANES)) for k in range(subset_count)] for t in slice_total
    ]
    tangents = [
        angle_facts(jnp.full((SUBLANES, LANES), angle_ref[subset_ref[k]], jnp.int32))[1] for k in range(subset_count)
    ]

    def one_group(group, carry):
        band = pl.ds(pl.multiple_of(group * SUBLANES, SUBLANES), SUBLANES)
        steps = []
        for member in range(subset_count):
            whole, fraction = shear_steps(group, row_count, tangents[member])
            place = lane + (half - 1 - whole)
            steps.append((jnp.bitwise_and(place, LANES - 1), place < LANES, 1.0 - fraction))

        def sheared(base_ref, bend, row, member):
            index, near, share = steps[member]
            before = None
            out = []
            for tile in range(tiles + 1):
                cut = slice(tile * LANES, (tile + 1) * LANES)
                low = pick(jnp.broadcast_to(base_ref[row : row + 1, cut], (SUBLANES, LANES)), index)
                rise = pick(jnp.broadcast_to(bend[row : row + 1, cut], (SUBLANES, LANES)), index)
                after = low + share * rise
                if tile:
                    out.append(jnp.where(near, before, after))
                before = after
            return out

        weight = [[zero] * tiles for _ in range(slab_depth)]
        for member in range(subset_count):
            line = sheared(edge_ref, bend_ref, member, member)
            for depth in range(slab_depth):
                for tile in range(tiles):
                    weight[depth][tile] = weight[depth][tile] + slice_total[depth][member] * line[tile]
        for depth in range(slab_depth):
            for tile in range(tiles):
                updated_ref[depth, band, tile * LANES : (tile + 1) * LANES] = jnp.maximum(
                    weight[depth][tile], LEN_FLOOR * subset_count / row_count
                )
        for depth in range(slab_depth):
            back = [zero] * tiles
            for member in range(subset_count):
                line = sheared(cell_ref, slope_ref, depth * subset_count + member, member)
                back = [b + a for b, a in zip(back, line)]
            for tile in range(tiles):
                cut = slice(tile * LANES, (tile + 1) * LANES)
                updated_ref[depth, band, cut] = volume_ref[depth, band, cut] + back[tile] / updated_ref[depth, band, cut]
        return carry

    lax.fori_loop(0, row_count // SUBLANES, one_group, 0)


def swapped(block):
    return lax.ppermute(block, "slab", [(i, i ^ 1) for i in range(lax.axis_size("slab"))])


def from_chip(block, distance):
    slabs = range(lax.axis_size("slab"))
    steps = [(i + 2 * distance * (1 - 2 * (i % 2)), i) for i in slabs]
    pairs = [p for p in steps if p[0] in slabs]
    idle = [i for i in slabs if i not in [p[0] for p in pairs]]
    unmet = [i for i in slabs if i not in [p[1] for p in pairs]]
    near = [i for i in idle if i ^ 1 in unmet]
    pairs += [(i, i ^ 1) for i in near]
    pairs += zip([i for i in idle if i not in near], [i for i in unmet if i ^ 1 not in near])
    return lax.ppermute(block, "slab", pairs)


def gathered(own, reach):
    received = {}
    for distance in range(1, reach // 2 + 2):
        for sign in (-1, 1):
            if 2 * distance - (sign > 0) <= reach:
                received[sign * distance] = from_chip(own, sign * distance)
    blocks = {0: own, 1: swapped(own)}
    for distance, block in received.items():
        if 2 * abs(distance) <= reach:
            blocks[2 * distance] = block
        if abs(1 - 2 * distance) <= reach:
            blocks[1 - 2 * distance] = swapped(block)
    assert sorted(blocks) == list(range(-reach, reach + 1))
    return blocks


def per_device(volume, measured, view_angle, view_lift, subset):
    slab_count = lax.axis_size("slab")
    slab_depth, row_count, cell_count = volume.shape
    row_share, view_count, column_count = measured.shape
    subset_count = subset.shape[0]
    tiles = cell_count // LANES
    reach = slab_reach(slab_count, slab_depth, row_share)
    smem, vmem = pl.BlockSpec(memory_space=pltpu.SMEM), pl.BlockSpec(memory_space=pltpu.VMEM)
    wide = (tiles + 1) * LANES
    block_shape = (2 * slab_depth + row_share, SUBLANES, column_count // 2)
    own, cover = pl.pallas_call(
        project_kernel,
        out_shape=(
            pltpu.VMEM(block_shape, F32),
            pltpu.VMEM((view_count, column_count), F32),
        ),
        in_specs=[smem, smem, vmem, vmem],
        out_specs=(vmem, vmem),
        scratch_shapes=[pltpu.VMEM((slab_depth + 1, view_count, SUBLANES, wide), F32)] * 2
        + [pltpu.VMEM((slab_depth + 1, SUBLANES, wide), F32)] * 2,
        name="project",
    )(view_angle, subset, volume, measured)
    blocks = gathered(own, reach)
    order = tuple(blocks)
    here = lambda x: pltpu.with_memory_space_constraint(x, pltpu.VMEM)
    return pl.pallas_call(
        functools.partial(update_kernel, slab_count, order),
        out_shape=(
            jax.ShapeDtypeStruct(measured.shape, F32),
            jax.ShapeDtypeStruct(volume.shape, F32),
        ),
        in_specs=[smem] * 3 + [vmem] * (3 + 1 + 2 * reach),
        out_specs=(vmem, vmem),
        scratch_shapes=[
            pltpu.VMEM((slab_depth + 2, SUBLANES, column_count // 2), F32),
            pltpu.VMEM((SUBLANES, column_count // 2), F32),
            pltpu.VMEM((SUBLANES, column_count), F32),
        ]
        + [pltpu.VMEM((SUBLANES, wide), F32)] * 4,
        name="update",
    )(view_angle, view_lift, subset, volume, measured, here(cover), *map(here, blocks.values()))


def solution(mesh):
    in_specs = (
        P(("scan", "slab"), None, None),
        P(("scan", "slab"), None, None),
        P("scan"),
        P("scan"),
        P("scan"),
    )
    out_specs = (P(("scan", "slab"), None, None), P(("scan", "slab"), None, None))
    return jax.shard_map(
        per_device, mesh=mesh, in_specs=in_specs, out_specs=out_specs, check_vma=False
    )
```

```python
import functools
import math

import jax
import jax.numpy as jnp
import numpy as np
from jax import lax
from jax.experimental import pallas as pl
from jax.experimental.pallas import tpu as pltpu
from jax.sharding import PartitionSpec as P

ANGLES = 180
LIFT = 6
PITCH = 0.9
MAG_BASE = 1.5
ECCENTRIC = 0.12
LEN_FLOOR = 0.25
LANES = 128
SUBLANES = 8
F32 = jnp.float32


def angle_table():
    radians = (np.arange(ANGLES) + 0.5) * (0.5 * math.pi / ANGLES) - 0.25 * math.pi
    magnify = MAG_BASE / (1.0 - ECCENTRIC * np.sin(2.0 * radians + 1.0))
    return np.cos(radians), magnify


def slab_reach(slab_count, slab_depth, row_share):
    _, magnify = angle_table()
    total_rows, total_slices = row_share * slab_count, slab_depth * slab_count
    rows = np.arange(total_rows)
    reach = 0
    for lift in range(-LIFT, LIFT + 1):
        sample = (rows[None] + 0.5 - total_rows / 2 - lift) / magnify[:, None] + total_slices / 2 - 0.5
        for tap in (np.floor(sample - 1e-3), np.floor(sample + 1e-3) + 1):
            inside = (tap >= 0) & (tap < total_slices)
            distance = np.abs(tap // slab_depth - rows[None] // row_share)
            reach = max(reach, int(distance[inside].max()))
    return reach


def lane_index():
    return lax.broadcasted_iota(jnp.int32, (SUBLANES, LANES), 1)


def sublane_index():
    return lax.broadcasted_iota(jnp.int32, (SUBLANES, LANES), 0)


def angle_facts(index):
    x = (index.astype(F32) + 0.5) * (0.5 * math.pi / ANGLES) - 0.25 * math.pi
    s = x * x
    sine = x * (1.0 + s * (-1 / 6 + s * (1 / 120 + s * (-1 / 5040 + s * (1 / 362880)))))
    cosine = 1.0 + s * (-1 / 2 + s * (1 / 24 + s * (-1 / 720 + s * (1 / 40320 + s * (-1 / 3628800)))))
    double = 2.0 * sine * cosine * math.cos(1.0) + (1.0 - 2.0 * sine * sine) * math.sin(1.0)
    return cosine, sine / cosine, (1.0 - ECCENTRIC * double) * (1.0 / MAG_BASE)


def spread_scalars(read, count, place):
    out = jnp.full((SUBLANES, LANES), read(0), jnp.int32)
    for item in range(1, count):
        out = jnp.where(place == item, read(item), out)
    return out


def pick(tile, index):
    return jnp.take_along_axis(tile, index, axis=1, mode="promise_in_bounds")


def next_lane(tile, following):
    lane = lane_index()
    return jnp.where(lane < LANES - 1, pltpu.roll(tile, LANES - 1, 1), pltpu.roll(following, LANES - 1, 1))


def rows_summed(parts):
    sub = sublane_index()
    step = SUBLANES // 2
    while step:
        low = jnp.bitwise_and(sub, step) == 0
        half = len(parts) // 2
        parts = [
            jnp.where(low, a, pltpu.roll(b, step, 0)) + jnp.where(low, pltpu.roll(a, SUBLANES - step, 0), b)
            for a, b in zip(parts[:half], parts[half:])
        ]
        step //= 2
    return parts[0]


def tile_of(ref, lead, tile):
    return ref[lead + (slice(None), slice(tile * LANES, (tile + 1) * LANES))]


def column_center(column, cosine, column_count, cell_count):
    return (column + 0.5 - column_count / 2) * (PITCH * cell_count / column_count) / cosine + (
        cell_count / 2 - 0.5
    )


def shear_steps(group, row_count, tangent):
    row = (sublane_index() + group * SUBLANES).astype(F32)
    offset = (row + 0.5 - row_count / 2) * tangent
    whole = jnp.floor(offset)
    return whole.astype(jnp.int32), offset - whole


def cone_sample(rows, lifts, flat, total_rows, total_slices):
    return (rows + 0.5 - total_rows / 2 - lifts) * flat + (total_slices / 2 - 0.5)


def cone_total(sample, total_slices):
    whole = jnp.floor(sample)
    fraction = sample - whole
    low = jnp.where((whole >= 0) & (whole < total_slices), 1.0 - fraction, 0.0)
    return low + jnp.where((whole >= -1) & (whole < total_slices - 1), fraction, 0.0)


def column_of(tile, at):
    return jnp.broadcast_to(tile[:, at : at + 1], (SUBLANES, LANES))


def subset_cone(slab, slab_count, order, slab_depth, row_share, flat, lifts):
    lane = lane_index()
    total_rows, total_slices = row_share * slab_count, slab_depth * slab_count
    origin = slabs_of(slab, order)
    source = sum(jnp.where(lane >= row_share * b, 1, 0) for b in range(1, len(order)))
    rows = spread_scalars(lambda b: origin[b], len(order), source) * row_share + (lane - source * row_share)
    real = (rows >= 0) & (rows < total_rows) & (lane < row_share * len(order))
    sample = cone_sample(rows.astype(F32), lifts, flat, total_rows, total_slices)
    weights = []
    for z in range(-1, slab_depth + 1):
        at = slab * slab_depth + z
        use = real & (at >= 0) & (at < total_slices)
        weights.append(jnp.where(use, jnp.maximum(0.0, 1.0 - jnp.abs(sample - at.astype(F32))), 0.0))
    return sample, weights


def slabs_of(slab, order):
    return [slab + (1 - 2 * lax.rem(slab, 2)) * away for away in order]


def adjoint_taps(tile, cosine, column_count, cell_count, half):
    spacing = PITCH * cell_count / column_count
    least = angle_table()[0].min()
    lane = lane_index()
    cell = (lane + (tile * LANES - half)).astype(F32)
    inside = (cell >= 0) & (cell < cell_count)
    first = jnp.floor((cell - (cell_count / 2 + 0.5)) * cosine * (1.0 / spacing) + (column_count / 2 - 0.5 - 1e-3)) + 1.0
    ends = [
        (tile * LANES - half + e - cell_count / 2 - 0.5) * c / spacing + column_count / 2 + 0.5
        for e in (0, LANES - 1)
        for c in (1.0, least)
    ]
    taps = []
    for tap in range(3):
        column = first + tap
        weight = jnp.maximum(0.0, 1.0 - jnp.abs(cell - column_center(column, cosine, column_count, cell_count)))
        weight = jnp.where(inside & (column >= 0) & (column < column_count), weight, 0.0)
        place = jnp.clip(column.astype(jnp.int32), 0, column_count - 1)
        low = min(max(math.floor(min(ends) + tap - 0.6), 0), column_count - 1) // LANES
        high = min(max(math.ceil(max(ends) + tap + 0.6), 0), column_count - 1) // LANES
        taps.append((place, weight, range(low, high + 1)))
    return taps


def store_line(line, base_ref, bend_ref):
    line = line + [jnp.zeros((SUBLANES, LANES), F32)]
    for tile in range(len(line) - 1):
        cut = slice(tile * LANES, (tile + 1) * LANES)
        base_ref[:, cut] = line[tile]
        bend_ref[:, cut] = next_lane(line[tile], line[tile + 1]) - line[tile]


def adjoint_steps(group, row_count, tangent):
    whole, fraction = shear_steps(group, row_count, tangent)
    place = lane_index() + (row_count // 2 - 1 - whole)
    return jnp.bitwise_and(place, LANES - 1), place < LANES, 1.0 - fraction


def sheared(base_ref, bend_ref, row, step, tiles):
    index, near, share = step
    before, out = None, []
    for tile in range(tiles + 1):
        cut = slice(tile * LANES, (tile + 1) * LANES)
        low = pick(jnp.broadcast_to(base_ref[row : row + 1, cut], (SUBLANES, LANES)), index)
        rise = pick(jnp.broadcast_to(bend_ref[row : row + 1, cut], (SUBLANES, LANES)), index)
        after = low + share * rise
        if tile:
            out.append(jnp.where(near, before, after))
        before = after
    return out


def subset_angles(angle_ref, lift_ref, subset_ref):
    members = subset_ref.shape[0]
    member = jnp.bitwise_and(sublane_index(), members - 1)
    cosine, _, flat = angle_facts(spread_scalars(lambda k: angle_ref[subset_ref[k]], members, member))
    lifts = spread_scalars(lambda k: lift_ref[subset_ref[k]], members, member).astype(F32)
    tangents = [
        angle_facts(jnp.full((SUBLANES, LANES), angle_ref[subset_ref[k]], jnp.int32))[1] for k in range(members)
    ]
    return cosine, flat, lifts, tangents


def project_kernel(
    angle_ref, subset_ref, volume_ref, measured_ref, block_ref, cover_ref, part_sum_ref, part_up_ref, cell_ref, slope_ref
):
    slab_depth, row_count, cell_count = volume_ref.shape
    row_share, view_count, column_count = measured_ref.shape
    subset_count = subset_ref.shape[0]
    half = row_count // 2
    tiles = cell_count // LANES
    groups = row_count // SUBLANES
    lane, sub = lane_index(), sublane_index()
    zero = jnp.zeros((SUBLANES, LANES), F32)
    width = column_count // 2

    for row in range(row_share):
        for member in range(subset_count):
            view = subset_ref[member]
            for side in range(2):
                block_ref[2 * slab_depth + row, side * subset_count + member : side * subset_count + member + 1, :] = (
                    measured_ref[row, pl.ds(view, 1), side * width : (side + 1) * width]
                )

    def one_view(view, carry):
        _, tangent, _ = angle_facts(jnp.full((SUBLANES, LANES), angle_ref[view], jnp.int32))
        first_sum, first_up, last_sum, last_up, all_up = zero, zero, zero, zero, zero
        for group in range(groups):
            whole, fraction = shear_steps(group, row_count, tangent)
            near = lane + (whole + half) < LANES
            first_sum += jnp.where(near, 0.0, 1.0)
            first_up += jnp.where(near, 0.0, fraction)
            last_sum += jnp.where(near, 1.0, 0.0)
            last_up += jnp.where(near, fraction, 0.0)
            all_up += fraction
        for tile, pair in ((0, (first_sum, first_up)), (tiles, (last_sum, last_up)), (1, (zero, all_up))):
            cut = slice(tile * LANES, (tile + 1) * LANES)
            part_sum_ref[slab_depth, view, :, cut], part_up_ref[slab_depth, view, :, cut] = pair
        for depth in range(slab_depth):
            sums, ups = [zero] * (tiles + 1), [zero] * (tiles + 1)
            for group in range(groups):
                whole, fraction = shear_steps(group, row_count, tangent)
                place = lane + (whole + half)
                index = jnp.bitwise_and(place, LANES - 1)
                near = place < LANES
                before = zero
                for tile in range(tiles + 1):
                    after = zero
                    if tile < tiles:
                        cells = volume_ref[
                            depth, group * SUBLANES : (group + 1) * SUBLANES, tile * LANES : (tile + 1) * LANES
                        ]
                        after = pick(cells, index)
                    moved = jnp.where(near, before, after)
                    sums[tile] = sums[tile] + moved
                    ups[tile] = ups[tile] + fraction * moved
                    before = after
            for tile in range(tiles + 1):
                cut = slice(tile * LANES, (tile + 1) * LANES)
                part_sum_ref[depth, view, :, cut] = sums[tile]
                part_up_ref[depth, view, :, cut] = ups[tile]
        return carry

    lax.fori_loop(0, view_count, one_view, 0)

    shift = LANES - half
    for depth in range(slab_depth + 1):
        collapsed = []
        held = lambda ref, tile: rows_summed([tile_of(ref, (depth, view), tile) for view in range(view_count)])
        if depth < slab_depth:
            sums = [held(part_sum_ref, tile) for tile in range(tiles + 1)]
            ups = [held(part_up_ref, tile) for tile in range(tiles + 1)]
        else:
            sums = [held(part_sum_ref, 0)] + [zero + float(row_count)] * (tiles - 1) + [held(part_sum_ref, tiles)]
            ups = [held(part_up_ref, 0)] + [held(part_up_ref, 1)] * (tiles - 1) + [held(part_up_ref, tiles)]
        ups.append(zero)
        for tile in range(tiles + 1):
            cells = sums[tile] - ups[tile] + next_lane(ups[tile], ups[tile + 1])
            cell = lane + (tile * LANES - shift)
            if tile in (0, tiles):
                cells = jnp.where((cell >= 0) & (cell < cell_count), cells, 0.0)
            collapsed.append(cells)
        collapsed.append(zero)
        for tile in range(tiles + 1):
            cut = slice(tile * LANES, (tile + 1) * LANES)
            cell_ref[depth, :, cut] = collapsed[tile]
            slope_ref[depth, :, cut] = next_lane(collapsed[tile], collapsed[tile + 1]) - collapsed[tile]

    cosine, _, _ = angle_facts(spread_scalars(lambda v: angle_ref[v], view_count, sub))
    factor = 1.0 / (row_count * cosine)
    least = angle_table()[0].min()
    for tile in range(column_count // LANES):
        column = (lane + tile * LANES).astype(F32)
        center = column_center(column, cosine, column_count, cell_count)
        whole = jnp.floor(center)
        fraction = center - whole
        place = jnp.clip(whole.astype(jnp.int32) + shift, shift - 2, shift + cell_count)
        block, index = jnp.right_shift(place, 7), jnp.bitwise_and(place, LANES - 1)
        ends = [column_center(tile * LANES + e, c, column_count, cell_count) for e in (0, LANES - 1) for c in (1.0, least)]
        low = min(max(math.floor(min(ends) - 1e-2) + shift, shift - 2), shift + cell_count) // LANES
        high = min(max(math.floor(max(ends) + 1e-2) + shift, shift - 2), shift + cell_count) // LANES
        for depth in range(slab_depth + 1):
            cells, slope = zero, zero
            for source in range(low, high + 1):
                here = block == source
                cells = jnp.where(here, pick(tile_of(cell_ref, (depth,), source), index), cells)
                slope = jnp.where(here, pick(tile_of(slope_ref, (depth,), source), index), slope)
            profile = (cells + fraction * slope) * factor
            if depth == slab_depth:
                cover_ref[:, tile * LANES : (tile + 1) * LANES] = profile
            else:
                side, inner = divmod(tile * LANES, width)
                block_ref[depth * 2 + side, :, inner : inner + LANES] = profile


def divisor_kernel(
    slab_count, order, angle_ref, lift_ref, subset_ref, cover_ref, bound_ref, own_ref, rows_ref, edge_ref, bend_ref, sub_ref
):
    slab_depth, row_count, cell_count = bound_ref.shape
    row_share, view_count, column_count = own_ref.shape
    subset_count = subset_ref.shape[0]
    total_rows, total_slices = row_share * slab_count, slab_depth * slab_count
    tiles, columns = cell_count // LANES, column_count // LANES
    width = column_count // 2
    sub = sublane_index()
    zero = jnp.zeros((SUBLANES, LANES), F32)
    slab = lax.axis_index("slab")

    _, _, flat = angle_facts(spread_scalars(lambda v: angle_ref[v], view_count, sub))
    lifts = spread_scalars(lambda v: lift_ref[v], view_count, sub).astype(F32)
    for row in range(row_share):
        sample = cone_sample((slab * row_share + row).astype(F32), lifts, flat, total_rows, total_slices)
        total = cone_total(sample, total_slices)
        for tile in range(columns):
            cut = slice(tile * LANES, (tile + 1) * LANES)
            own_ref[row, :, cut] = 1.0 / jnp.maximum(total * cover_ref[:, cut], LEN_FLOOR)

    cosine, flat, lifts, tangents = subset_angles(angle_ref, lift_ref, subset_ref)
    for member in range(subset_count):
        view = pl.ds(subset_ref[member], 1)
        for side in range(2):
            at = slice(side * subset_count + member, side * subset_count + member + 1)
            sub_ref[at, :] = cover_ref[view, side * width : (side + 1) * width]
    sample, weights = subset_cone(slab, slab_count, order, slab_depth, row_share, flat, lifts)
    total = cone_total(sample, total_slices)
    for place in range(row_share * len(order)):
        length = column_of(total, place)
        for tile in range(width // LANES):
            cut = slice(tile * LANES, (tile + 1) * LANES)
            rows_ref[place, :, cut] = 1.0 / jnp.maximum(length * sub_ref[:, cut], LEN_FLOOR)

    factor = 1.0 / (row_count * cosine)
    line = []
    for tile in range(tiles + 1):
        taps = adjoint_taps(tile, cosine, column_count, cell_count, row_count // 2)
        line.append(sum(weight for _, weight, _ in taps) * factor)
    store_line(line, edge_ref, bend_ref)
    slice_total = []
    for depth in range(slab_depth):
        t = jnp.sum(weights[1 + depth], axis=1, keepdims=True)
        slice_total.append([jnp.broadcast_to(t[k : k + 1], (SUBLANES, LANES)) for k in range(subset_count)])

    def one_group(group, carry):
        band = pl.ds(pl.multiple_of(group * SUBLANES, SUBLANES), SUBLANES)
        weight = [[zero] * tiles for _ in range(slab_depth)]
        for member in range(subset_count):
            line = sheared(edge_ref, bend_ref, member, adjoint_steps(group, row_count, tangents[member]), tiles)
            for depth in range(slab_depth):
                for tile in range(tiles):
                    weight[depth][tile] = weight[depth][tile] + slice_total[depth][member] * line[tile]
        for depth in range(slab_depth):
            for tile in range(tiles):
                bound_ref[depth, band, tile * LANES : (tile + 1) * LANES] = 1.0 / jnp.maximum(
                    weight[depth][tile], LEN_FLOOR * subset_count / row_count
                )
        return carry

    lax.fori_loop(0, row_count // SUBLANES, one_group, 0)


def update_kernel(
    slab_count,
    order,
    angle_ref,
    lift_ref,
    subset_ref,
    volume_ref,
    measured_ref,
    bound_ref,
    own_ref,
    rows_ref,
    *refs,
):
    blocks = refs[: len(order)]
    residual_ref, updated_ref, profile_ref, spread_ref, cell_ref, slope_ref = refs[len(order) :]
    slab_depth, row_count, cell_count = volume_ref.shape
    row_share, view_count, column_count = measured_ref.shape
    subset_count = subset_ref.shape[0]
    total_rows, total_slices = row_share * slab_count, slab_depth * slab_count
    tiles, columns = cell_count // LANES, column_count // LANES
    width = column_count // 2
    lane, sub = lane_index(), sublane_index()
    zero = jnp.zeros((SUBLANES, LANES), F32)
    slab = lax.axis_index("slab")
    odd = lax.rem(slab, 2)
    origin = slabs_of(slab, order)
    mate_block, other_block = (blocks[order.index(away)] for away in (1, -1))

    _, _, flat = angle_facts(spread_scalars(lambda v: angle_ref[v], view_count, sub))
    lifts = spread_scalars(lambda v: lift_ref[v], view_count, sub).astype(F32)
    source = sum(jnp.where(lane >= slab_depth * b, 1, 0) for b in range(1, len(order)))
    slices = spread_scalars(lambda b: origin[b], len(order), source) * slab_depth + (lane - source * slab_depth)
    held = (slices >= 0) & (slices < total_slices)
    slices = slices.astype(F32)
    for row in range(row_share):
        sample = cone_sample((slab * row_share + row).astype(F32), lifts, flat, total_rows, total_slices)
        weights = jnp.where(held, jnp.maximum(0.0, 1.0 - jnp.abs(sample - slices)), 0.0)
        image = [zero] * columns
        for place, block in enumerate(blocks):
            for depth in range(slab_depth):
                weight = column_of(weights, place * slab_depth + depth)
                for tile in range(columns):
                    side, inner = divmod(tile * LANES, width)
                    image[tile] = image[tile] + weight * block[depth * 2 + side, :, inner : inner + LANES]
        for tile in range(columns):
            cut = slice(tile * LANES, (tile + 1) * LANES)
            residual_ref[row, :, cut] = (measured_ref[row, :, cut] - image[tile]) * own_ref[row, :, cut]

    cosine, flat, lifts, tangents = subset_angles(angle_ref, lift_ref, subset_ref)
    factor = 1.0 / (row_count * cosine)
    for member in range(subset_count):
        view = pl.ds(subset_ref[member], 1)
        for side in range(2):
            at = slice(side * subset_count + member, side * subset_count + member + 1)
            other = other_block[(slab_depth - 1) * 2 + side, view, :], other_block[side, view, :]
            mate = mate_block[(slab_depth - 1) * 2 + side, view, :], mate_block[side, view, :]
            profile_ref[0, at, :] = jnp.where(odd == 0, other[0], mate[0])
            for depth in range(slab_depth):
                profile_ref[1 + depth, at, :] = blocks[0][depth * 2 + side, view, :]
            profile_ref[1 + slab_depth, at, :] = jnp.where(odd == 0, mate[1], other[1])

    _, weights = subset_cone(slab, slab_count, order, slab_depth, row_share, flat, lifts)
    inner_tiles = width // LANES
    spread = [[zero] * inner_tiles for _ in range(slab_depth)]
    for place in range(row_share * len(order)):
        weight = [column_of(w, place) for w in weights]
        block, row = blocks[place // row_share], place % row_share
        for tile in range(inner_tiles):
            cut = slice(tile * LANES, (tile + 1) * LANES)
            image = weight[0] * profile_ref[0, :, cut]
            for z in range(1, slab_depth + 2):
                image = image + weight[z] * profile_ref[z, :, cut]
            rest = (block[2 * slab_depth + row, :, cut] - image) * rows_ref[place, :, cut]
            for depth in range(slab_depth):
                spread[depth][tile] = spread[depth][tile] + weight[1 + depth] * rest
    for depth in range(slab_depth):
        for tile in range(inner_tiles):
            for side in range(2):
                spread_ref[
                    depth * subset_count : (depth + 1) * subset_count,
                    side * width + tile * LANES : side * width + (tile + 1) * LANES,
                ] = spread[depth][tile][side * subset_count : (side + 1) * subset_count]

    line = []
    for tile in range(tiles + 1):
        value = zero
        for place, weight, at_tiles in adjoint_taps(tile, cosine, column_count, cell_count, row_count // 2):
            block, index = jnp.right_shift(place, 7), jnp.bitwise_and(place, LANES - 1)
            found = zero
            for at in at_tiles:
                found = jnp.where(block == at, pick(tile_of(spread_ref, (), at), index), found)
            value = value + weight * found
        line.append(value * factor)
    store_line(line, cell_ref, slope_ref)

    def one_group(group, carry):
        band = pl.ds(pl.multiple_of(group * SUBLANES, SUBLANES), SUBLANES)
        steps = [adjoint_steps(group, row_count, tangent) for tangent in tangents]
        for depth in range(slab_depth):
            back = [zero] * tiles
            for member in range(subset_count):
                line = sheared(cell_ref, slope_ref, depth * subset_count + member, steps[member], tiles)
                back = [b + a for b, a in zip(back, line)]
            for tile in range(tiles):
                cut = slice(tile * LANES, (tile + 1) * LANES)
                updated_ref[depth, band, cut] = volume_ref[depth, band, cut] + back[tile] * bound_ref[depth, band, cut]
        return carry

    lax.fori_loop(0, row_count // SUBLANES, one_group, 0)


def swapped(block):
    return lax.ppermute(block, "slab", [(i, i ^ 1) for i in range(lax.axis_size("slab"))])


def from_chip(block, distance):
    slabs = range(lax.axis_size("slab"))
    steps = [(i + 2 * distance * (1 - 2 * (i % 2)), i) for i in slabs]
    pairs = [p for p in steps if p[0] in slabs]
    idle = [i for i in slabs if i not in [p[0] for p in pairs]]
    unmet = [i for i in slabs if i not in [p[1] for p in pairs]]
    near = [i for i in idle if i ^ 1 in unmet]
    pairs += [(i, i ^ 1) for i in near]
    pairs += zip([i for i in idle if i not in near], [i for i in unmet if i ^ 1 not in near])
    return lax.ppermute(block, "slab", pairs)


def fetches(reach):
    return [s * d for d in range(1, reach // 2 + 2) for s in (-1, 1) if 2 * d - (s > 0) <= reach]


def window(reach):
    order = [0, 1]
    for distance in fetches(reach):
        order += [at for at in (2 * distance, 1 - 2 * distance) if abs(at) <= reach]
    assert sorted(order) == list(range(-reach, reach + 1))
    return tuple(order)


def gathered(own, reach, meanwhile):
    received = [from_chip(own, distance) for distance in fetches(reach)]
    blocks = {0: own, 1: swapped(own)}
    done = meanwhile()
    received, done = lax.optimization_barrier((received, done))
    for distance, block in zip(fetches(reach), received):
        if 2 * abs(distance) <= reach:
            blocks[2 * distance] = block
        if abs(1 - 2 * distance) <= reach:
            blocks[1 - 2 * distance] = swapped(block)
    return [blocks[away] for away in window(reach)], done


def per_device(volume, measured, view_angle, view_lift, subset):
    slab_count = lax.axis_size("slab")
    slab_depth, row_count, cell_count = volume.shape
    row_share, view_count, column_count = measured.shape
    subset_count = subset.shape[0]
    tiles = cell_count // LANES
    reach = slab_reach(slab_count, slab_depth, row_share)
    smem, vmem = pl.BlockSpec(memory_space=pltpu.SMEM), pl.BlockSpec(memory_space=pltpu.VMEM)
    wide = (tiles + 1) * LANES
    block_shape = (2 * slab_depth + row_share, SUBLANES, column_count // 2)
    own, cover = pl.pallas_call(
        project_kernel,
        out_shape=(
            pltpu.VMEM(block_shape, F32),
            pltpu.VMEM((view_count, column_count), F32),
        ),
        in_specs=[smem, smem, vmem, vmem],
        out_specs=(vmem, vmem),
        scratch_shapes=[pltpu.VMEM((slab_depth + 1, view_count, SUBLANES, wide), F32)] * 2
        + [pltpu.VMEM((slab_depth + 1, SUBLANES, wide), F32)] * 2,
        name="project",
    )(view_angle, subset, volume, measured)
    here = lambda x: pltpu.with_memory_space_constraint(x, pltpu.VMEM)
    cover = here(cover)
    order = window(reach)
    divide = pl.pallas_call(
        functools.partial(divisor_kernel, slab_count, order),
        out_shape=(
            pltpu.VMEM(volume.shape, F32),
            pltpu.VMEM(measured.shape, F32),
            pltpu.VMEM((row_share * len(order), SUBLANES, column_count // 2), F32),
        ),
        in_specs=[smem] * 3 + [vmem],
        out_specs=(vmem,) * 3,
        scratch_shapes=[pltpu.VMEM((SUBLANES, wide), F32)] * 2 + [pltpu.VMEM((SUBLANES, column_count // 2), F32)],
        cost_estimate=pl.CostEstimate(flops=4_000_000, bytes_accessed=8_000_000, transcendentals=0),
        name="divisors",
    )
    blocks, divisors = gathered(own, reach, lambda: divide(view_angle, view_lift, subset, cover))
    return pl.pallas_call(
        functools.partial(update_kernel, slab_count, order),
        out_shape=(
            jax.ShapeDtypeStruct(measured.shape, F32),
            jax.ShapeDtypeStruct(volume.shape, F32),
        ),
        in_specs=[smem] * 3 + [vmem] * (5 + len(order)),
        out_specs=(vmem, vmem),
        scratch_shapes=[
            pltpu.VMEM((slab_depth + 2, SUBLANES, column_count // 2), F32),
            pltpu.VMEM((SUBLANES, column_count), F32),
        ]
        + [pltpu.VMEM((SUBLANES, wide), F32)] * 2,
        name="update",
    )(view_angle, view_lift, subset, volume, measured, *map(here, (*divisors, *blocks)))


def solution(mesh):
    in_specs = (
        P(("scan", "slab"), None, None),
        P(("scan", "slab"), None, None),
        P("scan"),
        P("scan"),
        P("scan"),
    )
    out_specs = (P(("scan", "slab"), None, None), P(("scan", "slab"), None, None))
    return jax.shard_map(
        per_device, mesh=mesh, in_specs=in_specs, out_specs=out_specs, check_vma=False
    )
```

```python
import functools
import math

import jax
import jax.numpy as jnp
import numpy as np
from jax import lax
from jax.experimental import pallas as pl
from jax.experimental.pallas import tpu as pltpu
from jax.sharding import PartitionSpec as P

ANGLES = 180
LIFT = 6
PITCH = 0.9
MAG_BASE = 1.5
ECCENTRIC = 0.12
LEN_FLOOR = 0.25
LANES = 128
SUBLANES = 8
F32 = jnp.float32


def angle_table():
    radians = (np.arange(ANGLES) + 0.5) * (0.5 * math.pi / ANGLES) - 0.25 * math.pi
    magnify = MAG_BASE / (1.0 - ECCENTRIC * np.sin(2.0 * radians + 1.0))
    return np.cos(radians), magnify


def slab_reach(slab_count, slab_depth, row_share):
    _, magnify = angle_table()
    total_rows, total_slices = row_share * slab_count, slab_depth * slab_count
    rows = np.arange(total_rows)
    reach = 0
    for lift in range(-LIFT, LIFT + 1):
        sample = (rows[None] + 0.5 - total_rows / 2 - lift) / magnify[:, None] + total_slices / 2 - 0.5
        for tap in (np.floor(sample - 1e-3), np.floor(sample + 1e-3) + 1):
            inside = (tap >= 0) & (tap < total_slices)
            distance = np.abs(tap // slab_depth - rows[None] // row_share)
            reach = max(reach, int(distance[inside].max()))
    return reach


def lane_index():
    return lax.broadcasted_iota(jnp.int32, (SUBLANES, LANES), 1)


def sublane_index():
    return lax.broadcasted_iota(jnp.int32, (SUBLANES, LANES), 0)


def angle_facts(index):
    x = (index.astype(F32) + 0.5) * (0.5 * math.pi / ANGLES) - 0.25 * math.pi
    s = x * x
    sine = x * (1.0 + s * (-1 / 6 + s * (1 / 120 + s * (-1 / 5040 + s * (1 / 362880)))))
    cosine = 1.0 + s * (-1 / 2 + s * (1 / 24 + s * (-1 / 720 + s * (1 / 40320 + s * (-1 / 3628800)))))
    double = 2.0 * sine * cosine * math.cos(1.0) + (1.0 - 2.0 * sine * sine) * math.sin(1.0)
    return cosine, sine / cosine, (1.0 - ECCENTRIC * double) * (1.0 / MAG_BASE)


def spread_scalars(read, count, place):
    out = jnp.full((SUBLANES, LANES), read(0), jnp.int32)
    for item in range(1, count):
        out = jnp.where(place == item, read(item), out)
    return out


def pick(tile, index):
    numbers = lax.GatherDimensionNumbers(
        offset_dims=(),
        collapsed_slice_dims=(1,),
        start_index_map=(1,),
        operand_batching_dims=(0,),
        start_indices_batching_dims=(0,),
    )
    return lax.gather(tile, index[..., None], numbers, (1, 1), mode=lax.GatherScatterMode.PROMISE_IN_BOUNDS)


def next_lane(tile, following):
    lane = lane_index()
    return jnp.where(lane < LANES - 1, pltpu.roll(tile, LANES - 1, 1), pltpu.roll(following, LANES - 1, 1))


def rows_summed(parts):
    sub = sublane_index()
    step = 1
    while step < SUBLANES:
        low = jnp.bitwise_and(sub, step) == 0
        parts = [
            jnp.where(low, a, b) + pltpu.roll(jnp.where(low, b, a), step, 0) for a, b in zip(parts[::2], parts[1::2])
        ]
        step *= 2
    return parts[0]


def tile_of(ref, lead, tile):
    whole = (slice(None),) * (len(ref.shape) - 1 - len(lead))
    return ref[lead + whole + (slice(tile * LANES, (tile + 1) * LANES),)]


def column_center(column, cosine, column_count, cell_count):
    return (column + 0.5 - column_count / 2) * (PITCH * cell_count / column_count) / cosine + (
        cell_count / 2 - 0.5
    )


def shear_steps(group, row_count, tangent):
    row = (sublane_index() + group * SUBLANES).astype(F32)
    offset = (row + 0.5 - row_count / 2) * tangent
    whole = jnp.floor(offset)
    return whole.astype(jnp.int32), offset - whole


def cone_sample(rows, lifts, flat, total_rows, total_slices):
    return (rows + 0.5 - total_rows / 2 - lifts) * flat + (total_slices / 2 - 0.5)


def cone_total(sample, total_slices):
    whole = jnp.floor(sample)
    fraction = sample - whole
    low = jnp.where((whole >= 0) & (whole < total_slices), 1.0 - fraction, 0.0)
    return low + jnp.where((whole >= -1) & (whole < total_slices - 1), fraction, 0.0)


def column_of(tile, at):
    return jnp.broadcast_to(tile[:, at : at + 1], (SUBLANES, LANES))


def subset_cone(slab, slab_count, order, slab_depth, row_share, flat, lifts):
    lane = lane_index()
    total_rows, total_slices = row_share * slab_count, slab_depth * slab_count
    origin = slabs_of(slab, order)
    source = sum(jnp.where(lane >= row_share * b, 1, 0) for b in range(1, len(order)))
    rows = spread_scalars(lambda b: origin[b], len(order), source) * row_share + (lane - source * row_share)
    real = (rows >= 0) & (rows < total_rows) & (lane < row_share * len(order))
    sample = cone_sample(rows.astype(F32), lifts, flat, total_rows, total_slices)
    weights = []
    for z in range(-1, slab_depth + 1):
        at = slab * slab_depth + z
        use = real & (at >= 0) & (at < total_slices)
        weights.append(jnp.where(use, jnp.maximum(0.0, 1.0 - jnp.abs(sample - at.astype(F32))), 0.0))
    return sample, weights


def slabs_of(slab, order):
    return [slab + (1 - 2 * lax.rem(slab, 2)) * away for away in order]


def adjoint_taps(tile, cosine, column_count, cell_count, half):
    spacing = PITCH * cell_count / column_count
    cell = (lane_index() + (tile * LANES - half)).astype(F32)
    inside = (cell >= 0) & (cell < cell_count)
    first = jnp.floor((cell - (cell_count / 2 + 0.5)) * cosine * (1.0 / spacing) + (column_count / 2 - 0.5 - 1e-3)) + 1.0
    taps = []
    for tap in range(3):
        column = first + tap
        weight = jnp.maximum(0.0, 1.0 - jnp.abs(cell - column_center(column, cosine, column_count, cell_count)))
        weight = jnp.where(inside & (column >= 0) & (column < column_count), weight, 0.0)
        taps.append((jnp.clip(column.astype(jnp.int32), 0, column_count - 1), weight))
    return taps


def adjoint_tiles(tile, tap, column_count, cell_count, half):
    spacing = PITCH * cell_count / column_count
    least = angle_table()[0].min()
    ends = [
        (tile * LANES - half + e - cell_count / 2 - 0.5) * c / spacing + column_count / 2 + 0.5
        for e in (0, LANES - 1)
        for c in (1.0, least)
    ]
    low = min(max(math.floor(min(ends) + tap - 0.6), 0), column_count - 1) // LANES
    high = min(max(math.ceil(max(ends) + tap + 0.6), 0), column_count - 1) // LANES
    return range(low, high + 1)


def store_line(line, base_ref, bend_ref):
    line = line + [jnp.zeros((SUBLANES, LANES), F32)]
    for tile in range(len(line) - 1):
        cut = slice(tile * LANES, (tile + 1) * LANES)
        base_ref[:, cut] = line[tile]
        bend_ref[:, cut] = next_lane(line[tile], line[tile + 1]) - line[tile]


def adjoint_steps(group, row_count, tangent):
    whole, fraction = shear_steps(group, row_count, tangent)
    place = lane_index() + (row_count // 2 - 1 - whole)
    return jnp.bitwise_and(place, LANES - 1), place < LANES, 1.0 - fraction


def sheared(base_ref, bend_ref, row, step, tiles):
    index, near, share = step
    before, out = None, []
    for tile in range(tiles + 1):
        cut = slice(tile * LANES, (tile + 1) * LANES)
        low = jnp.broadcast_to(base_ref[row : row + 1, cut], (SUBLANES, LANES))
        rise = jnp.broadcast_to(bend_ref[row : row + 1, cut], (SUBLANES, LANES))
        after = pick(low + share * rise, index)
        if tile:
            out.append(jnp.where(near, before, after))
        before = after
    return out


def subset_angles(angle_ref, lift_ref, subset_ref):
    members = subset_ref.shape[0]
    member = jnp.bitwise_and(sublane_index(), members - 1)
    cosine, _, flat = angle_facts(spread_scalars(lambda k: angle_ref[subset_ref[k]], members, member))
    lifts = spread_scalars(lambda k: lift_ref[subset_ref[k]], members, member).astype(F32)
    return cosine, flat, lifts


def member_tangents(angle_ref, subset_ref):
    indices = [angle_ref[subset_ref[k]] for k in range(subset_ref.shape[0])]
    return [angle_facts(jnp.full((SUBLANES, LANES), i, jnp.int32))[1] for i in indices]


def project_kernel(
    angle_ref,
    subset_ref,
    volume_ref,
    measured_ref,
    block_ref,
    cover_ref,
    rise_ref,
    first_ref,
    part_ref,
    end_ref,
    cell_ref,
    slope_ref,
):
    slab_depth, row_count, cell_count = volume_ref.shape
    row_share, view_count, column_count = measured_ref.shape
    subset_count = subset_ref.shape[0]
    half = row_count // 2
    tiles = cell_count // LANES
    groups = row_count // SUBLANES
    lane, sub = lane_index(), sublane_index()
    zero = jnp.zeros((SUBLANES, LANES), F32)
    width = column_count // 2

    for row in range(row_share):
        for member in range(subset_count):
            view = subset_ref[member]
            for side in range(2):
                block_ref[2 * slab_depth + row, side * subset_count + member : side * subset_count + member + 1, :] = (
                    measured_ref[row, pl.ds(view, 1), side * width : (side + 1) * width]
                )

    for depth in range(slab_depth):
        for group in range(groups):
            band = slice(group * SUBLANES, (group + 1) * SUBLANES)
            cells = [tile_of(volume_ref, (depth, band), tile) for tile in range(tiles)] + [zero]
            for tile in range(tiles):
                rise_ref[depth, band, tile * LANES : (tile + 1) * LANES] = (
                    next_lane(cells[tile], cells[tile + 1]) - cells[tile]
                )
            first_ref[depth, band, :] = column_of(cells[0], 0)

    def one_view(view, carry):
        _, tangent, _ = angle_facts(jnp.full((SUBLANES, LANES), angle_ref[view], jnp.int32))
        low_end, high_end = zero, zero
        sums = [[zero] * (tiles + 1) for _ in range(slab_depth)]
        for group in range(groups):
            band = slice(group * SUBLANES, (group + 1) * SUBLANES)
            whole, fraction = shear_steps(group, row_count, tangent)
            place = lane + (whole + half)
            index = jnp.bitwise_and(place, LANES - 1)
            near, last = place < LANES, index == LANES - 1
            enter = jnp.where(last, fraction, 0.0)
            low_end = low_end + jnp.where(near, enter, 1.0)
            high_end = high_end + jnp.where(near, 1.0 - enter, 0.0)
            for depth in range(slab_depth):
                before = enter * first_ref[depth, band, :]
                for tile in range(tiles + 1):
                    after = zero
                    if tile < tiles:
                        at = (depth, band)
                        after = pick(tile_of(volume_ref, at, tile) + fraction * tile_of(rise_ref, at, tile), index)
                    sums[depth][tile] = sums[depth][tile] + jnp.where(near, before, after)
                    before = after
        end_ref[0, view, :, :] = low_end
        end_ref[1, view, :, :] = high_end
        for depth in range(slab_depth):
            for tile in range(tiles + 1):
                part_ref[depth, view, :, tile * LANES : (tile + 1) * LANES] = sums[depth][tile]
        return carry

    lax.fori_loop(0, view_count, one_view, 0, unroll=4)

    shift = LANES - half
    inside = [None] * (tiles + 1)
    inside[0], inside[tiles] = lane >= shift, lane < shift

    def store(at, line):
        line = [jnp.where(mask, cells, 0.0) if mask is not None else cells for cells, mask in zip(line, inside)] + [zero]
        for tile in range(tiles + 1):
            cut = slice(tile * LANES, (tile + 1) * LANES)
            cell_ref[at, :, cut] = line[tile]
            slope_ref[at, :, cut] = next_lane(line[tile], line[tile + 1]) - line[tile]

    views = range(view_count)
    for depth in range(slab_depth):
        store(depth, [rows_summed([tile_of(part_ref, (depth, v), t) for v in views]) for t in range(tiles + 1)])
    flat = zero + float(row_count)
    ends = [rows_summed([end_ref[e, v, :, :] for v in views]) for e in range(2)]
    store(slab_depth, [ends[0]] + [flat] * (tiles - 1) + [ends[1]])

    cosine, _, _ = angle_facts(spread_scalars(lambda v: angle_ref[v], view_count, sub))
    factor = 1.0 / (row_count * cosine)
    least = angle_table()[0].min()
    for tile in range(column_count // LANES):
        column = (lane + tile * LANES).astype(F32)
        center = column_center(column, cosine, column_count, cell_count)
        whole = jnp.floor(center)
        fraction = center - whole
        place = jnp.clip(whole.astype(jnp.int32) + shift, shift - 2, shift + cell_count)
        block, index = jnp.right_shift(place, 7), jnp.bitwise_and(place, LANES - 1)
        ends = [column_center(tile * LANES + e, c, column_count, cell_count) for e in (0, LANES - 1) for c in (1.0, least)]
        low = min(max(math.floor(min(ends) - 1e-2) + shift, shift - 2), shift + cell_count) // LANES
        high = min(max(math.floor(max(ends) + 1e-2) + shift, shift - 2), shift + cell_count) // LANES
        cells, slopes = [zero] * slab_depth + [flat], [zero] * (slab_depth + 1)
        for source in range(low, high + 1):
            here = block == source
            for at in range(slab_depth + 1):
                if at == slab_depth and source not in (0, tiles):
                    continue
                cells[at] = jnp.where(here, pick(tile_of(cell_ref, (at,), source), index), cells[at])
                slopes[at] = jnp.where(here, pick(tile_of(slope_ref, (at,), source), index), slopes[at])
        profiles = [(c + fraction * s) * factor for c, s in zip(cells, slopes)]
        side, inner = divmod(tile * LANES, width)
        for depth in range(slab_depth):
            block_ref[depth * 2 + side, :, inner : inner + LANES] = profiles[depth]
        cover_ref[:, tile * LANES : (tile + 1) * LANES] = profiles[slab_depth]


def divisor_kernel(
    slab_count,
    order,
    angle_ref,
    lift_ref,
    subset_ref,
    cover_ref,
    bound_ref,
    own_ref,
    rows_ref,
    own_cone_ref,
    cone_ref,
    place_ref,
    tap_ref,
    edge_ref,
    bend_ref,
    sub_ref,
):
    slab_depth, row_count, cell_count = bound_ref.shape
    row_share, view_count, column_count = own_ref.shape
    subset_count = subset_ref.shape[0]
    total_rows, total_slices = row_share * slab_count, slab_depth * slab_count
    tiles, columns = cell_count // LANES, column_count // LANES
    width = column_count // 2
    sub = sublane_index()
    zero = jnp.zeros((SUBLANES, LANES), F32)
    slab = lax.axis_index("slab")

    _, _, flat = angle_facts(spread_scalars(lambda v: angle_ref[v], view_count, sub))
    lifts = spread_scalars(lambda v: lift_ref[v], view_count, sub).astype(F32)
    lane = lane_index()
    origin = slabs_of(slab, order)
    source = sum(jnp.where(lane >= slab_depth * b, 1, 0) for b in range(1, len(order)))
    slices = spread_scalars(lambda b: origin[b], len(order), source) * slab_depth + (lane - source * slab_depth)
    held = (slices >= 0) & (slices < total_slices)
    slices = slices.astype(F32)
    for row in range(row_share):
        sample = cone_sample((slab * row_share + row).astype(F32), lifts, flat, total_rows, total_slices)
        weights = jnp.where(held, jnp.maximum(0.0, 1.0 - jnp.abs(sample - slices)), 0.0)
        for place in range(slab_depth * len(order)):
            own_cone_ref[place, row, :, :] = column_of(weights, place)
        total = cone_total(sample, total_slices)
        for tile in range(columns):
            cut = slice(tile * LANES, (tile + 1) * LANES)
            own_ref[row, :, cut] = 1.0 / jnp.maximum(total * cover_ref[:, cut], LEN_FLOOR)

    cosine, flat, lifts = subset_angles(angle_ref, lift_ref, subset_ref)
    tangents = member_tangents(angle_ref, subset_ref)
    for member in range(subset_count):
        view = pl.ds(subset_ref[member], 1)
        for side in range(2):
            at = slice(side * subset_count + member, side * subset_count + member + 1)
            sub_ref[at, :] = cover_ref[view, side * width : (side + 1) * width]
    sample, weights = subset_cone(slab, slab_count, order, slab_depth, row_share, flat, lifts)
    total = cone_total(sample, total_slices)
    for place in range(row_share * len(order)):
        for z, w in enumerate(weights):
            cone_ref[place, z, :, :] = column_of(w, place)
        length = column_of(total, place)
        for tile in range(width // LANES):
            cut = slice(tile * LANES, (tile + 1) * LANES)
            rows_ref[place, :, cut] = 1.0 / jnp.maximum(length * sub_ref[:, cut], LEN_FLOOR)

    factor = 1.0 / (row_count * cosine)
    line = []
    for tile in range(tiles + 1):
        taps = adjoint_taps(tile, cosine, column_count, cell_count, row_count // 2)
        for tap, (place, weight) in enumerate(taps):
            place_ref[tile, tap, :, :] = place
            tap_ref[tile, tap, :, :] = weight * factor
        line.append(sum(weight for _, weight in taps) * factor)
    store_line(line, edge_ref, bend_ref)
    slice_total = []
    for depth in range(slab_depth):
        t = jnp.sum(weights[1 + depth], axis=1, keepdims=True)
        slice_total.append([jnp.broadcast_to(t[k : k + 1], (SUBLANES, LANES)) for k in range(subset_count)])

    def one_group(group, carry):
        band = pl.ds(pl.multiple_of(group * SUBLANES, SUBLANES), SUBLANES)
        weight = [[zero] * tiles for _ in range(slab_depth)]
        for member in range(subset_count):
            line = sheared(edge_ref, bend_ref, member, adjoint_steps(group, row_count, tangents[member]), tiles)
            for depth in range(slab_depth):
                for tile in range(tiles):
                    weight[depth][tile] = weight[depth][tile] + slice_total[depth][member] * line[tile]
        for depth in range(slab_depth):
            for tile in range(tiles):
                bound_ref[depth, band, tile * LANES : (tile + 1) * LANES] = 1.0 / jnp.maximum(
                    weight[depth][tile], LEN_FLOOR * subset_count / row_count
                )
        return carry

    lax.fori_loop(0, row_count // SUBLANES, one_group, 0)


def update_kernel(
    order,
    angle_ref,
    subset_ref,
    volume_ref,
    measured_ref,
    bound_ref,
    own_ref,
    rows_ref,
    own_cone_ref,
    cone_ref,
    place_ref,
    tap_ref,
    *refs,
):
    blocks = refs[: len(order)]
    residual_ref, updated_ref, profile_ref, spread_ref, cell_ref, slope_ref = refs[len(order) :]
    slab_depth, row_count, cell_count = volume_ref.shape
    row_share, view_count, column_count = measured_ref.shape
    subset_count = subset_ref.shape[0]
    tiles, columns = cell_count // LANES, column_count // LANES
    width = column_count // 2
    zero = jnp.zeros((SUBLANES, LANES), F32)
    odd = lax.rem(lax.axis_index("slab"), 2)
    mate_block, other_block = (blocks[order.index(away)] for away in (1, -1))

    for tile in range(columns):
        side, inner = divmod(tile * LANES, width)
        image = [zero] * row_share
        for place, block in enumerate(blocks):
            for depth in range(slab_depth):
                cells = block[depth * 2 + side, :, inner : inner + LANES]
                for row in range(row_share):
                    image[row] = image[row] + own_cone_ref[place * slab_depth + depth, row, :, :] * cells
        cut = slice(tile * LANES, (tile + 1) * LANES)
        for row in range(row_share):
            residual_ref[row, :, cut] = (measured_ref[row, :, cut] - image[row]) * own_ref[row, :, cut]

    for member in range(subset_count):
        view = pl.ds(subset_ref[member], 1)
        for side in range(2):
            at = slice(side * subset_count + member, side * subset_count + member + 1)
            other = other_block[(slab_depth - 1) * 2 + side, view, :], other_block[side, view, :]
            mate = mate_block[(slab_depth - 1) * 2 + side, view, :], mate_block[side, view, :]
            profile_ref[0, at, :] = jnp.where(odd == 0, other[0], mate[0])
            for depth in range(slab_depth):
                profile_ref[1 + depth, at, :] = blocks[0][depth * 2 + side, view, :]
            profile_ref[1 + slab_depth, at, :] = jnp.where(odd == 0, mate[1], other[1])

    inner_tiles = width // LANES
    spread = [[zero] * inner_tiles for _ in range(slab_depth)]
    for place in range(row_share * len(order)):
        weight = [cone_ref[place, z, :, :] for z in range(slab_depth + 2)]
        block, row = blocks[place // row_share], place % row_share
        for tile in range(inner_tiles):
            cut = slice(tile * LANES, (tile + 1) * LANES)
            image = weight[0] * profile_ref[0, :, cut]
            for z in range(1, slab_depth + 2):
                image = image + weight[z] * profile_ref[z, :, cut]
            rest = (block[2 * slab_depth + row, :, cut] - image) * rows_ref[place, :, cut]
            for depth in range(slab_depth):
                spread[depth][tile] = spread[depth][tile] + weight[1 + depth] * rest
    for depth in range(slab_depth):
        for tile in range(inner_tiles):
            for side in range(2):
                spread_ref[
                    depth * subset_count : (depth + 1) * subset_count,
                    side * width + tile * LANES : side * width + (tile + 1) * LANES,
                ] = spread[depth][tile][side * subset_count : (side + 1) * subset_count]

    line = []
    for tile in range(tiles + 1):
        value = zero
        for tap in range(3):
            place = place_ref[tile, tap, :, :]
            block, index = jnp.right_shift(place, 7), jnp.bitwise_and(place, LANES - 1)
            found = zero
            for at in adjoint_tiles(tile, tap, column_count, cell_count, row_count // 2):
                found = jnp.where(block == at, pick(tile_of(spread_ref, (), at), index), found)
            value = value + tap_ref[tile, tap, :, :] * found
        line.append(value)
    store_line(line, cell_ref, slope_ref)

    tangents = member_tangents(angle_ref, subset_ref)

    def one_group(group, carry):
        band = pl.ds(pl.multiple_of(group * SUBLANES, SUBLANES), SUBLANES)
        back = [[zero] * tiles for _ in range(slab_depth)]
        for member in range(subset_count):
            step = adjoint_steps(group, row_count, tangents[member])
            for depth in range(slab_depth):
                line = sheared(cell_ref, slope_ref, depth * subset_count + member, step, tiles)
                back[depth] = [b + a for b, a in zip(back[depth], line)]
        for depth in range(slab_depth):
            for tile in range(tiles):
                cut = slice(tile * LANES, (tile + 1) * LANES)
                updated_ref[depth, band, cut] = (
                    volume_ref[depth, band, cut] + back[depth][tile] * bound_ref[depth, band, cut]
                )
        return carry

    lax.fori_loop(0, row_count // SUBLANES, one_group, 0, unroll=2)


def swapped(block):
    return lax.ppermute(block, "slab", [(i, i ^ 1) for i in range(lax.axis_size("slab"))])


def from_chip(block, distance):
    slabs = range(lax.axis_size("slab"))
    steps = [(i + 2 * distance * (1 - 2 * (i % 2)), i) for i in slabs]
    pairs = [p for p in steps if p[0] in slabs]
    idle = [i for i in slabs if i not in [p[0] for p in pairs]]
    unmet = [i for i in slabs if i not in [p[1] for p in pairs]]
    near = [i for i in idle if i ^ 1 in unmet]
    pairs += [(i, i ^ 1) for i in near]
    pairs += zip([i for i in idle if i not in near], [i for i in unmet if i ^ 1 not in near])
    return lax.ppermute(block, "slab", pairs)


def fetches(reach):
    return [s * d for d in range(1, reach // 2 + 2) for s in (-1, 1) if 2 * d - (s > 0) <= reach]


def window(reach):
    order = [0, 1]
    for distance in fetches(reach):
        order += [at for at in (2 * distance, 1 - 2 * distance) if abs(at) <= reach]
    assert sorted(order) == list(range(-reach, reach + 1))
    return tuple(order)


def gathered(own, reach, meanwhile):
    received = [from_chip(own, distance) for distance in fetches(reach)]
    blocks = {0: own, 1: swapped(own)}
    done = meanwhile()
    received, done = lax.optimization_barrier((received, done))
    for distance, block in zip(fetches(reach), received):
        if 2 * abs(distance) <= reach:
            blocks[2 * distance] = block
        if abs(1 - 2 * distance) <= reach:
            blocks[1 - 2 * distance] = swapped(block)
    return [blocks[away] for away in window(reach)], done


def per_device(volume, measured, view_angle, view_lift, subset):
    slab_count = lax.axis_size("slab")
    slab_depth, row_count, cell_count = volume.shape
    row_share, view_count, column_count = measured.shape
    subset_count = subset.shape[0]
    tiles = cell_count // LANES
    reach = slab_reach(slab_count, slab_depth, row_share)
    smem, vmem = pl.BlockSpec(memory_space=pltpu.SMEM), pl.BlockSpec(memory_space=pltpu.VMEM)
    wide = (tiles + 1) * LANES
    block_shape = (2 * slab_depth + row_share, SUBLANES, column_count // 2)
    own, cover = pl.pallas_call(
        project_kernel,
        out_shape=(
            pltpu.VMEM(block_shape, F32),
            pltpu.VMEM((view_count, column_count), F32),
        ),
        in_specs=[smem, smem, vmem, vmem],
        out_specs=(vmem, vmem),
        scratch_shapes=[
            pltpu.VMEM(volume.shape, F32),
            pltpu.VMEM((slab_depth, row_count, LANES), F32),
            pltpu.VMEM((slab_depth, view_count, SUBLANES, wide), F32),
            pltpu.VMEM((2, view_count, SUBLANES, LANES), F32),
        ]
        + [pltpu.VMEM((slab_depth + 1, SUBLANES, wide), F32)] * 2,
        name="project",
    )(view_angle, subset, volume, measured)
    here = lambda x: pltpu.with_memory_space_constraint(x, pltpu.VMEM)
    cover = here(cover)
    order = window(reach)
    divide = pl.pallas_call(
        functools.partial(divisor_kernel, slab_count, order),
        out_shape=(
            pltpu.VMEM(volume.shape, F32),
            pltpu.VMEM(measured.shape, F32),
            pltpu.VMEM((row_share * len(order), SUBLANES, column_count // 2), F32),
            pltpu.VMEM((slab_depth * len(order), row_share, SUBLANES, LANES), F32),
            pltpu.VMEM((row_share * len(order), slab_depth + 2, SUBLANES, LANES), F32),
            pltpu.VMEM((tiles + 1, 3, SUBLANES, LANES), jnp.int32),
            pltpu.VMEM((tiles + 1, 3, SUBLANES, LANES), F32),
        ),
        in_specs=[smem] * 3 + [vmem],
        out_specs=(vmem,) * 7,
        scratch_shapes=[pltpu.VMEM((SUBLANES, wide), F32)] * 2 + [pltpu.VMEM((SUBLANES, column_count // 2), F32)],
        cost_estimate=pl.CostEstimate(flops=4_000_000, bytes_accessed=8_000_000, transcendentals=0),
        name="divisors",
    )
    blocks, divisors = gathered(own, reach, lambda: divide(view_angle, view_lift, subset, cover))
    return pl.pallas_call(
        functools.partial(update_kernel, order),
        out_shape=(
            jax.ShapeDtypeStruct(measured.shape, F32),
            jax.ShapeDtypeStruct(volume.shape, F32),
        ),
        in_specs=[smem] * 2 + [vmem] * (2 + len(divisors) + len(order)),
        out_specs=(vmem, vmem),
        scratch_shapes=[
            pltpu.VMEM((slab_depth + 2, SUBLANES, column_count // 2), F32),
            pltpu.VMEM((SUBLANES, column_count), F32),
        ]
        + [pltpu.VMEM((SUBLANES, wide), F32)] * 2,
        name="update",
    )(view_angle, subset, *map(here, (volume, measured, *divisors, *blocks)))


def solution(mesh):
    in_specs = (
        P(("scan", "slab"), None, None),
        P(("scan", "slab"), None, None),
        P("scan"),
        P("scan"),
        P("scan"),
    )
    out_specs = (P(("scan", "slab"), None, None), P(("scan", "slab"), None, None))
    return jax.shard_map(
        per_device, mesh=mesh, in_specs=in_specs, out_specs=out_specs, check_vma=False
    )
```

```python
import functools
import math

import jax
import jax.numpy as jnp
import numpy as np
from jax import lax
from jax.experimental import pallas as pl
from jax.experimental.pallas import tpu as pltpu
from jax.sharding import PartitionSpec as P

ANGLES = 180
LIFT = 6
PITCH = 0.9
MAG_BASE = 1.5
ECCENTRIC = 0.12
LEN_FLOOR = 0.25
LANES = 128
SUBLANES = 8
F32 = jnp.float32
VMEM_LIMIT = 8 * 1024 * 1024


def angle_table():
    radians = (np.arange(ANGLES) + 0.5) * (0.5 * math.pi / ANGLES) - 0.25 * math.pi
    magnify = MAG_BASE / (1.0 - ECCENTRIC * np.sin(2.0 * radians + 1.0))
    return np.cos(radians), magnify


def slab_reach(slab_count, slab_depth, row_share):
    _, magnify = angle_table()
    total_rows, total_slices = row_share * slab_count, slab_depth * slab_count
    rows = np.arange(total_rows)
    reach = 0
    for lift in range(-LIFT, LIFT + 1):
        sample = (rows[None] + 0.5 - total_rows / 2 - lift) / magnify[:, None] + total_slices / 2 - 0.5
        for tap in (np.floor(sample - 1e-3), np.floor(sample + 1e-3) + 1):
            inside = (tap >= 0) & (tap < total_slices)
            distance = np.abs(tap // slab_depth - rows[None] // row_share)
            reach = max(reach, int(distance[inside].max()))
    return reach


def lane_index():
    return lax.broadcasted_iota(jnp.int32, (SUBLANES, LANES), 1)


def sublane_index():
    return lax.broadcasted_iota(jnp.int32, (SUBLANES, LANES), 0)


def angle_facts(index):
    x = (index.astype(F32) + 0.5) * (0.5 * math.pi / ANGLES) - 0.25 * math.pi
    s = x * x
    sine = x * (1.0 + s * (-1 / 6 + s * (1 / 120 + s * (-1 / 5040 + s * (1 / 362880)))))
    cosine = 1.0 + s * (-1 / 2 + s * (1 / 24 + s * (-1 / 720 + s * (1 / 40320 + s * (-1 / 3628800)))))
    double = 2.0 * sine * cosine * math.cos(1.0) + (1.0 - 2.0 * sine * sine) * math.sin(1.0)
    return cosine, sine / cosine, (1.0 - ECCENTRIC * double) * (1.0 / MAG_BASE)


def spread_scalars(read, count, place):
    out = jnp.full((SUBLANES, LANES), read(0), jnp.int32)
    for item in range(1, count):
        out = jnp.where(place == item, read(item), out)
    return out


def pick(tile, index):
    numbers = lax.GatherDimensionNumbers(
        offset_dims=(),
        collapsed_slice_dims=(1,),
        start_index_map=(1,),
        operand_batching_dims=(0,),
        start_indices_batching_dims=(0,),
    )
    return lax.gather(tile, index[..., None], numbers, (1, 1), mode=lax.GatherScatterMode.PROMISE_IN_BOUNDS)


def next_lane(tile, following):
    lane = lane_index()
    return jnp.where(lane < LANES - 1, pltpu.roll(tile, LANES - 1, 1), pltpu.roll(following, LANES - 1, 1))


def rows_summed(parts):
    sub = sublane_index()
    step = 1
    while step < SUBLANES:
        low = jnp.bitwise_and(sub, step) == 0
        parts = [
            jnp.where(low, a, b) + pltpu.roll(jnp.where(low, b, a), step, 0) for a, b in zip(parts[::2], parts[1::2])
        ]
        step *= 2
    return parts[0]


def tile_of(ref, lead, tile):
    whole = (slice(None),) * (len(ref.shape) - 1 - len(lead))
    return ref[lead + whole + (slice(tile * LANES, (tile + 1) * LANES),)]


def column_center(column, cosine, column_count, cell_count):
    return (column + 0.5 - column_count / 2) * (PITCH * cell_count / column_count) / cosine + (
        cell_count / 2 - 0.5
    )


def shear_steps(group, row_count, tangent):
    row = (sublane_index() + group * SUBLANES).astype(F32)
    offset = (row + 0.5 - row_count / 2) * tangent
    whole = jnp.floor(offset)
    return whole.astype(jnp.int32), offset - whole


def cone_sample(rows, lifts, flat, total_rows, total_slices):
    return (rows + 0.5 - total_rows / 2 - lifts) * flat + (total_slices / 2 - 0.5)


def cone_total(sample, total_slices):
    whole = jnp.floor(sample)
    fraction = sample - whole
    low = jnp.where((whole >= 0) & (whole < total_slices), 1.0 - fraction, 0.0)
    return low + jnp.where((whole >= -1) & (whole < total_slices - 1), fraction, 0.0)


def column_of(tile, at):
    return jnp.broadcast_to(tile[:, at : at + 1], (SUBLANES, LANES))


def subset_cone(slab, slab_count, order, slab_depth, row_share, flat, lifts):
    lane = lane_index()
    total_rows, total_slices = row_share * slab_count, slab_depth * slab_count
    origin = slabs_of(slab, order)
    source = sum(jnp.where(lane >= row_share * b, 1, 0) for b in range(1, len(order)))
    rows = spread_scalars(lambda b: origin[b], len(order), source) * row_share + (lane - source * row_share)
    real = (rows >= 0) & (rows < total_rows) & (lane < row_share * len(order))
    sample = cone_sample(rows.astype(F32), lifts, flat, total_rows, total_slices)
    weights = []
    for z in range(-1, slab_depth + 1):
        at = slab * slab_depth + z
        use = real & (at >= 0) & (at < total_slices)
        weights.append(jnp.where(use, jnp.maximum(0.0, 1.0 - jnp.abs(sample - at.astype(F32))), 0.0))
    return sample, weights


def slabs_of(slab, order):
    return [slab + (1 - 2 * lax.rem(slab, 2)) * away for away in order]


def adjoint_taps(tile, cosine, column_count, cell_count, half):
    spacing = PITCH * cell_count / column_count
    cell = (lane_index() + (tile * LANES - half)).astype(F32)
    inside = (cell >= 0) & (cell < cell_count)
    first = jnp.floor((cell - (cell_count / 2 + 0.5)) * cosine * (1.0 / spacing) + (column_count / 2 - 0.5 - 1e-3)) + 1.0
    taps = []
    for tap in range(3):
        column = first + tap
        weight = jnp.maximum(0.0, 1.0 - jnp.abs(cell - column_center(column, cosine, column_count, cell_count)))
        weight = jnp.where(inside & (column >= 0) & (column < column_count), weight, 0.0)
        taps.append((jnp.clip(column.astype(jnp.int32), 0, column_count - 1), weight))
    return taps


def adjoint_tiles(tile, tap, column_count, cell_count, half):
    spacing = PITCH * cell_count / column_count
    least = angle_table()[0].min()
    ends = [
        (tile * LANES - half + e - cell_count / 2 - 0.5) * c / spacing + column_count / 2 + 0.5
        for e in (0, LANES - 1)
        for c in (1.0, least)
    ]
    low = min(max(math.floor(min(ends) + tap - 0.6), 0), column_count - 1) // LANES
    high = min(max(math.ceil(max(ends) + tap + 0.6), 0), column_count - 1) // LANES
    return range(low, high + 1)


def store_line(line, base_ref, bend_ref):
    line = line + [jnp.zeros((SUBLANES, LANES), F32)]
    for tile in range(len(line) - 1):
        cut = slice(tile * LANES, (tile + 1) * LANES)
        base_ref[:, cut] = line[tile]
        bend_ref[:, cut] = next_lane(line[tile], line[tile + 1]) - line[tile]


def adjoint_steps(group, row_count, tangent):
    whole, fraction = shear_steps(group, row_count, tangent)
    place = lane_index() + (row_count // 2 - 1 - whole)
    return jnp.bitwise_and(place, LANES - 1), place < LANES, 1.0 - fraction


def sheared(base_ref, bend_ref, row, step, tiles):
    index, near, share = step
    before, out = None, []
    for tile in range(tiles + 1):
        cut = slice(tile * LANES, (tile + 1) * LANES)
        low = jnp.broadcast_to(base_ref[row : row + 1, cut], (SUBLANES, LANES))
        rise = jnp.broadcast_to(bend_ref[row : row + 1, cut], (SUBLANES, LANES))
        after = pick(low + share * rise, index)
        if tile:
            out.append(jnp.where(near, before, after))
        before = after
    return out


def subset_angles(angle_ref, lift_ref, subset_ref):
    members = subset_ref.shape[0]
    member = jnp.bitwise_and(sublane_index(), members - 1)
    cosine, _, flat = angle_facts(spread_scalars(lambda k: angle_ref[subset_ref[k]], members, member))
    lifts = spread_scalars(lambda k: lift_ref[subset_ref[k]], members, member).astype(F32)
    return cosine, flat, lifts


def member_tangents(angle_ref, subset_ref):
    indices = [angle_ref[subset_ref[k]] for k in range(subset_ref.shape[0])]
    return [angle_facts(jnp.full((SUBLANES, LANES), i, jnp.int32))[1] for i in indices]


def project_kernel(
    angle_ref,
    subset_ref,
    volume_ref,
    measured_ref,
    block_ref,
    cover_ref,
    rise_ref,
    first_ref,
    part_ref,
    end_ref,
    cell_ref,
    slope_ref,
):
    slab_depth, row_count, cell_count = volume_ref.shape
    row_share, view_count, column_count = measured_ref.shape
    subset_count = subset_ref.shape[0]
    half = row_count // 2
    tiles = cell_count // LANES
    groups = row_count // SUBLANES
    lane, sub = lane_index(), sublane_index()
    zero = jnp.zeros((SUBLANES, LANES), F32)
    width = column_count // 2

    for row in range(row_share):
        for member in range(subset_count):
            view = subset_ref[member]
            for side in range(2):
                block_ref[2 * slab_depth + row, side * subset_count + member : side * subset_count + member + 1, :] = (
                    measured_ref[row, pl.ds(view, 1), side * width : (side + 1) * width]
                )

    for depth in range(slab_depth):
        for group in range(groups):
            band = slice(group * SUBLANES, (group + 1) * SUBLANES)
            cells = [tile_of(volume_ref, (depth, band), tile) for tile in range(tiles)] + [zero]
            for tile in range(tiles):
                rise_ref[depth, band, tile * LANES : (tile + 1) * LANES] = (
                    next_lane(cells[tile], cells[tile + 1]) - cells[tile]
                )
            first_ref[depth, band, :] = column_of(cells[0], 0)

    def one_view(view, carry):
        _, tangent, _ = angle_facts(jnp.full((SUBLANES, LANES), angle_ref[view], jnp.int32))
        low_end, high_end = zero, zero
        sums = [[zero] * (tiles + 1) for _ in range(slab_depth)]
        for group in range(groups):
            band = slice(group * SUBLANES, (group + 1) * SUBLANES)
            whole, fraction = shear_steps(group, row_count, tangent)
            place = lane + (whole + half)
            index = jnp.bitwise_and(place, LANES - 1)
            near, last = place < LANES, index == LANES - 1
            enter = jnp.where(last, fraction, 0.0)
            low_end = low_end + jnp.where(near, enter, 1.0)
            high_end = high_end + jnp.where(near, 1.0 - enter, 0.0)
            for depth in range(slab_depth):
                before = enter * first_ref[depth, band, :]
                for tile in range(tiles + 1):
                    after = zero
                    if tile < tiles:
                        at = (depth, band)
                        after = pick(tile_of(volume_ref, at, tile) + fraction * tile_of(rise_ref, at, tile), index)
                    sums[depth][tile] = sums[depth][tile] + jnp.where(near, before, after)
                    before = after
        end_ref[0, view, :, :] = low_end
        end_ref[1, view, :, :] = high_end
        for depth in range(slab_depth):
            for tile in range(tiles + 1):
                part_ref[depth, view, :, tile * LANES : (tile + 1) * LANES] = sums[depth][tile]
        return carry

    lax.fori_loop(0, view_count, one_view, 0, unroll=4)

    shift = LANES - half
    inside = [None] * (tiles + 1)
    inside[0], inside[tiles] = lane >= shift, lane < shift

    def store(at, line):
        line = [jnp.where(mask, cells, 0.0) if mask is not None else cells for cells, mask in zip(line, inside)] + [zero]
        for tile in range(tiles + 1):
            cut = slice(tile * LANES, (tile + 1) * LANES)
            cell_ref[at, :, cut] = line[tile]
            slope_ref[at, :, cut] = next_lane(line[tile], line[tile + 1]) - line[tile]

    views = range(view_count)
    for depth in range(slab_depth):
        store(depth, [rows_summed([tile_of(part_ref, (depth, v), t) for v in views]) for t in range(tiles + 1)])
    flat = zero + float(row_count)
    ends = [rows_summed([end_ref[e, v, :, :] for v in views]) for e in range(2)]
    store(slab_depth, [ends[0]] + [flat] * (tiles - 1) + [ends[1]])

    cosine, _, _ = angle_facts(spread_scalars(lambda v: angle_ref[v], view_count, sub))
    factor = 1.0 / (row_count * cosine)
    least = angle_table()[0].min()
    for tile in range(column_count // LANES):
        column = (lane + tile * LANES).astype(F32)
        center = column_center(column, cosine, column_count, cell_count)
        whole = jnp.floor(center)
        fraction = center - whole
        place = jnp.clip(whole.astype(jnp.int32) + shift, shift - 2, shift + cell_count)
        block, index = jnp.right_shift(place, 7), jnp.bitwise_and(place, LANES - 1)
        ends = [column_center(tile * LANES + e, c, column_count, cell_count) for e in (0, LANES - 1) for c in (1.0, least)]
        low = min(max(math.floor(min(ends) - 1e-2) + shift, shift - 2), shift + cell_count) // LANES
        high = min(max(math.floor(max(ends) + 1e-2) + shift, shift - 2), shift + cell_count) // LANES
        cells, slopes = [zero] * slab_depth + [flat], [zero] * (slab_depth + 1)
        for source in range(low, high + 1):
            here = block == source
            for at in range(slab_depth + 1):
                if at == slab_depth and source not in (0, tiles):
                    continue
                cells[at] = jnp.where(here, pick(tile_of(cell_ref, (at,), source), index), cells[at])
                slopes[at] = jnp.where(here, pick(tile_of(slope_ref, (at,), source), index), slopes[at])
        profiles = [(c + fraction * s) * factor for c, s in zip(cells, slopes)]
        side, inner = divmod(tile * LANES, width)
        for depth in range(slab_depth):
            block_ref[depth * 2 + side, :, inner : inner + LANES] = profiles[depth]
        cover_ref[:, tile * LANES : (tile + 1) * LANES] = profiles[slab_depth]


def divisor_kernel(
    slab_count,
    order,
    angle_ref,
    lift_ref,
    subset_ref,
    cover_ref,
    bound_ref,
    own_ref,
    rows_ref,
    own_cone_ref,
    cone_ref,
    place_ref,
    tap_ref,
    edge_ref,
    bend_ref,
    sub_ref,
):
    slab_depth, row_count, cell_count = bound_ref.shape
    row_share, view_count, column_count = own_ref.shape
    subset_count = subset_ref.shape[0]
    total_rows, total_slices = row_share * slab_count, slab_depth * slab_count
    tiles, columns = cell_count // LANES, column_count // LANES
    width = column_count // 2
    sub = sublane_index()
    zero = jnp.zeros((SUBLANES, LANES), F32)
    slab = lax.axis_index("slab")

    _, _, flat = angle_facts(spread_scalars(lambda v: angle_ref[v], view_count, sub))
    lifts = spread_scalars(lambda v: lift_ref[v], view_count, sub).astype(F32)
    lane = lane_index()
    origin = slabs_of(slab, order)
    source = sum(jnp.where(lane >= slab_depth * b, 1, 0) for b in range(1, len(order)))
    slices = spread_scalars(lambda b: origin[b], len(order), source) * slab_depth + (lane - source * slab_depth)
    held = (slices >= 0) & (slices < total_slices)
    slices = slices.astype(F32)
    for row in range(row_share):
        sample = cone_sample((slab * row_share + row).astype(F32), lifts, flat, total_rows, total_slices)
        weights = jnp.where(held, jnp.maximum(0.0, 1.0 - jnp.abs(sample - slices)), 0.0)
        for place in range(slab_depth * len(order)):
            own_cone_ref[place, row, :, :] = column_of(weights, place)
        total = cone_total(sample, total_slices)
        for tile in range(columns):
            cut = slice(tile * LANES, (tile + 1) * LANES)
            own_ref[row, :, cut] = 1.0 / jnp.maximum(total * cover_ref[:, cut], LEN_FLOOR)

    cosine, flat, lifts = subset_angles(angle_ref, lift_ref, subset_ref)
    tangents = member_tangents(angle_ref, subset_ref)
    for member in range(subset_count):
        view = pl.ds(subset_ref[member], 1)
        for side in range(2):
            at = slice(side * subset_count + member, side * subset_count + member + 1)
            sub_ref[at, :] = cover_ref[view, side * width : (side + 1) * width]
    sample, weights = subset_cone(slab, slab_count, order, slab_depth, row_share, flat, lifts)
    total = cone_total(sample, total_slices)
    for place in range(row_share * len(order)):
        for z, w in enumerate(weights):
            cone_ref[place, z, :, :] = column_of(w, place)
        length = column_of(total, place)
        for tile in range(width // LANES):
            cut = slice(tile * LANES, (tile + 1) * LANES)
            rows_ref[place, :, cut] = 1.0 / jnp.maximum(length * sub_ref[:, cut], LEN_FLOOR)

    factor = 1.0 / (row_count * cosine)
    line = []
    for tile in range(tiles + 1):
        taps = adjoint_taps(tile, cosine, column_count, cell_count, row_count // 2)
        for tap, (place, weight) in enumerate(taps):
            place_ref[tile, tap, :, :] = place
            tap_ref[tile, tap, :, :] = weight * factor
        line.append(sum(weight for _, weight in taps) * factor)
    store_line(line, edge_ref, bend_ref)
    slice_total = []
    for depth in range(slab_depth):
        t = jnp.sum(weights[1 + depth], axis=1, keepdims=True)
        slice_total.append([jnp.broadcast_to(t[k : k + 1], (SUBLANES, LANES)) for k in range(subset_count)])

    def one_group(group, carry):
        band = pl.ds(pl.multiple_of(group * SUBLANES, SUBLANES), SUBLANES)
        weight = [[zero] * tiles for _ in range(slab_depth)]
        for member in range(subset_count):
            line = sheared(edge_ref, bend_ref, member, adjoint_steps(group, row_count, tangents[member]), tiles)
            for depth in range(slab_depth):
                for tile in range(tiles):
                    weight[depth][tile] = weight[depth][tile] + slice_total[depth][member] * line[tile]
        for depth in range(slab_depth):
            for tile in range(tiles):
                bound_ref[depth, band, tile * LANES : (tile + 1) * LANES] = 1.0 / jnp.maximum(
                    weight[depth][tile], LEN_FLOOR * subset_count / row_count
                )
        return carry

    lax.fori_loop(0, row_count // SUBLANES, one_group, 0)


def update_kernel(
    order,
    angle_ref,
    subset_ref,
    volume_ref,
    measured_ref,
    bound_ref,
    own_ref,
    rows_ref,
    own_cone_ref,
    cone_ref,
    place_ref,
    tap_ref,
    *refs,
):
    blocks = refs[: len(order)]
    residual_ref, updated_ref, profile_ref, spread_ref, cell_ref, slope_ref = refs[len(order) :]
    slab_depth, row_count, cell_count = volume_ref.shape
    row_share, view_count, column_count = measured_ref.shape
    subset_count = subset_ref.shape[0]
    tiles, columns = cell_count // LANES, column_count // LANES
    width = column_count // 2
    zero = jnp.zeros((SUBLANES, LANES), F32)
    odd = lax.rem(lax.axis_index("slab"), 2)
    mate_block, other_block = (blocks[order.index(away)] for away in (1, -1))

    for tile in range(columns):
        side, inner = divmod(tile * LANES, width)
        image = [zero] * row_share
        for place, block in enumerate(blocks):
            for depth in range(slab_depth):
                cells = block[depth * 2 + side, :, inner : inner + LANES]
                for row in range(row_share):
                    image[row] = image[row] + own_cone_ref[place * slab_depth + depth, row, :, :] * cells
        cut = slice(tile * LANES, (tile + 1) * LANES)
        for row in range(row_share):
            residual_ref[row, :, cut] = (measured_ref[row, :, cut] - image[row]) * own_ref[row, :, cut]

    for member in range(subset_count):
        view = pl.ds(subset_ref[member], 1)
        for side in range(2):
            at = slice(side * subset_count + member, side * subset_count + member + 1)
            other = other_block[(slab_depth - 1) * 2 + side, view, :], other_block[side, view, :]
            mate = mate_block[(slab_depth - 1) * 2 + side, view, :], mate_block[side, view, :]
            profile_ref[0, at, :] = jnp.where(odd == 0, other[0], mate[0])
            for depth in range(slab_depth):
                profile_ref[1 + depth, at, :] = blocks[0][depth * 2 + side, view, :]
            profile_ref[1 + slab_depth, at, :] = jnp.where(odd == 0, mate[1], other[1])

    inner_tiles = width // LANES
    spread = [[zero] * inner_tiles for _ in range(slab_depth)]
    for place in range(row_share * len(order)):
        weight = [cone_ref[place, z, :, :] for z in range(slab_depth + 2)]
        block, row = blocks[place // row_share], place % row_share
        for tile in range(inner_tiles):
            cut = slice(tile * LANES, (tile + 1) * LANES)
            image = weight[0] * profile_ref[0, :, cut]
            for z in range(1, slab_depth + 2):
                image = image + weight[z] * profile_ref[z, :, cut]
            rest = (block[2 * slab_depth + row, :, cut] - image) * rows_ref[place, :, cut]
            for depth in range(slab_depth):
                spread[depth][tile] = spread[depth][tile] + weight[1 + depth] * rest
    for depth in range(slab_depth):
        for tile in range(inner_tiles):
            for side in range(2):
                spread_ref[
                    depth * subset_count : (depth + 1) * subset_count,
                    side * width + tile * LANES : side * width + (tile + 1) * LANES,
                ] = spread[depth][tile][side * subset_count : (side + 1) * subset_count]

    line = []
    for tile in range(tiles + 1):
        value = zero
        for tap in range(3):
            place = place_ref[tile, tap, :, :]
            block, index = jnp.right_shift(place, 7), jnp.bitwise_and(place, LANES - 1)
            found = zero
            for at in adjoint_tiles(tile, tap, column_count, cell_count, row_count // 2):
                found = jnp.where(block == at, pick(tile_of(spread_ref, (), at), index), found)
            value = value + tap_ref[tile, tap, :, :] * found
        line.append(value)
    store_line(line, cell_ref, slope_ref)

    tangents = member_tangents(angle_ref, subset_ref)

    def one_group(group, carry):
        band = pl.ds(pl.multiple_of(group * SUBLANES, SUBLANES), SUBLANES)
        back = [[zero] * tiles for _ in range(slab_depth)]
        for member in range(subset_count):
            step = adjoint_steps(group, row_count, tangents[member])
            for depth in range(slab_depth):
                line = sheared(cell_ref, slope_ref, depth * subset_count + member, step, tiles)
                back[depth] = [b + a for b, a in zip(back[depth], line)]
        for depth in range(slab_depth):
            for tile in range(tiles):
                cut = slice(tile * LANES, (tile + 1) * LANES)
                updated_ref[depth, band, cut] = (
                    volume_ref[depth, band, cut] + back[depth][tile] * bound_ref[depth, band, cut]
                )
        return carry

    lax.fori_loop(0, row_count // SUBLANES, one_group, 0, unroll=2)


def swapped(block):
    return lax.ppermute(block, "slab", [(i, i ^ 1) for i in range(lax.axis_size("slab"))])


def from_chip(block, distance):
    slabs = range(lax.axis_size("slab"))
    steps = [(i + 2 * distance * (1 - 2 * (i % 2)), i) for i in slabs]
    pairs = [p for p in steps if p[0] in slabs]
    idle = [i for i in slabs if i not in [p[0] for p in pairs]]
    unmet = [i for i in slabs if i not in [p[1] for p in pairs]]
    near = [i for i in idle if i ^ 1 in unmet]
    pairs += [(i, i ^ 1) for i in near]
    pairs += zip([i for i in idle if i not in near], [i for i in unmet if i ^ 1 not in near])
    return lax.ppermute(block, "slab", pairs)


def fetches(reach):
    return [s * d for d in range(1, reach // 2 + 2) for s in (-1, 1) if 2 * d - (s > 0) <= reach]


def window(reach):
    order = [0, 1]
    for distance in fetches(reach):
        order += [at for at in (2 * distance, 1 - 2 * distance) if abs(at) <= reach]
    assert sorted(order) == list(range(-reach, reach + 1))
    return tuple(order)


def gathered(own, reach, meanwhile):
    received = [from_chip(own, distance) for distance in fetches(reach)]
    blocks = {0: own, 1: swapped(own)}
    done = meanwhile()
    received, done = lax.optimization_barrier((received, done))
    for distance, block in zip(fetches(reach), received):
        if 2 * abs(distance) <= reach:
            blocks[2 * distance] = block
        if abs(1 - 2 * distance) <= reach:
            blocks[1 - 2 * distance] = swapped(block)
    return [blocks[away] for away in window(reach)], done


def per_device(volume, measured, view_angle, view_lift, subset):
    slab_count = lax.axis_size("slab")
    slab_depth, row_count, cell_count = volume.shape
    row_share, view_count, column_count = measured.shape
    subset_count = subset.shape[0]
    tiles = cell_count // LANES
    reach = slab_reach(slab_count, slab_depth, row_share)
    small = pltpu.CompilerParams(vmem_limit_bytes=VMEM_LIMIT)
    smem, vmem = pl.BlockSpec(memory_space=pltpu.SMEM), pl.BlockSpec(memory_space=pltpu.VMEM)
    wide = (tiles + 1) * LANES
    block_shape = (2 * slab_depth + row_share, SUBLANES, column_count // 2)
    own, cover = pl.pallas_call(
        project_kernel,
        out_shape=(
            pltpu.VMEM(block_shape, F32),
            pltpu.VMEM((view_count, column_count), F32),
        ),
        in_specs=[smem, smem, vmem, vmem],
        out_specs=(vmem, vmem),
        scratch_shapes=[
            pltpu.VMEM(volume.shape, F32),
            pltpu.VMEM((slab_depth, row_count, LANES), F32),
            pltpu.VMEM((slab_depth, view_count, SUBLANES, wide), F32),
            pltpu.VMEM((2, view_count, SUBLANES, LANES), F32),
        ]
        + [pltpu.VMEM((slab_depth + 1, SUBLANES, wide), F32)] * 2,
        compiler_params=small,
        name="project",
    )(view_angle, subset, volume, measured)
    here = lambda x: pltpu.with_memory_space_constraint(x, pltpu.VMEM)
    cover = here(cover)
    order = window(reach)
    divide = pl.pallas_call(
        functools.partial(divisor_kernel, slab_count, order),
        out_shape=(
            pltpu.VMEM(volume.shape, F32),
            pltpu.VMEM(measured.shape, F32),
            pltpu.VMEM((row_share * len(order), SUBLANES, column_count // 2), F32),
            pltpu.VMEM((slab_depth * len(order), row_share, SUBLANES, LANES), F32),
            pltpu.VMEM((row_share * len(order), slab_depth + 2, SUBLANES, LANES), F32),
            pltpu.VMEM((tiles + 1, 3, SUBLANES, LANES), jnp.int32),
            pltpu.VMEM((tiles + 1, 3, SUBLANES, LANES), F32),
        ),
        in_specs=[smem] * 3 + [vmem],
        out_specs=(vmem,) * 7,
        scratch_shapes=[pltpu.VMEM((SUBLANES, wide), F32)] * 2 + [pltpu.VMEM((SUBLANES, column_count // 2), F32)],
        cost_estimate=pl.CostEstimate(flops=4_000_000, bytes_accessed=8_000_000, transcendentals=0),
        compiler_params=small,
        name="divisors",
    )
    blocks, divisors = gathered(own, reach, lambda: divide(view_angle, view_lift, subset, cover))
    return pl.pallas_call(
        functools.partial(update_kernel, order),
        out_shape=(
            jax.ShapeDtypeStruct(measured.shape, F32),
            jax.ShapeDtypeStruct(volume.shape, F32),
        ),
        in_specs=[smem] * 2 + [vmem] * (2 + len(divisors) + len(order)),
        out_specs=(vmem, vmem),
        scratch_shapes=[
            pltpu.VMEM((slab_depth + 2, SUBLANES, column_count // 2), F32),
            pltpu.VMEM((SUBLANES, column_count), F32),
        ]
        + [pltpu.VMEM((SUBLANES, wide), F32)] * 2,
        compiler_params=small,
        name="update",
    )(view_angle, subset, *map(here, (volume, measured, *divisors, *blocks)))


def solution(mesh):
    in_specs = (
        P(("scan", "slab"), None, None),
        P(("scan", "slab"), None, None),
        P("scan"),
        P("scan"),
        P("scan"),
    )
    out_specs = (P(("scan", "slab"), None, None), P(("scan", "slab"), None, None))
    return jax.shard_map(
        per_device, mesh=mesh, in_specs=in_specs, out_specs=out_specs, check_vma=False
    )
```

```python
import functools
import math

import jax
import jax.numpy as jnp
import numpy as np
from jax import lax
from jax.experimental import pallas as pl
from jax.experimental.pallas import tpu as pltpu
from jax.sharding import PartitionSpec as P

ANGLES = 180
LIFT = 6
PITCH = 0.9
MAG_BASE = 1.5
ECCENTRIC = 0.12
LEN_FLOOR = 0.25
LANES = 128
SUBLANES = 8
F32 = jnp.float32
VMEM_LIMIT = 8 * 1024 * 1024


def angle_table():
    radians = (np.arange(ANGLES) + 0.5) * (0.5 * math.pi / ANGLES) - 0.25 * math.pi
    magnify = MAG_BASE / (1.0 - ECCENTRIC * np.sin(2.0 * radians + 1.0))
    return np.cos(radians), magnify


def slab_reach(slab_count, slab_depth, row_share):
    _, magnify = angle_table()
    total_rows, total_slices = row_share * slab_count, slab_depth * slab_count
    rows = np.arange(total_rows)
    reach = 0
    for lift in range(-LIFT, LIFT + 1):
        sample = (rows[None] + 0.5 - total_rows / 2 - lift) / magnify[:, None] + total_slices / 2 - 0.5
        for tap in (np.floor(sample - 1e-3), np.floor(sample + 1e-3) + 1):
            inside = (tap >= 0) & (tap < total_slices)
            distance = np.abs(tap // slab_depth - rows[None] // row_share)
            reach = max(reach, int(distance[inside].max()))
    return reach


def lane_index():
    return lax.broadcasted_iota(jnp.int32, (SUBLANES, LANES), 1)


def sublane_index():
    return lax.broadcasted_iota(jnp.int32, (SUBLANES, LANES), 0)


def angle_facts(index):
    x = (index.astype(F32) + 0.5) * (0.5 * math.pi / ANGLES) - 0.25 * math.pi
    s = x * x
    sine = x * (1.0 + s * (-1 / 6 + s * (1 / 120 + s * (-1 / 5040 + s * (1 / 362880)))))
    cosine = 1.0 + s * (-1 / 2 + s * (1 / 24 + s * (-1 / 720 + s * (1 / 40320 + s * (-1 / 3628800)))))
    double = 2.0 * sine * cosine * math.cos(1.0) + (1.0 - 2.0 * sine * sine) * math.sin(1.0)
    return cosine, sine / cosine, (1.0 - ECCENTRIC * double) * (1.0 / MAG_BASE)


def spread_scalars(read, count, place):
    out = jnp.full((SUBLANES, LANES), read(0), jnp.int32)
    for item in range(1, count):
        out = jnp.where(place == item, read(item), out)
    return out


def pick(tile, index):
    numbers = lax.GatherDimensionNumbers(
        offset_dims=(),
        collapsed_slice_dims=(1,),
        start_index_map=(1,),
        operand_batching_dims=(0,),
        start_indices_batching_dims=(0,),
    )
    return lax.gather(tile, index[..., None], numbers, (1, 1), mode=lax.GatherScatterMode.PROMISE_IN_BOUNDS)


def next_lane(tile, following):
    lane = lane_index()
    return jnp.where(lane < LANES - 1, pltpu.roll(tile, LANES - 1, 1), pltpu.roll(following, LANES - 1, 1))


def rows_summed(parts):
    sub = sublane_index()
    step = 1
    while step < SUBLANES:
        low = jnp.bitwise_and(sub, step) == 0
        parts = [
            jnp.where(low, a, b) + pltpu.roll(jnp.where(low, b, a), step, 0) for a, b in zip(parts[::2], parts[1::2])
        ]
        step *= 2
    return parts[0]


def tile_of(ref, lead, tile):
    whole = (slice(None),) * (len(ref.shape) - 1 - len(lead))
    return ref[lead + whole + (slice(tile * LANES, (tile + 1) * LANES),)]


def column_center(column, cosine, column_count, cell_count):
    return (column + 0.5 - column_count / 2) * (PITCH * cell_count / column_count) / cosine + (
        cell_count / 2 - 0.5
    )


def shear_steps(group, row_count, tangent):
    row = (sublane_index() + group * SUBLANES).astype(F32)
    offset = (row + 0.5 - row_count / 2) * tangent
    whole = jnp.floor(offset)
    return whole.astype(jnp.int32), offset - whole


def cone_sample(rows, lifts, flat, total_rows, total_slices):
    return (rows + 0.5 - total_rows / 2 - lifts) * flat + (total_slices / 2 - 0.5)


def cone_total(sample, total_slices):
    whole = jnp.floor(sample)
    fraction = sample - whole
    low = jnp.where((whole >= 0) & (whole < total_slices), 1.0 - fraction, 0.0)
    return low + jnp.where((whole >= -1) & (whole < total_slices - 1), fraction, 0.0)


def column_of(tile, at):
    return jnp.broadcast_to(tile[:, at : at + 1], (SUBLANES, LANES))


def subset_cone(slab, slab_count, order, slab_depth, row_share, flat, lifts):
    lane = lane_index()
    total_rows, total_slices = row_share * slab_count, slab_depth * slab_count
    origin = slabs_of(slab, order)
    source = sum(jnp.where(lane >= row_share * b, 1, 0) for b in range(1, len(order)))
    rows = spread_scalars(lambda b: origin[b], len(order), source) * row_share + (lane - source * row_share)
    real = (rows >= 0) & (rows < total_rows) & (lane < row_share * len(order))
    sample = cone_sample(rows.astype(F32), lifts, flat, total_rows, total_slices)
    weights = []
    for z in range(-1, slab_depth + 1):
        at = slab * slab_depth + z
        use = real & (at >= 0) & (at < total_slices)
        weights.append(jnp.where(use, jnp.maximum(0.0, 1.0 - jnp.abs(sample - at.astype(F32))), 0.0))
    return sample, weights


def slabs_of(slab, order):
    return [slab + (1 - 2 * lax.rem(slab, 2)) * away for away in order]


def adjoint_taps(tile, cosine, column_count, cell_count, half):
    spacing = PITCH * cell_count / column_count
    cell = (lane_index() + (tile * LANES - half)).astype(F32)
    inside = (cell >= 0) & (cell < cell_count)
    first = jnp.floor((cell - (cell_count / 2 + 0.5)) * cosine * (1.0 / spacing) + (column_count / 2 - 0.5 - 1e-3)) + 1.0
    taps = []
    for tap in range(3):
        column = first + tap
        weight = jnp.maximum(0.0, 1.0 - jnp.abs(cell - column_center(column, cosine, column_count, cell_count)))
        weight = jnp.where(inside & (column >= 0) & (column < column_count), weight, 0.0)
        taps.append((jnp.clip(column.astype(jnp.int32), 0, column_count - 1), weight))
    return taps


def adjoint_tiles(tile, tap, column_count, cell_count, half):
    spacing = PITCH * cell_count / column_count
    least = angle_table()[0].min()
    ends = [
        (tile * LANES - half + e - cell_count / 2 - 0.5) * c / spacing + column_count / 2 + 0.5
        for e in (0, LANES - 1)
        for c in (1.0, least)
    ]
    low = min(max(math.floor(min(ends) + tap - 0.6), 0), column_count - 1) // LANES
    high = min(max(math.ceil(max(ends) + tap + 0.6), 0), column_count - 1) // LANES
    return range(low, high + 1)


def store_line(line, base_ref, bend_ref):
    line = line + [jnp.zeros((SUBLANES, LANES), F32)]
    for tile in range(len(line) - 1):
        cut = slice(tile * LANES, (tile + 1) * LANES)
        base_ref[:, cut] = line[tile]
        bend_ref[:, cut] = next_lane(line[tile], line[tile + 1]) - line[tile]


def adjoint_steps(group, row_count, tangent):
    whole, fraction = shear_steps(group, row_count, tangent)
    place = lane_index() + (row_count // 2 - 1 - whole)
    return jnp.bitwise_and(place, LANES - 1), place < LANES, 1.0 - fraction


def sheared(base_ref, bend_ref, row, step, tiles):
    index, near, share = step
    before, out = None, []
    for tile in range(tiles + 1):
        cut = slice(tile * LANES, (tile + 1) * LANES)
        low = jnp.broadcast_to(base_ref[row : row + 1, cut], (SUBLANES, LANES))
        rise = jnp.broadcast_to(bend_ref[row : row + 1, cut], (SUBLANES, LANES))
        after = pick(low + share * rise, index)
        if tile:
            out.append(jnp.where(near, before, after))
        before = after
    return out


def subset_angles(angle_ref, lift_ref, subset_ref):
    members = subset_ref.shape[0]
    member = jnp.bitwise_and(sublane_index(), members - 1)
    cosine, _, flat = angle_facts(spread_scalars(lambda k: angle_ref[subset_ref[k]], members, member))
    lifts = spread_scalars(lambda k: lift_ref[subset_ref[k]], members, member).astype(F32)
    return cosine, flat, lifts


def member_tangents(angle_ref, subset_ref):
    indices = [angle_ref[subset_ref[k]] for k in range(subset_ref.shape[0])]
    return [angle_facts(jnp.full((SUBLANES, LANES), i, jnp.int32))[1] for i in indices]


def project_kernel(
    angle_ref,
    subset_ref,
    volume_ref,
    measured_ref,
    block_ref,
    cover_ref,
    rise_ref,
    first_ref,
    part_ref,
    end_ref,
    cell_ref,
    slope_ref,
):
    slab_depth, row_count, cell_count = volume_ref.shape
    row_share, view_count, column_count = measured_ref.shape
    subset_count = subset_ref.shape[0]
    half = row_count // 2
    tiles = cell_count // LANES
    groups = row_count // SUBLANES
    lane, sub = lane_index(), sublane_index()
    zero = jnp.zeros((SUBLANES, LANES), F32)
    width = column_count // 2

    for row in range(row_share):
        for member in range(subset_count):
            view = subset_ref[member]
            for side in range(2):
                block_ref[2 * slab_depth + row, side * subset_count + member : side * subset_count + member + 1, :] = (
                    measured_ref[row, pl.ds(view, 1), side * width : (side + 1) * width]
                )

    for depth in range(slab_depth):
        for group in range(groups):
            band = slice(group * SUBLANES, (group + 1) * SUBLANES)
            cells = [tile_of(volume_ref, (depth, band), tile) for tile in range(tiles)] + [zero]
            for tile in range(tiles):
                rise_ref[depth, band, tile * LANES : (tile + 1) * LANES] = (
                    next_lane(cells[tile], cells[tile + 1]) - cells[tile]
                )
            first_ref[depth, band, :] = column_of(cells[0], 0)

    def one_view(view, carry):
        _, tangent, _ = angle_facts(jnp.full((SUBLANES, LANES), angle_ref[view], jnp.int32))
        low_end, high_end = zero, zero
        sums = [[zero] * (tiles + 1) for _ in range(slab_depth)]
        for group in range(groups):
            band = slice(group * SUBLANES, (group + 1) * SUBLANES)
            whole, fraction = shear_steps(group, row_count, tangent)
            place = lane + (whole + half)
            index = jnp.bitwise_and(place, LANES - 1)
            near, last = place < LANES, index == LANES - 1
            enter = jnp.where(last, fraction, 0.0)
            low_end = low_end + jnp.where(near, enter, 1.0)
            high_end = high_end + jnp.where(near, 1.0 - enter, 0.0)
            for depth in range(slab_depth):
                before = enter * first_ref[depth, band, :]
                for tile in range(tiles + 1):
                    after = zero
                    if tile < tiles:
                        at = (depth, band)
                        after = pick(tile_of(volume_ref, at, tile) + fraction * tile_of(rise_ref, at, tile), index)
                    sums[depth][tile] = sums[depth][tile] + jnp.where(near, before, after)
                    before = after
        end_ref[0, view, :, :] = low_end
        end_ref[1, view, :, :] = high_end
        for depth in range(slab_depth):
            for tile in range(tiles + 1):
                part_ref[depth, view, :, tile * LANES : (tile + 1) * LANES] = sums[depth][tile]
        return carry

    lax.fori_loop(0, view_count, one_view, 0, unroll=4)

    shift = LANES - half
    inside = [None] * (tiles + 1)
    inside[0], inside[tiles] = lane >= shift, lane < shift

    def store(at, line):
        line = [jnp.where(mask, cells, 0.0) if mask is not None else cells for cells, mask in zip(line, inside)] + [zero]
        for tile in range(tiles + 1):
            cut = slice(tile * LANES, (tile + 1) * LANES)
            cell_ref[at, :, cut] = line[tile]
            slope_ref[at, :, cut] = next_lane(line[tile], line[tile + 1]) - line[tile]

    views = range(view_count)
    for depth in range(slab_depth):
        store(depth, [rows_summed([tile_of(part_ref, (depth, v), t) for v in views]) for t in range(tiles + 1)])
    flat = zero + float(row_count)
    ends = [rows_summed([end_ref[e, v, :, :] for v in views]) for e in range(2)]
    store(slab_depth, [ends[0]] + [flat] * (tiles - 1) + [ends[1]])

    cosine, _, _ = angle_facts(spread_scalars(lambda v: angle_ref[v], view_count, sub))
    factor = 1.0 / (row_count * cosine)
    least = angle_table()[0].min()
    for tile in range(column_count // LANES):
        column = (lane + tile * LANES).astype(F32)
        center = column_center(column, cosine, column_count, cell_count)
        whole = jnp.floor(center)
        fraction = center - whole
        place = jnp.clip(whole.astype(jnp.int32) + shift, shift - 2, shift + cell_count)
        block, index = jnp.right_shift(place, 7), jnp.bitwise_and(place, LANES - 1)
        ends = [column_center(tile * LANES + e, c, column_count, cell_count) for e in (0, LANES - 1) for c in (1.0, least)]
        low = min(max(math.floor(min(ends) - 1e-2) + shift, shift - 2), shift + cell_count) // LANES
        high = min(max(math.floor(max(ends) + 1e-2) + shift, shift - 2), shift + cell_count) // LANES
        cells, slopes = [zero] * slab_depth + [flat], [zero] * (slab_depth + 1)
        for source in range(low, high + 1):
            here = block == source
            for at in range(slab_depth + 1):
                if at == slab_depth and source not in (0, tiles):
                    continue
                cells[at] = jnp.where(here, pick(tile_of(cell_ref, (at,), source), index), cells[at])
                slopes[at] = jnp.where(here, pick(tile_of(slope_ref, (at,), source), index), slopes[at])
        profiles = [(c + fraction * s) * factor for c, s in zip(cells, slopes)]
        side, inner = divmod(tile * LANES, width)
        for depth in range(slab_depth):
            block_ref[depth * 2 + side, :, inner : inner + LANES] = profiles[depth]
        cover_ref[:, tile * LANES : (tile + 1) * LANES] = profiles[slab_depth]


def divisor_kernel(
    slab_count,
    order,
    angle_ref,
    lift_ref,
    subset_ref,
    cover_ref,
    bound_ref,
    own_ref,
    rows_ref,
    own_cone_ref,
    cone_ref,
    place_ref,
    tap_ref,
    edge_ref,
    bend_ref,
    sub_ref,
):
    slab_depth, row_count, cell_count = bound_ref.shape
    row_share, view_count, column_count = own_ref.shape
    subset_count = subset_ref.shape[0]
    total_rows, total_slices = row_share * slab_count, slab_depth * slab_count
    tiles, columns = cell_count // LANES, column_count // LANES
    width = column_count // 2
    sub = sublane_index()
    zero = jnp.zeros((SUBLANES, LANES), F32)
    slab = lax.axis_index("slab")

    _, _, flat = angle_facts(spread_scalars(lambda v: angle_ref[v], view_count, sub))
    lifts = spread_scalars(lambda v: lift_ref[v], view_count, sub).astype(F32)
    lane = lane_index()
    origin = slabs_of(slab, order)
    source = sum(jnp.where(lane >= slab_depth * b, 1, 0) for b in range(1, len(order)))
    slices = spread_scalars(lambda b: origin[b], len(order), source) * slab_depth + (lane - source * slab_depth)
    held = (slices >= 0) & (slices < total_slices)
    slices = slices.astype(F32)
    for row in range(row_share):
        sample = cone_sample((slab * row_share + row).astype(F32), lifts, flat, total_rows, total_slices)
        weights = jnp.where(held, jnp.maximum(0.0, 1.0 - jnp.abs(sample - slices)), 0.0)
        for place in range(slab_depth * len(order)):
            own_cone_ref[place, row, :, :] = column_of(weights, place)
        total = cone_total(sample, total_slices)
        for tile in range(columns):
            cut = slice(tile * LANES, (tile + 1) * LANES)
            own_ref[row, :, cut] = 1.0 / jnp.maximum(total * cover_ref[:, cut], LEN_FLOOR)

    cosine, flat, lifts = subset_angles(angle_ref, lift_ref, subset_ref)
    tangents = member_tangents(angle_ref, subset_ref)
    for member in range(subset_count):
        view = pl.ds(subset_ref[member], 1)
        for side in range(2):
            at = slice(side * subset_count + member, side * subset_count + member + 1)
            sub_ref[at, :] = cover_ref[view, side * width : (side + 1) * width]
    sample, weights = subset_cone(slab, slab_count, order, slab_depth, row_share, flat, lifts)
    total = cone_total(sample, total_slices)
    for place in range(row_share * len(order)):
        for z, w in enumerate(weights):
            cone_ref[place, z, :, :] = column_of(w, place)
        length = column_of(total, place)
        for tile in range(width // LANES):
            cut = slice(tile * LANES, (tile + 1) * LANES)
            rows_ref[place, :, cut] = 1.0 / jnp.maximum(length * sub_ref[:, cut], LEN_FLOOR)

    factor = 1.0 / (row_count * cosine)
    line = []
    for tile in range(tiles + 1):
        taps = adjoint_taps(tile, cosine, column_count, cell_count, row_count // 2)
        for tap, (place, weight) in enumerate(taps):
            place_ref[tile, tap, :, :] = place
            tap_ref[tile, tap, :, :] = weight * factor
        line.append(sum(weight for _, weight in taps) * factor)
    store_line(line, edge_ref, bend_ref)
    slice_total = []
    for depth in range(slab_depth):
        t = jnp.sum(weights[1 + depth], axis=1, keepdims=True)
        slice_total.append([jnp.broadcast_to(t[k : k + 1], (SUBLANES, LANES)) for k in range(subset_count)])

    def one_group(group, carry):
        band = pl.ds(pl.multiple_of(group * SUBLANES, SUBLANES), SUBLANES)
        weight = [[zero] * tiles for _ in range(slab_depth)]
        for member in range(subset_count):
            line = sheared(edge_ref, bend_ref, member, adjoint_steps(group, row_count, tangents[member]), tiles)
            for depth in range(slab_depth):
                for tile in range(tiles):
                    weight[depth][tile] = weight[depth][tile] + slice_total[depth][member] * line[tile]
        for depth in range(slab_depth):
            for tile in range(tiles):
                bound_ref[depth, band, tile * LANES : (tile + 1) * LANES] = 1.0 / jnp.maximum(
                    weight[depth][tile], LEN_FLOOR * subset_count / row_count
                )
        return carry

    lax.fori_loop(0, row_count // SUBLANES, one_group, 0)


def update_kernel(
    order,
    angle_ref,
    subset_ref,
    volume_ref,
    measured_ref,
    bound_ref,
    own_ref,
    rows_ref,
    own_cone_ref,
    cone_ref,
    place_ref,
    tap_ref,
    *refs,
):
    blocks = refs[: len(order)]
    residual_ref, updated_ref, profile_ref, spread_ref, cell_ref, slope_ref = refs[len(order) :]
    slab_depth, row_count, cell_count = volume_ref.shape
    row_share, view_count, column_count = measured_ref.shape
    subset_count = subset_ref.shape[0]
    tiles, columns = cell_count // LANES, column_count // LANES
    width = column_count // 2
    zero = jnp.zeros((SUBLANES, LANES), F32)
    odd = lax.rem(lax.axis_index("slab"), 2)
    mate_block, other_block = (blocks[order.index(away)] for away in (1, -1))

    for tile in range(columns):
        side, inner = divmod(tile * LANES, width)
        image = [zero] * row_share
        for place, block in enumerate(blocks):
            for depth in range(slab_depth):
                cells = block[depth * 2 + side, :, inner : inner + LANES]
                for row in range(row_share):
                    image[row] = image[row] + own_cone_ref[place * slab_depth + depth, row, :, :] * cells
        cut = slice(tile * LANES, (tile + 1) * LANES)
        for row in range(row_share):
            residual_ref[row, :, cut] = (measured_ref[row, :, cut] - image[row]) * own_ref[row, :, cut]

    for member in range(subset_count):
        view = pl.ds(subset_ref[member], 1)
        for side in range(2):
            at = slice(side * subset_count + member, side * subset_count + member + 1)
            other = other_block[(slab_depth - 1) * 2 + side, view, :], other_block[side, view, :]
            mate = mate_block[(slab_depth - 1) * 2 + side, view, :], mate_block[side, view, :]
            profile_ref[0, at, :] = jnp.where(odd == 0, other[0], mate[0])
            for depth in range(slab_depth):
                profile_ref[1 + depth, at, :] = blocks[0][depth * 2 + side, view, :]
            profile_ref[1 + slab_depth, at, :] = jnp.where(odd == 0, mate[1], other[1])

    inner_tiles = width // LANES
    spread = [[zero] * inner_tiles for _ in range(slab_depth)]
    for place in range(row_share * len(order)):
        weight = [cone_ref[place, z, :, :] for z in range(slab_depth + 2)]
        block, row = blocks[place // row_share], place % row_share
        for tile in range(inner_tiles):
            cut = slice(tile * LANES, (tile + 1) * LANES)
            image = weight[0] * profile_ref[0, :, cut]
            for z in range(1, slab_depth + 2):
                image = image + weight[z] * profile_ref[z, :, cut]
            rest = (block[2 * slab_depth + row, :, cut] - image) * rows_ref[place, :, cut]
            for depth in range(slab_depth):
                spread[depth][tile] = spread[depth][tile] + weight[1 + depth] * rest
    for depth in range(slab_depth):
        for tile in range(inner_tiles):
            for side in range(2):
                spread_ref[
                    depth * subset_count : (depth + 1) * subset_count,
                    side * width + tile * LANES : side * width + (tile + 1) * LANES,
                ] = spread[depth][tile][side * subset_count : (side + 1) * subset_count]

    line = []
    for tile in range(tiles + 1):
        value = zero
        for tap in range(3):
            place = place_ref[tile, tap, :, :]
            block, index = jnp.right_shift(place, 7), jnp.bitwise_and(place, LANES - 1)
            found = zero
            for at in adjoint_tiles(tile, tap, column_count, cell_count, row_count // 2):
                found = jnp.where(block == at, pick(tile_of(spread_ref, (), at), index), found)
            value = value + tap_ref[tile, tap, :, :] * found
        line.append(value)
    store_line(line, cell_ref, slope_ref)

    tangents = member_tangents(angle_ref, subset_ref)

    def one_group(group, carry):
        band = pl.ds(pl.multiple_of(group * SUBLANES, SUBLANES), SUBLANES)
        back = [[zero] * tiles for _ in range(slab_depth)]
        for member in range(subset_count):
            step = adjoint_steps(group, row_count, tangents[member])
            for depth in range(slab_depth):
                line = sheared(cell_ref, slope_ref, depth * subset_count + member, step, tiles)
                back[depth] = [b + a for b, a in zip(back[depth], line)]
        for depth in range(slab_depth):
            for tile in range(tiles):
                cut = slice(tile * LANES, (tile + 1) * LANES)
                updated_ref[depth, band, cut] = (
                    volume_ref[depth, band, cut] + back[depth][tile] * bound_ref[depth, band, cut]
                )
        return carry

    lax.fori_loop(0, row_count // SUBLANES, one_group, 0, unroll=2)


def swapped(block):
    return lax.ppermute(block, "slab", [(i, i ^ 1) for i in range(lax.axis_size("slab"))])


def from_chip(block, distance):
    slabs = range(lax.axis_size("slab"))
    steps = [(i + 2 * distance * (1 - 2 * (i % 2)), i) for i in slabs]
    pairs = [p for p in steps if p[0] in slabs]
    idle = [i for i in slabs if i not in [p[0] for p in pairs]]
    unmet = [i for i in slabs if i not in [p[1] for p in pairs]]
    near = [i for i in idle if i ^ 1 in unmet]
    pairs += [(i, i ^ 1) for i in near]
    pairs += zip([i for i in idle if i not in near], [i for i in unmet if i ^ 1 not in near])
    return lax.ppermute(block, "slab", pairs)


def fetches(reach):
    return [s * d for d in range(1, reach // 2 + 2) for s in (-1, 1) if 2 * d - (s > 0) <= reach]


def window(reach):
    order = [0, 1]
    for distance in fetches(reach):
        order += [at for at in (2 * distance, 1 - 2 * distance) if abs(at) <= reach]
    assert sorted(order) == list(range(-reach, reach + 1))
    return tuple(order)


def gathered(own, reach, meanwhile):
    received = [from_chip(own, distance) for distance in fetches(reach)]
    blocks = {0: own, 1: swapped(own)}
    done = meanwhile()
    received, done = lax.optimization_barrier((received, done))
    for distance, block in zip(fetches(reach), received):
        if 2 * abs(distance) <= reach:
            blocks[2 * distance] = block
        if abs(1 - 2 * distance) <= reach:
            blocks[1 - 2 * distance] = swapped(block)
    return [blocks[away] for away in window(reach)], done


def per_device(volume, measured, view_angle, view_lift, subset):
    slab_count = lax.axis_size("slab")
    slab_depth, row_count, cell_count = volume.shape
    row_share, view_count, column_count = measured.shape
    subset_count = subset.shape[0]
    tiles = cell_count // LANES
    reach = slab_reach(slab_count, slab_depth, row_share)
    here = lambda x: pltpu.with_memory_space_constraint(x, pltpu.VMEM)
    there = lambda x: pltpu.with_memory_space_constraint(x, pltpu.HBM)
    small = pltpu.CompilerParams(vmem_limit_bytes=VMEM_LIMIT)
    smem, vmem = pl.BlockSpec(memory_space=pltpu.SMEM), pl.BlockSpec(memory_space=pltpu.VMEM)
    wide = (tiles + 1) * LANES
    block_shape = (2 * slab_depth + row_share, SUBLANES, column_count // 2)
    own, cover = pl.pallas_call(
        project_kernel,
        out_shape=(
            pltpu.VMEM(block_shape, F32),
            pltpu.VMEM((view_count, column_count), F32),
        ),
        in_specs=[smem, smem, vmem, vmem],
        out_specs=(vmem, vmem),
        scratch_shapes=[
            pltpu.VMEM(volume.shape, F32),
            pltpu.VMEM((slab_depth, row_count, LANES), F32),
            pltpu.VMEM((slab_depth, view_count, SUBLANES, wide), F32),
            pltpu.VMEM((2, view_count, SUBLANES, LANES), F32),
        ]
        + [pltpu.VMEM((slab_depth + 1, SUBLANES, wide), F32)] * 2,
        compiler_params=small,
        name="project",
    )(*map(there, (view_angle, subset, volume, measured)))
    cover = here(cover)
    order = window(reach)
    divide = pl.pallas_call(
        functools.partial(divisor_kernel, slab_count, order),
        out_shape=(
            pltpu.VMEM(volume.shape, F32),
            pltpu.VMEM(measured.shape, F32),
            pltpu.VMEM((row_share * len(order), SUBLANES, column_count // 2), F32),
            pltpu.VMEM((slab_depth * len(order), row_share, SUBLANES, LANES), F32),
            pltpu.VMEM((row_share * len(order), slab_depth + 2, SUBLANES, LANES), F32),
            pltpu.VMEM((tiles + 1, 3, SUBLANES, LANES), jnp.int32),
            pltpu.VMEM((tiles + 1, 3, SUBLANES, LANES), F32),
        ),
        in_specs=[smem] * 3 + [vmem],
        out_specs=(vmem,) * 7,
        scratch_shapes=[pltpu.VMEM((SUBLANES, wide), F32)] * 2 + [pltpu.VMEM((SUBLANES, column_count // 2), F32)],
        cost_estimate=pl.CostEstimate(flops=4_000_000, bytes_accessed=8_000_000, transcendentals=0),
        compiler_params=small,
        name="divisors",
    )
    blocks, divisors = gathered(own, reach, lambda: divide(view_angle, view_lift, subset, cover))
    return pl.pallas_call(
        functools.partial(update_kernel, order),
        out_shape=(
            jax.ShapeDtypeStruct(measured.shape, F32),
            jax.ShapeDtypeStruct(volume.shape, F32),
        ),
        in_specs=[smem] * 2 + [vmem] * (2 + len(divisors) + len(order)),
        out_specs=(vmem, vmem),
        scratch_shapes=[
            pltpu.VMEM((slab_depth + 2, SUBLANES, column_count // 2), F32),
            pltpu.VMEM((SUBLANES, column_count), F32),
        ]
        + [pltpu.VMEM((SUBLANES, wide), F32)] * 2,
        compiler_params=small,
        name="update",
    )(view_angle, subset, *map(here, (volume, measured, *divisors, *blocks)))


def solution(mesh):
    in_specs = (
        P(("scan", "slab"), None, None),
        P(("scan", "slab"), None, None),
        P("scan"),
        P("scan"),
        P("scan"),
    )
    out_specs = (P(("scan", "slab"), None, None), P(("scan", "slab"), None, None))
    return jax.shard_map(
        per_device, mesh=mesh, in_specs=in_specs, out_specs=out_specs, check_vma=False
    )
```

```python
import functools
import math

import jax
import jax.numpy as jnp
import numpy as np
from jax import lax
from jax.experimental import pallas as pl
from jax.experimental.pallas import tpu as pltpu
from jax.sharding import PartitionSpec as P

ANGLES = 180
LIFT = 6
PITCH = 0.9
MAG_BASE = 1.5
ECCENTRIC = 0.12
LEN_FLOOR = 0.25
LANES = 128
SUBLANES = 8
F32 = jnp.float32
VMEM_LIMIT = 8 * 1024 * 1024


def angle_table():
    radians = (np.arange(ANGLES) + 0.5) * (0.5 * math.pi / ANGLES) - 0.25 * math.pi
    magnify = MAG_BASE / (1.0 - ECCENTRIC * np.sin(2.0 * radians + 1.0))
    return np.cos(radians), magnify


def slab_reach(slab_count, slab_depth, row_share):
    _, magnify = angle_table()
    total_rows, total_slices = row_share * slab_count, slab_depth * slab_count
    rows = np.arange(total_rows)
    reach = 0
    for lift in range(-LIFT, LIFT + 1):
        sample = (rows[None] + 0.5 - total_rows / 2 - lift) / magnify[:, None] + total_slices / 2 - 0.5
        for tap in (np.floor(sample - 1e-3), np.floor(sample + 1e-3) + 1):
            inside = (tap >= 0) & (tap < total_slices)
            distance = np.abs(tap // slab_depth - rows[None] // row_share)
            reach = max(reach, int(distance[inside].max()))
    return reach


def lane_index():
    return lax.broadcasted_iota(jnp.int32, (SUBLANES, LANES), 1)


def sublane_index():
    return lax.broadcasted_iota(jnp.int32, (SUBLANES, LANES), 0)


def angle_facts(index):
    x = (index.astype(F32) + 0.5) * (0.5 * math.pi / ANGLES) - 0.25 * math.pi
    s = x * x
    sine = x * (1.0 + s * (-1 / 6 + s * (1 / 120 + s * (-1 / 5040 + s * (1 / 362880)))))
    cosine = 1.0 + s * (-1 / 2 + s * (1 / 24 + s * (-1 / 720 + s * (1 / 40320 + s * (-1 / 3628800)))))
    double = 2.0 * sine * cosine * math.cos(1.0) + (1.0 - 2.0 * sine * sine) * math.sin(1.0)
    return cosine, sine / cosine, (1.0 - ECCENTRIC * double) * (1.0 / MAG_BASE)


def spread_scalars(read, count, place):
    out = jnp.full((SUBLANES, LANES), read(0), jnp.int32)
    for item in range(1, count):
        out = jnp.where(place == item, read(item), out)
    return out


def pick(tile, index):
    numbers = lax.GatherDimensionNumbers(
        offset_dims=(),
        collapsed_slice_dims=(1,),
        start_index_map=(1,),
        operand_batching_dims=(0,),
        start_indices_batching_dims=(0,),
    )
    return lax.gather(tile, index[..., None], numbers, (1, 1), mode=lax.GatherScatterMode.PROMISE_IN_BOUNDS)


def next_lane(tile, following):
    lane = lane_index()
    return jnp.where(lane < LANES - 1, pltpu.roll(tile, LANES - 1, 1), pltpu.roll(following, LANES - 1, 1))


def rows_summed(parts):
    sub = sublane_index()
    step = 1
    while step < SUBLANES:
        low = jnp.bitwise_and(sub, step) == 0
        parts = [
            jnp.where(low, a, b) + pltpu.roll(jnp.where(low, b, a), step, 0) for a, b in zip(parts[::2], parts[1::2])
        ]
        step *= 2
    return parts[0]


def tile_of(ref, lead, tile):
    whole = (slice(None),) * (len(ref.shape) - 1 - len(lead))
    return ref[lead + whole + (slice(tile * LANES, (tile + 1) * LANES),)]


def column_center(column, cosine, column_count, cell_count):
    return (column + 0.5 - column_count / 2) * (PITCH * cell_count / column_count) / cosine + (
        cell_count / 2 - 0.5
    )


def shear_steps(group, row_count, tangent):
    row = (sublane_index() + group * SUBLANES).astype(F32)
    offset = (row + 0.5 - row_count / 2) * tangent
    whole = jnp.floor(offset)
    return whole.astype(jnp.int32), offset - whole


def cone_sample(rows, lifts, flat, total_rows, total_slices):
    return (rows + 0.5 - total_rows / 2 - lifts) * flat + (total_slices / 2 - 0.5)


def cone_total(sample, total_slices):
    whole = jnp.floor(sample)
    fraction = sample - whole
    low = jnp.where((whole >= 0) & (whole < total_slices), 1.0 - fraction, 0.0)
    return low + jnp.where((whole >= -1) & (whole < total_slices - 1), fraction, 0.0)


def column_of(tile, at):
    return jnp.broadcast_to(tile[:, at : at + 1], (SUBLANES, LANES))


def subset_cone(slab, slab_count, order, slab_depth, row_share, flat, lifts):
    lane = lane_index()
    total_rows, total_slices = row_share * slab_count, slab_depth * slab_count
    origin = slabs_of(slab, order)
    source = sum(jnp.where(lane >= row_share * b, 1, 0) for b in range(1, len(order)))
    rows = spread_scalars(lambda b: origin[b], len(order), source) * row_share + (lane - source * row_share)
    real = (rows >= 0) & (rows < total_rows) & (lane < row_share * len(order))
    sample = cone_sample(rows.astype(F32), lifts, flat, total_rows, total_slices)
    weights = []
    for z in range(-1, slab_depth + 1):
        at = slab * slab_depth + z
        use = real & (at >= 0) & (at < total_slices)
        weights.append(jnp.where(use, jnp.maximum(0.0, 1.0 - jnp.abs(sample - at.astype(F32))), 0.0))
    return sample, weights


def slabs_of(slab, order):
    return [slab + (1 - 2 * lax.rem(slab, 2)) * away for away in order]


def adjoint_taps(tile, cosine, column_count, cell_count, half):
    spacing = PITCH * cell_count / column_count
    cell = (lane_index() + (tile * LANES - half)).astype(F32)
    inside = (cell >= 0) & (cell < cell_count)
    first = jnp.floor((cell - (cell_count / 2 + 0.5)) * cosine * (1.0 / spacing) + (column_count / 2 - 0.5 - 1e-3)) + 1.0
    taps = []
    for tap in range(3):
        column = first + tap
        weight = jnp.maximum(0.0, 1.0 - jnp.abs(cell - column_center(column, cosine, column_count, cell_count)))
        weight = jnp.where(inside & (column >= 0) & (column < column_count), weight, 0.0)
        taps.append((jnp.clip(column.astype(jnp.int32), 0, column_count - 1), weight))
    return taps


def adjoint_tiles(tile, tap, column_count, cell_count, half):
    spacing = PITCH * cell_count / column_count
    least = angle_table()[0].min()
    ends = [
        (tile * LANES - half + e - cell_count / 2 - 0.5) * c / spacing + column_count / 2 + 0.5
        for e in (0, LANES - 1)
        for c in (1.0, least)
    ]
    low = min(max(math.floor(min(ends) + tap - 0.6), 0), column_count - 1) // LANES
    high = min(max(math.ceil(max(ends) + tap + 0.6), 0), column_count - 1) // LANES
    return range(low, high + 1)


def store_line(line, base_ref, bend_ref):
    line = line + [jnp.zeros((SUBLANES, LANES), F32)]
    for tile in range(len(line) - 1):
        cut = slice(tile * LANES, (tile + 1) * LANES)
        base_ref[:, cut] = line[tile]
        bend_ref[:, cut] = next_lane(line[tile], line[tile + 1]) - line[tile]


def adjoint_steps(group, row_count, tangent):
    whole, fraction = shear_steps(group, row_count, tangent)
    place = lane_index() + (row_count // 2 - 1 - whole)
    return jnp.bitwise_and(place, LANES - 1), place < LANES, 1.0 - fraction


def sheared(base_ref, bend_ref, row, step, tiles):
    index, near, share = step
    before, out = None, []
    for tile in range(tiles + 1):
        cut = slice(tile * LANES, (tile + 1) * LANES)
        low = jnp.broadcast_to(base_ref[row : row + 1, cut], (SUBLANES, LANES))
        rise = jnp.broadcast_to(bend_ref[row : row + 1, cut], (SUBLANES, LANES))
        after = pick(low + share * rise, index)
        if tile:
            out.append(jnp.where(near, before, after))
        before = after
    return out


def subset_angles(angle_ref, lift_ref, subset_ref):
    members = subset_ref.shape[0]
    member = jnp.bitwise_and(sublane_index(), members - 1)
    cosine, _, flat = angle_facts(spread_scalars(lambda k: angle_ref[subset_ref[k]], members, member))
    lifts = spread_scalars(lambda k: lift_ref[subset_ref[k]], members, member).astype(F32)
    return cosine, flat, lifts


def member_tangents(angle_ref, subset_ref):
    indices = [angle_ref[subset_ref[k]] for k in range(subset_ref.shape[0])]
    return [angle_facts(jnp.full((SUBLANES, LANES), i, jnp.int32))[1] for i in indices]


def project_kernel(
    angle_ref,
    subset_ref,
    volume_ref,
    measured_ref,
    block_ref,
    cover_ref,
    rise_ref,
    first_ref,
    part_ref,
    end_ref,
    cell_ref,
    slope_ref,
):
    slab_depth, row_count, cell_count = volume_ref.shape
    row_share, view_count, column_count = measured_ref.shape
    subset_count = subset_ref.shape[0]
    half = row_count // 2
    tiles = cell_count // LANES
    groups = row_count // SUBLANES
    lane, sub = lane_index(), sublane_index()
    zero = jnp.zeros((SUBLANES, LANES), F32)
    width = column_count // 2

    for row in range(row_share):
        for member in range(subset_count):
            view = subset_ref[member]
            for side in range(2):
                block_ref[2 * slab_depth + row, side * subset_count + member : side * subset_count + member + 1, :] = (
                    measured_ref[row, pl.ds(view, 1), side * width : (side + 1) * width]
                )

    for depth in range(slab_depth):
        for group in range(groups):
            band = slice(group * SUBLANES, (group + 1) * SUBLANES)
            cells = [tile_of(volume_ref, (depth, band), tile) for tile in range(tiles)] + [zero]
            for tile in range(tiles):
                rise_ref[depth, band, tile * LANES : (tile + 1) * LANES] = (
                    next_lane(cells[tile], cells[tile + 1]) - cells[tile]
                )
            first_ref[depth, band, :] = column_of(cells[0], 0)

    def one_view(view, carry):
        _, tangent, _ = angle_facts(jnp.full((SUBLANES, LANES), angle_ref[view], jnp.int32))
        low_end, high_end = zero, zero
        sums = [[zero] * (tiles + 1) for _ in range(slab_depth)]
        for group in range(groups):
            band = slice(group * SUBLANES, (group + 1) * SUBLANES)
            whole, fraction = shear_steps(group, row_count, tangent)
            place = lane + (whole + half)
            index = jnp.bitwise_and(place, LANES - 1)
            near, last = place < LANES, index == LANES - 1
            enter = jnp.where(last, fraction, 0.0)
            low_end = low_end + jnp.where(near, enter, 1.0)
            high_end = high_end + jnp.where(near, 1.0 - enter, 0.0)
            for depth in range(slab_depth):
                before = enter * first_ref[depth, band, :]
                for tile in range(tiles + 1):
                    after = zero
                    if tile < tiles:
                        at = (depth, band)
                        after = pick(tile_of(volume_ref, at, tile) + fraction * tile_of(rise_ref, at, tile), index)
                    sums[depth][tile] = sums[depth][tile] + jnp.where(near, before, after)
                    before = after
        end_ref[0, view, :, :] = low_end
        end_ref[1, view, :, :] = high_end
        for depth in range(slab_depth):
            for tile in range(tiles + 1):
                part_ref[depth, view, :, tile * LANES : (tile + 1) * LANES] = sums[depth][tile]
        return carry

    lax.fori_loop(0, view_count, one_view, 0, unroll=4)

    shift = LANES - half
    inside = [None] * (tiles + 1)
    inside[0], inside[tiles] = lane >= shift, lane < shift

    def store(at, line):
        line = [jnp.where(mask, cells, 0.0) if mask is not None else cells for cells, mask in zip(line, inside)] + [zero]
        for tile in range(tiles + 1):
            cut = slice(tile * LANES, (tile + 1) * LANES)
            cell_ref[at, :, cut] = line[tile]
            slope_ref[at, :, cut] = next_lane(line[tile], line[tile + 1]) - line[tile]

    views = range(view_count)
    for depth in range(slab_depth):
        store(depth, [rows_summed([tile_of(part_ref, (depth, v), t) for v in views]) for t in range(tiles + 1)])
    flat = zero + float(row_count)
    ends = [rows_summed([end_ref[e, v, :, :] for v in views]) for e in range(2)]
    store(slab_depth, [ends[0]] + [flat] * (tiles - 1) + [ends[1]])

    cosine, _, _ = angle_facts(spread_scalars(lambda v: angle_ref[v], view_count, sub))
    factor = 1.0 / (row_count * cosine)
    least = angle_table()[0].min()
    for tile in range(column_count // LANES):
        column = (lane + tile * LANES).astype(F32)
        center = column_center(column, cosine, column_count, cell_count)
        whole = jnp.floor(center)
        fraction = center - whole
        place = jnp.clip(whole.astype(jnp.int32) + shift, shift - 2, shift + cell_count)
        block, index = jnp.right_shift(place, 7), jnp.bitwise_and(place, LANES - 1)
        ends = [column_center(tile * LANES + e, c, column_count, cell_count) for e in (0, LANES - 1) for c in (1.0, least)]
        low = min(max(math.floor(min(ends) - 1e-2) + shift, shift - 2), shift + cell_count) // LANES
        high = min(max(math.floor(max(ends) + 1e-2) + shift, shift - 2), shift + cell_count) // LANES
        cells, slopes = [zero] * slab_depth + [flat], [zero] * (slab_depth + 1)
        for source in range(low, high + 1):
            here = block == source
            for at in range(slab_depth + 1):
                if at == slab_depth and source not in (0, tiles):
                    continue
                cells[at] = jnp.where(here, pick(tile_of(cell_ref, (at,), source), index), cells[at])
                slopes[at] = jnp.where(here, pick(tile_of(slope_ref, (at,), source), index), slopes[at])
        profiles = [(c + fraction * s) * factor for c, s in zip(cells, slopes)]
        side, inner = divmod(tile * LANES, width)
        for depth in range(slab_depth):
            block_ref[depth * 2 + side, :, inner : inner + LANES] = profiles[depth]
        cover_ref[:, tile * LANES : (tile + 1) * LANES] = profiles[slab_depth]


def divisor_kernel(
    slab_count,
    order,
    angle_ref,
    lift_ref,
    subset_ref,
    cover_ref,
    bound_ref,
    own_ref,
    rows_ref,
    own_cone_ref,
    cone_ref,
    place_ref,
    tap_ref,
    edge_ref,
    bend_ref,
    sub_ref,
):
    slab_depth, row_count, cell_count = bound_ref.shape
    row_share, view_count, column_count = own_ref.shape
    subset_count = subset_ref.shape[0]
    total_rows, total_slices = row_share * slab_count, slab_depth * slab_count
    tiles, columns = cell_count // LANES, column_count // LANES
    width = column_count // 2
    sub = sublane_index()
    zero = jnp.zeros((SUBLANES, LANES), F32)
    slab = lax.axis_index("slab")

    _, _, flat = angle_facts(spread_scalars(lambda v: angle_ref[v], view_count, sub))
    lifts = spread_scalars(lambda v: lift_ref[v], view_count, sub).astype(F32)
    lane = lane_index()
    origin = slabs_of(slab, order)
    source = sum(jnp.where(lane >= slab_depth * b, 1, 0) for b in range(1, len(order)))
    slices = spread_scalars(lambda b: origin[b], len(order), source) * slab_depth + (lane - source * slab_depth)
    held = (slices >= 0) & (slices < total_slices)
    slices = slices.astype(F32)
    for row in range(row_share):
        sample = cone_sample((slab * row_share + row).astype(F32), lifts, flat, total_rows, total_slices)
        weights = jnp.where(held, jnp.maximum(0.0, 1.0 - jnp.abs(sample - slices)), 0.0)
        for place in range(slab_depth * len(order)):
            own_cone_ref[place, row, :, :] = column_of(weights, place)
        total = cone_total(sample, total_slices)
        for tile in range(columns):
            cut = slice(tile * LANES, (tile + 1) * LANES)
            own_ref[row, :, cut] = 1.0 / jnp.maximum(total * cover_ref[:, cut], LEN_FLOOR)

    cosine, flat, lifts = subset_angles(angle_ref, lift_ref, subset_ref)
    tangents = member_tangents(angle_ref, subset_ref)
    for member in range(subset_count):
        view = pl.ds(subset_ref[member], 1)
        for side in range(2):
            at = slice(side * subset_count + member, side * subset_count + member + 1)
            sub_ref[at, :] = cover_ref[view, side * width : (side + 1) * width]
    sample, weights = subset_cone(slab, slab_count, order, slab_depth, row_share, flat, lifts)
    total = cone_total(sample, total_slices)
    for place in range(row_share * len(order)):
        for z, w in enumerate(weights):
            cone_ref[place, z, :, :] = column_of(w, place)
        length = column_of(total, place)
        for tile in range(width // LANES):
            cut = slice(tile * LANES, (tile + 1) * LANES)
            rows_ref[place, :, cut] = 1.0 / jnp.maximum(length * sub_ref[:, cut], LEN_FLOOR)

    factor = 1.0 / (row_count * cosine)
    line = []
    for tile in range(tiles + 1):
        taps = adjoint_taps(tile, cosine, column_count, cell_count, row_count // 2)
        for tap, (place, weight) in enumerate(taps):
            place_ref[tile, tap, :, :] = place
            tap_ref[tile, tap, :, :] = weight * factor
        line.append(sum(weight for _, weight in taps) * factor)
    store_line(line, edge_ref, bend_ref)
    slice_total = []
    for depth in range(slab_depth):
        t = jnp.sum(weights[1 + depth], axis=1, keepdims=True)
        slice_total.append([jnp.broadcast_to(t[k : k + 1], (SUBLANES, LANES)) for k in range(subset_count)])

    def one_group(group, carry):
        band = pl.ds(pl.multiple_of(group * SUBLANES, SUBLANES), SUBLANES)
        weight = [[zero] * tiles for _ in range(slab_depth)]
        for member in range(subset_count):
            line = sheared(edge_ref, bend_ref, member, adjoint_steps(group, row_count, tangents[member]), tiles)
            for depth in range(slab_depth):
                for tile in range(tiles):
                    weight[depth][tile] = weight[depth][tile] + slice_total[depth][member] * line[tile]
        for depth in range(slab_depth):
            for tile in range(tiles):
                bound_ref[depth, band, tile * LANES : (tile + 1) * LANES] = 1.0 / jnp.maximum(
                    weight[depth][tile], LEN_FLOOR * subset_count / row_count
                )
        return carry

    lax.fori_loop(0, row_count // SUBLANES, one_group, 0)


def update_kernel(
    order,
    angle_ref,
    subset_ref,
    volume_ref,
    measured_ref,
    bound_ref,
    own_ref,
    rows_ref,
    own_cone_ref,
    cone_ref,
    place_ref,
    tap_ref,
    *refs,
):
    blocks = refs[: len(order)]
    residual_ref, updated_ref, profile_ref, spread_ref, cell_ref, slope_ref, rest_ref, new_ref, sent = refs[len(order) :]
    slab_depth, row_count, cell_count = volume_ref.shape
    row_share, view_count, column_count = measured_ref.shape
    subset_count = subset_ref.shape[0]
    tiles, columns = cell_count // LANES, column_count // LANES
    width = column_count // 2
    zero = jnp.zeros((SUBLANES, LANES), F32)
    odd = lax.rem(lax.axis_index("slab"), 2)
    mate_block, other_block = (blocks[order.index(away)] for away in (1, -1))

    groups = row_count // SUBLANES
    for tile in range(columns):
        side, inner = divmod(tile * LANES, width)
        image = [zero] * row_share
        for place, block in enumerate(blocks):
            for depth in range(slab_depth):
                cells = block[depth * 2 + side, :, inner : inner + LANES]
                for row in range(row_share):
                    image[row] = image[row] + own_cone_ref[place * slab_depth + depth, row, :, :] * cells
        cut = slice(tile * LANES, (tile + 1) * LANES)
        for row in range(row_share):
            rest_ref[row, :, cut] = (measured_ref[row, :, cut] - image[row]) * own_ref[row, :, cut]
    copies = [pltpu.make_async_copy(rest_ref, residual_ref, sent.at[groups])]
    copies[0].start()

    for member in range(subset_count):
        view = pl.ds(subset_ref[member], 1)
        for side in range(2):
            at = slice(side * subset_count + member, side * subset_count + member + 1)
            other = other_block[(slab_depth - 1) * 2 + side, view, :], other_block[side, view, :]
            mate = mate_block[(slab_depth - 1) * 2 + side, view, :], mate_block[side, view, :]
            profile_ref[0, at, :] = jnp.where(odd == 0, other[0], mate[0])
            for depth in range(slab_depth):
                profile_ref[1 + depth, at, :] = blocks[0][depth * 2 + side, view, :]
            profile_ref[1 + slab_depth, at, :] = jnp.where(odd == 0, mate[1], other[1])

    inner_tiles = width // LANES
    spread = [[zero] * inner_tiles for _ in range(slab_depth)]
    for place in range(row_share * len(order)):
        weight = [cone_ref[place, z, :, :] for z in range(slab_depth + 2)]
        block, row = blocks[place // row_share], place % row_share
        for tile in range(inner_tiles):
            cut = slice(tile * LANES, (tile + 1) * LANES)
            image = weight[0] * profile_ref[0, :, cut]
            for z in range(1, slab_depth + 2):
                image = image + weight[z] * profile_ref[z, :, cut]
            rest = (block[2 * slab_depth + row, :, cut] - image) * rows_ref[place, :, cut]
            for depth in range(slab_depth):
                spread[depth][tile] = spread[depth][tile] + weight[1 + depth] * rest
    for depth in range(slab_depth):
        for tile in range(inner_tiles):
            for side in range(2):
                spread_ref[
                    depth * subset_count : (depth + 1) * subset_count,
                    side * width + tile * LANES : side * width + (tile + 1) * LANES,
                ] = spread[depth][tile][side * subset_count : (side + 1) * subset_count]

    line = []
    for tile in range(tiles + 1):
        value = zero
        for tap in range(3):
            place = place_ref[tile, tap, :, :]
            block, index = jnp.right_shift(place, 7), jnp.bitwise_and(place, LANES - 1)
            found = zero
            for at in adjoint_tiles(tile, tap, column_count, cell_count, row_count // 2):
                found = jnp.where(block == at, pick(tile_of(spread_ref, (), at), index), found)
            value = value + tap_ref[tile, tap, :, :] * found
        line.append(value)
    store_line(line, cell_ref, slope_ref)

    tangents = member_tangents(angle_ref, subset_ref)
    for group in range(groups):
        band = slice(group * SUBLANES, (group + 1) * SUBLANES)
        back = [[zero] * tiles for _ in range(slab_depth)]
        for member in range(subset_count):
            step = adjoint_steps(group, row_count, tangents[member])
            for depth in range(slab_depth):
                line = sheared(cell_ref, slope_ref, depth * subset_count + member, step, tiles)
                back[depth] = [b + a for b, a in zip(back[depth], line)]
        for depth in range(slab_depth):
            for tile in range(tiles):
                cut = slice(tile * LANES, (tile + 1) * LANES)
                new_ref[depth, band, cut] = (
                    volume_ref[depth, band, cut] + back[depth][tile] * bound_ref[depth, band, cut]
                )
        copies.append(pltpu.make_async_copy(new_ref.at[:, band, :], updated_ref.at[:, band, :], sent.at[group]))
        copies[-1].start()
    for copy in copies:
        copy.wait()


def swapped(block):
    return lax.ppermute(block, "slab", [(i, i ^ 1) for i in range(lax.axis_size("slab"))])


def from_chip(block, distance):
    slabs = range(lax.axis_size("slab"))
    steps = [(i + 2 * distance * (1 - 2 * (i % 2)), i) for i in slabs]
    pairs = [p for p in steps if p[0] in slabs]
    idle = [i for i in slabs if i not in [p[0] for p in pairs]]
    unmet = [i for i in slabs if i not in [p[1] for p in pairs]]
    near = [i for i in idle if i ^ 1 in unmet]
    pairs += [(i, i ^ 1) for i in near]
    pairs += zip([i for i in idle if i not in near], [i for i in unmet if i ^ 1 not in near])
    return lax.ppermute(block, "slab", pairs)


def fetches(reach):
    return [s * d for d in range(1, reach // 2 + 2) for s in (-1, 1) if 2 * d - (s > 0) <= reach]


def window(reach):
    order = [0, 1]
    for distance in fetches(reach):
        order += [at for at in (2 * distance, 1 - 2 * distance) if abs(at) <= reach]
    assert sorted(order) == list(range(-reach, reach + 1))
    return tuple(order)


def gathered(own, reach, meanwhile):
    received = {distance: from_chip(own, distance) for distance in fetches(reach)}
    blocks = {0: own, 1: swapped(own)}
    done = meanwhile()
    for part in ([d for d in received if abs(d) > 1], [-1, 1]):
        arrived, done = lax.optimization_barrier(([received[d] for d in part], done))
        for distance, block in zip(part, arrived):
            if 2 * abs(distance) <= reach:
                blocks[2 * distance] = block
            if abs(1 - 2 * distance) <= reach:
                blocks[1 - 2 * distance] = swapped(block)
    return [blocks[away] for away in window(reach)], done


def per_device(volume, measured, view_angle, view_lift, subset):
    slab_count = lax.axis_size("slab")
    slab_depth, row_count, cell_count = volume.shape
    row_share, view_count, column_count = measured.shape
    subset_count = subset.shape[0]
    tiles = cell_count // LANES
    reach = slab_reach(slab_count, slab_depth, row_share)
    here = lambda x: pltpu.with_memory_space_constraint(x, pltpu.VMEM)
    there = lambda x: pltpu.with_memory_space_constraint(x, pltpu.HBM)
    small = pltpu.CompilerParams(vmem_limit_bytes=VMEM_LIMIT)
    smem, vmem = pl.BlockSpec(memory_space=pltpu.SMEM), pl.BlockSpec(memory_space=pltpu.VMEM)
    wide = (tiles + 1) * LANES
    block_shape = (2 * slab_depth + row_share, SUBLANES, column_count // 2)
    own, cover = pl.pallas_call(
        project_kernel,
        out_shape=(
            pltpu.VMEM(block_shape, F32),
            pltpu.VMEM((view_count, column_count), F32),
        ),
        in_specs=[smem, smem, vmem, vmem],
        out_specs=(vmem, vmem),
        scratch_shapes=[
            pltpu.VMEM(volume.shape, F32),
            pltpu.VMEM((slab_depth, row_count, LANES), F32),
            pltpu.VMEM((slab_depth, view_count, SUBLANES, wide), F32),
            pltpu.VMEM((2, view_count, SUBLANES, LANES), F32),
        ]
        + [pltpu.VMEM((slab_depth + 1, SUBLANES, wide), F32)] * 2,
        compiler_params=small,
        name="project",
    )(*map(there, (view_angle, subset, volume, measured)))
    cover = here(cover)
    order = window(reach)
    divide = pl.pallas_call(
        functools.partial(divisor_kernel, slab_count, order),
        out_shape=(
            pltpu.VMEM(volume.shape, F32),
            pltpu.VMEM(measured.shape, F32),
            pltpu.VMEM((row_share * len(order), SUBLANES, column_count // 2), F32),
            pltpu.VMEM((slab_depth * len(order), row_share, SUBLANES, LANES), F32),
            pltpu.VMEM((row_share * len(order), slab_depth + 2, SUBLANES, LANES), F32),
            pltpu.VMEM((tiles + 1, 3, SUBLANES, LANES), jnp.int32),
            pltpu.VMEM((tiles + 1, 3, SUBLANES, LANES), F32),
        ),
        in_specs=[smem] * 3 + [vmem],
        out_specs=(vmem,) * 7,
        scratch_shapes=[pltpu.VMEM((SUBLANES, wide), F32)] * 2 + [pltpu.VMEM((SUBLANES, column_count // 2), F32)],
        cost_estimate=pl.CostEstimate(flops=4_000_000, bytes_accessed=8_000_000, transcendentals=0),
        compiler_params=small,
        name="divisors",
    )
    blocks, divisors = gathered(own, reach, lambda: divide(view_angle, view_lift, subset, cover))
    return pl.pallas_call(
        functools.partial(update_kernel, order),
        out_shape=(
            jax.ShapeDtypeStruct(measured.shape, F32),
            jax.ShapeDtypeStruct(volume.shape, F32),
        ),
        in_specs=[smem] * 2 + [vmem] * (2 + len(divisors) + len(order)),
        out_specs=(pl.BlockSpec(memory_space=pl.ANY),) * 2,
        scratch_shapes=[
            pltpu.VMEM((slab_depth + 2, SUBLANES, column_count // 2), F32),
            pltpu.VMEM((SUBLANES, column_count), F32),
            pltpu.VMEM((SUBLANES, wide), F32),
            pltpu.VMEM((SUBLANES, wide), F32),
            pltpu.VMEM(measured.shape, F32),
            pltpu.VMEM(volume.shape, F32),
            pltpu.SemaphoreType.DMA((row_count // SUBLANES + 1,)),
        ],
        compiler_params=small,
        name="update",
    )(view_angle, subset, *map(here, (volume, measured, *divisors, *blocks)))


def solution(mesh):
    in_specs = (
        P(("scan", "slab"), None, None),
        P(("scan", "slab"), None, None),
        P("scan"),
        P("scan"),
        P("scan"),
    )
    out_specs = (P(("scan", "slab"), None, None), P(("scan", "slab"), None, None))
    return jax.shard_map(
        per_device, mesh=mesh, in_specs=in_specs, out_specs=out_specs, check_vma=False
    )
```

```python
import functools
import math

import jax
import jax.numpy as jnp
import numpy as np
from jax import lax
from jax.experimental import pallas as pl
from jax.experimental.pallas import tpu as pltpu
from jax.sharding import PartitionSpec as P

ANGLES = 180
LIFT = 6
PITCH = 0.9
MAG_BASE = 1.5
ECCENTRIC = 0.12
LEN_FLOOR = 0.25
LANES = 128
SUBLANES = 8
F32 = jnp.float32
FULL, NEAR, NEAR_SHARED, FAR = range(4)
VMEM_LIMIT = 8 * 1024 * 1024


def angle_table():
    radians = (np.arange(ANGLES) + 0.5) * (0.5 * math.pi / ANGLES) - 0.25 * math.pi
    magnify = MAG_BASE / (1.0 - ECCENTRIC * np.sin(2.0 * radians + 1.0))
    return np.cos(radians), magnify


def slab_reach(slab_count, slab_depth, row_share):
    _, magnify = angle_table()
    total_rows, total_slices = row_share * slab_count, slab_depth * slab_count
    rows = np.arange(total_rows)
    reach = 0
    for lift in range(-LIFT, LIFT + 1):
        sample = (rows[None] + 0.5 - total_rows / 2 - lift) / magnify[:, None] + total_slices / 2 - 0.5
        for tap in (np.floor(sample - 1e-3), np.floor(sample + 1e-3) + 1):
            inside = (tap >= 0) & (tap < total_slices)
            distance = np.abs(tap // slab_depth - rows[None] // row_share)
            reach = max(reach, int(distance[inside].max()))
    return reach


def lane_index():
    return lax.broadcasted_iota(jnp.int32, (SUBLANES, LANES), 1)


def sublane_index():
    return lax.broadcasted_iota(jnp.int32, (SUBLANES, LANES), 0)


def angle_facts(index):
    x = (index.astype(F32) + 0.5) * (0.5 * math.pi / ANGLES) - 0.25 * math.pi
    s = x * x
    sine = x * (1.0 + s * (-1 / 6 + s * (1 / 120 + s * (-1 / 5040 + s * (1 / 362880)))))
    cosine = 1.0 + s * (-1 / 2 + s * (1 / 24 + s * (-1 / 720 + s * (1 / 40320 + s * (-1 / 3628800)))))
    double = 2.0 * sine * cosine * math.cos(1.0) + (1.0 - 2.0 * sine * sine) * math.sin(1.0)
    return cosine, sine / cosine, (1.0 - ECCENTRIC * double) * (1.0 / MAG_BASE)


def spread_scalars(read, count, place):
    out = jnp.full((SUBLANES, LANES), read(0), jnp.int32)
    for item in range(1, count):
        out = jnp.where(place == item, read(item), out)
    return out


def pick(tile, index):
    numbers = lax.GatherDimensionNumbers(
        offset_dims=(),
        collapsed_slice_dims=(1,),
        start_index_map=(1,),
        operand_batching_dims=(0,),
        start_indices_batching_dims=(0,),
    )
    return lax.gather(tile, index[..., None], numbers, (1, 1), mode=lax.GatherScatterMode.PROMISE_IN_BOUNDS)


def next_lane(tile, following):
    lane = lane_index()
    return jnp.where(lane < LANES - 1, pltpu.roll(tile, LANES - 1, 1), pltpu.roll(following, LANES - 1, 1))


def rows_summed(parts):
    sub = sublane_index()
    step = 1
    while step < SUBLANES:
        low = jnp.bitwise_and(sub, step) == 0
        parts = [
            jnp.where(low, a, b) + pltpu.roll(jnp.where(low, b, a), step, 0) for a, b in zip(parts[::2], parts[1::2])
        ]
        step *= 2
    return parts[0]


def tile_of(ref, lead, tile):
    whole = (slice(None),) * (len(ref.shape) - 1 - len(lead))
    return ref[lead + whole + (slice(tile * LANES, (tile + 1) * LANES),)]


def column_center(column, cosine, column_count, cell_count):
    return (column + 0.5 - column_count / 2) * (PITCH * cell_count / column_count) / cosine + (
        cell_count / 2 - 0.5
    )


def shear_steps(group, row_count, tangent):
    row = (sublane_index() + group * SUBLANES).astype(F32)
    offset = (row + 0.5 - row_count / 2) * tangent
    whole = jnp.floor(offset)
    return whole.astype(jnp.int32), offset - whole


def cone_sample(rows, lifts, flat, total_rows, total_slices):
    return (rows + 0.5 - total_rows / 2 - lifts) * flat + (total_slices / 2 - 0.5)


def cone_total(sample, total_slices):
    whole = jnp.floor(sample)
    fraction = sample - whole
    low = jnp.where((whole >= 0) & (whole < total_slices), 1.0 - fraction, 0.0)
    return low + jnp.where((whole >= -1) & (whole < total_slices - 1), fraction, 0.0)


def column_of(tile, at):
    return jnp.broadcast_to(tile[:, at : at + 1], (SUBLANES, LANES))


def slabs_of(slab, order):
    return [slab + (1 - 2 * lax.rem(slab, 2)) * away for away in order]


def turned(slab, kinds):
    odd = lax.rem(slab, 2)
    return [{NEAR: 1 - odd, NEAR_SHARED: odd}.get(kind, 0) for kind in kinds]


def subset_cone(slab, slab_count, order, kinds, slab_depth, row_share, flat, lifts):
    lane = lane_index()
    total_rows, total_slices = row_share * slab_count, slab_depth * slab_count
    origin, turns = slabs_of(slab, order), turned(slab, kinds)
    source = sum(jnp.where(lane >= row_share * b, 1, 0) for b in range(1, len(order)))
    within = lane - source * row_share
    within = jnp.where(spread_scalars(lambda b: turns[b], len(order), source) == 1, row_share - 1 - within, within)
    rows = spread_scalars(lambda b: origin[b], len(order), source) * row_share + within
    real = (rows >= 0) & (rows < total_rows) & (lane < row_share * len(order))
    sample = cone_sample(rows.astype(F32), lifts, flat, total_rows, total_slices)
    weights = []
    for z in range(-1, slab_depth + 1):
        at = slab * slab_depth + z
        use = real & (at >= 0) & (at < total_slices)
        weights.append(jnp.where(use, jnp.maximum(0.0, 1.0 - jnp.abs(sample - at.astype(F32))), 0.0))
    return sample, weights


def adjoint_taps(tile, cosine, column_count, cell_count, half):
    spacing = PITCH * cell_count / column_count
    cell = (lane_index() + (tile * LANES - half)).astype(F32)
    inside = (cell >= 0) & (cell < cell_count)
    first = jnp.floor((cell - (cell_count / 2 + 0.5)) * cosine * (1.0 / spacing) + (column_count / 2 - 0.5 - 1e-3)) + 1.0
    taps = []
    for tap in range(3):
        column = first + tap
        weight = jnp.maximum(0.0, 1.0 - jnp.abs(cell - column_center(column, cosine, column_count, cell_count)))
        weight = jnp.where(inside & (column >= 0) & (column < column_count), weight, 0.0)
        taps.append((jnp.clip(column.astype(jnp.int32), 0, column_count - 1), weight))
    return taps


def adjoint_tiles(tile, tap, column_count, cell_count, half):
    spacing = PITCH * cell_count / column_count
    least = angle_table()[0].min()
    ends = [
        (tile * LANES - half + e - cell_count / 2 - 0.5) * c / spacing + column_count / 2 + 0.5
        for e in (0, LANES - 1)
        for c in (1.0, least)
    ]
    low = min(max(math.floor(min(ends) + tap - 0.6), 0), column_count - 1) // LANES
    high = min(max(math.ceil(max(ends) + tap + 0.6), 0), column_count - 1) // LANES
    return range(low, high + 1)


def store_line(line, base_ref, bend_ref):
    line = line + [jnp.zeros((SUBLANES, LANES), F32)]
    for tile in range(len(line) - 1):
        cut = slice(tile * LANES, (tile + 1) * LANES)
        base_ref[:, cut] = line[tile]
        bend_ref[:, cut] = next_lane(line[tile], line[tile + 1]) - line[tile]


def adjoint_steps(group, row_count, tangent):
    whole, fraction = shear_steps(group, row_count, tangent)
    place = lane_index() + (row_count // 2 - 1 - whole)
    return jnp.bitwise_and(place, LANES - 1), place < LANES, 1.0 - fraction


def sheared(base_ref, bend_ref, row, step, tiles):
    index, near, share = step
    before, out = None, []
    for tile in range(tiles + 1):
        cut = slice(tile * LANES, (tile + 1) * LANES)
        low = jnp.broadcast_to(base_ref[row : row + 1, cut], (SUBLANES, LANES))
        rise = jnp.broadcast_to(bend_ref[row : row + 1, cut], (SUBLANES, LANES))
        after = pick(low + share * rise, index)
        if tile:
            out.append(jnp.where(near, before, after))
        before = after
    return out


def subset_angles(angle_ref, lift_ref, subset_ref):
    members = subset_ref.shape[0]
    member = jnp.bitwise_and(sublane_index(), members - 1)
    cosine, _, flat = angle_facts(spread_scalars(lambda k: angle_ref[subset_ref[k]], members, member))
    lifts = spread_scalars(lambda k: lift_ref[subset_ref[k]], members, member).astype(F32)
    return cosine, flat, lifts


def member_tangents(angle_ref, subset_ref):
    indices = [angle_ref[subset_ref[k]] for k in range(subset_ref.shape[0])]
    return [angle_facts(jnp.full((SUBLANES, LANES), i, jnp.int32))[1] for i in indices]


def project_kernel(
    slab_count,
    angle_ref,
    lift_ref,
    subset_ref,
    volume_ref,
    measured_ref,
    block_ref,
    near_ref,
    low_ref,
    high_ref,
    cover_ref,
    rise_ref,
    first_ref,
    part_ref,
    end_ref,
    cell_ref,
    slope_ref,
):
    slab_depth, row_count, cell_count = volume_ref.shape
    row_share, view_count, column_count = measured_ref.shape
    subset_count = subset_ref.shape[0]
    half = row_count // 2
    tiles = cell_count // LANES
    groups = row_count // SUBLANES
    lane, sub = lane_index(), sublane_index()
    zero = jnp.zeros((SUBLANES, LANES), F32)
    width = column_count // 2

    assert (slab_depth, row_share) == (2, 3)
    slab = lax.axis_index("slab")
    odd = lax.rem(slab, 2)
    grows = odd == 1
    far_row = jnp.where(grows, 2, 0)
    for member in range(subset_count):
        view = pl.ds(subset_ref[member], 1)
        for side in range(2):
            at, cut = side * subset_count + member, slice(side * width, (side + 1) * width)
            rows = [measured_ref[row, view, cut] for row in range(row_share)]
            for row in range(row_share):
                block_ref[2 * slab_depth + row, at : at + 1, :] = rows[row]
            near_ref[2 * slab_depth, at : at + 1, :] = rows[1]
            near_ref[2 * slab_depth + 1, at : at + 1, :] = measured_ref[far_row, view, cut]
            low_ref[2 * slab_depth, at : at + 1, :] = rows[2]
            high_ref[2 * slab_depth, at : at + 1, :] = rows[2]

    cosine, _, flat = angle_facts(spread_scalars(lambda v: angle_ref[v], view_count, sub))
    lifts = spread_scalars(lambda v: lift_ref[v], view_count, sub).astype(F32)
    ends = [
        cone_sample((slab * row_share + row).astype(F32), lifts, flat, row_share * slab_count, slab_depth * slab_count)
        - (slab * slab_depth).astype(F32)
        for row in (0, row_share - 1)
    ]
    picked = sub == subset_ref[0]
    for member in range(1, subset_count):
        picked = picked | (sub == subset_ref[member])
    picked = jnp.where(picked, 1, 0)
    as_int = lambda mask: jnp.where(mask, 1, 0)
    near_up, near_down = picked * as_int(ends[1] > 0.75), picked * as_int(ends[0] < 0.25)
    far_up, far_down = picked * as_int(ends[1] > 2.5), picked * as_int(ends[0] < -1.5)
    near_places = [(near_up * odd) == 1, (near_down * (1 - odd)) == 1]
    high_places = (far_up * odd + far_down * (1 - odd)) == 1
    low_places = (far_up * (1 - odd) + far_down * odd) == 1

    for depth in range(slab_depth):
        for group in range(groups):
            band = slice(group * SUBLANES, (group + 1) * SUBLANES)
            cells = [tile_of(volume_ref, (depth, band), tile) for tile in range(tiles)] + [zero]
            for tile in range(tiles):
                rise_ref[depth, band, tile * LANES : (tile + 1) * LANES] = (
                    next_lane(cells[tile], cells[tile + 1]) - cells[tile]
                )
            first_ref[depth, band, :] = column_of(cells[0], 0)

    def one_view(view, carry):
        _, tangent, _ = angle_facts(jnp.full((SUBLANES, LANES), angle_ref[view], jnp.int32))
        low_end, high_end = zero, zero
        sums = [[zero] * (tiles + 1) for _ in range(slab_depth)]
        for group in range(groups):
            band = slice(group * SUBLANES, (group + 1) * SUBLANES)
            whole, fraction = shear_steps(group, row_count, tangent)
            place = lane + (whole + half)
            index = jnp.bitwise_and(place, LANES - 1)
            near, last = place < LANES, index == LANES - 1
            enter = jnp.where(last, fraction, 0.0)
            low_end = low_end + jnp.where(near, enter, 1.0)
            high_end = high_end + jnp.where(near, 1.0 - enter, 0.0)
            for depth in range(slab_depth):
                before = enter * first_ref[depth, band, :]
                for tile in range(tiles + 1):
                    after = zero
                    if tile < tiles:
                        at = (depth, band)
                        after = pick(tile_of(volume_ref, at, tile) + fraction * tile_of(rise_ref, at, tile), index)
                    sums[depth][tile] = sums[depth][tile] + jnp.where(near, before, after)
                    before = after
        end_ref[0, view, :, :] = low_end
        end_ref[1, view, :, :] = high_end
        for depth in range(slab_depth):
            for tile in range(tiles + 1):
                part_ref[depth, view, :, tile * LANES : (tile + 1) * LANES] = sums[depth][tile]
        return carry

    lax.fori_loop(0, view_count, one_view, 0, unroll=4)

    shift = LANES - half
    inside = [None] * (tiles + 1)
    inside[0], inside[tiles] = lane >= shift, lane < shift

    def store(at, line):
        line = [jnp.where(mask, cells, 0.0) if mask is not None else cells for cells, mask in zip(line, inside)] + [zero]
        for tile in range(tiles + 1):
            cut = slice(tile * LANES, (tile + 1) * LANES)
            cell_ref[at, :, cut] = line[tile]
            slope_ref[at, :, cut] = next_lane(line[tile], line[tile + 1]) - line[tile]

    views = range(view_count)
    for depth in range(slab_depth):
        store(depth, [rows_summed([tile_of(part_ref, (depth, v), t) for v in views]) for t in range(tiles + 1)])
    level = zero + float(row_count)
    ends = [rows_summed([end_ref[e, v, :, :] for v in views]) for e in range(2)]
    store(slab_depth, [ends[0]] + [level] * (tiles - 1) + [ends[1]])

    factor = 1.0 / (row_count * cosine)
    least = angle_table()[0].min()
    for tile in range(column_count // LANES):
        column = (lane + tile * LANES).astype(F32)
        center = column_center(column, cosine, column_count, cell_count)
        whole = jnp.floor(center)
        fraction = center - whole
        place = jnp.clip(whole.astype(jnp.int32) + shift, shift - 2, shift + cell_count)
        block, index = jnp.right_shift(place, 7), jnp.bitwise_and(place, LANES - 1)
        ends = [column_center(tile * LANES + e, c, column_count, cell_count) for e in (0, LANES - 1) for c in (1.0, least)]
        low = min(max(math.floor(min(ends) - 1e-2) + shift, shift - 2), shift + cell_count) // LANES
        high = min(max(math.floor(max(ends) + 1e-2) + shift, shift - 2), shift + cell_count) // LANES
        cells, slopes = [zero] * slab_depth + [level], [zero] * (slab_depth + 1)
        for source in range(low, high + 1):
            here = block == source
            for at in range(slab_depth + 1):
                if at == slab_depth and source not in (0, tiles):
                    continue
                cells[at] = jnp.where(here, pick(tile_of(cell_ref, (at,), source), index), cells[at])
                slopes[at] = jnp.where(here, pick(tile_of(slope_ref, (at,), source), index), slopes[at])
        profiles = [(c + fraction * s) * factor for c, s in zip(cells, slopes)]
        side, inner = divmod(tile * LANES, width)
        for depth in range(slab_depth):
            to = (depth * 2 + side, slice(None), slice(inner, inner + LANES))
            measured = tile_of(measured_ref, (depth,), tile)
            last = tile_of(measured_ref, (depth * (row_share - 1),), tile)
            block_ref[to] = profiles[depth]
            near_ref[to] = jnp.where(near_places[depth], last, profiles[depth])
            low_ref[to] = jnp.where(low_places, measured, profiles[depth])
            high_ref[to] = jnp.where(high_places, measured, profiles[depth])
        cover_ref[:, tile * LANES : (tile + 1) * LANES] = profiles[slab_depth]


def divisor_kernel(
    slab_count,
    order,
    kinds,
    angle_ref,
    lift_ref,
    subset_ref,
    cover_ref,
    bound_ref,
    own_ref,
    rows_ref,
    own_cone_ref,
    cone_ref,
    place_ref,
    tap_ref,
    edge_ref,
    bend_ref,
    sub_ref,
):
    slab_depth, row_count, cell_count = bound_ref.shape
    row_share, view_count, column_count = own_ref.shape
    subset_count = subset_ref.shape[0]
    total_rows, total_slices = row_share * slab_count, slab_depth * slab_count
    tiles, columns = cell_count // LANES, column_count // LANES
    width = column_count // 2
    sub = sublane_index()
    zero = jnp.zeros((SUBLANES, LANES), F32)
    slab = lax.axis_index("slab")

    _, _, flat = angle_facts(spread_scalars(lambda v: angle_ref[v], view_count, sub))
    lifts = spread_scalars(lambda v: lift_ref[v], view_count, sub).astype(F32)
    lane = lane_index()
    origin = slabs_of(slab, order)
    source = sum(jnp.where(lane >= slab_depth * b, 1, 0) for b in range(1, len(order)))
    slices = spread_scalars(lambda b: origin[b], len(order), source) * slab_depth + (lane - source * slab_depth)
    held = (slices >= 0) & (slices < total_slices)
    slices = slices.astype(F32)
    for row in range(row_share):
        sample = cone_sample((slab * row_share + row).astype(F32), lifts, flat, total_rows, total_slices)
        weights = jnp.where(held, jnp.maximum(0.0, 1.0 - jnp.abs(sample - slices)), 0.0)
        for place in range(slab_depth * len(order)):
            own_cone_ref[place, row, :, :] = column_of(weights, place)
        total = cone_total(sample, total_slices)
        for tile in range(columns):
            cut = slice(tile * LANES, (tile + 1) * LANES)
            own_ref[row, :, cut] = 1.0 / jnp.maximum(total * cover_ref[:, cut], LEN_FLOOR)

    cosine, flat, lifts = subset_angles(angle_ref, lift_ref, subset_ref)
    tangents = member_tangents(angle_ref, subset_ref)
    for member in range(subset_count):
        view = pl.ds(subset_ref[member], 1)
        for side in range(2):
            at = slice(side * subset_count + member, side * subset_count + member + 1)
            sub_ref[at, :] = cover_ref[view, side * width : (side + 1) * width]
    sample, weights = subset_cone(slab, slab_count, order, kinds, slab_depth, row_share, flat, lifts)
    total = cone_total(sample, total_slices)
    for place in range(row_share * len(order)):
        for z, w in enumerate(weights):
            cone_ref[place, z, :, :] = column_of(w, place)
        length = column_of(total, place)
        for tile in range(width // LANES):
            cut = slice(tile * LANES, (tile + 1) * LANES)
            rows_ref[place, :, cut] = 1.0 / jnp.maximum(length * sub_ref[:, cut], LEN_FLOOR)

    factor = 1.0 / (row_count * cosine)
    line = []
    for tile in range(tiles + 1):
        taps = adjoint_taps(tile, cosine, column_count, cell_count, row_count // 2)
        for tap, (place, weight) in enumerate(taps):
            place_ref[tile, tap, :, :] = place
            tap_ref[tile, tap, :, :] = weight * factor
        line.append(sum(weight for _, weight in taps) * factor)
    store_line(line, edge_ref, bend_ref)
    slice_total = []
    for depth in range(slab_depth):
        t = jnp.sum(weights[1 + depth], axis=1, keepdims=True)
        slice_total.append([jnp.broadcast_to(t[k : k + 1], (SUBLANES, LANES)) for k in range(subset_count)])

    def one_group(group, carry):
        band = pl.ds(pl.multiple_of(group * SUBLANES, SUBLANES), SUBLANES)
        weight = [[zero] * tiles for _ in range(slab_depth)]
        for member in range(subset_count):
            line = sheared(edge_ref, bend_ref, member, adjoint_steps(group, row_count, tangents[member]), tiles)
            for depth in range(slab_depth):
                for tile in range(tiles):
                    weight[depth][tile] = weight[depth][tile] + slice_total[depth][member] * line[tile]
        for depth in range(slab_depth):
            for tile in range(tiles):
                bound_ref[depth, band, tile * LANES : (tile + 1) * LANES] = 1.0 / jnp.maximum(
                    weight[depth][tile], LEN_FLOOR * subset_count / row_count
                )
        return carry

    lax.fori_loop(0, row_count // SUBLANES, one_group, 0)


def update_kernel(
    order,
    kinds,
    angle_ref,
    subset_ref,
    volume_ref,
    measured_ref,
    bound_ref,
    own_ref,
    rows_ref,
    own_cone_ref,
    cone_ref,
    place_ref,
    tap_ref,
    *refs,
):
    blocks = refs[: len(order)]
    residual_ref, updated_ref, profile_ref, spread_ref, cell_ref, slope_ref, rest_ref, new_ref, row_ref, sent = refs[len(order) :]
    slab_depth, row_count, cell_count = volume_ref.shape
    row_share, view_count, column_count = measured_ref.shape
    subset_count = subset_ref.shape[0]
    tiles, columns = cell_count // LANES, column_count // LANES
    width = column_count // 2
    zero = jnp.zeros((SUBLANES, LANES), F32)
    slab = lax.axis_index("slab")
    odd = lax.rem(slab, 2)
    turns = turned(slab, kinds)
    mate_block, other_block = (blocks[order.index(away)] for away in (1, -1))

    groups = row_count // SUBLANES
    for tile in range(columns):
        side, inner = divmod(tile * LANES, width)
        image = [zero] * row_share
        for place, block in enumerate(blocks):
            for depth in range(slab_depth):
                cells = block[depth * 2 + side, :, inner : inner + LANES]
                for row in range(row_share):
                    image[row] = image[row] + own_cone_ref[place * slab_depth + depth, row, :, :] * cells
        cut = slice(tile * LANES, (tile + 1) * LANES)
        for row in range(row_share):
            rest_ref[row, :, cut] = (measured_ref[row, :, cut] - image[row]) * own_ref[row, :, cut]
    copies = [pltpu.make_async_copy(rest_ref, residual_ref, sent.at[groups])]
    copies[0].start()

    for member in range(subset_count):
        view = pl.ds(subset_ref[member], 1)
        for side in range(2):
            at = slice(side * subset_count + member, side * subset_count + member + 1)
            other = other_block[(slab_depth - 1) * 2 + side, view, :], other_block[side, view, :]
            mate = mate_block[(slab_depth - 1) * 2 + side, view, :], mate_block[side, view, :]
            profile_ref[0, at, :] = jnp.where(odd == 0, other[0], mate[0])
            for depth in range(slab_depth):
                profile_ref[1 + depth, at, :] = blocks[0][depth * 2 + side, view, :]
            profile_ref[1 + slab_depth, at, :] = jnp.where(odd == 0, mate[1], other[1])

    moved = [(b, j) for b, kind in enumerate(kinds) for j in range({FULL: 0, FAR: 2}.get(kind, 1))]
    for at_row, (b, j) in enumerate(moved):
        depth = turns[b] if kinds[b] in (NEAR, NEAR_SHARED) else j
        for member in range(subset_count):
            view = pl.ds(subset_ref[member], 1)
            for side in range(2):
                at = slice(side * subset_count + member, side * subset_count + member + 1)
                row_ref[at_row, at, :] = blocks[b][depth * 2 + side, view, :]

    inner_tiles = width // LANES
    spread = [[zero] * inner_tiles for _ in range(slab_depth)]
    for place in range(row_share * len(order)):
        weight = [cone_ref[place, z, :, :] for z in range(slab_depth + 2)]
        block, row = divmod(place, row_share)
        here = (block, row) in moved
        held = row_ref if here else blocks[block]
        at_row = moved.index((block, row)) if here else 2 * slab_depth + row - sum(b == block for b, _ in moved)
        for tile in range(inner_tiles):
            cut = slice(tile * LANES, (tile + 1) * LANES)
            image = weight[0] * profile_ref[0, :, cut]
            for z in range(1, slab_depth + 2):
                image = image + weight[z] * profile_ref[z, :, cut]
            rest = (held[at_row, :, cut] - image) * rows_ref[place, :, cut]
            for depth in range(slab_depth):
                spread[depth][tile] = spread[depth][tile] + weight[1 + depth] * rest
    for depth in range(slab_depth):
        for tile in range(inner_tiles):
            for side in range(2):
                spread_ref[
                    depth * subset_count : (depth + 1) * subset_count,
                    side * width + tile * LANES : side * width + (tile + 1) * LANES,
                ] = spread[depth][tile][side * subset_count : (side + 1) * subset_count]

    line = []
    for tile in range(tiles + 1):
        value = zero
        for tap in range(3):
            place = place_ref[tile, tap, :, :]
            block, index = jnp.right_shift(place, 7), jnp.bitwise_and(place, LANES - 1)
            found = zero
            for at in adjoint_tiles(tile, tap, column_count, cell_count, row_count // 2):
                found = jnp.where(block == at, pick(tile_of(spread_ref, (), at), index), found)
            value = value + tap_ref[tile, tap, :, :] * found
        line.append(value)
    store_line(line, cell_ref, slope_ref)

    tangents = member_tangents(angle_ref, subset_ref)
    for group in range(groups):
        band = slice(group * SUBLANES, (group + 1) * SUBLANES)
        back = [[zero] * tiles for _ in range(slab_depth)]
        for member in range(subset_count):
            step = adjoint_steps(group, row_count, tangents[member])
            for depth in range(slab_depth):
                line = sheared(cell_ref, slope_ref, depth * subset_count + member, step, tiles)
                back[depth] = [b + a for b, a in zip(back[depth], line)]
        for depth in range(slab_depth):
            for tile in range(tiles):
                cut = slice(tile * LANES, (tile + 1) * LANES)
                new_ref[depth, band, cut] = (
                    volume_ref[depth, band, cut] + back[depth][tile] * bound_ref[depth, band, cut]
                )
        copies.append(pltpu.make_async_copy(new_ref.at[:, band, :], updated_ref.at[:, band, :], sent.at[group]))
        copies[-1].start()
    for copy in copies:
        copy.wait()


def swapped(block):
    return lax.ppermute(block, "slab", [(i, i ^ 1) for i in range(lax.axis_size("slab"))])


def from_chip(block, distance):
    slabs = range(lax.axis_size("slab"))
    steps = [(i + 2 * distance * (1 - 2 * (i % 2)), i) for i in slabs]
    pairs = [p for p in steps if p[0] in slabs]
    idle = [i for i in slabs if i not in [p[0] for p in pairs]]
    unmet = [i for i in slabs if i not in [p[1] for p in pairs]]
    near = [i for i in idle if i ^ 1 in unmet]
    pairs += [(i, i ^ 1) for i in near]
    pairs += zip([i for i in idle if i not in near], [i for i in unmet if i ^ 1 not in near])
    return lax.ppermute(block, "slab", pairs)


def fetches(reach):
    return [s * d for d in range(1, reach // 2 + 2) for s in (-1, 1) if 2 * d - (s > 0) <= reach]


def window(reach):
    order, kinds = [0, 1], [FULL, FULL]
    for distance in fetches(reach):
        near = distance == 1
        for away, kind in ((2 * distance, NEAR if near else FAR), (1 - 2 * distance, NEAR_SHARED if near else FAR)):
            if abs(away) <= reach:
                order.append(away)
                kinds.append(kind)
    assert sorted(order) == list(range(-reach, reach + 1))
    return tuple(order), tuple(kinds)


def gathered(own, near, low, high, reach, meanwhile):
    sent = {distance: near if distance == 1 else high if distance > 0 else low for distance in fetches(reach)}
    received = {distance: from_chip(block, distance) for distance, block in sent.items()}
    blocks = {0: own, 1: swapped(own)}
    done = meanwhile()
    arrived, done = lax.optimization_barrier((list(received.values()), done))
    for distance, block in zip(received, arrived):
        if 2 * abs(distance) <= reach:
            blocks[2 * distance] = block
        if abs(1 - 2 * distance) <= reach:
            blocks[1 - 2 * distance] = swapped(block)
    return [blocks[away] for away in window(reach)[0]], done


def per_device(volume, measured, view_angle, view_lift, subset):
    slab_count = lax.axis_size("slab")
    slab_depth, row_count, cell_count = volume.shape
    row_share, view_count, column_count = measured.shape
    subset_count = subset.shape[0]
    tiles = cell_count // LANES
    reach = slab_reach(slab_count, slab_depth, row_share)
    here = lambda x: pltpu.with_memory_space_constraint(x, pltpu.VMEM)
    there = lambda x: pltpu.with_memory_space_constraint(x, pltpu.HBM)
    small = pltpu.CompilerParams(vmem_limit_bytes=VMEM_LIMIT)
    smem, vmem = pl.BlockSpec(memory_space=pltpu.SMEM), pl.BlockSpec(memory_space=pltpu.VMEM)
    wide = (tiles + 1) * LANES
    block_of = lambda rows: pltpu.VMEM((2 * slab_depth + rows, SUBLANES, column_count // 2), F32)
    own, near, low, high, cover = pl.pallas_call(
        functools.partial(project_kernel, slab_count),
        out_shape=(
            block_of(row_share),
            block_of(2),
            block_of(1),
            block_of(1),
            pltpu.VMEM((view_count, column_count), F32),
        ),
        in_specs=[smem] * 3 + [vmem] * 2,
        out_specs=(vmem,) * 5,
        scratch_shapes=[
            pltpu.VMEM(volume.shape, F32),
            pltpu.VMEM((slab_depth, row_count, LANES), F32),
            pltpu.VMEM((slab_depth, view_count, SUBLANES, wide), F32),
            pltpu.VMEM((2, view_count, SUBLANES, LANES), F32),
        ]
        + [pltpu.VMEM((slab_depth + 1, SUBLANES, wide), F32)] * 2,
        compiler_params=small,
        name="project",
    )(*map(there, (view_angle, view_lift, subset, volume, measured)))
    cover = here(cover)
    order, kinds = window(reach)
    divide = pl.pallas_call(
        functools.partial(divisor_kernel, slab_count, order, kinds),
        out_shape=(
            pltpu.VMEM(volume.shape, F32),
            pltpu.VMEM(measured.shape, F32),
            pltpu.VMEM((row_share * len(order), SUBLANES, column_count // 2), F32),
            pltpu.VMEM((slab_depth * len(order), row_share, SUBLANES, LANES), F32),
            pltpu.VMEM((row_share * len(order), slab_depth + 2, SUBLANES, LANES), F32),
            pltpu.VMEM((tiles + 1, 3, SUBLANES, LANES), jnp.int32),
            pltpu.VMEM((tiles + 1, 3, SUBLANES, LANES), F32),
        ),
        in_specs=[smem] * 3 + [vmem],
        out_specs=(vmem,) * 7,
        scratch_shapes=[pltpu.VMEM((SUBLANES, wide), F32)] * 2 + [pltpu.VMEM((SUBLANES, column_count // 2), F32)],
        cost_estimate=pl.CostEstimate(flops=4_000_000, bytes_accessed=8_000_000, transcendentals=0),
        compiler_params=small,
        name="divisors",
    )
    blocks, divisors = gathered(own, near, low, high, reach, lambda: divide(view_angle, view_lift, subset, cover))
    return pl.pallas_call(
        functools.partial(update_kernel, order, kinds),
        out_shape=(
            jax.ShapeDtypeStruct(measured.shape, F32),
            jax.ShapeDtypeStruct(volume.shape, F32),
        ),
        in_specs=[smem] * 2 + [vmem] * (2 + len(divisors) + len(order)),
        out_specs=(pl.BlockSpec(memory_space=pl.ANY),) * 2,
        scratch_shapes=[
            pltpu.VMEM((slab_depth + 2, SUBLANES, column_count // 2), F32),
            pltpu.VMEM((SUBLANES, column_count), F32),
            pltpu.VMEM((SUBLANES, wide), F32),
            pltpu.VMEM((SUBLANES, wide), F32),
            pltpu.VMEM(measured.shape, F32),
            pltpu.VMEM(volume.shape, F32),
            pltpu.VMEM((2 * len(order), SUBLANES, column_count // 2), F32),
            pltpu.SemaphoreType.DMA((row_count // SUBLANES + 1,)),
        ],
        compiler_params=small,
        name="update",
    )(view_angle, subset, *map(here, (volume, measured, *divisors, *blocks)))


def solution(mesh):
    in_specs = (
        P(("scan", "slab"), None, None),
        P(("scan", "slab"), None, None),
        P("scan"),
        P("scan"),
        P("scan"),
    )
    out_specs = (P(("scan", "slab"), None, None), P(("scan", "slab"), None, None))
    return jax.shard_map(
        per_device, mesh=mesh, in_specs=in_specs, out_specs=out_specs, check_vma=False
    )
```

```python
import functools
import math

import jax
import jax.numpy as jnp
import numpy as np
from jax import lax
from jax.experimental import pallas as pl
from jax.experimental.pallas import tpu as pltpu
from jax.sharding import PartitionSpec as P

ANGLES = 180
LIFT = 6
PITCH = 0.9
MAG_BASE = 1.5
ECCENTRIC = 0.12
LEN_FLOOR = 0.25
LANES = 128
SUBLANES = 8
F32 = jnp.float32
FULL, NEAR, NEAR_SHARED, FAR = range(4)
VMEM_LIMIT = 8 * 1024 * 1024


def angle_table():
    radians = (np.arange(ANGLES) + 0.5) * (0.5 * math.pi / ANGLES) - 0.25 * math.pi
    magnify = MAG_BASE / (1.0 - ECCENTRIC * np.sin(2.0 * radians + 1.0))
    return np.cos(radians), magnify


def slab_reach(slab_count, slab_depth, row_share):
    _, magnify = angle_table()
    total_rows, total_slices = row_share * slab_count, slab_depth * slab_count
    rows = np.arange(total_rows)
    reach = 0
    for lift in range(-LIFT, LIFT + 1):
        sample = (rows[None] + 0.5 - total_rows / 2 - lift) / magnify[:, None] + total_slices / 2 - 0.5
        for tap in (np.floor(sample - 1e-3), np.floor(sample + 1e-3) + 1):
            inside = (tap >= 0) & (tap < total_slices)
            distance = np.abs(tap // slab_depth - rows[None] // row_share)
            reach = max(reach, int(distance[inside].max()))
    return reach


def lane_index():
    return lax.broadcasted_iota(jnp.int32, (SUBLANES, LANES), 1)


def sublane_index():
    return lax.broadcasted_iota(jnp.int32, (SUBLANES, LANES), 0)


def angle_facts(index):
    x = (index.astype(F32) + 0.5) * (0.5 * math.pi / ANGLES) - 0.25 * math.pi
    s = x * x
    sine = x * (1.0 + s * (-1 / 6 + s * (1 / 120 + s * (-1 / 5040 + s * (1 / 362880)))))
    cosine = 1.0 + s * (-1 / 2 + s * (1 / 24 + s * (-1 / 720 + s * (1 / 40320 + s * (-1 / 3628800)))))
    double = 2.0 * sine * cosine * math.cos(1.0) + (1.0 - 2.0 * sine * sine) * math.sin(1.0)
    return cosine, sine / cosine, (1.0 - ECCENTRIC * double) * (1.0 / MAG_BASE)


def spread_scalars(read, count, place):
    out = jnp.full((SUBLANES, LANES), read(0), jnp.int32)
    for item in range(1, count):
        out = jnp.where(place == item, read(item), out)
    return out


def pick(tile, index):
    numbers = lax.GatherDimensionNumbers(
        offset_dims=(),
        collapsed_slice_dims=(1,),
        start_index_map=(1,),
        operand_batching_dims=(0,),
        start_indices_batching_dims=(0,),
    )
    return lax.gather(tile, index[..., None], numbers, (1, 1), mode=lax.GatherScatterMode.PROMISE_IN_BOUNDS)


def next_lane(tile, following):
    lane = lane_index()
    return jnp.where(lane < LANES - 1, pltpu.roll(tile, LANES - 1, 1), pltpu.roll(following, LANES - 1, 1))


def rows_summed(parts):
    sub = sublane_index()
    step = 1
    while step < SUBLANES:
        low = jnp.bitwise_and(sub, step) == 0
        parts = [
            jnp.where(low, a, b) + pltpu.roll(jnp.where(low, b, a), step, 0) for a, b in zip(parts[::2], parts[1::2])
        ]
        step *= 2
    return parts[0]


def tile_of(ref, lead, tile):
    whole = (slice(None),) * (len(ref.shape) - 1 - len(lead))
    return ref[lead + whole + (slice(tile * LANES, (tile + 1) * LANES),)]


def column_center(column, cosine, column_count, cell_count):
    return (column + 0.5 - column_count / 2) * (PITCH * cell_count / column_count) / cosine + (
        cell_count / 2 - 0.5
    )


def shear_steps(group, row_count, tangent):
    row = (sublane_index() + group * SUBLANES).astype(F32)
    offset = (row + 0.5 - row_count / 2) * tangent
    whole = jnp.floor(offset)
    return whole.astype(jnp.int32), offset - whole


def cone_sample(rows, lifts, flat, total_rows, total_slices):
    return (rows + 0.5 - total_rows / 2 - lifts) * flat + (total_slices / 2 - 0.5)


def cone_total(sample, total_slices):
    whole = jnp.floor(sample)
    fraction = sample - whole
    low = jnp.where((whole >= 0) & (whole < total_slices), 1.0 - fraction, 0.0)
    return low + jnp.where((whole >= -1) & (whole < total_slices - 1), fraction, 0.0)


def column_of(tile, at):
    return jnp.broadcast_to(tile[:, at : at + 1], (SUBLANES, LANES))


def slabs_of(slab, order):
    return [slab + (1 - 2 * lax.rem(slab, 2)) * away for away in order]


def turned(slab, kinds):
    odd = lax.rem(slab, 2)
    return [{NEAR: 1 - odd, NEAR_SHARED: odd}.get(kind, 0) for kind in kinds]


def subset_cone(slab, slab_count, order, kinds, slab_depth, row_share, flat, lifts):
    lane = lane_index()
    total_rows, total_slices = row_share * slab_count, slab_depth * slab_count
    origin, turns = slabs_of(slab, order), turned(slab, kinds)
    source = sum(jnp.where(lane >= row_share * b, 1, 0) for b in range(1, len(order)))
    within = lane - source * row_share
    within = jnp.where(spread_scalars(lambda b: turns[b], len(order), source) == 1, row_share - 1 - within, within)
    rows = spread_scalars(lambda b: origin[b], len(order), source) * row_share + within
    real = (rows >= 0) & (rows < total_rows) & (lane < row_share * len(order))
    sample = cone_sample(rows.astype(F32), lifts, flat, total_rows, total_slices)
    weights = []
    for z in range(-1, slab_depth + 1):
        at = slab * slab_depth + z
        use = real & (at >= 0) & (at < total_slices)
        weights.append(jnp.where(use, jnp.maximum(0.0, 1.0 - jnp.abs(sample - at.astype(F32))), 0.0))
    return sample, weights


def adjoint_taps(tile, cosine, column_count, cell_count, half):
    spacing = PITCH * cell_count / column_count
    cell = (lane_index() + (tile * LANES - half)).astype(F32)
    inside = (cell >= 0) & (cell < cell_count)
    first = jnp.floor((cell - (cell_count / 2 + 0.5)) * cosine * (1.0 / spacing) + (column_count / 2 - 0.5 - 1e-3)) + 1.0
    taps = []
    for tap in range(3):
        column = first + tap
        weight = jnp.maximum(0.0, 1.0 - jnp.abs(cell - column_center(column, cosine, column_count, cell_count)))
        weight = jnp.where(inside & (column >= 0) & (column < column_count), weight, 0.0)
        taps.append((jnp.clip(column.astype(jnp.int32), 0, column_count - 1), weight))
    return taps


def adjoint_tiles(tile, tap, column_count, cell_count, half):
    spacing = PITCH * cell_count / column_count
    least = angle_table()[0].min()
    ends = [
        (tile * LANES - half + e - cell_count / 2 - 0.5) * c / spacing + column_count / 2 + 0.5
        for e in (0, LANES - 1)
        for c in (1.0, least)
    ]
    low = min(max(math.floor(min(ends) + tap - 0.6), 0), column_count - 1) // LANES
    high = min(max(math.ceil(max(ends) + tap + 0.6), 0), column_count - 1) // LANES
    return range(low, high + 1)


def store_line(line, base_ref, bend_ref):
    line = line + [jnp.zeros((SUBLANES, LANES), F32)]
    for tile in range(len(line) - 1):
        cut = slice(tile * LANES, (tile + 1) * LANES)
        base_ref[:, cut] = line[tile]
        bend_ref[:, cut] = next_lane(line[tile], line[tile + 1]) - line[tile]


def adjoint_steps(group, row_count, tangent):
    whole, fraction = shear_steps(group, row_count, tangent)
    place = lane_index() + (row_count // 2 - 1 - whole)
    return jnp.bitwise_and(place, LANES - 1), place < LANES, 1.0 - fraction


def sheared(base_ref, bend_ref, row, step, tiles):
    index, near, share = step
    before, out = None, []
    for tile in range(tiles + 1):
        cut = slice(tile * LANES, (tile + 1) * LANES)
        low = jnp.broadcast_to(base_ref[row : row + 1, cut], (SUBLANES, LANES))
        rise = jnp.broadcast_to(bend_ref[row : row + 1, cut], (SUBLANES, LANES))
        after = pick(low + share * rise, index)
        if tile:
            out.append(jnp.where(near, before, after))
        before = after
    return out


def subset_angles(angle_ref, lift_ref, subset_ref):
    members = subset_ref.shape[0]
    member = jnp.bitwise_and(sublane_index(), members - 1)
    cosine, _, flat = angle_facts(spread_scalars(lambda k: angle_ref[subset_ref[k]], members, member))
    lifts = spread_scalars(lambda k: lift_ref[subset_ref[k]], members, member).astype(F32)
    return cosine, flat, lifts


def member_tangents(angle_ref, subset_ref):
    indices = [angle_ref[subset_ref[k]] for k in range(subset_ref.shape[0])]
    return [angle_facts(jnp.full((SUBLANES, LANES), i, jnp.int32))[1] for i in indices]


def project_kernel(
    slab_count,
    angle_ref,
    lift_ref,
    subset_ref,
    volume_ref,
    measured_ref,
    block_ref,
    near_ref,
    low_ref,
    high_ref,
    cover_ref,
    rise_ref,
    first_ref,
    part_ref,
    end_ref,
    cell_ref,
    slope_ref,
):
    slab_depth, row_count, cell_count = volume_ref.shape
    row_share, view_count, column_count = measured_ref.shape
    subset_count = subset_ref.shape[0]
    half = row_count // 2
    tiles = cell_count // LANES
    groups = row_count // SUBLANES
    lane, sub = lane_index(), sublane_index()
    zero = jnp.zeros((SUBLANES, LANES), F32)
    width = column_count // 2

    assert (slab_depth, row_share) == (2, 3)
    slab = lax.axis_index("slab")
    odd = lax.rem(slab, 2)
    grows = odd == 1
    far_row = jnp.where(grows, 2, 0)
    for member in range(subset_count):
        view = pl.ds(subset_ref[member], 1)
        for side in range(2):
            at, cut = side * subset_count + member, slice(side * width, (side + 1) * width)
            rows = [measured_ref[row, view, cut] for row in range(row_share)]
            for row in range(row_share):
                block_ref[2 * slab_depth + row, at : at + 1, :] = rows[row]
            near_ref[2 * slab_depth, at : at + 1, :] = rows[1]
            near_ref[2 * slab_depth + 1, at : at + 1, :] = measured_ref[far_row, view, cut]
            low_ref[2 * slab_depth, at : at + 1, :] = rows[2]
            high_ref[2 * slab_depth, at : at + 1, :] = rows[2]

    cosine, _, flat = angle_facts(spread_scalars(lambda v: angle_ref[v], view_count, sub))
    lifts = spread_scalars(lambda v: lift_ref[v], view_count, sub).astype(F32)
    ends = [
        cone_sample((slab * row_share + row).astype(F32), lifts, flat, row_share * slab_count, slab_depth * slab_count)
        - (slab * slab_depth).astype(F32)
        for row in (0, row_share - 1)
    ]
    picked = sub == subset_ref[0]
    for member in range(1, subset_count):
        picked = picked | (sub == subset_ref[member])
    picked = jnp.where(picked, 1, 0)
    as_int = lambda mask: jnp.where(mask, 1, 0)
    near_up, near_down = picked * as_int(ends[1] > 0.75), picked * as_int(ends[0] < 0.25)
    far_up, far_down = picked * as_int(ends[1] > 2.5), picked * as_int(ends[0] < -1.5)
    near_places = [(near_up * odd) == 1, (near_down * (1 - odd)) == 1]
    high_places = (far_up * odd + far_down * (1 - odd)) == 1
    low_places = (far_up * (1 - odd) + far_down * odd) == 1

    for depth in range(slab_depth):
        for group in range(groups):
            band = slice(group * SUBLANES, (group + 1) * SUBLANES)
            cells = [tile_of(volume_ref, (depth, band), tile) for tile in range(tiles)] + [zero]
            for tile in range(tiles):
                rise_ref[depth, band, tile * LANES : (tile + 1) * LANES] = (
                    next_lane(cells[tile], cells[tile + 1]) - cells[tile]
                )
            first_ref[depth, band, :] = column_of(cells[0], 0)

    def one_view(view, carry):
        _, tangent, _ = angle_facts(jnp.full((SUBLANES, LANES), angle_ref[view], jnp.int32))
        low_end, high_end = zero, zero
        sums = [[zero] * (tiles + 1) for _ in range(slab_depth)]
        for group in range(groups):
            band = slice(group * SUBLANES, (group + 1) * SUBLANES)
            whole, fraction = shear_steps(group, row_count, tangent)
            place = lane + (whole + half)
            index = jnp.bitwise_and(place, LANES - 1)
            near, last = place < LANES, index == LANES - 1
            enter = jnp.where(last, fraction, 0.0)
            low_end = low_end + jnp.where(near, enter, 1.0)
            high_end = high_end + jnp.where(near, 1.0 - enter, 0.0)
            for depth in range(slab_depth):
                before = enter * first_ref[depth, band, :]
                for tile in range(tiles + 1):
                    after = zero
                    if tile < tiles:
                        at = (depth, band)
                        after = pick(tile_of(volume_ref, at, tile) + fraction * tile_of(rise_ref, at, tile), index)
                    sums[depth][tile] = sums[depth][tile] + jnp.where(near, before, after)
                    before = after
        end_ref[0, view, :, :] = low_end
        end_ref[1, view, :, :] = high_end
        for depth in range(slab_depth):
            for tile in range(tiles + 1):
                part_ref[depth, view, :, tile * LANES : (tile + 1) * LANES] = sums[depth][tile]
        return carry

    lax.fori_loop(0, view_count, one_view, 0, unroll=4)

    shift = LANES - half
    inside = [None] * (tiles + 1)
    inside[0], inside[tiles] = lane >= shift, lane < shift

    def store(at, line):
        line = [jnp.where(mask, cells, 0.0) if mask is not None else cells for cells, mask in zip(line, inside)] + [zero]
        for tile in range(tiles + 1):
            cut = slice(tile * LANES, (tile + 1) * LANES)
            cell_ref[at, :, cut] = line[tile]
            slope_ref[at, :, cut] = next_lane(line[tile], line[tile + 1]) - line[tile]

    views = range(view_count)
    for depth in range(slab_depth):
        store(depth, [rows_summed([tile_of(part_ref, (depth, v), t) for v in views]) for t in range(tiles + 1)])
    level = zero + float(row_count)
    ends = [rows_summed([end_ref[e, v, :, :] for v in views]) for e in range(2)]
    store(slab_depth, [ends[0]] + [level] * (tiles - 1) + [ends[1]])

    factor = 1.0 / (row_count * cosine)
    least = angle_table()[0].min()
    for tile in range(column_count // LANES):
        column = (lane + tile * LANES).astype(F32)
        center = column_center(column, cosine, column_count, cell_count)
        whole = jnp.floor(center)
        fraction = center - whole
        place = jnp.clip(whole.astype(jnp.int32) + shift, shift - 2, shift + cell_count)
        block, index = jnp.right_shift(place, 7), jnp.bitwise_and(place, LANES - 1)
        ends = [column_center(tile * LANES + e, c, column_count, cell_count) for e in (0, LANES - 1) for c in (1.0, least)]
        low = min(max(math.floor(min(ends) - 1e-2) + shift, shift - 2), shift + cell_count) // LANES
        high = min(max(math.floor(max(ends) + 1e-2) + shift, shift - 2), shift + cell_count) // LANES
        cells, slopes = [zero] * slab_depth + [level], [zero] * (slab_depth + 1)
        for source in range(low, high + 1):
            here = block == source
            for at in range(slab_depth + 1):
                if at == slab_depth and source not in (0, tiles):
                    continue
                cells[at] = jnp.where(here, pick(tile_of(cell_ref, (at,), source), index), cells[at])
                slopes[at] = jnp.where(here, pick(tile_of(slope_ref, (at,), source), index), slopes[at])
        profiles = [(c + fraction * s) * factor for c, s in zip(cells, slopes)]
        side, inner = divmod(tile * LANES, width)
        for depth in range(slab_depth):
            to = (depth * 2 + side, slice(None), slice(inner, inner + LANES))
            measured = tile_of(measured_ref, (depth,), tile)
            last = tile_of(measured_ref, (depth * (row_share - 1),), tile)
            block_ref[to] = profiles[depth]
            near_ref[to] = jnp.where(near_places[depth], last, profiles[depth])
            low_ref[to] = jnp.where(low_places, measured, profiles[depth])
            high_ref[to] = jnp.where(high_places, measured, profiles[depth])
        cover_ref[:, tile * LANES : (tile + 1) * LANES] = profiles[slab_depth]


def divisor_kernel(
    slab_count,
    order,
    kinds,
    angle_ref,
    lift_ref,
    subset_ref,
    cover_ref,
    bound_ref,
    own_ref,
    rows_ref,
    own_cone_ref,
    cone_ref,
    place_ref,
    tap_ref,
    edge_ref,
    bend_ref,
    sub_ref,
):
    slab_depth, row_count, cell_count = bound_ref.shape
    row_share, view_count, column_count = own_ref.shape
    subset_count = subset_ref.shape[0]
    total_rows, total_slices = row_share * slab_count, slab_depth * slab_count
    tiles, columns = cell_count // LANES, column_count // LANES
    width = column_count // 2
    sub = sublane_index()
    zero = jnp.zeros((SUBLANES, LANES), F32)
    slab = lax.axis_index("slab")

    _, _, flat = angle_facts(spread_scalars(lambda v: angle_ref[v], view_count, sub))
    lifts = spread_scalars(lambda v: lift_ref[v], view_count, sub).astype(F32)
    lane = lane_index()
    origin = slabs_of(slab, order)
    source = sum(jnp.where(lane >= slab_depth * b, 1, 0) for b in range(1, len(order)))
    slices = spread_scalars(lambda b: origin[b], len(order), source) * slab_depth + (lane - source * slab_depth)
    held = (slices >= 0) & (slices < total_slices)
    slices = slices.astype(F32)
    for row in range(row_share):
        sample = cone_sample((slab * row_share + row).astype(F32), lifts, flat, total_rows, total_slices)
        weights = jnp.where(held, jnp.maximum(0.0, 1.0 - jnp.abs(sample - slices)), 0.0)
        for place in range(slab_depth * len(order)):
            own_cone_ref[place, row, :, :] = column_of(weights, place)
        total = cone_total(sample, total_slices)
        for tile in range(columns):
            cut = slice(tile * LANES, (tile + 1) * LANES)
            own_ref[row, :, cut] = 1.0 / jnp.maximum(total * cover_ref[:, cut], LEN_FLOOR)

    cosine, flat, lifts = subset_angles(angle_ref, lift_ref, subset_ref)
    tangents = member_tangents(angle_ref, subset_ref)
    for member in range(subset_count):
        view = pl.ds(subset_ref[member], 1)
        for side in range(2):
            at = slice(side * subset_count + member, side * subset_count + member + 1)
            sub_ref[at, :] = cover_ref[view, side * width : (side + 1) * width]
    sample, weights = subset_cone(slab, slab_count, order, kinds, slab_depth, row_share, flat, lifts)
    total = cone_total(sample, total_slices)
    for place in range(row_share * len(order)):
        for z, w in enumerate(weights):
            cone_ref[place, z, :, :] = column_of(w, place)
        length = column_of(total, place)
        for tile in range(width // LANES):
            cut = slice(tile * LANES, (tile + 1) * LANES)
            rows_ref[place, :, cut] = 1.0 / jnp.maximum(length * sub_ref[:, cut], LEN_FLOOR)

    factor = 1.0 / (row_count * cosine)
    line = []
    for tile in range(tiles + 1):
        taps = adjoint_taps(tile, cosine, column_count, cell_count, row_count // 2)
        for tap, (place, weight) in enumerate(taps):
            place_ref[tile, tap, :, :] = place
            tap_ref[tile, tap, :, :] = weight * factor
        line.append(sum(weight for _, weight in taps) * factor)
    store_line(line, edge_ref, bend_ref)
    slice_total = []
    for depth in range(slab_depth):
        t = jnp.sum(weights[1 + depth], axis=1, keepdims=True)
        slice_total.append([jnp.broadcast_to(t[k : k + 1], (SUBLANES, LANES)) for k in range(subset_count)])

    def one_group(group, carry):
        band = pl.ds(pl.multiple_of(group * SUBLANES, SUBLANES), SUBLANES)
        weight = [[zero] * tiles for _ in range(slab_depth)]
        for member in range(subset_count):
            line = sheared(edge_ref, bend_ref, member, adjoint_steps(group, row_count, tangents[member]), tiles)
            for depth in range(slab_depth):
                for tile in range(tiles):
                    weight[depth][tile] = weight[depth][tile] + slice_total[depth][member] * line[tile]
        for depth in range(slab_depth):
            for tile in range(tiles):
                bound_ref[depth, band, tile * LANES : (tile + 1) * LANES] = 1.0 / jnp.maximum(
                    weight[depth][tile], LEN_FLOOR * subset_count / row_count
                )
        return carry

    lax.fori_loop(0, row_count // SUBLANES, one_group, 0)


def update_kernel(
    order,
    kinds,
    angle_ref,
    subset_ref,
    volume_ref,
    measured_ref,
    bound_ref,
    own_ref,
    rows_ref,
    own_cone_ref,
    cone_ref,
    place_ref,
    tap_ref,
    *refs,
):
    blocks = refs[: len(order)]
    residual_ref, updated_ref, profile_ref, spread_ref, cell_ref, slope_ref, rest_ref, new_ref, row_ref, sent = refs[len(order) :]
    slab_depth, row_count, cell_count = volume_ref.shape
    row_share, view_count, column_count = measured_ref.shape
    subset_count = subset_ref.shape[0]
    tiles, columns = cell_count // LANES, column_count // LANES
    width = column_count // 2
    zero = jnp.zeros((SUBLANES, LANES), F32)
    slab = lax.axis_index("slab")
    odd = lax.rem(slab, 2)
    turns = turned(slab, kinds)
    mate_block, other_block = (blocks[order.index(away)] for away in (1, -1))

    groups = row_count // SUBLANES
    for tile in range(columns):
        side, inner = divmod(tile * LANES, width)
        image = [zero] * row_share
        for place, block in enumerate(blocks):
            for depth in range(slab_depth):
                cells = block[depth * 2 + side, :, inner : inner + LANES]
                for row in range(row_share):
                    image[row] = image[row] + own_cone_ref[place * slab_depth + depth, row, :, :] * cells
        cut = slice(tile * LANES, (tile + 1) * LANES)
        for row in range(row_share):
            rest_ref[row, :, cut] = (measured_ref[row, :, cut] - image[row]) * own_ref[row, :, cut]
    copies = [pltpu.make_async_copy(rest_ref, residual_ref, sent.at[groups])]
    copies[0].start()

    for member in range(subset_count):
        view = pl.ds(subset_ref[member], 1)
        for side in range(2):
            at = slice(side * subset_count + member, side * subset_count + member + 1)
            other = other_block[(slab_depth - 1) * 2 + side, view, :], other_block[side, view, :]
            mate = mate_block[(slab_depth - 1) * 2 + side, view, :], mate_block[side, view, :]
            profile_ref[0, at, :] = jnp.where(odd == 0, other[0], mate[0])
            for depth in range(slab_depth):
                profile_ref[1 + depth, at, :] = blocks[0][depth * 2 + side, view, :]
            profile_ref[1 + slab_depth, at, :] = jnp.where(odd == 0, mate[1], other[1])

    moved = [(b, j) for b, kind in enumerate(kinds) for j in range({FULL: 0, FAR: 2}.get(kind, 1))]
    for at_row, (b, j) in enumerate(moved):
        depth = turns[b] if kinds[b] in (NEAR, NEAR_SHARED) else j
        for member in range(subset_count):
            view = pl.ds(subset_ref[member], 1)
            for side in range(2):
                at = slice(side * subset_count + member, side * subset_count + member + 1)
                row_ref[at_row, at, :] = blocks[b][depth * 2 + side, view, :]

    inner_tiles = width // LANES
    spread = [[zero] * inner_tiles for _ in range(slab_depth)]
    for place in range(row_share * len(order)):
        weight = [cone_ref[place, z, :, :] for z in range(slab_depth + 2)]
        block, row = divmod(place, row_share)
        here = (block, row) in moved
        held = row_ref if here else blocks[block]
        at_row = moved.index((block, row)) if here else 2 * slab_depth + row - sum(b == block for b, _ in moved)
        for tile in range(inner_tiles):
            cut = slice(tile * LANES, (tile + 1) * LANES)
            image = weight[0] * profile_ref[0, :, cut]
            for z in range(1, slab_depth + 2):
                image = image + weight[z] * profile_ref[z, :, cut]
            rest = (held[at_row, :, cut] - image) * rows_ref[place, :, cut]
            for depth in range(slab_depth):
                spread[depth][tile] = spread[depth][tile] + weight[1 + depth] * rest
    for depth in range(slab_depth):
        for tile in range(inner_tiles):
            for side in range(2):
                spread_ref[
                    depth * subset_count : (depth + 1) * subset_count,
                    side * width + tile * LANES : side * width + (tile + 1) * LANES,
                ] = spread[depth][tile][side * subset_count : (side + 1) * subset_count]

    line = []
    for tile in range(tiles + 1):
        value = zero
        for tap in range(3):
            place = place_ref[tile, tap, :, :]
            block, index = jnp.right_shift(place, 7), jnp.bitwise_and(place, LANES - 1)
            found = zero
            for at in adjoint_tiles(tile, tap, column_count, cell_count, row_count // 2):
                found = jnp.where(block == at, pick(tile_of(spread_ref, (), at), index), found)
            value = value + tap_ref[tile, tap, :, :] * found
        line.append(value)
    store_line(line, cell_ref, slope_ref)

    tangents = member_tangents(angle_ref, subset_ref)
    for group in range(groups):
        band = slice(group * SUBLANES, (group + 1) * SUBLANES)
        back = [[zero] * tiles for _ in range(slab_depth)]
        for member in range(subset_count):
            step = adjoint_steps(group, row_count, tangents[member])
            for depth in range(slab_depth):
                line = sheared(cell_ref, slope_ref, depth * subset_count + member, step, tiles)
                back[depth] = [b + a for b, a in zip(back[depth], line)]
        for depth in range(slab_depth):
            for tile in range(tiles):
                cut = slice(tile * LANES, (tile + 1) * LANES)
                new_ref[depth, band, cut] = (
                    volume_ref[depth, band, cut] + back[depth][tile] * bound_ref[depth, band, cut]
                )
        copies.append(pltpu.make_async_copy(new_ref.at[:, band, :], updated_ref.at[:, band, :], sent.at[group]))
        copies[-1].start()
    for copy in copies:
        copy.wait()


def swapped(block):
    return lax.ppermute(block, "slab", [(i, i ^ 1) for i in range(lax.axis_size("slab"))])


def from_chip(block, distance):
    slabs = range(lax.axis_size("slab"))
    steps = [(i + 2 * distance * (1 - 2 * (i % 2)), i) for i in slabs]
    pairs = [p for p in steps if p[0] in slabs]
    idle = [i for i in slabs if i not in [p[0] for p in pairs]]
    unmet = [i for i in slabs if i not in [p[1] for p in pairs]]
    near = [i for i in idle if i ^ 1 in unmet]
    pairs += [(i, i ^ 1) for i in near]
    pairs += zip([i for i in idle if i not in near], [i for i in unmet if i ^ 1 not in near])
    return lax.ppermute(block, "slab", pairs)


def fetches(reach):
    return [s * d for d in range(1, reach // 2 + 2) for s in (-1, 1) if 2 * d - (s > 0) <= reach]


def window(reach):
    order, kinds = [0, 1], [FULL, FULL]
    for distance in fetches(reach):
        near = distance == 1
        for away, kind in ((2 * distance, NEAR if near else FAR), (1 - 2 * distance, NEAR_SHARED if near else FAR)):
            if abs(away) <= reach:
                order.append(away)
                kinds.append(kind)
    assert sorted(order) == list(range(-reach, reach + 1))
    return tuple(order), tuple(kinds)


def gathered(own, near, low, high, reach, meanwhile):
    sent = {distance: near if distance == 1 else high if distance > 0 else low for distance in fetches(reach)}
    received = {distance: from_chip(block, distance) for distance, block in sent.items()}
    done = meanwhile()
    own, done = lax.optimization_barrier((own, done))
    blocks = {0: own, 1: swapped(own)}
    arrived, done = lax.optimization_barrier((list(received.values()), done))
    for distance, block in zip(received, arrived):
        if 2 * abs(distance) <= reach:
            blocks[2 * distance] = block
        if abs(1 - 2 * distance) <= reach:
            blocks[1 - 2 * distance] = swapped(block)
    return [blocks[away] for away in window(reach)[0]], done


def per_device(volume, measured, view_angle, view_lift, subset):
    slab_count = lax.axis_size("slab")
    slab_depth, row_count, cell_count = volume.shape
    row_share, view_count, column_count = measured.shape
    subset_count = subset.shape[0]
    tiles = cell_count // LANES
    reach = slab_reach(slab_count, slab_depth, row_share)
    here = lambda x: pltpu.with_memory_space_constraint(x, pltpu.VMEM)
    there = lambda x: pltpu.with_memory_space_constraint(x, pltpu.HBM)
    small = pltpu.CompilerParams(vmem_limit_bytes=VMEM_LIMIT)
    smem, vmem = pl.BlockSpec(memory_space=pltpu.SMEM), pl.BlockSpec(memory_space=pltpu.VMEM)
    wide = (tiles + 1) * LANES
    block_of = lambda rows: pltpu.VMEM((2 * slab_depth + rows, SUBLANES, column_count // 2), F32)
    own, near, low, high, cover = pl.pallas_call(
        functools.partial(project_kernel, slab_count),
        out_shape=(
            block_of(row_share),
            block_of(2),
            block_of(1),
            block_of(1),
            pltpu.VMEM((view_count, column_count), F32),
        ),
        in_specs=[smem] * 3 + [vmem] * 2,
        out_specs=(vmem,) * 5,
        scratch_shapes=[
            pltpu.VMEM(volume.shape, F32),
            pltpu.VMEM((slab_depth, row_count, LANES), F32),
            pltpu.VMEM((slab_depth, view_count, SUBLANES, wide), F32),
            pltpu.VMEM((2, view_count, SUBLANES, LANES), F32),
        ]
        + [pltpu.VMEM((slab_depth + 1, SUBLANES, wide), F32)] * 2,
        compiler_params=small,
        name="project",
    )(*map(there, (view_angle, view_lift, subset, volume, measured)))
    cover = here(cover)
    order, kinds = window(reach)
    divide = pl.pallas_call(
        functools.partial(divisor_kernel, slab_count, order, kinds),
        out_shape=(
            pltpu.VMEM(volume.shape, F32),
            pltpu.VMEM(measured.shape, F32),
            pltpu.VMEM((row_share * len(order), SUBLANES, column_count // 2), F32),
            pltpu.VMEM((slab_depth * len(order), row_share, SUBLANES, LANES), F32),
            pltpu.VMEM((row_share * len(order), slab_depth + 2, SUBLANES, LANES), F32),
            pltpu.VMEM((tiles + 1, 3, SUBLANES, LANES), jnp.int32),
            pltpu.VMEM((tiles + 1, 3, SUBLANES, LANES), F32),
        ),
        in_specs=[smem] * 3 + [vmem],
        out_specs=(vmem,) * 7,
        scratch_shapes=[pltpu.VMEM((SUBLANES, wide), F32)] * 2 + [pltpu.VMEM((SUBLANES, column_count // 2), F32)],
        cost_estimate=pl.CostEstimate(flops=4_000_000, bytes_accessed=8_000_000, transcendentals=0),
        compiler_params=small,
        name="divisors",
    )
    blocks, divisors = gathered(own, near, low, high, reach, lambda: divide(view_angle, view_lift, subset, cover))
    return pl.pallas_call(
        functools.partial(update_kernel, order, kinds),
        out_shape=(
            jax.ShapeDtypeStruct(measured.shape, F32),
            jax.ShapeDtypeStruct(volume.shape, F32),
        ),
        in_specs=[smem] * 2 + [vmem] * (2 + len(divisors) + len(order)),
        out_specs=(pl.BlockSpec(memory_space=pl.ANY),) * 2,
        scratch_shapes=[
            pltpu.VMEM((slab_depth + 2, SUBLANES, column_count // 2), F32),
            pltpu.VMEM((SUBLANES, column_count), F32),
            pltpu.VMEM((SUBLANES, wide), F32),
            pltpu.VMEM((SUBLANES, wide), F32),
            pltpu.VMEM(measured.shape, F32),
            pltpu.VMEM(volume.shape, F32),
            pltpu.VMEM((2 * len(order), SUBLANES, column_count // 2), F32),
            pltpu.SemaphoreType.DMA((row_count // SUBLANES + 1,)),
        ],
        compiler_params=small,
        name="update",
    )(view_angle, subset, *map(here, (volume, measured, *divisors, *blocks)))


def solution(mesh):
    in_specs = (
        P(("scan", "slab"), None, None),
        P(("scan", "slab"), None, None),
        P("scan"),
        P("scan"),
        P("scan"),
    )
    out_specs = (P(("scan", "slab"), None, None), P(("scan", "slab"), None, None))
    return jax.shard_map(
        per_device, mesh=mesh, in_specs=in_specs, out_specs=out_specs, check_vma=False
    )
```

```python
import functools
import math

import jax
import jax.numpy as jnp
import numpy as np
from jax import lax
from jax.experimental import pallas as pl
from jax.experimental.pallas import tpu as pltpu
from jax.sharding import PartitionSpec as P

ANGLES = 180
LIFT = 6
PITCH = 0.9
MAG_BASE = 1.5
ECCENTRIC = 0.12
LEN_FLOOR = 0.25
LANES = 128
SUBLANES = 8
F32 = jnp.float32
FULL, NEAR, NEAR_SHARED, FAR = range(4)
VMEM_LIMIT = 8 * 1024 * 1024


def angle_table():
    radians = (np.arange(ANGLES) + 0.5) * (0.5 * math.pi / ANGLES) - 0.25 * math.pi
    magnify = MAG_BASE / (1.0 - ECCENTRIC * np.sin(2.0 * radians + 1.0))
    return np.cos(radians), magnify


def slab_reach(slab_count, slab_depth, row_share):
    _, magnify = angle_table()
    total_rows, total_slices = row_share * slab_count, slab_depth * slab_count
    rows = np.arange(total_rows)
    reach = 0
    for lift in range(-LIFT, LIFT + 1):
        sample = (rows[None] + 0.5 - total_rows / 2 - lift) / magnify[:, None] + total_slices / 2 - 0.5
        for tap in (np.floor(sample - 1e-3), np.floor(sample + 1e-3) + 1):
            inside = (tap >= 0) & (tap < total_slices)
            distance = np.abs(tap // slab_depth - rows[None] // row_share)
            reach = max(reach, int(distance[inside].max()))
    return reach


def lane_index():
    return lax.broadcasted_iota(jnp.int32, (SUBLANES, LANES), 1)


def sublane_index():
    return lax.broadcasted_iota(jnp.int32, (SUBLANES, LANES), 0)


def angle_facts(index):
    x = (index.astype(F32) + 0.5) * (0.5 * math.pi / ANGLES) - 0.25 * math.pi
    s = x * x
    sine = x * (1.0 + s * (-1 / 6 + s * (1 / 120 + s * (-1 / 5040 + s * (1 / 362880)))))
    cosine = 1.0 + s * (-1 / 2 + s * (1 / 24 + s * (-1 / 720 + s * (1 / 40320 + s * (-1 / 3628800)))))
    double = 2.0 * sine * cosine * math.cos(1.0) + (1.0 - 2.0 * sine * sine) * math.sin(1.0)
    return cosine, sine / cosine, (1.0 - ECCENTRIC * double) * (1.0 / MAG_BASE)


def spread_scalars(read, count, place):
    out = jnp.full((SUBLANES, LANES), read(0), jnp.int32)
    for item in range(1, count):
        out = jnp.where(place == item, read(item), out)
    return out


def pick(tile, index):
    numbers = lax.GatherDimensionNumbers(
        offset_dims=(),
        collapsed_slice_dims=(1,),
        start_index_map=(1,),
        operand_batching_dims=(0,),
        start_indices_batching_dims=(0,),
    )
    return lax.gather(tile, index[..., None], numbers, (1, 1), mode=lax.GatherScatterMode.PROMISE_IN_BOUNDS)


def next_lane(tile, following):
    lane = lane_index()
    return jnp.where(lane < LANES - 1, pltpu.roll(tile, LANES - 1, 1), pltpu.roll(following, LANES - 1, 1))


def rows_summed(parts):
    sub = sublane_index()
    step = 1
    while step < SUBLANES:
        low = jnp.bitwise_and(sub, step) == 0
        parts = [
            jnp.where(low, a, b) + pltpu.roll(jnp.where(low, b, a), step, 0) for a, b in zip(parts[::2], parts[1::2])
        ]
        step *= 2
    return parts[0]


def tile_of(ref, lead, tile):
    whole = (slice(None),) * (len(ref.shape) - 1 - len(lead))
    return ref[lead + whole + (slice(tile * LANES, (tile + 1) * LANES),)]


def column_center(column, cosine, column_count, cell_count):
    return (column + 0.5 - column_count / 2) * (PITCH * cell_count / column_count) / cosine + (
        cell_count / 2 - 0.5
    )


def shear_steps(group, row_count, tangent):
    row = (sublane_index() + group * SUBLANES).astype(F32)
    offset = (row + 0.5 - row_count / 2) * tangent
    whole = jnp.floor(offset)
    return whole.astype(jnp.int32), offset - whole


def cone_sample(rows, lifts, flat, total_rows, total_slices):
    return (rows + 0.5 - total_rows / 2 - lifts) * flat + (total_slices / 2 - 0.5)


def cone_total(sample, total_slices):
    whole = jnp.floor(sample)
    fraction = sample - whole
    low = jnp.where((whole >= 0) & (whole < total_slices), 1.0 - fraction, 0.0)
    return low + jnp.where((whole >= -1) & (whole < total_slices - 1), fraction, 0.0)


def column_of(tile, at):
    return jnp.broadcast_to(tile[:, at : at + 1], (SUBLANES, LANES))


def slabs_of(slab, order):
    return [slab + (1 - 2 * lax.rem(slab, 2)) * away for away in order]


def turned(slab, kinds):
    odd = lax.rem(slab, 2)
    return [{NEAR: 1 - odd, NEAR_SHARED: odd}.get(kind, 0) for kind in kinds]


def subset_cone(slab, slab_count, order, kinds, slab_depth, row_share, flat, lifts):
    lane = lane_index()
    total_rows, total_slices = row_share * slab_count, slab_depth * slab_count
    origin, turns = slabs_of(slab, order), turned(slab, kinds)
    source = sum(jnp.where(lane >= row_share * b, 1, 0) for b in range(1, len(order)))
    within = lane - source * row_share
    within = jnp.where(spread_scalars(lambda b: turns[b], len(order), source) == 1, row_share - 1 - within, within)
    rows = spread_scalars(lambda b: origin[b], len(order), source) * row_share + within
    real = (rows >= 0) & (rows < total_rows) & (lane < row_share * len(order))
    sample = cone_sample(rows.astype(F32), lifts, flat, total_rows, total_slices)
    weights = []
    for z in range(-1, slab_depth + 1):
        at = slab * slab_depth + z
        use = real & (at >= 0) & (at < total_slices)
        weights.append(jnp.where(use, jnp.maximum(0.0, 1.0 - jnp.abs(sample - at.astype(F32))), 0.0))
    return sample, weights


def adjoint_taps(tile, cosine, column_count, cell_count, half):
    spacing = PITCH * cell_count / column_count
    cell = (lane_index() + (tile * LANES - half)).astype(F32)
    inside = (cell >= 0) & (cell < cell_count)
    first = jnp.floor((cell - (cell_count / 2 + 0.5)) * cosine * (1.0 / spacing) + (column_count / 2 - 0.5 - 1e-3)) + 1.0
    taps = []
    for tap in range(3):
        column = first + tap
        weight = jnp.maximum(0.0, 1.0 - jnp.abs(cell - column_center(column, cosine, column_count, cell_count)))
        weight = jnp.where(inside & (column >= 0) & (column < column_count), weight, 0.0)
        taps.append((jnp.clip(column.astype(jnp.int32), 0, column_count - 1), weight))
    return taps


def adjoint_tiles(tile, tap, column_count, cell_count, half):
    spacing = PITCH * cell_count / column_count
    least = angle_table()[0].min()
    ends = [
        (tile * LANES - half + e - cell_count / 2 - 0.5) * c / spacing + column_count / 2 + 0.5
        for e in (0, LANES - 1)
        for c in (1.0, least)
    ]
    low = min(max(math.floor(min(ends) + tap - 0.6), 0), column_count - 1) // LANES
    high = min(max(math.ceil(max(ends) + tap + 0.6), 0), column_count - 1) // LANES
    return range(low, high + 1)


def store_line(line, base_ref, bend_ref):
    line = line + [jnp.zeros((SUBLANES, LANES), F32)]
    for tile in range(len(line) - 1):
        cut = slice(tile * LANES, (tile + 1) * LANES)
        base_ref[:, cut] = line[tile]
        bend_ref[:, cut] = next_lane(line[tile], line[tile + 1]) - line[tile]


def adjoint_steps(group, row_count, tangent):
    whole, fraction = shear_steps(group, row_count, tangent)
    place = lane_index() + (row_count // 2 - 1 - whole)
    return jnp.bitwise_and(place, LANES - 1), place < LANES, 1.0 - fraction


def sheared(base_ref, bend_ref, row, step, tiles):
    index, near, share = step
    before, out = None, []
    for tile in range(tiles + 1):
        cut = slice(tile * LANES, (tile + 1) * LANES)
        low = jnp.broadcast_to(base_ref[row : row + 1, cut], (SUBLANES, LANES))
        rise = jnp.broadcast_to(bend_ref[row : row + 1, cut], (SUBLANES, LANES))
        after = pick(low + share * rise, index)
        if tile:
            out.append(jnp.where(near, before, after))
        before = after
    return out


def subset_angles(angle_ref, lift_ref, subset_ref):
    members = subset_ref.shape[0]
    member = jnp.bitwise_and(sublane_index(), members - 1)
    cosine, _, flat = angle_facts(spread_scalars(lambda k: angle_ref[subset_ref[k]], members, member))
    lifts = spread_scalars(lambda k: lift_ref[subset_ref[k]], members, member).astype(F32)
    return cosine, flat, lifts


def member_tangents(angle_ref, subset_ref):
    indices = [angle_ref[subset_ref[k]] for k in range(subset_ref.shape[0])]
    return [angle_facts(jnp.full((SUBLANES, LANES), i, jnp.int32))[1] for i in indices]


def project_kernel(
    slab_count,
    angle_ref,
    lift_ref,
    subset_ref,
    volume_ref,
    measured_ref,
    block_ref,
    near_ref,
    low_ref,
    high_ref,
    cover_ref,
    rise_ref,
    first_ref,
    part_ref,
    end_ref,
    cell_ref,
    slope_ref,
):
    slab_depth, row_count, cell_count = volume_ref.shape
    row_share, view_count, column_count = measured_ref.shape
    subset_count = subset_ref.shape[0]
    half = row_count // 2
    tiles = cell_count // LANES
    groups = row_count // SUBLANES
    lane, sub = lane_index(), sublane_index()
    zero = jnp.zeros((SUBLANES, LANES), F32)
    width = column_count // 2

    assert (slab_depth, row_share) == (2, 3)
    slab = lax.axis_index("slab")
    odd = lax.rem(slab, 2)
    grows = odd == 1
    far_row = jnp.where(grows, 2, 0)
    for member in range(subset_count):
        view = pl.ds(subset_ref[member], 1)
        for side in range(2):
            at, cut = side * subset_count + member, slice(side * width, (side + 1) * width)
            rows = [measured_ref[row, view, cut] for row in range(row_share)]
            for row in range(row_share):
                block_ref[2 * slab_depth + row, at : at + 1, :] = rows[row]
            near_ref[2 * slab_depth, at : at + 1, :] = rows[1]
            near_ref[2 * slab_depth + 1, at : at + 1, :] = measured_ref[far_row, view, cut]
            low_ref[2 * slab_depth, at : at + 1, :] = rows[2]
            high_ref[2 * slab_depth, at : at + 1, :] = rows[2]

    cosine, _, flat = angle_facts(spread_scalars(lambda v: angle_ref[v], view_count, sub))
    lifts = spread_scalars(lambda v: lift_ref[v], view_count, sub).astype(F32)
    ends = [
        cone_sample((slab * row_share + row).astype(F32), lifts, flat, row_share * slab_count, slab_depth * slab_count)
        - (slab * slab_depth).astype(F32)
        for row in (0, row_share - 1)
    ]
    picked = sub == subset_ref[0]
    for member in range(1, subset_count):
        picked = picked | (sub == subset_ref[member])
    picked = jnp.where(picked, 1, 0)
    as_int = lambda mask: jnp.where(mask, 1, 0)
    near_up, near_down = picked * as_int(ends[1] > 0.75), picked * as_int(ends[0] < 0.25)
    far_up, far_down = picked * as_int(ends[1] > 2.5), picked * as_int(ends[0] < -1.5)
    near_places = [(near_up * odd) == 1, (near_down * (1 - odd)) == 1]
    high_places = (far_up * odd + far_down * (1 - odd)) == 1
    low_places = (far_up * (1 - odd) + far_down * odd) == 1

    for depth in range(slab_depth):
        for group in range(groups):
            band = slice(group * SUBLANES, (group + 1) * SUBLANES)
            cells = [tile_of(volume_ref, (depth, band), tile) for tile in range(tiles)] + [zero]
            for tile in range(tiles):
                rise_ref[depth, band, tile * LANES : (tile + 1) * LANES] = (
                    next_lane(cells[tile], cells[tile + 1]) - cells[tile]
                )
            first_ref[depth, band, :] = column_of(cells[0], 0)

    def one_view(view, carry):
        _, tangent, _ = angle_facts(jnp.full((SUBLANES, LANES), angle_ref[view], jnp.int32))
        low_end, high_end = zero, zero
        sums = [[zero] * (tiles + 1) for _ in range(slab_depth)]
        for group in range(groups):
            band = slice(group * SUBLANES, (group + 1) * SUBLANES)
            whole, fraction = shear_steps(group, row_count, tangent)
            place = lane + (whole + half)
            index = jnp.bitwise_and(place, LANES - 1)
            near, last = place < LANES, index == LANES - 1
            enter = jnp.where(last, fraction, 0.0)
            low_end = low_end + jnp.where(near, enter, 1.0)
            high_end = high_end + jnp.where(near, 1.0 - enter, 0.0)
            for depth in range(slab_depth):
                before = enter * first_ref[depth, band, :]
                for tile in range(tiles + 1):
                    after = zero
                    if tile < tiles:
                        at = (depth, band)
                        after = pick(tile_of(volume_ref, at, tile) + fraction * tile_of(rise_ref, at, tile), index)
                    sums[depth][tile] = sums[depth][tile] + jnp.where(near, before, after)
                    before = after
        end_ref[0, view, :, :] = low_end
        end_ref[1, view, :, :] = high_end
        for depth in range(slab_depth):
            for tile in range(tiles + 1):
                part_ref[depth, view, :, tile * LANES : (tile + 1) * LANES] = sums[depth][tile]
        return carry

    lax.fori_loop(0, view_count, one_view, 0, unroll=4)

    shift = LANES - half
    inside = [None] * (tiles + 1)
    inside[0], inside[tiles] = lane >= shift, lane < shift

    def store(at, line):
        line = [jnp.where(mask, cells, 0.0) if mask is not None else cells for cells, mask in zip(line, inside)] + [zero]
        for tile in range(tiles + 1):
            cut = slice(tile * LANES, (tile + 1) * LANES)
            cell_ref[at, :, cut] = line[tile]
            slope_ref[at, :, cut] = next_lane(line[tile], line[tile + 1]) - line[tile]

    views = range(view_count)
    for depth in range(slab_depth):
        store(depth, [rows_summed([tile_of(part_ref, (depth, v), t) for v in views]) for t in range(tiles + 1)])
    level = zero + float(row_count)
    ends = [rows_summed([end_ref[e, v, :, :] for v in views]) for e in range(2)]
    store(slab_depth, [ends[0]] + [level] * (tiles - 1) + [ends[1]])

    factor = 1.0 / (row_count * cosine)
    least = angle_table()[0].min()
    for tile in range(column_count // LANES):
        column = (lane + tile * LANES).astype(F32)
        center = column_center(column, cosine, column_count, cell_count)
        whole = jnp.floor(center)
        fraction = center - whole
        place = jnp.clip(whole.astype(jnp.int32) + shift, shift - 2, shift + cell_count)
        block, index = jnp.right_shift(place, 7), jnp.bitwise_and(place, LANES - 1)
        ends = [column_center(tile * LANES + e, c, column_count, cell_count) for e in (0, LANES - 1) for c in (1.0, least)]
        low = min(max(math.floor(min(ends) - 1e-2) + shift, shift - 2), shift + cell_count) // LANES
        high = min(max(math.floor(max(ends) + 1e-2) + shift, shift - 2), shift + cell_count) // LANES
        cells, slopes = [zero] * slab_depth + [level], [zero] * (slab_depth + 1)
        for source in range(low, high + 1):
            here = block == source
            for at in range(slab_depth + 1):
                if at == slab_depth and source not in (0, tiles):
                    continue
                cells[at] = jnp.where(here, pick(tile_of(cell_ref, (at,), source), index), cells[at])
                slopes[at] = jnp.where(here, pick(tile_of(slope_ref, (at,), source), index), slopes[at])
        profiles = [(c + fraction * s) * factor for c, s in zip(cells, slopes)]
        side, inner = divmod(tile * LANES, width)
        for depth in range(slab_depth):
            to = (depth * 2 + side, slice(None), slice(inner, inner + LANES))
            measured = tile_of(measured_ref, (depth,), tile)
            last = tile_of(measured_ref, (depth * (row_share - 1),), tile)
            block_ref[to] = profiles[depth]
            near_ref[to] = jnp.where(near_places[depth], last, profiles[depth])
            low_ref[to] = jnp.where(low_places, measured, profiles[depth])
            high_ref[to] = jnp.where(high_places, measured, profiles[depth])
        cover_ref[:, tile * LANES : (tile + 1) * LANES] = profiles[slab_depth]


def divisor_kernel(
    slab_count,
    order,
    kinds,
    angle_ref,
    lift_ref,
    subset_ref,
    cover_ref,
    bound_ref,
    own_ref,
    rows_ref,
    own_cone_ref,
    cone_ref,
    place_ref,
    tap_ref,
    edge_ref,
    bend_ref,
    sub_ref,
):
    slab_depth, row_count, cell_count = bound_ref.shape
    row_share, view_count, column_count = own_ref.shape
    subset_count = subset_ref.shape[0]
    total_rows, total_slices = row_share * slab_count, slab_depth * slab_count
    tiles, columns = cell_count // LANES, column_count // LANES
    width = column_count // 2
    sub = sublane_index()
    zero = jnp.zeros((SUBLANES, LANES), F32)
    slab = lax.axis_index("slab")

    _, _, flat = angle_facts(spread_scalars(lambda v: angle_ref[v], view_count, sub))
    lifts = spread_scalars(lambda v: lift_ref[v], view_count, sub).astype(F32)
    lane = lane_index()
    origin = slabs_of(slab, order)
    source = sum(jnp.where(lane >= slab_depth * b, 1, 0) for b in range(1, len(order)))
    slices = spread_scalars(lambda b: origin[b], len(order), source) * slab_depth + (lane - source * slab_depth)
    held = (slices >= 0) & (slices < total_slices)
    slices = slices.astype(F32)
    for row in range(row_share):
        sample = cone_sample((slab * row_share + row).astype(F32), lifts, flat, total_rows, total_slices)
        weights = jnp.where(held, jnp.maximum(0.0, 1.0 - jnp.abs(sample - slices)), 0.0)
        for place in range(slab_depth * len(order)):
            own_cone_ref[place, row, :, :] = column_of(weights, place)
        total = cone_total(sample, total_slices)
        for tile in range(columns):
            cut = slice(tile * LANES, (tile + 1) * LANES)
            own_ref[row, :, cut] = 1.0 / jnp.maximum(total * cover_ref[:, cut], LEN_FLOOR)

    cosine, flat, lifts = subset_angles(angle_ref, lift_ref, subset_ref)
    tangents = member_tangents(angle_ref, subset_ref)
    for member in range(subset_count):
        view = pl.ds(subset_ref[member], 1)
        for side in range(2):
            at = slice(side * subset_count + member, side * subset_count + member + 1)
            sub_ref[at, :] = cover_ref[view, side * width : (side + 1) * width]
    sample, weights = subset_cone(slab, slab_count, order, kinds, slab_depth, row_share, flat, lifts)
    total = cone_total(sample, total_slices)
    for place in range(row_share * len(order)):
        for z, w in enumerate(weights):
            cone_ref[place, z, :, :] = column_of(w, place)
        length = column_of(total, place)
        for tile in range(width // LANES):
            cut = slice(tile * LANES, (tile + 1) * LANES)
            rows_ref[place, :, cut] = 1.0 / jnp.maximum(length * sub_ref[:, cut], LEN_FLOOR)

    factor = 1.0 / (row_count * cosine)
    line = []
    for tile in range(tiles + 1):
        taps = adjoint_taps(tile, cosine, column_count, cell_count, row_count // 2)
        for tap, (place, weight) in enumerate(taps):
            place_ref[tile, tap, :, :] = place
            tap_ref[tile, tap, :, :] = weight * factor
        line.append(sum(weight for _, weight in taps) * factor)
    store_line(line, edge_ref, bend_ref)
    slice_total = []
    for depth in range(slab_depth):
        t = jnp.sum(weights[1 + depth], axis=1, keepdims=True)
        slice_total.append([jnp.broadcast_to(t[k : k + 1], (SUBLANES, LANES)) for k in range(subset_count)])

    def one_group(group, carry):
        band = pl.ds(pl.multiple_of(group * SUBLANES, SUBLANES), SUBLANES)
        weight = [[zero] * tiles for _ in range(slab_depth)]
        for member in range(subset_count):
            line = sheared(edge_ref, bend_ref, member, adjoint_steps(group, row_count, tangents[member]), tiles)
            for depth in range(slab_depth):
                for tile in range(tiles):
                    weight[depth][tile] = weight[depth][tile] + slice_total[depth][member] * line[tile]
        for depth in range(slab_depth):
            for tile in range(tiles):
                bound_ref[depth, band, tile * LANES : (tile + 1) * LANES] = 1.0 / jnp.maximum(
                    weight[depth][tile], LEN_FLOOR * subset_count / row_count
                )
        return carry

    lax.fori_loop(0, row_count // SUBLANES, one_group, 0)


def update_kernel(
    order,
    kinds,
    angle_ref,
    subset_ref,
    volume_ref,
    measured_ref,
    bound_ref,
    own_ref,
    rows_ref,
    own_cone_ref,
    cone_ref,
    place_ref,
    tap_ref,
    *refs,
):
    blocks = refs[: len(order)]
    residual_ref, updated_ref, profile_ref, spread_ref, cell_ref, slope_ref, rest_ref, new_ref, row_ref, sent = refs[len(order) :]
    slab_depth, row_count, cell_count = volume_ref.shape
    row_share, view_count, column_count = measured_ref.shape
    subset_count = subset_ref.shape[0]
    tiles, columns = cell_count // LANES, column_count // LANES
    width = column_count // 2
    zero = jnp.zeros((SUBLANES, LANES), F32)
    slab = lax.axis_index("slab")
    odd = lax.rem(slab, 2)
    turns = turned(slab, kinds)
    mate_block, other_block = (blocks[order.index(away)] for away in (1, -1))

    groups = row_count // SUBLANES
    for tile in range(columns):
        side, inner = divmod(tile * LANES, width)
        image = [zero] * row_share
        for place, block in enumerate(blocks):
            for depth in range(slab_depth):
                cells = block[depth * 2 + side, :, inner : inner + LANES]
                for row in range(row_share):
                    image[row] = image[row] + own_cone_ref[place * slab_depth + depth, row, :, :] * cells
        cut = slice(tile * LANES, (tile + 1) * LANES)
        for row in range(row_share):
            rest_ref[row, :, cut] = (measured_ref[row, :, cut] - image[row]) * own_ref[row, :, cut]
    copies = [pltpu.make_async_copy(rest_ref, residual_ref, sent.at[groups])]
    copies[0].start()

    for member in range(subset_count):
        view = pl.ds(subset_ref[member], 1)
        for side in range(2):
            at = slice(side * subset_count + member, side * subset_count + member + 1)
            other = other_block[(slab_depth - 1) * 2 + side, view, :], other_block[side, view, :]
            mate = mate_block[(slab_depth - 1) * 2 + side, view, :], mate_block[side, view, :]
            profile_ref[0, at, :] = jnp.where(odd == 0, other[0], mate[0])
            for depth in range(slab_depth):
                profile_ref[1 + depth, at, :] = blocks[0][depth * 2 + side, view, :]
            profile_ref[1 + slab_depth, at, :] = jnp.where(odd == 0, mate[1], other[1])

    moved = [(b, j) for b, kind in enumerate(kinds) for j in range({FULL: 0, FAR: 2}.get(kind, 1))]
    for at_row, (b, j) in enumerate(moved):
        depth = turns[b] if kinds[b] in (NEAR, NEAR_SHARED) else j
        for member in range(subset_count):
            view = pl.ds(subset_ref[member], 1)
            for side in range(2):
                at = slice(side * subset_count + member, side * subset_count + member + 1)
                row_ref[at_row, at, :] = blocks[b][depth * 2 + side, view, :]

    inner_tiles = width // LANES
    spread = [[zero] * inner_tiles for _ in range(slab_depth)]
    for place in range(row_share * len(order)):
        weight = [cone_ref[place, z, :, :] for z in range(slab_depth + 2)]
        block, row = divmod(place, row_share)
        here = (block, row) in moved
        held = row_ref if here else blocks[block]
        at_row = moved.index((block, row)) if here else 2 * slab_depth + row - sum(b == block for b, _ in moved)
        for tile in range(inner_tiles):
            cut = slice(tile * LANES, (tile + 1) * LANES)
            image = weight[0] * profile_ref[0, :, cut]
            for z in range(1, slab_depth + 2):
                image = image + weight[z] * profile_ref[z, :, cut]
            rest = (held[at_row, :, cut] - image) * rows_ref[place, :, cut]
            for depth in range(slab_depth):
                spread[depth][tile] = spread[depth][tile] + weight[1 + depth] * rest
    for depth in range(slab_depth):
        for tile in range(inner_tiles):
            for side in range(2):
                spread_ref[
                    depth * subset_count : (depth + 1) * subset_count,
                    side * width + tile * LANES : side * width + (tile + 1) * LANES,
                ] = spread[depth][tile][side * subset_count : (side + 1) * subset_count]

    line = []
    for tile in range(tiles + 1):
        value = zero
        for tap in range(3):
            place = place_ref[tile, tap, :, :]
            block, index = jnp.right_shift(place, 7), jnp.bitwise_and(place, LANES - 1)
            found = zero
            for at in adjoint_tiles(tile, tap, column_count, cell_count, row_count // 2):
                found = jnp.where(block == at, pick(tile_of(spread_ref, (), at), index), found)
            value = value + tap_ref[tile, tap, :, :] * found
        line.append(value)
    store_line(line, cell_ref, slope_ref)

    tangents = member_tangents(angle_ref, subset_ref)
    for group in range(groups):
        band = slice(group * SUBLANES, (group + 1) * SUBLANES)
        back = [[zero] * tiles for _ in range(slab_depth)]
        for member in range(subset_count):
            step = adjoint_steps(group, row_count, tangents[member])
            for depth in range(slab_depth):
                line = sheared(cell_ref, slope_ref, depth * subset_count + member, step, tiles)
                back[depth] = [b + a for b, a in zip(back[depth], line)]
        for depth in range(slab_depth):
            for tile in range(tiles):
                cut = slice(tile * LANES, (tile + 1) * LANES)
                new_ref[depth, band, cut] = (
                    volume_ref[depth, band, cut] + back[depth][tile] * bound_ref[depth, band, cut]
                )
        copies.append(pltpu.make_async_copy(new_ref.at[:, band, :], updated_ref.at[:, band, :], sent.at[group]))
        copies[-1].start()
    for copy in copies:
        copy.wait()


def swapped(block):
    return lax.ppermute(block, "slab", [(i, i ^ 1) for i in range(lax.axis_size("slab"))])


def from_chip(block, distance):
    slabs = range(lax.axis_size("slab"))
    steps = [(i + 2 * distance * (1 - 2 * (i % 2)), i) for i in slabs]
    pairs = [p for p in steps if p[0] in slabs]
    idle = [i for i in slabs if i not in [p[0] for p in pairs]]
    unmet = [i for i in slabs if i not in [p[1] for p in pairs]]
    near = [i for i in idle if i ^ 1 in unmet]
    pairs += [(i, i ^ 1) for i in near]
    pairs += zip([i for i in idle if i not in near], [i for i in unmet if i ^ 1 not in near])
    return lax.ppermute(block, "slab", pairs)


def fetches(reach):
    return [s * d for d in range(reach // 2 + 1, 0, -1) for s in (1, -1) if 2 * d - (s > 0) <= reach]


def window(reach):
    order, kinds = [0, 1], [FULL, FULL]
    for distance in fetches(reach):
        near = distance == 1
        for away, kind in ((2 * distance, NEAR if near else FAR), (1 - 2 * distance, NEAR_SHARED if near else FAR)):
            if abs(away) <= reach:
                order.append(away)
                kinds.append(kind)
    assert sorted(order) == list(range(-reach, reach + 1))
    return tuple(order), tuple(kinds)


def gathered(own, near, low, high, reach, meanwhile):
    sent = {distance: near if distance == 1 else high if distance > 0 else low for distance in fetches(reach)}
    received = {distance: from_chip(block, distance) for distance, block in sent.items()}
    done = meanwhile()
    own, done = lax.optimization_barrier((own, done))
    blocks = {0: own, 1: swapped(own)}
    arrived, done = lax.optimization_barrier((list(received.values()), done))
    for distance, block in zip(received, arrived):
        if 2 * abs(distance) <= reach:
            blocks[2 * distance] = block
        if abs(1 - 2 * distance) <= reach:
            blocks[1 - 2 * distance] = swapped(block)
    return [blocks[away] for away in window(reach)[0]], done


def per_device(volume, measured, view_angle, view_lift, subset):
    slab_count = lax.axis_size("slab")
    slab_depth, row_count, cell_count = volume.shape
    row_share, view_count, column_count = measured.shape
    subset_count = subset.shape[0]
    tiles = cell_count // LANES
    reach = slab_reach(slab_count, slab_depth, row_share)
    here = lambda x: pltpu.with_memory_space_constraint(x, pltpu.VMEM)
    there = lambda x: pltpu.with_memory_space_constraint(x, pltpu.HBM)
    small = pltpu.CompilerParams(vmem_limit_bytes=VMEM_LIMIT)
    smem, vmem = pl.BlockSpec(memory_space=pltpu.SMEM), pl.BlockSpec(memory_space=pltpu.VMEM)
    wide = (tiles + 1) * LANES
    block_of = lambda rows: pltpu.VMEM((2 * slab_depth + rows, SUBLANES, column_count // 2), F32)
    own, near, low, high, cover = pl.pallas_call(
        functools.partial(project_kernel, slab_count),
        out_shape=(
            block_of(row_share),
            block_of(2),
            block_of(1),
            block_of(1),
            pltpu.VMEM((view_count, column_count), F32),
        ),
        in_specs=[smem] * 3 + [vmem] * 2,
        out_specs=(vmem,) * 5,
        scratch_shapes=[
            pltpu.VMEM(volume.shape, F32),
            pltpu.VMEM((slab_depth, row_count, LANES), F32),
            pltpu.VMEM((slab_depth, view_count, SUBLANES, wide), F32),
            pltpu.VMEM((2, view_count, SUBLANES, LANES), F32),
        ]
        + [pltpu.VMEM((slab_depth + 1, SUBLANES, wide), F32)] * 2,
        compiler_params=small,
        name="project",
    )(*map(there, (view_angle, view_lift, subset, volume, measured)))
    cover = here(cover)
    order, kinds = window(reach)
    divide = pl.pallas_call(
        functools.partial(divisor_kernel, slab_count, order, kinds),
        out_shape=(
            pltpu.VMEM(volume.shape, F32),
            pltpu.VMEM(measured.shape, F32),
            pltpu.VMEM((row_share * len(order), SUBLANES, column_count // 2), F32),
            pltpu.VMEM((slab_depth * len(order), row_share, SUBLANES, LANES), F32),
            pltpu.VMEM((row_share * len(order), slab_depth + 2, SUBLANES, LANES), F32),
            pltpu.VMEM((tiles + 1, 3, SUBLANES, LANES), jnp.int32),
            pltpu.VMEM((tiles + 1, 3, SUBLANES, LANES), F32),
        ),
        in_specs=[smem] * 3 + [vmem],
        out_specs=(vmem,) * 7,
        scratch_shapes=[pltpu.VMEM((SUBLANES, wide), F32)] * 2 + [pltpu.VMEM((SUBLANES, column_count // 2), F32)],
        cost_estimate=pl.CostEstimate(flops=4_000_000, bytes_accessed=8_000_000, transcendentals=0),
        compiler_params=small,
        name="divisors",
    )
    blocks, divisors = gathered(own, near, low, high, reach, lambda: divide(view_angle, view_lift, subset, cover))
    return pl.pallas_call(
        functools.partial(update_kernel, order, kinds),
        out_shape=(
            jax.ShapeDtypeStruct(measured.shape, F32),
            jax.ShapeDtypeStruct(volume.shape, F32),
        ),
        in_specs=[smem] * 2 + [vmem] * (2 + len(divisors) + len(order)),
        out_specs=(pl.BlockSpec(memory_space=pl.ANY),) * 2,
        scratch_shapes=[
            pltpu.VMEM((slab_depth + 2, SUBLANES, column_count // 2), F32),
            pltpu.VMEM((SUBLANES, column_count), F32),
            pltpu.VMEM((SUBLANES, wide), F32),
            pltpu.VMEM((SUBLANES, wide), F32),
            pltpu.VMEM(measured.shape, F32),
            pltpu.VMEM(volume.shape, F32),
            pltpu.VMEM((2 * len(order), SUBLANES, column_count // 2), F32),
            pltpu.SemaphoreType.DMA((row_count // SUBLANES + 1,)),
        ],
        compiler_params=small,
        name="update",
    )(view_angle, subset, *map(here, (volume, measured, *divisors, *blocks)))


def solution(mesh):
    in_specs = (
        P(("scan", "slab"), None, None),
        P(("scan", "slab"), None, None),
        P("scan"),
        P("scan"),
        P("scan"),
    )
    out_specs = (P(("scan", "slab"), None, None), P(("scan", "slab"), None, None))
    return jax.shard_map(
        per_device, mesh=mesh, in_specs=in_specs, out_specs=out_specs, check_vma=False
    )
```

```python
import functools
import math

import jax
import jax.numpy as jnp
import numpy as np
from jax import lax
from jax.experimental import pallas as pl
from jax.experimental.pallas import tpu as pltpu
from jax.sharding import PartitionSpec as P

ANGLES = 180
LIFT = 6
PITCH = 0.9
MAG_BASE = 1.5
ECCENTRIC = 0.12
LEN_FLOOR = 0.25
LANES = 128
SUBLANES = 8
F32 = jnp.float32
FULL, NEAR, NEAR_SHARED, FAR = range(4)
VMEM_LIMIT = 8 * 1024 * 1024


def angle_table():
    radians = (np.arange(ANGLES) + 0.5) * (0.5 * math.pi / ANGLES) - 0.25 * math.pi
    magnify = MAG_BASE / (1.0 - ECCENTRIC * np.sin(2.0 * radians + 1.0))
    return np.cos(radians), magnify


def slab_reach(slab_count, slab_depth, row_share):
    _, magnify = angle_table()
    total_rows, total_slices = row_share * slab_count, slab_depth * slab_count
    rows = np.arange(total_rows)
    reach = 0
    for lift in range(-LIFT, LIFT + 1):
        sample = (rows[None] + 0.5 - total_rows / 2 - lift) / magnify[:, None] + total_slices / 2 - 0.5
        for tap in (np.floor(sample - 1e-3), np.floor(sample + 1e-3) + 1):
            inside = (tap >= 0) & (tap < total_slices)
            distance = np.abs(tap // slab_depth - rows[None] // row_share)
            reach = max(reach, int(distance[inside].max()))
    return reach


def lane_index():
    return lax.broadcasted_iota(jnp.int32, (SUBLANES, LANES), 1)


def sublane_index():
    return lax.broadcasted_iota(jnp.int32, (SUBLANES, LANES), 0)


def angle_facts(index):
    x = (index.astype(F32) + 0.5) * (0.5 * math.pi / ANGLES) - 0.25 * math.pi
    s = x * x
    sine = x * (1.0 + s * (-1 / 6 + s * (1 / 120 + s * (-1 / 5040 + s * (1 / 362880)))))
    cosine = 1.0 + s * (-1 / 2 + s * (1 / 24 + s * (-1 / 720 + s * (1 / 40320 + s * (-1 / 3628800)))))
    double = 2.0 * sine * cosine * math.cos(1.0) + (1.0 - 2.0 * sine * sine) * math.sin(1.0)
    return cosine, sine / cosine, (1.0 - ECCENTRIC * double) * (1.0 / MAG_BASE)


def spread_scalars(read, count, place):
    out = jnp.full((SUBLANES, LANES), read(0), jnp.int32)
    for item in range(1, count):
        out = jnp.where(place == item, read(item), out)
    return out


def pick(tile, index):
    numbers = lax.GatherDimensionNumbers(
        offset_dims=(),
        collapsed_slice_dims=(1,),
        start_index_map=(1,),
        operand_batching_dims=(0,),
        start_indices_batching_dims=(0,),
    )
    return lax.gather(tile, index[..., None], numbers, (1, 1), mode=lax.GatherScatterMode.PROMISE_IN_BOUNDS)


def next_lane(tile, following):
    lane = lane_index()
    return jnp.where(lane < LANES - 1, pltpu.roll(tile, LANES - 1, 1), pltpu.roll(following, LANES - 1, 1))


def rows_summed(parts):
    sub = sublane_index()
    step = 1
    while step < SUBLANES:
        low = jnp.bitwise_and(sub, step) == 0
        parts = [
            jnp.where(low, a, b) + pltpu.roll(jnp.where(low, b, a), step, 0) for a, b in zip(parts[::2], parts[1::2])
        ]
        step *= 2
    return parts[0]


def tile_of(ref, lead, tile):
    whole = (slice(None),) * (len(ref.shape) - 1 - len(lead))
    return ref[lead + whole + (slice(tile * LANES, (tile + 1) * LANES),)]


def column_center(column, cosine, column_count, cell_count):
    return (column + 0.5 - column_count / 2) * (PITCH * cell_count / column_count) / cosine + (
        cell_count / 2 - 0.5
    )


def shear_steps(group, row_count, tangent):
    row = (sublane_index() + group * SUBLANES).astype(F32)
    offset = (row + 0.5 - row_count / 2) * tangent
    whole = jnp.floor(offset)
    return whole.astype(jnp.int32), offset - whole


def cone_sample(rows, lifts, flat, total_rows, total_slices):
    return (rows + 0.5 - total_rows / 2 - lifts) * flat + (total_slices / 2 - 0.5)


def cone_total(sample, total_slices):
    whole = jnp.floor(sample)
    fraction = sample - whole
    low = jnp.where((whole >= 0) & (whole < total_slices), 1.0 - fraction, 0.0)
    return low + jnp.where((whole >= -1) & (whole < total_slices - 1), fraction, 0.0)


def column_of(tile, at):
    return jnp.broadcast_to(tile[:, at : at + 1], (SUBLANES, LANES))


def slabs_of(slab, order):
    return [slab + (1 - 2 * lax.rem(slab, 2)) * away for away in order]


def turned(slab, kinds):
    odd = lax.rem(slab, 2)
    return [{NEAR: 1 - odd, NEAR_SHARED: odd}.get(kind, 0) for kind in kinds]


def subset_cone(slab, slab_count, order, kinds, slab_depth, row_share, flat, lifts):
    lane = lane_index()
    total_rows, total_slices = row_share * slab_count, slab_depth * slab_count
    origin, turns = slabs_of(slab, order), turned(slab, kinds)
    source = sum(jnp.where(lane >= row_share * b, 1, 0) for b in range(1, len(order)))
    within = lane - source * row_share
    within = jnp.where(spread_scalars(lambda b: turns[b], len(order), source) == 1, row_share - 1 - within, within)
    rows = spread_scalars(lambda b: origin[b], len(order), source) * row_share + within
    real = (rows >= 0) & (rows < total_rows) & (lane < row_share * len(order))
    sample = cone_sample(rows.astype(F32), lifts, flat, total_rows, total_slices)
    weights = []
    for z in range(-1, slab_depth + 1):
        at = slab * slab_depth + z
        use = real & (at >= 0) & (at < total_slices)
        weights.append(jnp.where(use, jnp.maximum(0.0, 1.0 - jnp.abs(sample - at.astype(F32))), 0.0))
    return sample, weights


def adjoint_taps(tile, cosine, column_count, cell_count, half):
    spacing = PITCH * cell_count / column_count
    cell = (lane_index() + (tile * LANES - half)).astype(F32)
    inside = (cell >= 0) & (cell < cell_count)
    first = jnp.floor((cell - (cell_count / 2 + 0.5)) * cosine * (1.0 / spacing) + (column_count / 2 - 0.5 - 1e-3)) + 1.0
    taps = []
    for tap in range(3):
        column = first + tap
        weight = jnp.maximum(0.0, 1.0 - jnp.abs(cell - column_center(column, cosine, column_count, cell_count)))
        weight = jnp.where(inside & (column >= 0) & (column < column_count), weight, 0.0)
        taps.append((jnp.clip(column.astype(jnp.int32), 0, column_count - 1), weight))
    return taps


def adjoint_tiles(tile, tap, column_count, cell_count, half):
    spacing = PITCH * cell_count / column_count
    least = angle_table()[0].min()
    ends = [
        (tile * LANES - half + e - cell_count / 2 - 0.5) * c / spacing + column_count / 2 + 0.5
        for e in (0, LANES - 1)
        for c in (1.0, least)
    ]
    low = min(max(math.floor(min(ends) + tap - 0.6), 0), column_count - 1) // LANES
    high = min(max(math.ceil(max(ends) + tap + 0.6), 0), column_count - 1) // LANES
    return range(low, high + 1)


def store_line(line, base_ref, bend_ref):
    line = line + [jnp.zeros((SUBLANES, LANES), F32)]
    for tile in range(len(line) - 1):
        cut = slice(tile * LANES, (tile + 1) * LANES)
        base_ref[:, cut] = line[tile]
        bend_ref[:, cut] = next_lane(line[tile], line[tile + 1]) - line[tile]


def adjoint_steps(group, row_count, tangent):
    whole, fraction = shear_steps(group, row_count, tangent)
    place = lane_index() + (row_count // 2 - 1 - whole)
    return jnp.bitwise_and(place, LANES - 1), place < LANES, 1.0 - fraction


def sheared(base_ref, bend_ref, row, step, tiles):
    index, near, share = step
    before, out = None, []
    for tile in range(tiles + 1):
        cut = slice(tile * LANES, (tile + 1) * LANES)
        low = jnp.broadcast_to(base_ref[row : row + 1, cut], (SUBLANES, LANES))
        rise = jnp.broadcast_to(bend_ref[row : row + 1, cut], (SUBLANES, LANES))
        after = pick(low + share * rise, index)
        if tile:
            out.append(jnp.where(near, before, after))
        before = after
    return out


def subset_angles(angle_ref, lift_ref, subset_ref):
    members = subset_ref.shape[0]
    member = jnp.bitwise_and(sublane_index(), members - 1)
    cosine, _, flat = angle_facts(spread_scalars(lambda k: angle_ref[subset_ref[k]], members, member))
    lifts = spread_scalars(lambda k: lift_ref[subset_ref[k]], members, member).astype(F32)
    return cosine, flat, lifts


def member_tangents(angle_ref, subset_ref):
    indices = [angle_ref[subset_ref[k]] for k in range(subset_ref.shape[0])]
    return [angle_facts(jnp.full((SUBLANES, LANES), i, jnp.int32))[1] for i in indices]


def project_kernel(
    slab_count,
    angle_ref,
    lift_ref,
    subset_ref,
    volume_ref,
    measured_ref,
    block_ref,
    near_ref,
    low_ref,
    high_ref,
    cover_ref,
    rise_ref,
    first_ref,
    part_ref,
    end_ref,
    cell_ref,
    slope_ref,
):
    slab_depth, row_count, cell_count = volume_ref.shape
    row_share, view_count, column_count = measured_ref.shape
    subset_count = subset_ref.shape[0]
    half = row_count // 2
    tiles = cell_count // LANES
    groups = row_count // SUBLANES
    lane, sub = lane_index(), sublane_index()
    zero = jnp.zeros((SUBLANES, LANES), F32)
    width = column_count // 2

    assert (slab_depth, row_share) == (2, 3)
    slab = lax.axis_index("slab")
    odd = lax.rem(slab, 2)
    grows = odd == 1
    far_row = jnp.where(grows, 2, 0)
    for member in range(subset_count):
        view = pl.ds(subset_ref[member], 1)
        for side in range(2):
            at, cut = side * subset_count + member, slice(side * width, (side + 1) * width)
            rows = [measured_ref[row, view, cut] for row in range(row_share)]
            for row in range(row_share):
                block_ref[2 * slab_depth + row, at : at + 1, :] = rows[row]
            near_ref[2 * slab_depth, at : at + 1, :] = rows[1]
            near_ref[2 * slab_depth + 1, at : at + 1, :] = measured_ref[far_row, view, cut]
            low_ref[2 * slab_depth, at : at + 1, :] = rows[2]
            for more in range(2):
                high_ref[2 * slab_depth + more, at : at + 1, :] = rows[2]

    cosine, _, flat = angle_facts(spread_scalars(lambda v: angle_ref[v], view_count, sub))
    lifts = spread_scalars(lambda v: lift_ref[v], view_count, sub).astype(F32)
    ends = [
        cone_sample((slab * row_share + row).astype(F32), lifts, flat, row_share * slab_count, slab_depth * slab_count)
        - (slab * slab_depth).astype(F32)
        for row in (0, row_share - 1)
    ]
    picked = sub == subset_ref[0]
    for member in range(1, subset_count):
        picked = picked | (sub == subset_ref[member])
    picked = jnp.where(picked, 1, 0)
    as_int = lambda mask: jnp.where(mask, 1, 0)
    near_up, near_down = picked * as_int(ends[1] > 0.75), picked * as_int(ends[0] < 0.25)
    far_up, far_down = picked * as_int(ends[1] > 2.5), picked * as_int(ends[0] < -1.5)
    near_places = [(near_up * odd) == 1, (near_down * (1 - odd)) == 1]
    high_places = (far_up * odd + far_down * (1 - odd)) == 1
    low_places = (far_up * (1 - odd) + far_down * odd) == 1

    for depth in range(slab_depth):
        for group in range(groups):
            band = slice(group * SUBLANES, (group + 1) * SUBLANES)
            cells = [tile_of(volume_ref, (depth, band), tile) for tile in range(tiles)] + [zero]
            for tile in range(tiles):
                rise_ref[depth, band, tile * LANES : (tile + 1) * LANES] = (
                    next_lane(cells[tile], cells[tile + 1]) - cells[tile]
                )
            first_ref[depth, band, :] = column_of(cells[0], 0)

    def one_view(view, carry):
        _, tangent, _ = angle_facts(jnp.full((SUBLANES, LANES), angle_ref[view], jnp.int32))
        low_end, high_end = zero, zero
        sums = [[zero] * (tiles + 1) for _ in range(slab_depth)]
        for group in range(groups):
            band = slice(group * SUBLANES, (group + 1) * SUBLANES)
            whole, fraction = shear_steps(group, row_count, tangent)
            place = lane + (whole + half)
            index = jnp.bitwise_and(place, LANES - 1)
            near, last = place < LANES, index == LANES - 1
            enter = jnp.where(last, fraction, 0.0)
            low_end = low_end + jnp.where(near, enter, 1.0)
            high_end = high_end + jnp.where(near, 1.0 - enter, 0.0)
            for depth in range(slab_depth):
                before = enter * first_ref[depth, band, :]
                for tile in range(tiles + 1):
                    after = zero
                    if tile < tiles:
                        at = (depth, band)
                        after = pick(tile_of(volume_ref, at, tile) + fraction * tile_of(rise_ref, at, tile), index)
                    sums[depth][tile] = sums[depth][tile] + jnp.where(near, before, after)
                    before = after
        end_ref[0, view, :, :] = low_end
        end_ref[1, view, :, :] = high_end
        for depth in range(slab_depth):
            for tile in range(tiles + 1):
                part_ref[depth, view, :, tile * LANES : (tile + 1) * LANES] = sums[depth][tile]
        return carry

    lax.fori_loop(0, view_count, one_view, 0, unroll=4)

    shift = LANES - half
    inside = [None] * (tiles + 1)
    inside[0], inside[tiles] = lane >= shift, lane < shift

    def store(at, line):
        line = [jnp.where(mask, cells, 0.0) if mask is not None else cells for cells, mask in zip(line, inside)] + [zero]
        for tile in range(tiles + 1):
            cut = slice(tile * LANES, (tile + 1) * LANES)
            cell_ref[at, :, cut] = line[tile]
            slope_ref[at, :, cut] = next_lane(line[tile], line[tile + 1]) - line[tile]

    views = range(view_count)
    for depth in range(slab_depth):
        store(depth, [rows_summed([tile_of(part_ref, (depth, v), t) for v in views]) for t in range(tiles + 1)])
    level = zero + float(row_count)
    ends = [rows_summed([end_ref[e, v, :, :] for v in views]) for e in range(2)]
    store(slab_depth, [ends[0]] + [level] * (tiles - 1) + [ends[1]])

    factor = 1.0 / (row_count * cosine)
    least = angle_table()[0].min()
    for tile in range(column_count // LANES):
        column = (lane + tile * LANES).astype(F32)
        center = column_center(column, cosine, column_count, cell_count)
        whole = jnp.floor(center)
        fraction = center - whole
        place = jnp.clip(whole.astype(jnp.int32) + shift, shift - 2, shift + cell_count)
        block, index = jnp.right_shift(place, 7), jnp.bitwise_and(place, LANES - 1)
        ends = [column_center(tile * LANES + e, c, column_count, cell_count) for e in (0, LANES - 1) for c in (1.0, least)]
        low = min(max(math.floor(min(ends) - 1e-2) + shift, shift - 2), shift + cell_count) // LANES
        high = min(max(math.floor(max(ends) + 1e-2) + shift, shift - 2), shift + cell_count) // LANES
        cells, slopes = [zero] * slab_depth + [level], [zero] * (slab_depth + 1)
        for source in range(low, high + 1):
            here = block == source
            for at in range(slab_depth + 1):
                if at == slab_depth and source not in (0, tiles):
                    continue
                cells[at] = jnp.where(here, pick(tile_of(cell_ref, (at,), source), index), cells[at])
                slopes[at] = jnp.where(here, pick(tile_of(slope_ref, (at,), source), index), slopes[at])
        profiles = [(c + fraction * s) * factor for c, s in zip(cells, slopes)]
        side, inner = divmod(tile * LANES, width)
        for depth in range(slab_depth):
            to = (depth * 2 + side, slice(None), slice(inner, inner + LANES))
            measured = tile_of(measured_ref, (depth,), tile)
            last = tile_of(measured_ref, (depth * (row_share - 1),), tile)
            block_ref[to] = profiles[depth]
            near_ref[to] = jnp.where(near_places[depth], last, profiles[depth])
            low_ref[to] = jnp.where(low_places, measured, profiles[depth])
            high_ref[to] = jnp.where(high_places, measured, profiles[depth])
        cover_ref[:, tile * LANES : (tile + 1) * LANES] = profiles[slab_depth]


def divisor_kernel(
    slab_count,
    order,
    kinds,
    angle_ref,
    lift_ref,
    subset_ref,
    cover_ref,
    bound_ref,
    own_ref,
    rows_ref,
    own_cone_ref,
    cone_ref,
    place_ref,
    tap_ref,
    edge_ref,
    bend_ref,
    sub_ref,
):
    slab_depth, row_count, cell_count = bound_ref.shape
    row_share, view_count, column_count = own_ref.shape
    subset_count = subset_ref.shape[0]
    total_rows, total_slices = row_share * slab_count, slab_depth * slab_count
    tiles, columns = cell_count // LANES, column_count // LANES
    width = column_count // 2
    sub = sublane_index()
    zero = jnp.zeros((SUBLANES, LANES), F32)
    slab = lax.axis_index("slab")

    _, _, flat = angle_facts(spread_scalars(lambda v: angle_ref[v], view_count, sub))
    lifts = spread_scalars(lambda v: lift_ref[v], view_count, sub).astype(F32)
    lane = lane_index()
    origin = slabs_of(slab, order)
    source = sum(jnp.where(lane >= slab_depth * b, 1, 0) for b in range(1, len(order)))
    slices = spread_scalars(lambda b: origin[b], len(order), source) * slab_depth + (lane - source * slab_depth)
    held = (slices >= 0) & (slices < total_slices)
    slices = slices.astype(F32)
    for row in range(row_share):
        sample = cone_sample((slab * row_share + row).astype(F32), lifts, flat, total_rows, total_slices)
        weights = jnp.where(held, jnp.maximum(0.0, 1.0 - jnp.abs(sample - slices)), 0.0)
        for place in range(slab_depth * len(order)):
            own_cone_ref[place, row, :, :] = column_of(weights, place)
        total = cone_total(sample, total_slices)
        for tile in range(columns):
            cut = slice(tile * LANES, (tile + 1) * LANES)
            own_ref[row, :, cut] = 1.0 / jnp.maximum(total * cover_ref[:, cut], LEN_FLOOR)

    cosine, flat, lifts = subset_angles(angle_ref, lift_ref, subset_ref)
    tangents = member_tangents(angle_ref, subset_ref)
    for member in range(subset_count):
        view = pl.ds(subset_ref[member], 1)
        for side in range(2):
            at = slice(side * subset_count + member, side * subset_count + member + 1)
            sub_ref[at, :] = cover_ref[view, side * width : (side + 1) * width]
    sample, weights = subset_cone(slab, slab_count, order, kinds, slab_depth, row_share, flat, lifts)
    total = cone_total(sample, total_slices)
    for place in range(row_share * len(order)):
        for z, w in enumerate(weights):
            cone_ref[place, z, :, :] = column_of(w, place)
        length = column_of(total, place)
        for tile in range(width // LANES):
            cut = slice(tile * LANES, (tile + 1) * LANES)
            rows_ref[place, :, cut] = 1.0 / jnp.maximum(length * sub_ref[:, cut], LEN_FLOOR)

    factor = 1.0 / (row_count * cosine)
    line = []
    for tile in range(tiles + 1):
        taps = adjoint_taps(tile, cosine, column_count, cell_count, row_count // 2)
        for tap, (place, weight) in enumerate(taps):
            place_ref[tile, tap, :, :] = place
            tap_ref[tile, tap, :, :] = weight * factor
        line.append(sum(weight for _, weight in taps) * factor)
    store_line(line, edge_ref, bend_ref)
    slice_total = []
    for depth in range(slab_depth):
        t = jnp.sum(weights[1 + depth], axis=1, keepdims=True)
        slice_total.append([jnp.broadcast_to(t[k : k + 1], (SUBLANES, LANES)) for k in range(subset_count)])

    def one_group(group, carry):
        band = pl.ds(pl.multiple_of(group * SUBLANES, SUBLANES), SUBLANES)
        weight = [[zero] * tiles for _ in range(slab_depth)]
        for member in range(subset_count):
            line = sheared(edge_ref, bend_ref, member, adjoint_steps(group, row_count, tangents[member]), tiles)
            for depth in range(slab_depth):
                for tile in range(tiles):
                    weight[depth][tile] = weight[depth][tile] + slice_total[depth][member] * line[tile]
        for depth in range(slab_depth):
            for tile in range(tiles):
                bound_ref[depth, band, tile * LANES : (tile + 1) * LANES] = 1.0 / jnp.maximum(
                    weight[depth][tile], LEN_FLOOR * subset_count / row_count
                )
        return carry

    lax.fori_loop(0, row_count // SUBLANES, one_group, 0)


def update_kernel(
    order,
    kinds,
    angle_ref,
    subset_ref,
    volume_ref,
    measured_ref,
    bound_ref,
    own_ref,
    rows_ref,
    own_cone_ref,
    cone_ref,
    place_ref,
    tap_ref,
    *refs,
):
    blocks = refs[: len(order)]
    residual_ref, updated_ref, profile_ref, spread_ref, cell_ref, slope_ref, rest_ref, new_ref, row_ref, sent = refs[len(order) :]
    slab_depth, row_count, cell_count = volume_ref.shape
    row_share, view_count, column_count = measured_ref.shape
    subset_count = subset_ref.shape[0]
    tiles, columns = cell_count // LANES, column_count // LANES
    width = column_count // 2
    zero = jnp.zeros((SUBLANES, LANES), F32)
    slab = lax.axis_index("slab")
    odd = lax.rem(slab, 2)
    turns = turned(slab, kinds)
    mate_block, other_block = (blocks[order.index(away)] for away in (1, -1))

    groups = row_count // SUBLANES
    for tile in range(columns):
        side, inner = divmod(tile * LANES, width)
        image = [zero] * row_share
        for place, block in enumerate(blocks):
            for depth in range(slab_depth):
                cells = block[depth * 2 + side, :, inner : inner + LANES]
                for row in range(row_share):
                    image[row] = image[row] + own_cone_ref[place * slab_depth + depth, row, :, :] * cells
        cut = slice(tile * LANES, (tile + 1) * LANES)
        for row in range(row_share):
            rest_ref[row, :, cut] = (measured_ref[row, :, cut] - image[row]) * own_ref[row, :, cut]
    copies = [pltpu.make_async_copy(rest_ref, residual_ref, sent.at[groups])]
    copies[0].start()

    for member in range(subset_count):
        view = pl.ds(subset_ref[member], 1)
        for side in range(2):
            at = slice(side * subset_count + member, side * subset_count + member + 1)
            other = other_block[(slab_depth - 1) * 2 + side, view, :], other_block[side, view, :]
            mate = mate_block[(slab_depth - 1) * 2 + side, view, :], mate_block[side, view, :]
            profile_ref[0, at, :] = jnp.where(odd == 0, other[0], mate[0])
            for depth in range(slab_depth):
                profile_ref[1 + depth, at, :] = blocks[0][depth * 2 + side, view, :]
            profile_ref[1 + slab_depth, at, :] = jnp.where(odd == 0, mate[1], other[1])

    moved = [(b, j) for b, kind in enumerate(kinds) for j in range({FULL: 0, FAR: 2}.get(kind, 1))]
    for at_row, (b, j) in enumerate(moved):
        depth = turns[b] if kinds[b] in (NEAR, NEAR_SHARED) else j
        for member in range(subset_count):
            view = pl.ds(subset_ref[member], 1)
            for side in range(2):
                at = slice(side * subset_count + member, side * subset_count + member + 1)
                row_ref[at_row, at, :] = blocks[b][depth * 2 + side, view, :]

    inner_tiles = width // LANES
    spread = [[zero] * inner_tiles for _ in range(slab_depth)]
    for place in range(row_share * len(order)):
        weight = [cone_ref[place, z, :, :] for z in range(slab_depth + 2)]
        block, row = divmod(place, row_share)
        here = (block, row) in moved
        held = row_ref if here else blocks[block]
        at_row = moved.index((block, row)) if here else 2 * slab_depth + row - sum(b == block for b, _ in moved)
        for tile in range(inner_tiles):
            cut = slice(tile * LANES, (tile + 1) * LANES)
            image = weight[0] * profile_ref[0, :, cut]
            for z in range(1, slab_depth + 2):
                image = image + weight[z] * profile_ref[z, :, cut]
            rest = (held[at_row, :, cut] - image) * rows_ref[place, :, cut]
            for depth in range(slab_depth):
                spread[depth][tile] = spread[depth][tile] + weight[1 + depth] * rest
    for depth in range(slab_depth):
        for tile in range(inner_tiles):
            for side in range(2):
                spread_ref[
                    depth * subset_count : (depth + 1) * subset_count,
                    side * width + tile * LANES : side * width + (tile + 1) * LANES,
                ] = spread[depth][tile][side * subset_count : (side + 1) * subset_count]

    line = []
    for tile in range(tiles + 1):
        value = zero
        for tap in range(3):
            place = place_ref[tile, tap, :, :]
            block, index = jnp.right_shift(place, 7), jnp.bitwise_and(place, LANES - 1)
            found = zero
            for at in adjoint_tiles(tile, tap, column_count, cell_count, row_count // 2):
                found = jnp.where(block == at, pick(tile_of(spread_ref, (), at), index), found)
            value = value + tap_ref[tile, tap, :, :] * found
        line.append(value)
    store_line(line, cell_ref, slope_ref)

    tangents = member_tangents(angle_ref, subset_ref)
    for group in range(groups):
        band = slice(group * SUBLANES, (group + 1) * SUBLANES)
        back = [[zero] * tiles for _ in range(slab_depth)]
        for member in range(subset_count):
            step = adjoint_steps(group, row_count, tangents[member])
            for depth in range(slab_depth):
                line = sheared(cell_ref, slope_ref, depth * subset_count + member, step, tiles)
                back[depth] = [b + a for b, a in zip(back[depth], line)]
        for depth in range(slab_depth):
            for tile in range(tiles):
                cut = slice(tile * LANES, (tile + 1) * LANES)
                new_ref[depth, band, cut] = (
                    volume_ref[depth, band, cut] + back[depth][tile] * bound_ref[depth, band, cut]
                )
        copies.append(pltpu.make_async_copy(new_ref.at[:, band, :], updated_ref.at[:, band, :], sent.at[group]))
        copies[-1].start()
    for copy in copies:
        copy.wait()


def swapped(block):
    return lax.ppermute(block, "slab", [(i, i ^ 1) for i in range(lax.axis_size("slab"))])


def from_chip(block, distance):
    slabs = range(lax.axis_size("slab"))
    steps = [(i + 2 * distance * (1 - 2 * (i % 2)), i) for i in slabs]
    pairs = [p for p in steps if p[0] in slabs]
    idle = [i for i in slabs if i not in [p[0] for p in pairs]]
    unmet = [i for i in slabs if i not in [p[1] for p in pairs]]
    near = [i for i in idle if i ^ 1 in unmet]
    pairs += [(i, i ^ 1) for i in near]
    pairs += zip([i for i in idle if i not in near], [i for i in unmet if i ^ 1 not in near])
    return lax.ppermute(block, "slab", pairs)


def fetches(reach):
    return [s * d for d in range(reach // 2 + 1, 0, -1) for s in (1, -1) if 2 * d - (s > 0) <= reach]


def window(reach):
    order, kinds = [0, 1], [FULL, FULL]
    for distance in fetches(reach):
        near = distance == 1
        for away, kind in ((2 * distance, NEAR if near else FAR), (1 - 2 * distance, NEAR_SHARED if near else FAR)):
            if abs(away) <= reach:
                order.append(away)
                kinds.append(kind)
    assert sorted(order) == list(range(-reach, reach + 1))
    return tuple(order), tuple(kinds)


def gathered(own, near, low, high, reach, meanwhile):
    sent = {distance: near if distance == 1 else high if distance > 0 else low for distance in fetches(reach)}
    received = {distance: from_chip(block, distance) for distance, block in sent.items()}
    done = meanwhile()
    own, done = lax.optimization_barrier((own, done))
    blocks = {0: own, 1: swapped(own)}
    arrived, done = lax.optimization_barrier((list(received.values()), done))
    for distance, block in zip(received, arrived):
        if 2 * abs(distance) <= reach:
            blocks[2 * distance] = block
        if abs(1 - 2 * distance) <= reach:
            blocks[1 - 2 * distance] = swapped(block)
    return [blocks[away] for away in window(reach)[0]], done


def per_device(volume, measured, view_angle, view_lift, subset):
    slab_count = lax.axis_size("slab")
    slab_depth, row_count, cell_count = volume.shape
    row_share, view_count, column_count = measured.shape
    subset_count = subset.shape[0]
    tiles = cell_count // LANES
    reach = slab_reach(slab_count, slab_depth, row_share)
    here = lambda x: pltpu.with_memory_space_constraint(x, pltpu.VMEM)
    there = lambda x: pltpu.with_memory_space_constraint(x, pltpu.HBM)
    small = pltpu.CompilerParams(vmem_limit_bytes=VMEM_LIMIT)
    smem, vmem = pl.BlockSpec(memory_space=pltpu.SMEM), pl.BlockSpec(memory_space=pltpu.VMEM)
    wide = (tiles + 1) * LANES
    block_of = lambda rows: pltpu.VMEM((2 * slab_depth + rows, SUBLANES, column_count // 2), F32)
    own, near, low, high, cover = pl.pallas_call(
        functools.partial(project_kernel, slab_count),
        out_shape=(
            block_of(row_share),
            block_of(2),
            block_of(1),
            block_of(2),
            pltpu.VMEM((view_count, column_count), F32),
        ),
        in_specs=[smem] * 3 + [vmem] * 2,
        out_specs=(vmem,) * 5,
        scratch_shapes=[
            pltpu.VMEM(volume.shape, F32),
            pltpu.VMEM((slab_depth, row_count, LANES), F32),
            pltpu.VMEM((slab_depth, view_count, SUBLANES, wide), F32),
            pltpu.VMEM((2, view_count, SUBLANES, LANES), F32),
        ]
        + [pltpu.VMEM((slab_depth + 1, SUBLANES, wide), F32)] * 2,
        compiler_params=small,
        name="project",
    )(*map(there, (view_angle, view_lift, subset, volume, measured)))
    cover = here(cover)
    order, kinds = window(reach)
    divide = pl.pallas_call(
        functools.partial(divisor_kernel, slab_count, order, kinds),
        out_shape=(
            pltpu.VMEM(volume.shape, F32),
            pltpu.VMEM(measured.shape, F32),
            pltpu.VMEM((row_share * len(order), SUBLANES, column_count // 2), F32),
            pltpu.VMEM((slab_depth * len(order), row_share, SUBLANES, LANES), F32),
            pltpu.VMEM((row_share * len(order), slab_depth + 2, SUBLANES, LANES), F32),
            pltpu.VMEM((tiles + 1, 3, SUBLANES, LANES), jnp.int32),
            pltpu.VMEM((tiles + 1, 3, SUBLANES, LANES), F32),
        ),
        in_specs=[smem] * 3 + [vmem],
        out_specs=(vmem,) * 7,
        scratch_shapes=[pltpu.VMEM((SUBLANES, wide), F32)] * 2 + [pltpu.VMEM((SUBLANES, column_count // 2), F32)],
        cost_estimate=pl.CostEstimate(flops=4_000_000, bytes_accessed=8_000_000, transcendentals=0),
        compiler_params=small,
        name="divisors",
    )
    blocks, divisors = gathered(own, near, low, high, reach, lambda: divide(view_angle, view_lift, subset, cover))
    return pl.pallas_call(
        functools.partial(update_kernel, order, kinds),
        out_shape=(
            jax.ShapeDtypeStruct(measured.shape, F32),
            jax.ShapeDtypeStruct(volume.shape, F32),
        ),
        in_specs=[smem] * 2 + [vmem] * (2 + len(divisors) + len(order)),
        out_specs=(pl.BlockSpec(memory_space=pl.ANY),) * 2,
        scratch_shapes=[
            pltpu.VMEM((slab_depth + 2, SUBLANES, column_count // 2), F32),
            pltpu.VMEM((SUBLANES, column_count), F32),
            pltpu.VMEM((SUBLANES, wide), F32),
            pltpu.VMEM((SUBLANES, wide), F32),
            pltpu.VMEM(measured.shape, F32),
            pltpu.VMEM(volume.shape, F32),
            pltpu.VMEM((2 * len(order), SUBLANES, column_count // 2), F32),
            pltpu.SemaphoreType.DMA((row_count // SUBLANES + 1,)),
        ],
        compiler_params=small,
        name="update",
    )(view_angle, subset, *map(here, (volume, measured, *divisors, *blocks)))


def solution(mesh):
    in_specs = (
        P(("scan", "slab"), None, None),
        P(("scan", "slab"), None, None),
        P("scan"),
        P("scan"),
        P("scan"),
    )
    out_specs = (P(("scan", "slab"), None, None), P(("scan", "slab"), None, None))
    return jax.shard_map(
        per_device, mesh=mesh, in_specs=in_specs, out_specs=out_specs, check_vma=False
    )
```

```python
import functools
import math

import jax
import jax.numpy as jnp
import numpy as np
from jax import lax
from jax.experimental import pallas as pl
from jax.experimental.pallas import tpu as pltpu
from jax.sharding import PartitionSpec as P

ANGLES = 180
LIFT = 6
PITCH = 0.9
MAG_BASE = 1.5
ECCENTRIC = 0.12
LEN_FLOOR = 0.25
LANES = 128
SUBLANES = 8
F32 = jnp.float32
FULL, NEAR, NEAR_SHARED, FAR = range(4)
VMEM_LIMIT = 8 * 1024 * 1024


def angle_table():
    radians = (np.arange(ANGLES) + 0.5) * (0.5 * math.pi / ANGLES) - 0.25 * math.pi
    magnify = MAG_BASE / (1.0 - ECCENTRIC * np.sin(2.0 * radians + 1.0))
    return np.cos(radians), magnify


def slab_reach(slab_count, slab_depth, row_share):
    _, magnify = angle_table()
    total_rows, total_slices = row_share * slab_count, slab_depth * slab_count
    rows = np.arange(total_rows)
    reach = 0
    for lift in range(-LIFT, LIFT + 1):
        sample = (rows[None] + 0.5 - total_rows / 2 - lift) / magnify[:, None] + total_slices / 2 - 0.5
        for tap in (np.floor(sample - 1e-3), np.floor(sample + 1e-3) + 1):
            inside = (tap >= 0) & (tap < total_slices)
            distance = np.abs(tap // slab_depth - rows[None] // row_share)
            reach = max(reach, int(distance[inside].max()))
    return reach


def lane_index():
    return lax.broadcasted_iota(jnp.int32, (SUBLANES, LANES), 1)


def sublane_index():
    return lax.broadcasted_iota(jnp.int32, (SUBLANES, LANES), 0)


def angle_facts(index):
    x = (index.astype(F32) + 0.5) * (0.5 * math.pi / ANGLES) - 0.25 * math.pi
    s = x * x
    sine = x * (1.0 + s * (-1 / 6 + s * (1 / 120 + s * (-1 / 5040 + s * (1 / 362880)))))
    cosine = 1.0 + s * (-1 / 2 + s * (1 / 24 + s * (-1 / 720 + s * (1 / 40320 + s * (-1 / 3628800)))))
    double = 2.0 * sine * cosine * math.cos(1.0) + (1.0 - 2.0 * sine * sine) * math.sin(1.0)
    return cosine, sine / cosine, (1.0 - ECCENTRIC * double) * (1.0 / MAG_BASE)


def spread_scalars(read, count, place):
    out = jnp.full((SUBLANES, LANES), read(0), jnp.int32)
    for item in range(1, count):
        out = jnp.where(place == item, read(item), out)
    return out


def pick(tile, index):
    numbers = lax.GatherDimensionNumbers(
        offset_dims=(),
        collapsed_slice_dims=(1,),
        start_index_map=(1,),
        operand_batching_dims=(0,),
        start_indices_batching_dims=(0,),
    )
    return lax.gather(tile, index[..., None], numbers, (1, 1), mode=lax.GatherScatterMode.PROMISE_IN_BOUNDS)


def next_lane(tile, following):
    lane = lane_index()
    return jnp.where(lane < LANES - 1, pltpu.roll(tile, LANES - 1, 1), pltpu.roll(following, LANES - 1, 1))


def rows_summed(parts):
    sub = sublane_index()
    step = 1
    while step < SUBLANES:
        low = jnp.bitwise_and(sub, step) == 0
        parts = [
            jnp.where(low, a, b) + pltpu.roll(jnp.where(low, b, a), step, 0) for a, b in zip(parts[::2], parts[1::2])
        ]
        step *= 2
    return parts[0]


def tile_of(ref, lead, tile):
    whole = (slice(None),) * (len(ref.shape) - 1 - len(lead))
    return ref[lead + whole + (slice(tile * LANES, (tile + 1) * LANES),)]


def column_center(column, cosine, column_count, cell_count):
    return (column + 0.5 - column_count / 2) * (PITCH * cell_count / column_count) / cosine + (
        cell_count / 2 - 0.5
    )


def shear_steps(group, row_count, tangent):
    row = (sublane_index() + group * SUBLANES).astype(F32)
    offset = (row + 0.5 - row_count / 2) * tangent
    whole = jnp.floor(offset)
    return whole.astype(jnp.int32), offset - whole


def cone_sample(rows, lifts, flat, total_rows, total_slices):
    return (rows + 0.5 - total_rows / 2 - lifts) * flat + (total_slices / 2 - 0.5)


def cone_total(sample, total_slices):
    whole = jnp.floor(sample)
    fraction = sample - whole
    low = jnp.where((whole >= 0) & (whole < total_slices), 1.0 - fraction, 0.0)
    return low + jnp.where((whole >= -1) & (whole < total_slices - 1), fraction, 0.0)


def column_of(tile, at):
    return jnp.broadcast_to(tile[:, at : at + 1], (SUBLANES, LANES))


def slabs_of(slab, order):
    return [slab + (1 - 2 * lax.rem(slab, 2)) * away for away in order]


def turned(slab, kinds):
    odd = lax.rem(slab, 2)
    return [{NEAR: 1 - odd, NEAR_SHARED: odd}.get(kind, 0) for kind in kinds]


def subset_cone(slab, slab_count, order, kinds, slab_depth, row_share, flat, lifts):
    lane = lane_index()
    total_rows, total_slices = row_share * slab_count, slab_depth * slab_count
    origin, turns = slabs_of(slab, order), turned(slab, kinds)
    source = sum(jnp.where(lane >= row_share * b, 1, 0) for b in range(1, len(order)))
    within = lane - source * row_share
    within = jnp.where(spread_scalars(lambda b: turns[b], len(order), source) == 1, row_share - 1 - within, within)
    rows = spread_scalars(lambda b: origin[b], len(order), source) * row_share + within
    real = (rows >= 0) & (rows < total_rows) & (lane < row_share * len(order))
    sample = cone_sample(rows.astype(F32), lifts, flat, total_rows, total_slices)
    weights = []
    for z in range(-1, slab_depth + 1):
        at = slab * slab_depth + z
        use = real & (at >= 0) & (at < total_slices)
        weights.append(jnp.where(use, jnp.maximum(0.0, 1.0 - jnp.abs(sample - at.astype(F32))), 0.0))
    return sample, weights


def adjoint_taps(tile, cosine, column_count, cell_count, half):
    spacing = PITCH * cell_count / column_count
    cell = (lane_index() + (tile * LANES - half)).astype(F32)
    inside = (cell >= 0) & (cell < cell_count)
    first = jnp.floor((cell - (cell_count / 2 + 0.5)) * cosine * (1.0 / spacing) + (column_count / 2 - 0.5 - 1e-3)) + 1.0
    taps = []
    for tap in range(3):
        column = first + tap
        weight = jnp.maximum(0.0, 1.0 - jnp.abs(cell - column_center(column, cosine, column_count, cell_count)))
        weight = jnp.where(inside & (column >= 0) & (column < column_count), weight, 0.0)
        taps.append((jnp.clip(column.astype(jnp.int32), 0, column_count - 1), weight))
    return taps


def adjoint_tiles(tile, tap, column_count, cell_count, half):
    spacing = PITCH * cell_count / column_count
    least = angle_table()[0].min()
    ends = [
        (tile * LANES - half + e - cell_count / 2 - 0.5) * c / spacing + column_count / 2 + 0.5
        for e in (0, LANES - 1)
        for c in (1.0, least)
    ]
    low = min(max(math.floor(min(ends) + tap - 0.6), 0), column_count - 1) // LANES
    high = min(max(math.ceil(max(ends) + tap + 0.6), 0), column_count - 1) // LANES
    return range(low, high + 1)


def store_line(line, base_ref, bend_ref):
    line = line + [jnp.zeros((SUBLANES, LANES), F32)]
    for tile in range(len(line) - 1):
        cut = slice(tile * LANES, (tile + 1) * LANES)
        base_ref[:, cut] = line[tile]
        bend_ref[:, cut] = next_lane(line[tile], line[tile + 1]) - line[tile]


def adjoint_steps(group, row_count, tangent):
    whole, fraction = shear_steps(group, row_count, tangent)
    place = lane_index() + (row_count // 2 - 1 - whole)
    return jnp.bitwise_and(place, LANES - 1), place < LANES, 1.0 - fraction


def sheared(base_ref, bend_ref, row, step, tiles):
    index, near, share = step
    before, out = None, []
    for tile in range(tiles + 1):
        cut = slice(tile * LANES, (tile + 1) * LANES)
        low = jnp.broadcast_to(base_ref[row : row + 1, cut], (SUBLANES, LANES))
        rise = jnp.broadcast_to(bend_ref[row : row + 1, cut], (SUBLANES, LANES))
        after = pick(low + share * rise, index)
        if tile:
            out.append(jnp.where(near, before, after))
        before = after
    return out


def subset_angles(angle_ref, lift_ref, subset_ref):
    members = subset_ref.shape[0]
    member = jnp.bitwise_and(sublane_index(), members - 1)
    cosine, _, flat = angle_facts(spread_scalars(lambda k: angle_ref[subset_ref[k]], members, member))
    lifts = spread_scalars(lambda k: lift_ref[subset_ref[k]], members, member).astype(F32)
    return cosine, flat, lifts


def member_tangents(angle_ref, subset_ref):
    indices = [angle_ref[subset_ref[k]] for k in range(subset_ref.shape[0])]
    return [angle_facts(jnp.full((SUBLANES, LANES), i, jnp.int32))[1] for i in indices]


def project_kernel(
    slab_count,
    angle_ref,
    lift_ref,
    subset_ref,
    volume_ref,
    measured_ref,
    block_ref,
    near_ref,
    low_ref,
    high_ref,
    cover_ref,
    rise_ref,
    first_ref,
    part_ref,
    end_ref,
    cell_ref,
    slope_ref,
):
    slab_depth, row_count, cell_count = volume_ref.shape
    row_share, view_count, column_count = measured_ref.shape
    subset_count = subset_ref.shape[0]
    half = row_count // 2
    tiles = cell_count // LANES
    groups = row_count // SUBLANES
    lane, sub = lane_index(), sublane_index()
    zero = jnp.zeros((SUBLANES, LANES), F32)
    width = column_count // 2

    assert (slab_depth, row_share) == (2, 3)
    slab = lax.axis_index("slab")
    odd = lax.rem(slab, 2)
    grows = odd == 1
    far_row = jnp.where(grows, 2, 0)
    for member in range(subset_count):
        view = pl.ds(subset_ref[member], 1)
        for side in range(2):
            at, cut = side * subset_count + member, slice(side * width, (side + 1) * width)
            rows = [measured_ref[row, view, cut] for row in range(row_share)]
            for row in range(row_share):
                block_ref[2 * slab_depth + row, at : at + 1, :] = rows[row]
            near_ref[2 * slab_depth, at : at + 1, :] = rows[1]
            near_ref[2 * slab_depth + 1, at : at + 1, :] = measured_ref[far_row, view, cut]
            low_ref[2 * slab_depth, at : at + 1, :] = rows[2]
            for more in range(2):
                high_ref[2 * slab_depth + more, at : at + 1, :] = rows[2]

    cosine, _, flat = angle_facts(spread_scalars(lambda v: angle_ref[v], view_count, sub))
    lifts = spread_scalars(lambda v: lift_ref[v], view_count, sub).astype(F32)
    ends = [
        cone_sample((slab * row_share + row).astype(F32), lifts, flat, row_share * slab_count, slab_depth * slab_count)
        - (slab * slab_depth).astype(F32)
        for row in (0, row_share - 1)
    ]
    picked = sub == subset_ref[0]
    for member in range(1, subset_count):
        picked = picked | (sub == subset_ref[member])
    picked = jnp.where(picked, 1, 0)
    as_int = lambda mask: jnp.where(mask, 1, 0)
    near_up, near_down = picked * as_int(ends[1] > 0.75), picked * as_int(ends[0] < 0.25)
    far_up, far_down = picked * as_int(ends[1] > 2.5), picked * as_int(ends[0] < -1.5)
    near_places = [(near_up * odd) == 1, (near_down * (1 - odd)) == 1]
    high_places = (far_up * odd + far_down * (1 - odd)) == 1
    low_places = (far_up * (1 - odd) + far_down * odd) == 1

    for depth in range(slab_depth):
        for group in range(groups):
            band = slice(group * SUBLANES, (group + 1) * SUBLANES)
            cells = [tile_of(volume_ref, (depth, band), tile) for tile in range(tiles)] + [zero]
            for tile in range(tiles):
                rise_ref[depth, band, tile * LANES : (tile + 1) * LANES] = (
                    next_lane(cells[tile], cells[tile + 1]) - cells[tile]
                )
            first_ref[depth, band, :] = column_of(cells[0], 0)

    def one_view(view, carry):
        _, tangent, _ = angle_facts(jnp.full((SUBLANES, LANES), angle_ref[view], jnp.int32))
        low_end, high_end = zero, zero
        sums = [[zero] * (tiles + 1) for _ in range(slab_depth)]
        for group in range(groups):
            band = slice(group * SUBLANES, (group + 1) * SUBLANES)
            whole, fraction = shear_steps(group, row_count, tangent)
            place = lane + (whole + half)
            index = jnp.bitwise_and(place, LANES - 1)
            near, last = place < LANES, index == LANES - 1
            enter = jnp.where(last, fraction, 0.0)
            low_end = low_end + jnp.where(near, enter, 1.0)
            high_end = high_end + jnp.where(near, 1.0 - enter, 0.0)
            for depth in range(slab_depth):
                before = enter * first_ref[depth, band, :]
                for tile in range(tiles + 1):
                    after = zero
                    if tile < tiles:
                        at = (depth, band)
                        after = pick(tile_of(volume_ref, at, tile) + fraction * tile_of(rise_ref, at, tile), index)
                    sums[depth][tile] = sums[depth][tile] + jnp.where(near, before, after)
                    before = after
        end_ref[0, view, :, :] = low_end
        end_ref[1, view, :, :] = high_end
        for depth in range(slab_depth):
            for tile in range(tiles + 1):
                part_ref[depth, view, :, tile * LANES : (tile + 1) * LANES] = sums[depth][tile]
        return carry

    lax.fori_loop(0, view_count, one_view, 0, unroll=8)

    shift = LANES - half
    inside = [None] * (tiles + 1)
    inside[0], inside[tiles] = lane >= shift, lane < shift

    def store(at, line):
        line = [jnp.where(mask, cells, 0.0) if mask is not None else cells for cells, mask in zip(line, inside)] + [zero]
        for tile in range(tiles + 1):
            cut = slice(tile * LANES, (tile + 1) * LANES)
            cell_ref[at, :, cut] = line[tile]
            slope_ref[at, :, cut] = next_lane(line[tile], line[tile + 1]) - line[tile]

    views = range(view_count)
    for depth in range(slab_depth):
        store(depth, [rows_summed([tile_of(part_ref, (depth, v), t) for v in views]) for t in range(tiles + 1)])
    level = zero + float(row_count)
    ends = [rows_summed([end_ref[e, v, :, :] for v in views]) for e in range(2)]
    store(slab_depth, [ends[0]] + [level] * (tiles - 1) + [ends[1]])

    factor = 1.0 / (row_count * cosine)
    least = angle_table()[0].min()
    for tile in range(column_count // LANES):
        column = (lane + tile * LANES).astype(F32)
        center = column_center(column, cosine, column_count, cell_count)
        whole = jnp.floor(center)
        fraction = center - whole
        place = jnp.clip(whole.astype(jnp.int32) + shift, shift - 2, shift + cell_count)
        block, index = jnp.right_shift(place, 7), jnp.bitwise_and(place, LANES - 1)
        ends = [column_center(tile * LANES + e, c, column_count, cell_count) for e in (0, LANES - 1) for c in (1.0, least)]
        low = min(max(math.floor(min(ends) - 1e-2) + shift, shift - 2), shift + cell_count) // LANES
        high = min(max(math.floor(max(ends) + 1e-2) + shift, shift - 2), shift + cell_count) // LANES
        cells, slopes = [zero] * slab_depth + [level], [zero] * (slab_depth + 1)
        for source in range(low, high + 1):
            here = block == source
            for at in range(slab_depth + 1):
                if at == slab_depth and source not in (0, tiles):
                    continue
                cells[at] = jnp.where(here, pick(tile_of(cell_ref, (at,), source), index), cells[at])
                slopes[at] = jnp.where(here, pick(tile_of(slope_ref, (at,), source), index), slopes[at])
        profiles = [(c + fraction * s) * factor for c, s in zip(cells, slopes)]
        side, inner = divmod(tile * LANES, width)
        for depth in range(slab_depth):
            to = (depth * 2 + side, slice(None), slice(inner, inner + LANES))
            measured = tile_of(measured_ref, (depth,), tile)
            last = tile_of(measured_ref, (depth * (row_share - 1),), tile)
            block_ref[to] = profiles[depth]
            near_ref[to] = jnp.where(near_places[depth], last, profiles[depth])
            low_ref[to] = jnp.where(low_places, measured, profiles[depth])
            high_ref[to] = jnp.where(high_places, measured, profiles[depth])
        cover_ref[:, tile * LANES : (tile + 1) * LANES] = profiles[slab_depth]


def divisor_kernel(
    slab_count,
    order,
    kinds,
    angle_ref,
    lift_ref,
    subset_ref,
    cover_ref,
    bound_ref,
    own_ref,
    rows_ref,
    own_cone_ref,
    cone_ref,
    place_ref,
    tap_ref,
    edge_ref,
    bend_ref,
    sub_ref,
):
    slab_depth, row_count, cell_count = bound_ref.shape
    row_share, view_count, column_count = own_ref.shape
    subset_count = subset_ref.shape[0]
    total_rows, total_slices = row_share * slab_count, slab_depth * slab_count
    tiles, columns = cell_count // LANES, column_count // LANES
    width = column_count // 2
    sub = sublane_index()
    zero = jnp.zeros((SUBLANES, LANES), F32)
    slab = lax.axis_index("slab")

    _, _, flat = angle_facts(spread_scalars(lambda v: angle_ref[v], view_count, sub))
    lifts = spread_scalars(lambda v: lift_ref[v], view_count, sub).astype(F32)
    lane = lane_index()
    origin = slabs_of(slab, order)
    source = sum(jnp.where(lane >= slab_depth * b, 1, 0) for b in range(1, len(order)))
    slices = spread_scalars(lambda b: origin[b], len(order), source) * slab_depth + (lane - source * slab_depth)
    held = (slices >= 0) & (slices < total_slices)
    slices = slices.astype(F32)
    for row in range(row_share):
        sample = cone_sample((slab * row_share + row).astype(F32), lifts, flat, total_rows, total_slices)
        weights = jnp.where(held, jnp.maximum(0.0, 1.0 - jnp.abs(sample - slices)), 0.0)
        for place in range(slab_depth * len(order)):
            own_cone_ref[place, row, :, :] = column_of(weights, place)
        total = cone_total(sample, total_slices)
        for tile in range(columns):
            cut = slice(tile * LANES, (tile + 1) * LANES)
            own_ref[row, :, cut] = 1.0 / jnp.maximum(total * cover_ref[:, cut], LEN_FLOOR)

    cosine, flat, lifts = subset_angles(angle_ref, lift_ref, subset_ref)
    tangents = member_tangents(angle_ref, subset_ref)
    for member in range(subset_count):
        view = pl.ds(subset_ref[member], 1)
        for side in range(2):
            at = slice(side * subset_count + member, side * subset_count + member + 1)
            sub_ref[at, :] = cover_ref[view, side * width : (side + 1) * width]
    sample, weights = subset_cone(slab, slab_count, order, kinds, slab_depth, row_share, flat, lifts)
    total = cone_total(sample, total_slices)
    for place in range(row_share * len(order)):
        for z, w in enumerate(weights):
            cone_ref[place, z, :, :] = column_of(w, place)
        length = column_of(total, place)
        for tile in range(width // LANES):
            cut = slice(tile * LANES, (tile + 1) * LANES)
            rows_ref[place, :, cut] = 1.0 / jnp.maximum(length * sub_ref[:, cut], LEN_FLOOR)

    factor = 1.0 / (row_count * cosine)
    line = []
    for tile in range(tiles + 1):
        taps = adjoint_taps(tile, cosine, column_count, cell_count, row_count // 2)
        for tap, (place, weight) in enumerate(taps):
            place_ref[tile, tap, :, :] = place
            tap_ref[tile, tap, :, :] = weight * factor
        line.append(sum(weight for _, weight in taps) * factor)
    store_line(line, edge_ref, bend_ref)
    slice_total = []
    for depth in range(slab_depth):
        t = jnp.sum(weights[1 + depth], axis=1, keepdims=True)
        slice_total.append([jnp.broadcast_to(t[k : k + 1], (SUBLANES, LANES)) for k in range(subset_count)])

    def one_group(group, carry):
        band = pl.ds(pl.multiple_of(group * SUBLANES, SUBLANES), SUBLANES)
        weight = [[zero] * tiles for _ in range(slab_depth)]
        for member in range(subset_count):
            line = sheared(edge_ref, bend_ref, member, adjoint_steps(group, row_count, tangents[member]), tiles)
            for depth in range(slab_depth):
                for tile in range(tiles):
                    weight[depth][tile] = weight[depth][tile] + slice_total[depth][member] * line[tile]
        for depth in range(slab_depth):
            for tile in range(tiles):
                bound_ref[depth, band, tile * LANES : (tile + 1) * LANES] = 1.0 / jnp.maximum(
                    weight[depth][tile], LEN_FLOOR * subset_count / row_count
                )
        return carry

    lax.fori_loop(0, row_count // SUBLANES, one_group, 0)


def update_kernel(
    order,
    kinds,
    angle_ref,
    subset_ref,
    volume_ref,
    measured_ref,
    bound_ref,
    own_ref,
    rows_ref,
    own_cone_ref,
    cone_ref,
    place_ref,
    tap_ref,
    *refs,
):
    blocks = refs[: len(order)]
    residual_ref, updated_ref, profile_ref, spread_ref, cell_ref, slope_ref, rest_ref, new_ref, row_ref, sent = refs[len(order) :]
    slab_depth, row_count, cell_count = volume_ref.shape
    row_share, view_count, column_count = measured_ref.shape
    subset_count = subset_ref.shape[0]
    tiles, columns = cell_count // LANES, column_count // LANES
    width = column_count // 2
    zero = jnp.zeros((SUBLANES, LANES), F32)
    slab = lax.axis_index("slab")
    odd = lax.rem(slab, 2)
    turns = turned(slab, kinds)
    mate_block, other_block = (blocks[order.index(away)] for away in (1, -1))

    groups = row_count // SUBLANES
    for tile in range(columns):
        side, inner = divmod(tile * LANES, width)
        image = [zero] * row_share
        for place, block in enumerate(blocks):
            for depth in range(slab_depth):
                cells = block[depth * 2 + side, :, inner : inner + LANES]
                for row in range(row_share):
                    image[row] = image[row] + own_cone_ref[place * slab_depth + depth, row, :, :] * cells
        cut = slice(tile * LANES, (tile + 1) * LANES)
        for row in range(row_share):
            rest_ref[row, :, cut] = (measured_ref[row, :, cut] - image[row]) * own_ref[row, :, cut]
    copies = [pltpu.make_async_copy(rest_ref, residual_ref, sent.at[groups])]
    copies[0].start()

    for member in range(subset_count):
        view = pl.ds(subset_ref[member], 1)
        for side in range(2):
            at = slice(side * subset_count + member, side * subset_count + member + 1)
            other = other_block[(slab_depth - 1) * 2 + side, view, :], other_block[side, view, :]
            mate = mate_block[(slab_depth - 1) * 2 + side, view, :], mate_block[side, view, :]
            profile_ref[0, at, :] = jnp.where(odd == 0, other[0], mate[0])
            for depth in range(slab_depth):
                profile_ref[1 + depth, at, :] = blocks[0][depth * 2 + side, view, :]
            profile_ref[1 + slab_depth, at, :] = jnp.where(odd == 0, mate[1], other[1])

    moved = [(b, j) for b, kind in enumerate(kinds) for j in range({FULL: 0, FAR: 2}.get(kind, 1))]
    for at_row, (b, j) in enumerate(moved):
        depth = turns[b] if kinds[b] in (NEAR, NEAR_SHARED) else j
        for member in range(subset_count):
            view = pl.ds(subset_ref[member], 1)
            for side in range(2):
                at = slice(side * subset_count + member, side * subset_count + member + 1)
                row_ref[at_row, at, :] = blocks[b][depth * 2 + side, view, :]

    inner_tiles = width // LANES
    spread = [[zero] * inner_tiles for _ in range(slab_depth)]
    for place in range(row_share * len(order)):
        weight = [cone_ref[place, z, :, :] for z in range(slab_depth + 2)]
        block, row = divmod(place, row_share)
        here = (block, row) in moved
        held = row_ref if here else blocks[block]
        at_row = moved.index((block, row)) if here else 2 * slab_depth + row - sum(b == block for b, _ in moved)
        for tile in range(inner_tiles):
            cut = slice(tile * LANES, (tile + 1) * LANES)
            image = weight[0] * profile_ref[0, :, cut]
            for z in range(1, slab_depth + 2):
                image = image + weight[z] * profile_ref[z, :, cut]
            rest = (held[at_row, :, cut] - image) * rows_ref[place, :, cut]
            for depth in range(slab_depth):
                spread[depth][tile] = spread[depth][tile] + weight[1 + depth] * rest
    for depth in range(slab_depth):
        for tile in range(inner_tiles):
            for side in range(2):
                spread_ref[
                    depth * subset_count : (depth + 1) * subset_count,
                    side * width + tile * LANES : side * width + (tile + 1) * LANES,
                ] = spread[depth][tile][side * subset_count : (side + 1) * subset_count]

    line = []
    for tile in range(tiles + 1):
        value = zero
        for tap in range(3):
            place = place_ref[tile, tap, :, :]
            block, index = jnp.right_shift(place, 7), jnp.bitwise_and(place, LANES - 1)
            found = zero
            for at in adjoint_tiles(tile, tap, column_count, cell_count, row_count // 2):
                found = jnp.where(block == at, pick(tile_of(spread_ref, (), at), index), found)
            value = value + tap_ref[tile, tap, :, :] * found
        line.append(value)
    store_line(line, cell_ref, slope_ref)

    tangents = member_tangents(angle_ref, subset_ref)
    for group in range(groups):
        band = slice(group * SUBLANES, (group + 1) * SUBLANES)
        back = [[zero] * tiles for _ in range(slab_depth)]
        for member in range(subset_count):
            step = adjoint_steps(group, row_count, tangents[member])
            for depth in range(slab_depth):
                line = sheared(cell_ref, slope_ref, depth * subset_count + member, step, tiles)
                back[depth] = [b + a for b, a in zip(back[depth], line)]
        for depth in range(slab_depth):
            for tile in range(tiles):
                cut = slice(tile * LANES, (tile + 1) * LANES)
                new_ref[depth, band, cut] = (
                    volume_ref[depth, band, cut] + back[depth][tile] * bound_ref[depth, band, cut]
                )
        copies.append(pltpu.make_async_copy(new_ref.at[:, band, :], updated_ref.at[:, band, :], sent.at[group]))
        copies[-1].start()
    for copy in copies:
        copy.wait()


def swapped(block):
    return lax.ppermute(block, "slab", [(i, i ^ 1) for i in range(lax.axis_size("slab"))])


def from_chip(block, distance):
    slabs = range(lax.axis_size("slab"))
    steps = [(i + 2 * distance * (1 - 2 * (i % 2)), i) for i in slabs]
    pairs = [p for p in steps if p[0] in slabs]
    idle = [i for i in slabs if i not in [p[0] for p in pairs]]
    unmet = [i for i in slabs if i not in [p[1] for p in pairs]]
    near = [i for i in idle if i ^ 1 in unmet]
    pairs += [(i, i ^ 1) for i in near]
    pairs += zip([i for i in idle if i not in near], [i for i in unmet if i ^ 1 not in near])
    return lax.ppermute(block, "slab", pairs)


def fetches(reach):
    return [s * d for d in range(reach // 2 + 1, 0, -1) for s in (1, -1) if 2 * d - (s > 0) <= reach]


def window(reach):
    order, kinds = [0, 1], [FULL, FULL]
    for distance in fetches(reach):
        near = distance == 1
        for away, kind in ((2 * distance, NEAR if near else FAR), (1 - 2 * distance, NEAR_SHARED if near else FAR)):
            if abs(away) <= reach:
                order.append(away)
                kinds.append(kind)
    assert sorted(order) == list(range(-reach, reach + 1))
    return tuple(order), tuple(kinds)


def gathered(own, near, low, high, reach, meanwhile):
    sent = {distance: near if distance == 1 else high if distance > 0 else low for distance in fetches(reach)}
    received = {distance: from_chip(block, distance) for distance, block in sent.items()}
    done = meanwhile()
    own, done = lax.optimization_barrier((own, done))
    blocks = {0: own, 1: swapped(own)}
    arrived, done = lax.optimization_barrier((list(received.values()), done))
    for distance, block in zip(received, arrived):
        if 2 * abs(distance) <= reach:
            blocks[2 * distance] = block
        if abs(1 - 2 * distance) <= reach:
            blocks[1 - 2 * distance] = swapped(block)
    return [blocks[away] for away in window(reach)[0]], done


def per_device(volume, measured, view_angle, view_lift, subset):
    slab_count = lax.axis_size("slab")
    slab_depth, row_count, cell_count = volume.shape
    row_share, view_count, column_count = measured.shape
    subset_count = subset.shape[0]
    tiles = cell_count // LANES
    reach = slab_reach(slab_count, slab_depth, row_share)
    here = lambda x: pltpu.with_memory_space_constraint(x, pltpu.VMEM)
    there = lambda x: pltpu.with_memory_space_constraint(x, pltpu.HBM)
    small = pltpu.CompilerParams(vmem_limit_bytes=VMEM_LIMIT)
    smem, vmem = pl.BlockSpec(memory_space=pltpu.SMEM), pl.BlockSpec(memory_space=pltpu.VMEM)
    wide = (tiles + 1) * LANES
    block_of = lambda rows: pltpu.VMEM((2 * slab_depth + rows, SUBLANES, column_count // 2), F32)
    own, near, low, high, cover = pl.pallas_call(
        functools.partial(project_kernel, slab_count),
        out_shape=(
            block_of(row_share),
            block_of(2),
            block_of(1),
            block_of(2),
            pltpu.VMEM((view_count, column_count), F32),
        ),
        in_specs=[smem] * 3 + [vmem] * 2,
        out_specs=(vmem,) * 5,
        scratch_shapes=[
            pltpu.VMEM(volume.shape, F32),
            pltpu.VMEM((slab_depth, row_count, LANES), F32),
            pltpu.VMEM((slab_depth, view_count, SUBLANES, wide), F32),
            pltpu.VMEM((2, view_count, SUBLANES, LANES), F32),
        ]
        + [pltpu.VMEM((slab_depth + 1, SUBLANES, wide), F32)] * 2,
        compiler_params=small,
        name="project",
    )(*map(there, (view_angle, view_lift, subset, volume, measured)))
    cover = here(cover)
    order, kinds = window(reach)
    divide = pl.pallas_call(
        functools.partial(divisor_kernel, slab_count, order, kinds),
        out_shape=(
            pltpu.VMEM(volume.shape, F32),
            pltpu.VMEM(measured.shape, F32),
            pltpu.VMEM((row_share * len(order), SUBLANES, column_count // 2), F32),
            pltpu.VMEM((slab_depth * len(order), row_share, SUBLANES, LANES), F32),
            pltpu.VMEM((row_share * len(order), slab_depth + 2, SUBLANES, LANES), F32),
            pltpu.VMEM((tiles + 1, 3, SUBLANES, LANES), jnp.int32),
            pltpu.VMEM((tiles + 1, 3, SUBLANES, LANES), F32),
        ),
        in_specs=[smem] * 3 + [vmem],
        out_specs=(vmem,) * 7,
        scratch_shapes=[pltpu.VMEM((SUBLANES, wide), F32)] * 2 + [pltpu.VMEM((SUBLANES, column_count // 2), F32)],
        cost_estimate=pl.CostEstimate(flops=4_000_000, bytes_accessed=8_000_000, transcendentals=0),
        compiler_params=small,
        name="divisors",
    )
    blocks, divisors = gathered(own, near, low, high, reach, lambda: divide(view_angle, view_lift, subset, cover))
    return pl.pallas_call(
        functools.partial(update_kernel, order, kinds),
        out_shape=(
            jax.ShapeDtypeStruct(measured.shape, F32),
            jax.ShapeDtypeStruct(volume.shape, F32),
        ),
        in_specs=[smem] * 2 + [vmem] * (2 + len(divisors) + len(order)),
        out_specs=(pl.BlockSpec(memory_space=pl.ANY),) * 2,
        scratch_shapes=[
            pltpu.VMEM((slab_depth + 2, SUBLANES, column_count // 2), F32),
            pltpu.VMEM((SUBLANES, column_count), F32),
            pltpu.VMEM((SUBLANES, wide), F32),
            pltpu.VMEM((SUBLANES, wide), F32),
            pltpu.VMEM(measured.shape, F32),
            pltpu.VMEM(volume.shape, F32),
            pltpu.VMEM((2 * len(order), SUBLANES, column_count // 2), F32),
            pltpu.SemaphoreType.DMA((row_count // SUBLANES + 1,)),
        ],
        compiler_params=small,
        name="update",
    )(view_angle, subset, *map(here, (volume, measured, *divisors, *blocks)))


def solution(mesh):
    in_specs = (
        P(("scan", "slab"), None, None),
        P(("scan", "slab"), None, None),
        P("scan"),
        P("scan"),
        P("scan"),
    )
    out_specs = (P(("scan", "slab"), None, None), P(("scan", "slab"), None, None))
    return jax.shard_map(
        per_device, mesh=mesh, in_specs=in_specs, out_specs=out_specs, check_vma=False
    )
```

```python
import functools
import math

import jax
import jax.numpy as jnp
import numpy as np
from jax import lax
from jax.experimental import pallas as pl
from jax.experimental.pallas import tpu as pltpu
from jax.sharding import PartitionSpec as P

ANGLES = 180
LIFT = 6
PITCH = 0.9
MAG_BASE = 1.5
ECCENTRIC = 0.12
LEN_FLOOR = 0.25
LANES = 128
SUBLANES = 8
F32 = jnp.float32
FULL, NEAR, NEAR_SHARED, FAR = range(4)
VMEM_LIMIT = 8 * 1024 * 1024


def angle_table():
    radians = (np.arange(ANGLES) + 0.5) * (0.5 * math.pi / ANGLES) - 0.25 * math.pi
    magnify = MAG_BASE / (1.0 - ECCENTRIC * np.sin(2.0 * radians + 1.0))
    return np.cos(radians), magnify


def slab_reach(slab_count, slab_depth, row_share):
    _, magnify = angle_table()
    total_rows, total_slices = row_share * slab_count, slab_depth * slab_count
    rows = np.arange(total_rows)
    reach = 0
    for lift in range(-LIFT, LIFT + 1):
        sample = (rows[None] + 0.5 - total_rows / 2 - lift) / magnify[:, None] + total_slices / 2 - 0.5
        for tap in (np.floor(sample - 1e-3), np.floor(sample + 1e-3) + 1):
            inside = (tap >= 0) & (tap < total_slices)
            distance = np.abs(tap // slab_depth - rows[None] // row_share)
            reach = max(reach, int(distance[inside].max()))
    return reach


def lane_index():
    return lax.broadcasted_iota(jnp.int32, (SUBLANES, LANES), 1)


def sublane_index():
    return lax.broadcasted_iota(jnp.int32, (SUBLANES, LANES), 0)


def angle_facts(index):
    x = (index.astype(F32) + 0.5) * (0.5 * math.pi / ANGLES) - 0.25 * math.pi
    s = x * x
    sine = x * (1.0 + s * (-1 / 6 + s * (1 / 120 + s * (-1 / 5040 + s * (1 / 362880)))))
    cosine = 1.0 + s * (-1 / 2 + s * (1 / 24 + s * (-1 / 720 + s * (1 / 40320 + s * (-1 / 3628800)))))
    double = 2.0 * sine * cosine * math.cos(1.0) + (1.0 - 2.0 * sine * sine) * math.sin(1.0)
    return cosine, sine / cosine, (1.0 - ECCENTRIC * double) * (1.0 / MAG_BASE)


def spread_scalars(read, count, place):
    out = jnp.full((SUBLANES, LANES), read(0), jnp.int32)
    for item in range(1, count):
        out = jnp.where(place == item, read(item), out)
    return out


def pick(tile, index):
    numbers = lax.GatherDimensionNumbers(
        offset_dims=(),
        collapsed_slice_dims=(1,),
        start_index_map=(1,),
        operand_batching_dims=(0,),
        start_indices_batching_dims=(0,),
    )
    return lax.gather(tile, index[..., None], numbers, (1, 1), mode=lax.GatherScatterMode.PROMISE_IN_BOUNDS)


def pick_rows(tile, index):
    numbers = lax.GatherDimensionNumbers(
        offset_dims=(),
        collapsed_slice_dims=(0,),
        start_index_map=(0,),
        operand_batching_dims=(1,),
        start_indices_batching_dims=(1,),
    )
    return lax.gather(tile, index[..., None], numbers, (1, 1), mode=lax.GatherScatterMode.PROMISE_IN_BOUNDS)


def next_lane(tile, following):
    lane = lane_index()
    return jnp.where(lane < LANES - 1, pltpu.roll(tile, LANES - 1, 1), pltpu.roll(following, LANES - 1, 1))


def rows_summed(parts):
    sub = sublane_index()
    step = 1
    while step < SUBLANES:
        low = jnp.bitwise_and(sub, step) == 0
        parts = [
            jnp.where(low, a, b) + pltpu.roll(jnp.where(low, b, a), step, 0) for a, b in zip(parts[::2], parts[1::2])
        ]
        step *= 2
    return parts[0]


def tile_of(ref, lead, tile):
    whole = (slice(None),) * (len(ref.shape) - 1 - len(lead))
    return ref[lead + whole + (slice(tile * LANES, (tile + 1) * LANES),)]


def column_center(column, cosine, column_count, cell_count):
    return (column + 0.5 - column_count / 2) * (PITCH * cell_count / column_count) / cosine + (
        cell_count / 2 - 0.5
    )


def shear_steps(group, row_count, tangent):
    row = (sublane_index() + group * SUBLANES).astype(F32)
    offset = (row + 0.5 - row_count / 2) * tangent
    whole = jnp.floor(offset)
    return whole.astype(jnp.int32), offset - whole


def cone_sample(rows, lifts, flat, total_rows, total_slices):
    return (rows + 0.5 - total_rows / 2 - lifts) * flat + (total_slices / 2 - 0.5)


def cone_total(sample, total_slices):
    whole = jnp.floor(sample)
    fraction = sample - whole
    low = jnp.where((whole >= 0) & (whole < total_slices), 1.0 - fraction, 0.0)
    return low + jnp.where((whole >= -1) & (whole < total_slices - 1), fraction, 0.0)


def column_of(tile, at):
    return jnp.broadcast_to(tile[:, at : at + 1], (SUBLANES, LANES))


def slabs_of(slab, order):
    return [slab + (1 - 2 * lax.rem(slab, 2)) * away for away in order]


def turned(slab, kinds):
    odd = lax.rem(slab, 2)
    return [{NEAR: 1 - odd, NEAR_SHARED: odd}.get(kind, 0) for kind in kinds]


def subset_cone(slab, slab_count, order, kinds, slab_depth, row_share, flat, lifts):
    lane = lane_index()
    total_rows, total_slices = row_share * slab_count, slab_depth * slab_count
    origin, turns = slabs_of(slab, order), turned(slab, kinds)
    source = sum(jnp.where(lane >= row_share * b, 1, 0) for b in range(1, len(order)))
    within = lane - source * row_share
    within = jnp.where(spread_scalars(lambda b: turns[b], len(order), source) == 1, row_share - 1 - within, within)
    rows = spread_scalars(lambda b: origin[b], len(order), source) * row_share + within
    real = (rows >= 0) & (rows < total_rows) & (lane < row_share * len(order))
    sample = cone_sample(rows.astype(F32), lifts, flat, total_rows, total_slices)
    weights = []
    for z in range(-1, slab_depth + 1):
        at = slab * slab_depth + z
        use = real & (at >= 0) & (at < total_slices)
        weights.append(jnp.where(use, jnp.maximum(0.0, 1.0 - jnp.abs(sample - at.astype(F32))), 0.0))
    return sample, weights


def adjoint_taps(tile, cosine, column_count, cell_count, half):
    spacing = PITCH * cell_count / column_count
    cell = (lane_index() + (tile * LANES - half)).astype(F32)
    inside = (cell >= 0) & (cell < cell_count)
    first = jnp.floor((cell - (cell_count / 2 + 0.5)) * cosine * (1.0 / spacing) + (column_count / 2 - 0.5 - 1e-3)) + 1.0
    taps = []
    for tap in range(3):
        column = first + tap
        weight = jnp.maximum(0.0, 1.0 - jnp.abs(cell - column_center(column, cosine, column_count, cell_count)))
        weight = jnp.where(inside & (column >= 0) & (column < column_count), weight, 0.0)
        taps.append((jnp.clip(column.astype(jnp.int32), 0, column_count - 1), weight))
    return taps


def adjoint_tiles(tile, tap, column_count, cell_count, half):
    spacing = PITCH * cell_count / column_count
    least = angle_table()[0].min()
    ends = [
        (tile * LANES - half + e - cell_count / 2 - 0.5) * c / spacing + column_count / 2 + 0.5
        for e in (0, LANES - 1)
        for c in (1.0, least)
    ]
    low = min(max(math.floor(min(ends) + tap - 0.6), 0), column_count - 1) // LANES
    high = min(max(math.ceil(max(ends) + tap + 0.6), 0), column_count - 1) // LANES
    return range(low, high + 1)


def store_line(line, base_ref, bend_ref):
    line = line + [jnp.zeros((SUBLANES, LANES), F32)]
    for tile in range(len(line) - 1):
        cut = slice(tile * LANES, (tile + 1) * LANES)
        base_ref[:, cut] = line[tile]
        bend_ref[:, cut] = next_lane(line[tile], line[tile + 1]) - line[tile]


def adjoint_steps(group, row_count, tangent):
    whole, fraction = shear_steps(group, row_count, tangent)
    place = lane_index() + (row_count // 2 - 1 - whole)
    return jnp.bitwise_and(place, LANES - 1), place < LANES, 1.0 - fraction


def sheared(base_ref, bend_ref, row, step, tiles):
    index, near, share = step
    before, out = None, []
    for tile in range(tiles + 1):
        cut = slice(tile * LANES, (tile + 1) * LANES)
        low = jnp.broadcast_to(base_ref[row : row + 1, cut], (SUBLANES, LANES))
        rise = jnp.broadcast_to(bend_ref[row : row + 1, cut], (SUBLANES, LANES))
        after = pick(low + share * rise, index)
        if tile:
            out.append(jnp.where(near, before, after))
        before = after
    return out


def subset_angles(angle_ref, lift_ref, subset_ref):
    members = subset_ref.shape[0]
    member = jnp.bitwise_and(sublane_index(), members - 1)
    cosine, _, flat = angle_facts(spread_scalars(lambda k: angle_ref[subset_ref[k]], members, member))
    lifts = spread_scalars(lambda k: lift_ref[subset_ref[k]], members, member).astype(F32)
    return cosine, flat, lifts


def member_tangents(angle_ref, subset_ref):
    indices = [angle_ref[subset_ref[k]] for k in range(subset_ref.shape[0])]
    return [angle_facts(jnp.full((SUBLANES, LANES), i, jnp.int32))[1] for i in indices]


def project_kernel(
    slab_count,
    angle_ref,
    lift_ref,
    subset_ref,
    volume_ref,
    measured_ref,
    block_ref,
    near_ref,
    low_ref,
    high_ref,
    cover_ref,
    rise_ref,
    first_ref,
    part_ref,
    end_ref,
    cell_ref,
    slope_ref,
):
    slab_depth, row_count, cell_count = volume_ref.shape
    row_share, view_count, column_count = measured_ref.shape
    subset_count = subset_ref.shape[0]
    half = row_count // 2
    tiles = cell_count // LANES
    groups = row_count // SUBLANES
    lane, sub = lane_index(), sublane_index()
    zero = jnp.zeros((SUBLANES, LANES), F32)
    width = column_count // 2

    assert (slab_depth, row_share) == (2, 3)
    slab = lax.axis_index("slab")
    odd = lax.rem(slab, 2)
    grows = odd == 1
    far_row = jnp.where(grows, 2, 0)
    for member in range(subset_count):
        view = pl.ds(subset_ref[member], 1)
        for side in range(2):
            at, cut = side * subset_count + member, slice(side * width, (side + 1) * width)
            rows = [measured_ref[row, view, cut] for row in range(row_share)]
            for row in range(row_share):
                block_ref[2 * slab_depth + row, at : at + 1, :] = rows[row]
            near_ref[2 * slab_depth, at : at + 1, :] = rows[1]
            near_ref[2 * slab_depth + 1, at : at + 1, :] = measured_ref[far_row, view, cut]
            low_ref[2 * slab_depth, at : at + 1, :] = rows[2]
            for more in range(2):
                high_ref[2 * slab_depth + more, at : at + 1, :] = rows[2]

    cosine, _, flat = angle_facts(spread_scalars(lambda v: angle_ref[v], view_count, sub))
    lifts = spread_scalars(lambda v: lift_ref[v], view_count, sub).astype(F32)
    ends = [
        cone_sample((slab * row_share + row).astype(F32), lifts, flat, row_share * slab_count, slab_depth * slab_count)
        - (slab * slab_depth).astype(F32)
        for row in (0, row_share - 1)
    ]
    picked = sub == subset_ref[0]
    for member in range(1, subset_count):
        picked = picked | (sub == subset_ref[member])
    picked = jnp.where(picked, 1, 0)
    as_int = lambda mask: jnp.where(mask, 1, 0)
    near_up, near_down = picked * as_int(ends[1] > 0.75), picked * as_int(ends[0] < 0.25)
    far_up, far_down = picked * as_int(ends[1] > 2.5), picked * as_int(ends[0] < -1.5)
    near_places = [(near_up * odd) == 1, (near_down * (1 - odd)) == 1]
    high_places = (far_up * odd + far_down * (1 - odd)) == 1
    low_places = (far_up * (1 - odd) + far_down * odd) == 1

    for depth in range(slab_depth):
        for group in range(groups):
            band = slice(group * SUBLANES, (group + 1) * SUBLANES)
            cells = [tile_of(volume_ref, (depth, band), tile) for tile in range(tiles)] + [zero]
            for tile in range(tiles):
                rise_ref[depth, band, tile * LANES : (tile + 1) * LANES] = (
                    next_lane(cells[tile], cells[tile + 1]) - cells[tile]
                )
            first_ref[depth, band, :] = column_of(cells[0], 0)

    def one_view(view, carry):
        _, tangent, _ = angle_facts(jnp.full((SUBLANES, LANES), angle_ref[view], jnp.int32))
        low_end, high_end = zero, zero
        sums = [[zero] * (tiles + 1) for _ in range(slab_depth)]
        for group in range(groups):
            band = slice(group * SUBLANES, (group + 1) * SUBLANES)
            whole, fraction = shear_steps(group, row_count, tangent)
            place = lane + (whole + half)
            index = jnp.bitwise_and(place, LANES - 1)
            near, last = place < LANES, index == LANES - 1
            enter = jnp.where(last, fraction, 0.0)
            low_end = low_end + jnp.where(near, enter, 1.0)
            high_end = high_end + jnp.where(near, 1.0 - enter, 0.0)
            for depth in range(slab_depth):
                before = enter * first_ref[depth, band, :]
                for tile in range(tiles + 1):
                    after = zero
                    if tile < tiles:
                        at = (depth, band)
                        after = pick(tile_of(volume_ref, at, tile) + fraction * tile_of(rise_ref, at, tile), index)
                    sums[depth][tile] = sums[depth][tile] + jnp.where(near, before, after)
                    before = after
        end_ref[0, view, :, :] = low_end
        end_ref[1, view, :, :] = high_end
        for depth in range(slab_depth):
            for tile in range(tiles + 1):
                part_ref[depth, view, :, tile * LANES : (tile + 1) * LANES] = sums[depth][tile]
        return carry

    lax.fori_loop(0, view_count, one_view, 0, unroll=8)

    shift = LANES - half
    inside = [None] * (tiles + 1)
    inside[0], inside[tiles] = lane >= shift, lane < shift

    def store(at, line):
        line = [jnp.where(mask, cells, 0.0) if mask is not None else cells for cells, mask in zip(line, inside)] + [zero]
        for tile in range(tiles + 1):
            cut = slice(tile * LANES, (tile + 1) * LANES)
            cell_ref[at, :, cut] = line[tile]
            slope_ref[at, :, cut] = next_lane(line[tile], line[tile + 1]) - line[tile]

    views = range(view_count)
    for depth in range(slab_depth):
        store(depth, [rows_summed([tile_of(part_ref, (depth, v), t) for v in views]) for t in range(tiles + 1)])
    level = zero + float(row_count)
    ends = [rows_summed([end_ref[e, v, :, :] for v in views]) for e in range(2)]
    store(slab_depth, [ends[0]] + [level] * (tiles - 1) + [ends[1]])

    factor = 1.0 / (row_count * cosine)
    least = angle_table()[0].min()
    for tile in range(column_count // LANES):
        column = (lane + tile * LANES).astype(F32)
        center = column_center(column, cosine, column_count, cell_count)
        whole = jnp.floor(center)
        fraction = center - whole
        place = jnp.clip(whole.astype(jnp.int32) + shift, shift - 2, shift + cell_count)
        block, index = jnp.right_shift(place, 7), jnp.bitwise_and(place, LANES - 1)
        ends = [column_center(tile * LANES + e, c, column_count, cell_count) for e in (0, LANES - 1) for c in (1.0, least)]
        low = min(max(math.floor(min(ends) - 1e-2) + shift, shift - 2), shift + cell_count) // LANES
        high = min(max(math.floor(max(ends) + 1e-2) + shift, shift - 2), shift + cell_count) // LANES
        cells, slopes = [zero] * slab_depth + [level], [zero] * (slab_depth + 1)
        for source in range(low, high + 1):
            here = block == source
            for at in range(slab_depth + 1):
                if at == slab_depth and source not in (0, tiles):
                    continue
                cells[at] = jnp.where(here, pick(tile_of(cell_ref, (at,), source), index), cells[at])
                slopes[at] = jnp.where(here, pick(tile_of(slope_ref, (at,), source), index), slopes[at])
        profiles = [(c + fraction * s) * factor for c, s in zip(cells, slopes)]
        side, inner = divmod(tile * LANES, width)
        for depth in range(slab_depth):
            to = (depth * 2 + side, slice(None), slice(inner, inner + LANES))
            measured = tile_of(measured_ref, (depth,), tile)
            last = tile_of(measured_ref, (depth * (row_share - 1),), tile)
            block_ref[to] = profiles[depth]
            near_ref[to] = jnp.where(near_places[depth], last, profiles[depth])
            low_ref[to] = jnp.where(low_places, measured, profiles[depth])
            high_ref[to] = jnp.where(high_places, measured, profiles[depth])
        cover_ref[:, tile * LANES : (tile + 1) * LANES] = profiles[slab_depth]


def divisor_kernel(
    slab_count,
    order,
    kinds,
    angle_ref,
    lift_ref,
    subset_ref,
    cover_ref,
    bound_ref,
    own_ref,
    rows_ref,
    own_cone_ref,
    cone_ref,
    place_ref,
    tap_ref,
    tangent_ref,
    view_ref,
    edge_ref,
    bend_ref,
    sub_ref,
):
    slab_depth, row_count, cell_count = bound_ref.shape
    row_share, view_count, column_count = own_ref.shape
    subset_count = subset_ref.shape[0]
    total_rows, total_slices = row_share * slab_count, slab_depth * slab_count
    tiles, columns = cell_count // LANES, column_count // LANES
    width = column_count // 2
    sub = sublane_index()
    zero = jnp.zeros((SUBLANES, LANES), F32)
    slab = lax.axis_index("slab")

    _, _, flat = angle_facts(spread_scalars(lambda v: angle_ref[v], view_count, sub))
    lifts = spread_scalars(lambda v: lift_ref[v], view_count, sub).astype(F32)
    lane = lane_index()
    origin = slabs_of(slab, order)
    source = sum(jnp.where(lane >= slab_depth * b, 1, 0) for b in range(1, len(order)))
    slices = spread_scalars(lambda b: origin[b], len(order), source) * slab_depth + (lane - source * slab_depth)
    held = (slices >= 0) & (slices < total_slices)
    slices = slices.astype(F32)
    for row in range(row_share):
        sample = cone_sample((slab * row_share + row).astype(F32), lifts, flat, total_rows, total_slices)
        weights = jnp.where(held, jnp.maximum(0.0, 1.0 - jnp.abs(sample - slices)), 0.0)
        for place in range(slab_depth * len(order)):
            own_cone_ref[place, row, :, :] = column_of(weights, place)
        total = cone_total(sample, total_slices)
        for tile in range(columns):
            cut = slice(tile * LANES, (tile + 1) * LANES)
            own_ref[row, :, cut] = 1.0 / jnp.maximum(total * cover_ref[:, cut], LEN_FLOOR)

    cosine, flat, lifts = subset_angles(angle_ref, lift_ref, subset_ref)
    tangents = member_tangents(angle_ref, subset_ref)
    for member in range(subset_count):
        tangent_ref[member, :, :] = tangents[member]
    view_ref[...] = spread_scalars(lambda k: subset_ref[k], subset_count, jnp.bitwise_and(sub, subset_count - 1))
    for member in range(subset_count):
        view = pl.ds(subset_ref[member], 1)
        for side in range(2):
            at = slice(side * subset_count + member, side * subset_count + member + 1)
            sub_ref[at, :] = cover_ref[view, side * width : (side + 1) * width]
    sample, weights = subset_cone(slab, slab_count, order, kinds, slab_depth, row_share, flat, lifts)
    total = cone_total(sample, total_slices)
    for place in range(row_share * len(order)):
        for z, w in enumerate(weights):
            cone_ref[place, z, :, :] = column_of(w, place)
        length = column_of(total, place)
        for tile in range(width // LANES):
            cut = slice(tile * LANES, (tile + 1) * LANES)
            rows_ref[place, :, cut] = 1.0 / jnp.maximum(length * sub_ref[:, cut], LEN_FLOOR)

    factor = 1.0 / (row_count * cosine)
    line = []
    for tile in range(tiles + 1):
        taps = adjoint_taps(tile, cosine, column_count, cell_count, row_count // 2)
        for tap, (place, weight) in enumerate(taps):
            place_ref[tile, tap, :, :] = place
            tap_ref[tile, tap, :, :] = weight * factor
        line.append(sum(weight for _, weight in taps) * factor)
    store_line(line, edge_ref, bend_ref)
    slice_total = []
    for depth in range(slab_depth):
        t = jnp.sum(weights[1 + depth], axis=1, keepdims=True)
        slice_total.append([jnp.broadcast_to(t[k : k + 1], (SUBLANES, LANES)) for k in range(subset_count)])

    def one_group(group, carry):
        band = pl.ds(pl.multiple_of(group * SUBLANES, SUBLANES), SUBLANES)
        weight = [[zero] * tiles for _ in range(slab_depth)]
        for member in range(subset_count):
            line = sheared(edge_ref, bend_ref, member, adjoint_steps(group, row_count, tangents[member]), tiles)
            for depth in range(slab_depth):
                for tile in range(tiles):
                    weight[depth][tile] = weight[depth][tile] + slice_total[depth][member] * line[tile]
        for depth in range(slab_depth):
            for tile in range(tiles):
                bound_ref[depth, band, tile * LANES : (tile + 1) * LANES] = 1.0 / jnp.maximum(
                    weight[depth][tile], LEN_FLOOR * subset_count / row_count
                )
        return carry

    lax.fori_loop(0, row_count // SUBLANES, one_group, 0)


def update_kernel(
    order,
    kinds,
    volume_ref,
    measured_ref,
    bound_ref,
    own_ref,
    rows_ref,
    own_cone_ref,
    cone_ref,
    place_ref,
    tap_ref,
    tangent_ref,
    view_ref,
    *refs,
):
    blocks = refs[: len(order)]
    residual_ref, updated_ref, profile_ref, spread_ref, cell_ref, slope_ref, rest_ref, new_ref, row_ref, sent = refs[len(order) :]
    slab_depth, row_count, cell_count = volume_ref.shape
    row_share, view_count, column_count = measured_ref.shape
    subset_count = tangent_ref.shape[0]
    tiles, columns = cell_count // LANES, column_count // LANES
    width = column_count // 2
    zero = jnp.zeros((SUBLANES, LANES), F32)
    slab = lax.axis_index("slab")
    odd = lax.rem(slab, 2)
    turns = turned(slab, kinds)
    mate_block, other_block = (blocks[order.index(away)] for away in (1, -1))

    groups = row_count // SUBLANES
    for tile in range(columns):
        side, inner = divmod(tile * LANES, width)
        image = [zero] * row_share
        for place, block in enumerate(blocks):
            for depth in range(slab_depth):
                cells = block[depth * 2 + side, :, inner : inner + LANES]
                for row in range(row_share):
                    image[row] = image[row] + own_cone_ref[place * slab_depth + depth, row, :, :] * cells
        cut = slice(tile * LANES, (tile + 1) * LANES)
        for row in range(row_share):
            rest_ref[row, :, cut] = (measured_ref[row, :, cut] - image[row]) * own_ref[row, :, cut]
    copies = [pltpu.make_async_copy(rest_ref, residual_ref, sent.at[groups])]
    copies[0].start()

    chosen, first_side = view_ref[...], sublane_index() < subset_count

    def of_members(read, tile):
        return jnp.where(first_side, pick_rows(read(0, tile), chosen), pick_rows(read(1, tile), chosen))

    inner_tiles = width // LANES
    for tile in range(inner_tiles):
        cut = slice(tile * LANES, (tile + 1) * LANES)
        last, first = (slab_depth - 1) * 2, 0
        below = lambda side, t: jnp.where(
            odd == 0, tile_of(other_block, (last + side,), t), tile_of(mate_block, (last + side,), t)
        )
        above = lambda side, t: jnp.where(
            odd == 0, tile_of(mate_block, (first + side,), t), tile_of(other_block, (first + side,), t)
        )
        profile_ref[0, :, cut] = of_members(below, tile)
        for depth in range(slab_depth):
            profile_ref[1 + depth, :, cut] = of_members(
                lambda side, t: tile_of(blocks[0], (depth * 2 + side,), t), tile
            )
        profile_ref[1 + slab_depth, :, cut] = of_members(above, tile)

    moved = [(b, j) for b, kind in enumerate(kinds) for j in range({FULL: 0, FAR: 2}.get(kind, 1))]
    for at_row, (b, j) in enumerate(moved):
        depth = turns[b] if kinds[b] in (NEAR, NEAR_SHARED) else j
        for tile in range(inner_tiles):
            row_ref[at_row, :, tile * LANES : (tile + 1) * LANES] = of_members(
                lambda side, t: tile_of(blocks[b], (depth * 2 + side,), t), tile
            )

    spread = [[zero] * inner_tiles for _ in range(slab_depth)]
    for place in range(row_share * len(order)):
        weight = [cone_ref[place, z, :, :] for z in range(slab_depth + 2)]
        block, row = divmod(place, row_share)
        here = (block, row) in moved
        held = row_ref if here else blocks[block]
        at_row = moved.index((block, row)) if here else 2 * slab_depth + row - sum(b == block for b, _ in moved)
        for tile in range(inner_tiles):
            cut = slice(tile * LANES, (tile + 1) * LANES)
            image = weight[0] * profile_ref[0, :, cut]
            for z in range(1, slab_depth + 2):
                image = image + weight[z] * profile_ref[z, :, cut]
            rest = (held[at_row, :, cut] - image) * rows_ref[place, :, cut]
            for depth in range(slab_depth):
                spread[depth][tile] = spread[depth][tile] + weight[1 + depth] * rest
    for depth in range(slab_depth):
        for tile in range(inner_tiles):
            for side in range(2):
                spread_ref[
                    depth * subset_count : (depth + 1) * subset_count,
                    side * width + tile * LANES : side * width + (tile + 1) * LANES,
                ] = spread[depth][tile][side * subset_count : (side + 1) * subset_count]

    line = []
    for tile in range(tiles + 1):
        value = zero
        for tap in range(3):
            place = place_ref[tile, tap, :, :]
            block, index = jnp.right_shift(place, 7), jnp.bitwise_and(place, LANES - 1)
            found = zero
            for at in adjoint_tiles(tile, tap, column_count, cell_count, row_count // 2):
                found = jnp.where(block == at, pick(tile_of(spread_ref, (), at), index), found)
            value = value + tap_ref[tile, tap, :, :] * found
        line.append(value)
    store_line(line, cell_ref, slope_ref)

    tangents = [tangent_ref[member, :, :] for member in range(subset_count)]
    for group in range(groups):
        band = slice(group * SUBLANES, (group + 1) * SUBLANES)
        back = [[zero] * tiles for _ in range(slab_depth)]
        for member in range(subset_count):
            step = adjoint_steps(group, row_count, tangents[member])
            for depth in range(slab_depth):
                line = sheared(cell_ref, slope_ref, depth * subset_count + member, step, tiles)
                back[depth] = [b + a for b, a in zip(back[depth], line)]
        for depth in range(slab_depth):
            for tile in range(tiles):
                cut = slice(tile * LANES, (tile + 1) * LANES)
                new_ref[depth, band, cut] = (
                    volume_ref[depth, band, cut] + back[depth][tile] * bound_ref[depth, band, cut]
                )
        copies.append(pltpu.make_async_copy(new_ref.at[:, band, :], updated_ref.at[:, band, :], sent.at[group]))
        copies[-1].start()
    for copy in copies:
        copy.wait()


def swapped(block):
    return lax.ppermute(block, "slab", [(i, i ^ 1) for i in range(lax.axis_size("slab"))])


def from_chip(block, distance):
    slabs = range(lax.axis_size("slab"))
    steps = [(i + 2 * distance * (1 - 2 * (i % 2)), i) for i in slabs]
    pairs = [p for p in steps if p[0] in slabs]
    idle = [i for i in slabs if i not in [p[0] for p in pairs]]
    unmet = [i for i in slabs if i not in [p[1] for p in pairs]]
    near = [i for i in idle if i ^ 1 in unmet]
    pairs += [(i, i ^ 1) for i in near]
    pairs += zip([i for i in idle if i not in near], [i for i in unmet if i ^ 1 not in near])
    return lax.ppermute(block, "slab", pairs)


def fetches(reach):
    return [s * d for d in range(reach // 2 + 1, 0, -1) for s in (1, -1) if 2 * d - (s > 0) <= reach]


def window(reach):
    order, kinds = [0, 1], [FULL, FULL]
    for distance in fetches(reach):
        near = distance == 1
        for away, kind in ((2 * distance, NEAR if near else FAR), (1 - 2 * distance, NEAR_SHARED if near else FAR)):
            if abs(away) <= reach:
                order.append(away)
                kinds.append(kind)
    assert sorted(order) == list(range(-reach, reach + 1))
    return tuple(order), tuple(kinds)


def gathered(own, near, low, high, reach, meanwhile):
    sent = {distance: near if distance == 1 else high if distance > 0 else low for distance in fetches(reach)}
    received = {distance: from_chip(block, distance) for distance, block in sent.items()}
    done = meanwhile()
    own, done = lax.optimization_barrier((own, done))
    blocks = {0: own, 1: swapped(own)}
    arrived, done = lax.optimization_barrier((list(received.values()), done))
    for distance, block in zip(received, arrived):
        if 2 * abs(distance) <= reach:
            blocks[2 * distance] = block
        if abs(1 - 2 * distance) <= reach:
            blocks[1 - 2 * distance] = swapped(block)
    return [blocks[away] for away in window(reach)[0]], done


def per_device(volume, measured, view_angle, view_lift, subset):
    slab_count = lax.axis_size("slab")
    slab_depth, row_count, cell_count = volume.shape
    row_share, view_count, column_count = measured.shape
    subset_count = subset.shape[0]
    tiles = cell_count // LANES
    reach = slab_reach(slab_count, slab_depth, row_share)
    here = lambda x: pltpu.with_memory_space_constraint(x, pltpu.VMEM)
    there = lambda x: pltpu.with_memory_space_constraint(x, pltpu.HBM)
    small = pltpu.CompilerParams(vmem_limit_bytes=VMEM_LIMIT)
    smem, vmem = pl.BlockSpec(memory_space=pltpu.SMEM), pl.BlockSpec(memory_space=pltpu.VMEM)
    wide = (tiles + 1) * LANES
    block_of = lambda rows: pltpu.VMEM((2 * slab_depth + rows, SUBLANES, column_count // 2), F32)
    own, near, low, high, cover = pl.pallas_call(
        functools.partial(project_kernel, slab_count),
        out_shape=(
            block_of(row_share),
            block_of(2),
            block_of(1),
            block_of(2),
            pltpu.VMEM((view_count, column_count), F32),
        ),
        in_specs=[smem] * 3 + [vmem] * 2,
        out_specs=(vmem,) * 5,
        scratch_shapes=[
            pltpu.VMEM(volume.shape, F32),
            pltpu.VMEM((slab_depth, row_count, LANES), F32),
            pltpu.VMEM((slab_depth, view_count, SUBLANES, wide), F32),
            pltpu.VMEM((2, view_count, SUBLANES, LANES), F32),
        ]
        + [pltpu.VMEM((slab_depth + 1, SUBLANES, wide), F32)] * 2,
        compiler_params=small,
        name="project",
    )(*map(there, (view_angle, view_lift, subset, volume, measured)))
    cover = here(cover)
    order, kinds = window(reach)
    divide = pl.pallas_call(
        functools.partial(divisor_kernel, slab_count, order, kinds),
        out_shape=(
            pltpu.VMEM(volume.shape, F32),
            pltpu.VMEM(measured.shape, F32),
            pltpu.VMEM((row_share * len(order), SUBLANES, column_count // 2), F32),
            pltpu.VMEM((slab_depth * len(order), row_share, SUBLANES, LANES), F32),
            pltpu.VMEM((row_share * len(order), slab_depth + 2, SUBLANES, LANES), F32),
            pltpu.VMEM((tiles + 1, 3, SUBLANES, LANES), jnp.int32),
            pltpu.VMEM((tiles + 1, 3, SUBLANES, LANES), F32),
            pltpu.VMEM((subset_count, SUBLANES, LANES), F32),
            pltpu.VMEM((SUBLANES, LANES), jnp.int32),
        ),
        in_specs=[smem] * 3 + [vmem],
        out_specs=(vmem,) * 9,
        scratch_shapes=[pltpu.VMEM((SUBLANES, wide), F32)] * 2 + [pltpu.VMEM((SUBLANES, column_count // 2), F32)],
        cost_estimate=pl.CostEstimate(flops=4_000_000, bytes_accessed=8_000_000, transcendentals=0),
        compiler_params=small,
        name="divisors",
    )
    blocks, divisors = gathered(own, near, low, high, reach, lambda: divide(view_angle, view_lift, subset, cover))
    return pl.pallas_call(
        functools.partial(update_kernel, order, kinds),
        out_shape=(
            jax.ShapeDtypeStruct(measured.shape, F32),
            jax.ShapeDtypeStruct(volume.shape, F32),
        ),
        in_specs=[vmem] * (2 + len(divisors) + len(order)),
        out_specs=(pl.BlockSpec(memory_space=pl.ANY),) * 2,
        scratch_shapes=[
            pltpu.VMEM((slab_depth + 2, SUBLANES, column_count // 2), F32),
            pltpu.VMEM((SUBLANES, column_count), F32),
            pltpu.VMEM((SUBLANES, wide), F32),
            pltpu.VMEM((SUBLANES, wide), F32),
            pltpu.VMEM(measured.shape, F32),
            pltpu.VMEM(volume.shape, F32),
            pltpu.VMEM((2 * len(order), SUBLANES, column_count // 2), F32),
            pltpu.SemaphoreType.DMA((row_count // SUBLANES + 1,)),
        ],
        compiler_params=small,
        name="update",
    )(*map(here, (volume, measured, *divisors, *blocks)))


def solution(mesh):
    in_specs = (
        P(("scan", "slab"), None, None),
        P(("scan", "slab"), None, None),
        P("scan"),
        P("scan"),
        P("scan"),
    )
    out_specs = (P(("scan", "slab"), None, None), P(("scan", "slab"), None, None))
    return jax.shard_map(
        per_device, mesh=mesh, in_specs=in_specs, out_specs=out_specs, check_vma=False
    )
```

```python
import functools
import math

import jax
import jax.numpy as jnp
import numpy as np
from jax import lax
from jax.experimental import pallas as pl
from jax.experimental.pallas import tpu as pltpu
from jax.sharding import PartitionSpec as P

ANGLES = 180
LIFT = 6
PITCH = 0.9
MAG_BASE = 1.5
ECCENTRIC = 0.12
LEN_FLOOR = 0.25
LANES = 128
SUBLANES = 8
F32 = jnp.float32
FULL, NEAR, NEAR_SHARED, FAR = range(4)
VMEM_LIMIT = 8 * 1024 * 1024


def angle_table():
    radians = (np.arange(ANGLES) + 0.5) * (0.5 * math.pi / ANGLES) - 0.25 * math.pi
    magnify = MAG_BASE / (1.0 - ECCENTRIC * np.sin(2.0 * radians + 1.0))
    return np.cos(radians), magnify


def slab_reach(slab_count, slab_depth, row_share):
    _, magnify = angle_table()
    total_rows, total_slices = row_share * slab_count, slab_depth * slab_count
    rows = np.arange(total_rows)
    reach = 0
    for lift in range(-LIFT, LIFT + 1):
        sample = (rows[None] + 0.5 - total_rows / 2 - lift) / magnify[:, None] + total_slices / 2 - 0.5
        for tap in (np.floor(sample - 1e-3), np.floor(sample + 1e-3) + 1):
            inside = (tap >= 0) & (tap < total_slices)
            distance = np.abs(tap // slab_depth - rows[None] // row_share)
            reach = max(reach, int(distance[inside].max()))
    return reach


def lane_index():
    return lax.broadcasted_iota(jnp.int32, (SUBLANES, LANES), 1)


def sublane_index():
    return lax.broadcasted_iota(jnp.int32, (SUBLANES, LANES), 0)


def angle_facts(index):
    x = (index.astype(F32) + 0.5) * (0.5 * math.pi / ANGLES) - 0.25 * math.pi
    s = x * x
    sine = x * (1.0 + s * (-1 / 6 + s * (1 / 120 + s * (-1 / 5040 + s * (1 / 362880)))))
    cosine = 1.0 + s * (-1 / 2 + s * (1 / 24 + s * (-1 / 720 + s * (1 / 40320 + s * (-1 / 3628800)))))
    double = 2.0 * sine * cosine * math.cos(1.0) + (1.0 - 2.0 * sine * sine) * math.sin(1.0)
    return cosine, sine / cosine, (1.0 - ECCENTRIC * double) * (1.0 / MAG_BASE)


def spread_scalars(read, count, place):
    out = jnp.full((SUBLANES, LANES), read(0), jnp.int32)
    for item in range(1, count):
        out = jnp.where(place == item, read(item), out)
    return out


def pick(tile, index):
    numbers = lax.GatherDimensionNumbers(
        offset_dims=(),
        collapsed_slice_dims=(1,),
        start_index_map=(1,),
        operand_batching_dims=(0,),
        start_indices_batching_dims=(0,),
    )
    return lax.gather(tile, index[..., None], numbers, (1, 1), mode=lax.GatherScatterMode.PROMISE_IN_BOUNDS)


def pick_rows(tile, index):
    numbers = lax.GatherDimensionNumbers(
        offset_dims=(),
        collapsed_slice_dims=(0,),
        start_index_map=(0,),
        operand_batching_dims=(1,),
        start_indices_batching_dims=(1,),
    )
    return lax.gather(tile, index[..., None], numbers, (1, 1), mode=lax.GatherScatterMode.PROMISE_IN_BOUNDS)


def next_lane(tile, following):
    lane = lane_index()
    return jnp.where(lane < LANES - 1, pltpu.roll(tile, LANES - 1, 1), pltpu.roll(following, LANES - 1, 1))


def rows_summed(parts):
    sub = sublane_index()
    step = 1
    while step < SUBLANES:
        low = jnp.bitwise_and(sub, step) == 0
        parts = [
            jnp.where(low, a, b) + pltpu.roll(jnp.where(low, b, a), step, 0) for a, b in zip(parts[::2], parts[1::2])
        ]
        step *= 2
    return parts[0]


def tile_of(ref, lead, tile):
    whole = (slice(None),) * (len(ref.shape) - 1 - len(lead))
    return ref[lead + whole + (slice(tile * LANES, (tile + 1) * LANES),)]


def column_center(column, cosine, column_count, cell_count):
    return (column + 0.5 - column_count / 2) * (PITCH * cell_count / column_count) / cosine + (
        cell_count / 2 - 0.5
    )


def shear_steps(group, row_count, tangent):
    row = (sublane_index() + group * SUBLANES).astype(F32)
    offset = (row + 0.5 - row_count / 2) * tangent
    whole = jnp.floor(offset)
    return whole.astype(jnp.int32), offset - whole


def cone_sample(rows, lifts, flat, total_rows, total_slices):
    return (rows + 0.5 - total_rows / 2 - lifts) * flat + (total_slices / 2 - 0.5)


def cone_total(sample, total_slices):
    whole = jnp.floor(sample)
    fraction = sample - whole
    low = jnp.where((whole >= 0) & (whole < total_slices), 1.0 - fraction, 0.0)
    return low + jnp.where((whole >= -1) & (whole < total_slices - 1), fraction, 0.0)


def column_of(tile, at):
    return jnp.broadcast_to(tile[:, at : at + 1], (SUBLANES, LANES))


def slabs_of(slab, order):
    return [slab + (1 - 2 * lax.rem(slab, 2)) * away for away in order]


def turned(slab, kinds):
    odd = lax.rem(slab, 2)
    return [{NEAR: 1 - odd, NEAR_SHARED: odd}.get(kind, 0) for kind in kinds]


def subset_cone(slab, slab_count, order, kinds, slab_depth, row_share, flat, lifts):
    lane = lane_index()
    total_rows, total_slices = row_share * slab_count, slab_depth * slab_count
    origin, turns = slabs_of(slab, order), turned(slab, kinds)
    source = sum(jnp.where(lane >= row_share * b, 1, 0) for b in range(1, len(order)))
    within = lane - source * row_share
    within = jnp.where(spread_scalars(lambda b: turns[b], len(order), source) == 1, row_share - 1 - within, within)
    rows = spread_scalars(lambda b: origin[b], len(order), source) * row_share + within
    real = (rows >= 0) & (rows < total_rows) & (lane < row_share * len(order))
    sample = cone_sample(rows.astype(F32), lifts, flat, total_rows, total_slices)
    weights = []
    for z in range(-1, slab_depth + 1):
        at = slab * slab_depth + z
        use = real & (at >= 0) & (at < total_slices)
        weights.append(jnp.where(use, jnp.maximum(0.0, 1.0 - jnp.abs(sample - at.astype(F32))), 0.0))
    return sample, weights


def adjoint_taps(tile, cosine, column_count, cell_count, half):
    spacing = PITCH * cell_count / column_count
    cell = (lane_index() + (tile * LANES - half)).astype(F32)
    inside = (cell >= 0) & (cell < cell_count)
    first = jnp.floor((cell - (cell_count / 2 + 0.5)) * cosine * (1.0 / spacing) + (column_count / 2 - 0.5 - 1e-3)) + 1.0
    taps = []
    for tap in range(3):
        column = first + tap
        weight = jnp.maximum(0.0, 1.0 - jnp.abs(cell - column_center(column, cosine, column_count, cell_count)))
        weight = jnp.where(inside & (column >= 0) & (column < column_count), weight, 0.0)
        taps.append((jnp.clip(column.astype(jnp.int32), 0, column_count - 1), weight))
    return taps


def adjoint_tiles(tile, tap, column_count, cell_count, half):
    spacing = PITCH * cell_count / column_count
    least = angle_table()[0].min()
    ends = [
        (tile * LANES - half + e - cell_count / 2 - 0.5) * c / spacing + column_count / 2 + 0.5
        for e in (0, LANES - 1)
        for c in (1.0, least)
    ]
    low = min(max(math.floor(min(ends) + tap - 0.6), 0), column_count - 1) // LANES
    high = min(max(math.ceil(max(ends) + tap + 0.6), 0), column_count - 1) // LANES
    return range(low, high + 1)


def store_line(line, base_ref, bend_ref):
    line = line + [jnp.zeros((SUBLANES, LANES), F32)]
    for tile in range(len(line) - 1):
        cut = slice(tile * LANES, (tile + 1) * LANES)
        base_ref[:, cut] = line[tile]
        bend_ref[:, cut] = next_lane(line[tile], line[tile + 1]) - line[tile]


def adjoint_steps(group, row_count, tangent):
    whole, fraction = shear_steps(group, row_count, tangent)
    place = lane_index() + (row_count // 2 - 1 - whole)
    return jnp.bitwise_and(place, LANES - 1), place < LANES, 1.0 - fraction


def sheared(base_ref, bend_ref, row, step, tiles):
    index, near, share = step
    before, out = None, []
    for tile in range(tiles + 1):
        cut = slice(tile * LANES, (tile + 1) * LANES)
        low = jnp.broadcast_to(base_ref[row : row + 1, cut], (SUBLANES, LANES))
        rise = jnp.broadcast_to(bend_ref[row : row + 1, cut], (SUBLANES, LANES))
        after = pick(low + share * rise, index)
        if tile:
            out.append(jnp.where(near, before, after))
        before = after
    return out


def subset_angles(angle_ref, lift_ref, subset_ref):
    members = subset_ref.shape[0]
    member = jnp.bitwise_and(sublane_index(), members - 1)
    cosine, _, flat = angle_facts(spread_scalars(lambda k: angle_ref[subset_ref[k]], members, member))
    lifts = spread_scalars(lambda k: lift_ref[subset_ref[k]], members, member).astype(F32)
    return cosine, flat, lifts


def member_tangents(angle_ref, subset_ref):
    indices = [angle_ref[subset_ref[k]] for k in range(subset_ref.shape[0])]
    return [angle_facts(jnp.full((SUBLANES, LANES), i, jnp.int32))[1] for i in indices]


def store_cells(line, at, half, cell_ref, slope_ref):
    lane, shift = lane_index(), LANES - half
    zero = jnp.zeros((SUBLANES, LANES), F32)
    line = [jnp.where(lane >= shift, line[0], 0.0)] + line[1:-1] + [jnp.where(lane < shift, line[-1], 0.0), zero]
    for tile in range(len(line) - 1):
        cut = slice(tile * LANES, (tile + 1) * LANES)
        cell_ref[at, :, cut] = line[tile]
        slope_ref[at, :, cut] = next_lane(line[tile], line[tile + 1]) - line[tile]


def forward_tap(tile, cosine, column_count, cell_count, shift):
    least = angle_table()[0].min()
    column = (lane_index() + tile * LANES).astype(F32)
    center = column_center(column, cosine, column_count, cell_count)
    whole = jnp.floor(center)
    place = jnp.clip(whole.astype(jnp.int32) + shift, shift - 2, shift + cell_count)
    ends = [column_center(tile * LANES + e, c, column_count, cell_count) for e in (0, LANES - 1) for c in (1.0, least)]
    low = min(max(math.floor(min(ends) - 1e-2) + shift, shift - 2), shift + cell_count) // LANES
    high = min(max(math.floor(max(ends) + 1e-2) + shift, shift - 2), shift + cell_count) // LANES
    return place, center - whole, range(low, high + 1)


def resampled(at, place, fraction, sources, level, cell_ref, slope_ref):
    block, index = jnp.right_shift(place, 7), jnp.bitwise_and(place, LANES - 1)
    cells, slope = level, jnp.zeros((SUBLANES, LANES), F32)
    for source in sources:
        here = block == source
        cells = jnp.where(here, pick(tile_of(cell_ref, (at,), source), index), cells)
        slope = jnp.where(here, pick(tile_of(slope_ref, (at,), source), index), slope)
    return cells + fraction * slope


def project_kernel(
    slab_count,
    angle_ref,
    lift_ref,
    subset_ref,
    volume_ref,
    measured_ref,
    block_ref,
    near_ref,
    low_ref,
    high_ref,
    rise_ref,
    first_ref,
    part_ref,
    cell_ref,
    slope_ref,
):
    slab_depth, row_count, cell_count = volume_ref.shape
    row_share, view_count, column_count = measured_ref.shape
    subset_count = subset_ref.shape[0]
    half = row_count // 2
    tiles = cell_count // LANES
    groups = row_count // SUBLANES
    lane, sub = lane_index(), sublane_index()
    zero = jnp.zeros((SUBLANES, LANES), F32)
    width = column_count // 2

    assert (slab_depth, row_share) == (2, 3)
    slab = lax.axis_index("slab")
    odd = lax.rem(slab, 2)
    grows = odd == 1
    far_row = jnp.where(grows, 2, 0)
    for member in range(subset_count):
        view = pl.ds(subset_ref[member], 1)
        for side in range(2):
            at, cut = side * subset_count + member, slice(side * width, (side + 1) * width)
            rows = [measured_ref[row, view, cut] for row in range(row_share)]
            for row in range(row_share):
                block_ref[2 * slab_depth + row, at : at + 1, :] = rows[row]
            near_ref[2 * slab_depth, at : at + 1, :] = rows[1]
            near_ref[2 * slab_depth + 1, at : at + 1, :] = measured_ref[far_row, view, cut]
            low_ref[2 * slab_depth, at : at + 1, :] = rows[2]
            for more in range(2):
                high_ref[2 * slab_depth + more, at : at + 1, :] = rows[2]

    cosine, _, flat = angle_facts(spread_scalars(lambda v: angle_ref[v], view_count, sub))
    lifts = spread_scalars(lambda v: lift_ref[v], view_count, sub).astype(F32)
    ends = [
        cone_sample((slab * row_share + row).astype(F32), lifts, flat, row_share * slab_count, slab_depth * slab_count)
        - (slab * slab_depth).astype(F32)
        for row in (0, row_share - 1)
    ]
    picked = sub == subset_ref[0]
    for member in range(1, subset_count):
        picked = picked | (sub == subset_ref[member])
    picked = jnp.where(picked, 1, 0)
    as_int = lambda mask: jnp.where(mask, 1, 0)
    near_up, near_down = picked * as_int(ends[1] > 0.75), picked * as_int(ends[0] < 0.25)
    far_up, far_down = picked * as_int(ends[1] > 2.5), picked * as_int(ends[0] < -1.5)
    near_places = [(near_up * odd) == 1, (near_down * (1 - odd)) == 1]
    high_places = (far_up * odd + far_down * (1 - odd)) == 1
    low_places = (far_up * (1 - odd) + far_down * odd) == 1

    for depth in range(slab_depth):
        for group in range(groups):
            band = slice(group * SUBLANES, (group + 1) * SUBLANES)
            cells = [tile_of(volume_ref, (depth, band), tile) for tile in range(tiles)] + [zero]
            for tile in range(tiles):
                rise_ref[depth, band, tile * LANES : (tile + 1) * LANES] = (
                    next_lane(cells[tile], cells[tile + 1]) - cells[tile]
                )
            first_ref[depth, band, :] = column_of(cells[0], 0)

    def one_view(view, carry):
        _, tangent, _ = angle_facts(jnp.full((SUBLANES, LANES), angle_ref[view], jnp.int32))
        sums = [[zero] * (tiles + 1) for _ in range(slab_depth)]
        for group in range(groups):
            band = slice(group * SUBLANES, (group + 1) * SUBLANES)
            whole, fraction = shear_steps(group, row_count, tangent)
            place = lane + (whole + half)
            index = jnp.bitwise_and(place, LANES - 1)
            near, last = place < LANES, index == LANES - 1
            enter = jnp.where(last, fraction, 0.0)
            for depth in range(slab_depth):
                before = enter * first_ref[depth, band, :]
                for tile in range(tiles + 1):
                    after = zero
                    if tile < tiles:
                        at = (depth, band)
                        after = pick(tile_of(volume_ref, at, tile) + fraction * tile_of(rise_ref, at, tile), index)
                    sums[depth][tile] = sums[depth][tile] + jnp.where(near, before, after)
                    before = after
        for depth in range(slab_depth):
            for tile in range(tiles + 1):
                part_ref[depth, view, :, tile * LANES : (tile + 1) * LANES] = sums[depth][tile]
        return carry

    lax.fori_loop(0, view_count, one_view, 0, unroll=8)

    for depth in range(slab_depth):
        line = [
            rows_summed([tile_of(part_ref, (depth, view), tile) for view in range(view_count)])
            for tile in range(tiles + 1)
        ]
        store_cells(line, depth, half, cell_ref, slope_ref)

    factor = 1.0 / (row_count * cosine)
    for tile in range(column_count // LANES):
        place, fraction, sources = forward_tap(tile, cosine, column_count, cell_count, LANES - half)
        side, inner = divmod(tile * LANES, width)
        for depth in range(slab_depth):
            profile = resampled(depth, place, fraction, sources, zero, cell_ref, slope_ref) * factor
            to = (depth * 2 + side, slice(None), slice(inner, inner + LANES))
            measured = tile_of(measured_ref, (depth,), tile)
            last = tile_of(measured_ref, (depth * (row_share - 1),), tile)
            block_ref[to] = profile
            near_ref[to] = jnp.where(near_places[depth], last, profile)
            low_ref[to] = jnp.where(low_places, measured, profile)
            high_ref[to] = jnp.where(high_places, measured, profile)


def divisor_kernel(
    slab_count,
    order,
    kinds,
    angle_ref,
    lift_ref,
    subset_ref,
    _,
    bound_ref,
    own_ref,
    rows_ref,
    own_cone_ref,
    cone_ref,
    place_ref,
    tap_ref,
    tangent_ref,
    view_ref,
    edge_ref,
    bend_ref,
    sub_ref,
    cover_ref,
    cell_ref,
    slope_ref,
):
    slab_depth, row_count, cell_count = bound_ref.shape
    row_share, view_count, column_count = own_ref.shape
    subset_count = subset_ref.shape[0]
    total_rows, total_slices = row_share * slab_count, slab_depth * slab_count
    tiles, columns = cell_count // LANES, column_count // LANES
    width = column_count // 2
    sub = sublane_index()
    zero = jnp.zeros((SUBLANES, LANES), F32)
    slab = lax.axis_index("slab")

    cosine, _, flat = angle_facts(spread_scalars(lambda v: angle_ref[v], view_count, sub))
    lifts = spread_scalars(lambda v: lift_ref[v], view_count, sub).astype(F32)
    lane = lane_index()

    half = row_count // 2
    ends = [], []
    for view in range(view_count):
        _, tangent, _ = angle_facts(jnp.full((SUBLANES, LANES), angle_ref[view], jnp.int32))
        low_end, high_end = zero, zero
        for group in range(row_count // SUBLANES):
            whole, fraction = shear_steps(group, row_count, tangent)
            place = lane + (whole + half)
            near = place < LANES
            enter = jnp.where(jnp.bitwise_and(place, LANES - 1) == LANES - 1, fraction, 0.0)
            low_end = low_end + jnp.where(near, enter, 1.0)
            high_end = high_end + jnp.where(near, 1.0 - enter, 0.0)
        ends[0].append(low_end)
        ends[1].append(high_end)
    level = zero + float(row_count)
    store_cells([rows_summed(ends[0])] + [level] * (tiles - 1) + [rows_summed(ends[1])], 0, half, cell_ref, slope_ref)
    for tile in range(columns):
        place, fraction, sources = forward_tap(tile, cosine, column_count, cell_count, LANES - half)
        sources = [source for source in sources if source in (0, tiles)]
        cover_ref[:, tile * LANES : (tile + 1) * LANES] = resampled(
            0, place, fraction, sources, level, cell_ref, slope_ref
        ) * (1.0 / (row_count * cosine))
    origin = slabs_of(slab, order)
    source = sum(jnp.where(lane >= slab_depth * b, 1, 0) for b in range(1, len(order)))
    slices = spread_scalars(lambda b: origin[b], len(order), source) * slab_depth + (lane - source * slab_depth)
    held = (slices >= 0) & (slices < total_slices)
    slices = slices.astype(F32)
    for row in range(row_share):
        sample = cone_sample((slab * row_share + row).astype(F32), lifts, flat, total_rows, total_slices)
        weights = jnp.where(held, jnp.maximum(0.0, 1.0 - jnp.abs(sample - slices)), 0.0)
        for place in range(slab_depth * len(order)):
            own_cone_ref[place, row, :, :] = column_of(weights, place)
        total = cone_total(sample, total_slices)
        for tile in range(columns):
            cut = slice(tile * LANES, (tile + 1) * LANES)
            own_ref[row, :, cut] = 1.0 / jnp.maximum(total * cover_ref[:, cut], LEN_FLOOR)

    cosine, flat, lifts = subset_angles(angle_ref, lift_ref, subset_ref)
    tangents = member_tangents(angle_ref, subset_ref)
    for member in range(subset_count):
        tangent_ref[member, :, :] = tangents[member]
    view_ref[...] = spread_scalars(lambda k: subset_ref[k], subset_count, jnp.bitwise_and(sub, subset_count - 1))
    for member in range(subset_count):
        view = pl.ds(subset_ref[member], 1)
        for side in range(2):
            at = slice(side * subset_count + member, side * subset_count + member + 1)
            sub_ref[at, :] = cover_ref[view, side * width : (side + 1) * width]
    sample, weights = subset_cone(slab, slab_count, order, kinds, slab_depth, row_share, flat, lifts)
    total = cone_total(sample, total_slices)
    for place in range(row_share * len(order)):
        for z, w in enumerate(weights):
            cone_ref[place, z, :, :] = column_of(w, place)
        length = column_of(total, place)
        for tile in range(width // LANES):
            cut = slice(tile * LANES, (tile + 1) * LANES)
            rows_ref[place, :, cut] = 1.0 / jnp.maximum(length * sub_ref[:, cut], LEN_FLOOR)

    factor = 1.0 / (row_count * cosine)
    line = []
    for tile in range(tiles + 1):
        taps = adjoint_taps(tile, cosine, column_count, cell_count, row_count // 2)
        for tap, (place, weight) in enumerate(taps):
            place_ref[tile, tap, :, :] = place
            tap_ref[tile, tap, :, :] = weight * factor
        line.append(sum(weight for _, weight in taps) * factor)
    store_line(line, edge_ref, bend_ref)
    slice_total = []
    for depth in range(slab_depth):
        t = jnp.sum(weights[1 + depth], axis=1, keepdims=True)
        slice_total.append([jnp.broadcast_to(t[k : k + 1], (SUBLANES, LANES)) for k in range(subset_count)])

    def one_group(group, carry):
        band = pl.ds(pl.multiple_of(group * SUBLANES, SUBLANES), SUBLANES)
        weight = [[zero] * tiles for _ in range(slab_depth)]
        for member in range(subset_count):
            line = sheared(edge_ref, bend_ref, member, adjoint_steps(group, row_count, tangents[member]), tiles)
            for depth in range(slab_depth):
                for tile in range(tiles):
                    weight[depth][tile] = weight[depth][tile] + slice_total[depth][member] * line[tile]
        for depth in range(slab_depth):
            for tile in range(tiles):
                bound_ref[depth, band, tile * LANES : (tile + 1) * LANES] = 1.0 / jnp.maximum(
                    weight[depth][tile], LEN_FLOOR * subset_count / row_count
                )
        return carry

    lax.fori_loop(0, row_count // SUBLANES, one_group, 0)


def update_kernel(
    order,
    kinds,
    volume_ref,
    measured_ref,
    bound_ref,
    own_ref,
    rows_ref,
    own_cone_ref,
    cone_ref,
    place_ref,
    tap_ref,
    tangent_ref,
    view_ref,
    *refs,
):
    blocks = refs[: len(order)]
    residual_ref, updated_ref, profile_ref, spread_ref, cell_ref, slope_ref, rest_ref, new_ref, row_ref, sent = refs[len(order) :]
    slab_depth, row_count, cell_count = volume_ref.shape
    row_share, view_count, column_count = measured_ref.shape
    subset_count = tangent_ref.shape[0]
    tiles, columns = cell_count // LANES, column_count // LANES
    width = column_count // 2
    zero = jnp.zeros((SUBLANES, LANES), F32)
    slab = lax.axis_index("slab")
    odd = lax.rem(slab, 2)
    turns = turned(slab, kinds)
    mate_block, other_block = (blocks[order.index(away)] for away in (1, -1))

    groups = row_count // SUBLANES
    for tile in range(columns):
        side, inner = divmod(tile * LANES, width)
        image = [zero] * row_share
        for place, block in enumerate(blocks):
            for depth in range(slab_depth):
                cells = block[depth * 2 + side, :, inner : inner + LANES]
                for row in range(row_share):
                    image[row] = image[row] + own_cone_ref[place * slab_depth + depth, row, :, :] * cells
        cut = slice(tile * LANES, (tile + 1) * LANES)
        for row in range(row_share):
            rest_ref[row, :, cut] = (measured_ref[row, :, cut] - image[row]) * own_ref[row, :, cut]
    copies = [pltpu.make_async_copy(rest_ref, residual_ref, sent.at[groups])]
    copies[0].start()

    chosen, first_side = view_ref[...], sublane_index() < subset_count

    def of_members(read, tile):
        return jnp.where(first_side, pick_rows(read(0, tile), chosen), pick_rows(read(1, tile), chosen))

    inner_tiles = width // LANES
    for tile in range(inner_tiles):
        cut = slice(tile * LANES, (tile + 1) * LANES)
        last, first = (slab_depth - 1) * 2, 0
        below = lambda side, t: jnp.where(
            odd == 0, tile_of(other_block, (last + side,), t), tile_of(mate_block, (last + side,), t)
        )
        above = lambda side, t: jnp.where(
            odd == 0, tile_of(mate_block, (first + side,), t), tile_of(other_block, (first + side,), t)
        )
        profile_ref[0, :, cut] = of_members(below, tile)
        for depth in range(slab_depth):
            profile_ref[1 + depth, :, cut] = of_members(
                lambda side, t: tile_of(blocks[0], (depth * 2 + side,), t), tile
            )
        profile_ref[1 + slab_depth, :, cut] = of_members(above, tile)

    moved = [(b, j) for b, kind in enumerate(kinds) for j in range({FULL: 0, FAR: 2}.get(kind, 1))]
    for at_row, (b, j) in enumerate(moved):
        depth = turns[b] if kinds[b] in (NEAR, NEAR_SHARED) else j
        for tile in range(inner_tiles):
            row_ref[at_row, :, tile * LANES : (tile + 1) * LANES] = of_members(
                lambda side, t: tile_of(blocks[b], (depth * 2 + side,), t), tile
            )

    spread = [[zero] * inner_tiles for _ in range(slab_depth)]
    for place in range(row_share * len(order)):
        weight = [cone_ref[place, z, :, :] for z in range(slab_depth + 2)]
        block, row = divmod(place, row_share)
        here = (block, row) in moved
        held = row_ref if here else blocks[block]
        at_row = moved.index((block, row)) if here else 2 * slab_depth + row - sum(b == block for b, _ in moved)
        for tile in range(inner_tiles):
            cut = slice(tile * LANES, (tile + 1) * LANES)
            image = weight[0] * profile_ref[0, :, cut]
            for z in range(1, slab_depth + 2):
                image = image + weight[z] * profile_ref[z, :, cut]
            rest = (held[at_row, :, cut] - image) * rows_ref[place, :, cut]
            for depth in range(slab_depth):
                spread[depth][tile] = spread[depth][tile] + weight[1 + depth] * rest
    for depth in range(slab_depth):
        for tile in range(inner_tiles):
            for side in range(2):
                spread_ref[
                    depth * subset_count : (depth + 1) * subset_count,
                    side * width + tile * LANES : side * width + (tile + 1) * LANES,
                ] = spread[depth][tile][side * subset_count : (side + 1) * subset_count]

    line = []
    for tile in range(tiles + 1):
        value = zero
        for tap in range(3):
            place = place_ref[tile, tap, :, :]
            block, index = jnp.right_shift(place, 7), jnp.bitwise_and(place, LANES - 1)
            found = zero
            for at in adjoint_tiles(tile, tap, column_count, cell_count, row_count // 2):
                found = jnp.where(block == at, pick(tile_of(spread_ref, (), at), index), found)
            value = value + tap_ref[tile, tap, :, :] * found
        line.append(value)
    store_line(line, cell_ref, slope_ref)

    tangents = [tangent_ref[member, :, :] for member in range(subset_count)]
    for group in range(groups):
        band = slice(group * SUBLANES, (group + 1) * SUBLANES)
        back = [[zero] * tiles for _ in range(slab_depth)]
        for member in range(subset_count):
            step = adjoint_steps(group, row_count, tangents[member])
            for depth in range(slab_depth):
                line = sheared(cell_ref, slope_ref, depth * subset_count + member, step, tiles)
                back[depth] = [b + a for b, a in zip(back[depth], line)]
        for depth in range(slab_depth):
            for tile in range(tiles):
                cut = slice(tile * LANES, (tile + 1) * LANES)
                new_ref[depth, band, cut] = (
                    volume_ref[depth, band, cut] + back[depth][tile] * bound_ref[depth, band, cut]
                )
        copies.append(pltpu.make_async_copy(new_ref.at[:, band, :], updated_ref.at[:, band, :], sent.at[group]))
        copies[-1].start()
    for copy in copies:
        copy.wait()


def swapped(block):
    return lax.ppermute(block, "slab", [(i, i ^ 1) for i in range(lax.axis_size("slab"))])


def from_chip(block, distance):
    slabs = range(lax.axis_size("slab"))
    steps = [(i + 2 * distance * (1 - 2 * (i % 2)), i) for i in slabs]
    pairs = [p for p in steps if p[0] in slabs]
    idle = [i for i in slabs if i not in [p[0] for p in pairs]]
    unmet = [i for i in slabs if i not in [p[1] for p in pairs]]
    near = [i for i in idle if i ^ 1 in unmet]
    pairs += [(i, i ^ 1) for i in near]
    pairs += zip([i for i in idle if i not in near], [i for i in unmet if i ^ 1 not in near])
    return lax.ppermute(block, "slab", pairs)


def fetches(reach):
    return [s * d for d in range(reach // 2 + 1, 0, -1) for s in (1, -1) if 2 * d - (s > 0) <= reach]


def window(reach):
    order, kinds = [0, 1], [FULL, FULL]
    for distance in fetches(reach):
        near = distance == 1
        for away, kind in ((2 * distance, NEAR if near else FAR), (1 - 2 * distance, NEAR_SHARED if near else FAR)):
            if abs(away) <= reach:
                order.append(away)
                kinds.append(kind)
    assert sorted(order) == list(range(-reach, reach + 1))
    return tuple(order), tuple(kinds)


def gathered(own, near, low, high, reach, meanwhile):
    sent = {distance: near if distance == 1 else high if distance > 0 else low for distance in fetches(reach)}
    received = {distance: from_chip(block, distance) for distance, block in sent.items()}
    done = meanwhile()
    own, done = lax.optimization_barrier((own, done))
    blocks = {0: own, 1: swapped(own)}
    arrived, done = lax.optimization_barrier((list(received.values()), done))
    for distance, block in zip(received, arrived):
        if 2 * abs(distance) <= reach:
            blocks[2 * distance] = block
        if abs(1 - 2 * distance) <= reach:
            blocks[1 - 2 * distance] = swapped(block)
    return [blocks[away] for away in window(reach)[0]], done


def per_device(volume, measured, view_angle, view_lift, subset):
    slab_count = lax.axis_size("slab")
    slab_depth, row_count, cell_count = volume.shape
    row_share, view_count, column_count = measured.shape
    subset_count = subset.shape[0]
    tiles = cell_count // LANES
    reach = slab_reach(slab_count, slab_depth, row_share)
    here = lambda x: pltpu.with_memory_space_constraint(x, pltpu.VMEM)
    there = lambda x: pltpu.with_memory_space_constraint(x, pltpu.HBM)
    small = pltpu.CompilerParams(vmem_limit_bytes=VMEM_LIMIT)
    smem, vmem = pl.BlockSpec(memory_space=pltpu.SMEM), pl.BlockSpec(memory_space=pltpu.VMEM)
    wide = (tiles + 1) * LANES
    block_of = lambda rows: pltpu.VMEM((2 * slab_depth + rows, SUBLANES, column_count // 2), F32)
    own, near, low, high = pl.pallas_call(
        functools.partial(project_kernel, slab_count),
        out_shape=(
            block_of(row_share),
            block_of(2),
            block_of(1),
            block_of(2),
        ),
        in_specs=[smem] * 3 + [vmem] * 2,
        out_specs=(vmem,) * 4,
        scratch_shapes=[
            pltpu.VMEM(volume.shape, F32),
            pltpu.VMEM((slab_depth, row_count, LANES), F32),
            pltpu.VMEM((slab_depth, view_count, SUBLANES, wide), F32),
        ]
        + [pltpu.VMEM((slab_depth, SUBLANES, wide), F32)] * 2,
        compiler_params=small,
        name="project",
    )(*map(there, (view_angle, view_lift, subset, volume, measured)))
    order, kinds = window(reach)
    divide = pl.pallas_call(
        functools.partial(divisor_kernel, slab_count, order, kinds),
        out_shape=(
            pltpu.VMEM(volume.shape, F32),
            pltpu.VMEM(measured.shape, F32),
            pltpu.VMEM((row_share * len(order), SUBLANES, column_count // 2), F32),
            pltpu.VMEM((slab_depth * len(order), row_share, SUBLANES, LANES), F32),
            pltpu.VMEM((row_share * len(order), slab_depth + 2, SUBLANES, LANES), F32),
            pltpu.VMEM((tiles + 1, 3, SUBLANES, LANES), jnp.int32),
            pltpu.VMEM((tiles + 1, 3, SUBLANES, LANES), F32),
            pltpu.VMEM((subset_count, SUBLANES, LANES), F32),
            pltpu.VMEM((SUBLANES, LANES), jnp.int32),
        ),
        in_specs=[smem] * 3 + [pl.BlockSpec(memory_space=pl.ANY)],
        out_specs=(vmem,) * 9,
        scratch_shapes=[pltpu.VMEM((SUBLANES, wide), F32)] * 2
        + [pltpu.VMEM((SUBLANES, column_count // 2), F32), pltpu.VMEM((view_count, column_count), F32)]
        + [pltpu.VMEM((1, SUBLANES, wide), F32)] * 2,
        cost_estimate=pl.CostEstimate(flops=4_000_000, bytes_accessed=8_000_000, transcendentals=0),
        compiler_params=small,
        name="divisors",
    )
    blocks, divisors = gathered(own, near, low, high, reach, lambda: divide(view_angle, view_lift, subset, own))
    return pl.pallas_call(
        functools.partial(update_kernel, order, kinds),
        out_shape=(
            jax.ShapeDtypeStruct(measured.shape, F32),
            jax.ShapeDtypeStruct(volume.shape, F32),
        ),
        in_specs=[vmem] * (2 + len(divisors) + len(order)),
        out_specs=(pl.BlockSpec(memory_space=pl.ANY),) * 2,
        scratch_shapes=[
            pltpu.VMEM((slab_depth + 2, SUBLANES, column_count // 2), F32),
            pltpu.VMEM((SUBLANES, column_count), F32),
            pltpu.VMEM((SUBLANES, wide), F32),
            pltpu.VMEM((SUBLANES, wide), F32),
            pltpu.VMEM(measured.shape, F32),
            pltpu.VMEM(volume.shape, F32),
            pltpu.VMEM((2 * len(order), SUBLANES, column_count // 2), F32),
            pltpu.SemaphoreType.DMA((row_count // SUBLANES + 1,)),
        ],
        compiler_params=small,
        name="update",
    )(*map(here, (volume, measured, *divisors, *blocks)))


def solution(mesh):
    in_specs = (
        P(("scan", "slab"), None, None),
        P(("scan", "slab"), None, None),
        P("scan"),
        P("scan"),
        P("scan"),
    )
    out_specs = (P(("scan", "slab"), None, None), P(("scan", "slab"), None, None))
    return jax.shard_map(
        per_device, mesh=mesh, in_specs=in_specs, out_specs=out_specs, check_vma=False
    )
```

```python
import functools
import math

import jax
import jax.numpy as jnp
import numpy as np
from jax import lax
from jax.experimental import pallas as pl
from jax.experimental.pallas import tpu as pltpu
from jax.sharding import PartitionSpec as P

ANGLES = 180
LIFT = 6
PITCH = 0.9
MAG_BASE = 1.5
ECCENTRIC = 0.12
LEN_FLOOR = 0.25
LANES = 128
SUBLANES = 8
F32 = jnp.float32
FULL, NEAR, NEAR_SHARED, FAR = range(4)
VMEM_LIMIT = 8 * 1024 * 1024


def angle_table():
    radians = (np.arange(ANGLES) + 0.5) * (0.5 * math.pi / ANGLES) - 0.25 * math.pi
    magnify = MAG_BASE / (1.0 - ECCENTRIC * np.sin(2.0 * radians + 1.0))
    return np.cos(radians), magnify


def slab_reach(slab_count, slab_depth, row_share):
    _, magnify = angle_table()
    total_rows, total_slices = row_share * slab_count, slab_depth * slab_count
    rows = np.arange(total_rows)
    reach = 0
    for lift in range(-LIFT, LIFT + 1):
        sample = (rows[None] + 0.5 - total_rows / 2 - lift) / magnify[:, None] + total_slices / 2 - 0.5
        for tap in (np.floor(sample - 1e-3), np.floor(sample + 1e-3) + 1):
            inside = (tap >= 0) & (tap < total_slices)
            distance = np.abs(tap // slab_depth - rows[None] // row_share)
            reach = max(reach, int(distance[inside].max()))
    return reach


def lane_index():
    return lax.broadcasted_iota(jnp.int32, (SUBLANES, LANES), 1)


def sublane_index():
    return lax.broadcasted_iota(jnp.int32, (SUBLANES, LANES), 0)


def angle_facts(index):
    x = (index.astype(F32) + 0.5) * (0.5 * math.pi / ANGLES) - 0.25 * math.pi
    s = x * x
    sine = x * (1.0 + s * (-1 / 6 + s * (1 / 120 + s * (-1 / 5040 + s * (1 / 362880)))))
    cosine = 1.0 + s * (-1 / 2 + s * (1 / 24 + s * (-1 / 720 + s * (1 / 40320 + s * (-1 / 3628800)))))
    double = 2.0 * sine * cosine * math.cos(1.0) + (1.0 - 2.0 * sine * sine) * math.sin(1.0)
    return cosine, sine / cosine, (1.0 - ECCENTRIC * double) * (1.0 / MAG_BASE)


def spread_scalars(read, count, place):
    out = jnp.full((SUBLANES, LANES), read(0), jnp.int32)
    for item in range(1, count):
        out = jnp.where(place == item, read(item), out)
    return out


def pick(tile, index):
    numbers = lax.GatherDimensionNumbers(
        offset_dims=(),
        collapsed_slice_dims=(1,),
        start_index_map=(1,),
        operand_batching_dims=(0,),
        start_indices_batching_dims=(0,),
    )
    return lax.gather(tile, index[..., None], numbers, (1, 1), mode=lax.GatherScatterMode.PROMISE_IN_BOUNDS)


def pick_rows(tile, index):
    numbers = lax.GatherDimensionNumbers(
        offset_dims=(),
        collapsed_slice_dims=(0,),
        start_index_map=(0,),
        operand_batching_dims=(1,),
        start_indices_batching_dims=(1,),
    )
    return lax.gather(tile, index[..., None], numbers, (1, 1), mode=lax.GatherScatterMode.PROMISE_IN_BOUNDS)


def next_lane(tile, following):
    lane = lane_index()
    return jnp.where(lane < LANES - 1, pltpu.roll(tile, LANES - 1, 1), pltpu.roll(following, LANES - 1, 1))


def rows_summed(parts):
    sub = sublane_index()
    step = 1
    while step < SUBLANES:
        low = jnp.bitwise_and(sub, step) == 0
        parts = [
            jnp.where(low, a, b) + pltpu.roll(jnp.where(low, b, a), step, 0) for a, b in zip(parts[::2], parts[1::2])
        ]
        step *= 2
    return parts[0]


def tile_of(ref, lead, tile):
    whole = (slice(None),) * (len(ref.shape) - 1 - len(lead))
    return ref[lead + whole + (slice(tile * LANES, (tile + 1) * LANES),)]


def column_center(column, cosine, column_count, cell_count):
    return (column + 0.5 - column_count / 2) * (PITCH * cell_count / column_count) / cosine + (
        cell_count / 2 - 0.5
    )


def shear_steps(group, row_count, tangent):
    row = (sublane_index() + group * SUBLANES).astype(F32)
    offset = (row + 0.5 - row_count / 2) * tangent
    whole = jnp.floor(offset)
    return whole.astype(jnp.int32), offset - whole


def cone_sample(rows, lifts, flat, total_rows, total_slices):
    return (rows + 0.5 - total_rows / 2 - lifts) * flat + (total_slices / 2 - 0.5)


def cone_total(sample, total_slices):
    whole = jnp.floor(sample)
    fraction = sample - whole
    low = jnp.where((whole >= 0) & (whole < total_slices), 1.0 - fraction, 0.0)
    return low + jnp.where((whole >= -1) & (whole < total_slices - 1), fraction, 0.0)


def column_of(tile, at):
    return jnp.broadcast_to(tile[:, at : at + 1], (SUBLANES, LANES))


def slabs_of(slab, order):
    return [slab + (1 - 2 * lax.rem(slab, 2)) * away for away in order]


def turned(slab, kinds):
    odd = lax.rem(slab, 2)
    return [{NEAR: 1 - odd, NEAR_SHARED: odd}.get(kind, 0) for kind in kinds]


def subset_cone(slab, slab_count, order, kinds, slab_depth, row_share, flat, lifts):
    lane = lane_index()
    total_rows, total_slices = row_share * slab_count, slab_depth * slab_count
    origin, turns = slabs_of(slab, order), turned(slab, kinds)
    source = sum(jnp.where(lane >= row_share * b, 1, 0) for b in range(1, len(order)))
    within = lane - source * row_share
    within = jnp.where(spread_scalars(lambda b: turns[b], len(order), source) == 1, row_share - 1 - within, within)
    rows = spread_scalars(lambda b: origin[b], len(order), source) * row_share + within
    real = (rows >= 0) & (rows < total_rows) & (lane < row_share * len(order))
    sample = cone_sample(rows.astype(F32), lifts, flat, total_rows, total_slices)
    weights = []
    for z in range(-1, slab_depth + 1):
        at = slab * slab_depth + z
        use = real & (at >= 0) & (at < total_slices)
        weights.append(jnp.where(use, jnp.maximum(0.0, 1.0 - jnp.abs(sample - at.astype(F32))), 0.0))
    return sample, weights


def adjoint_taps(tile, cosine, column_count, cell_count, half):
    spacing = PITCH * cell_count / column_count
    cell = (lane_index() + (tile * LANES - half)).astype(F32)
    inside = (cell >= 0) & (cell < cell_count)
    first = jnp.floor((cell - (cell_count / 2 + 0.5)) * cosine * (1.0 / spacing) + (column_count / 2 - 0.5 - 1e-3)) + 1.0
    taps = []
    for tap in range(3):
        column = first + tap
        weight = jnp.maximum(0.0, 1.0 - jnp.abs(cell - column_center(column, cosine, column_count, cell_count)))
        weight = jnp.where(inside & (column >= 0) & (column < column_count), weight, 0.0)
        taps.append((jnp.clip(column.astype(jnp.int32), 0, column_count - 1), weight))
    return taps


def adjoint_tiles(tile, tap, column_count, cell_count, half):
    spacing = PITCH * cell_count / column_count
    least = angle_table()[0].min()
    ends = [
        (tile * LANES - half + e - cell_count / 2 - 0.5) * c / spacing + column_count / 2 + 0.5
        for e in (0, LANES - 1)
        for c in (1.0, least)
    ]
    low = min(max(math.floor(min(ends) + tap - 0.6), 0), column_count - 1) // LANES
    high = min(max(math.ceil(max(ends) + tap + 0.6), 0), column_count - 1) // LANES
    return range(low, high + 1)


def store_line(line, base_ref, bend_ref):
    line = line + [jnp.zeros((SUBLANES, LANES), F32)]
    for tile in range(len(line) - 1):
        cut = slice(tile * LANES, (tile + 1) * LANES)
        base_ref[:, cut] = line[tile]
        bend_ref[:, cut] = next_lane(line[tile], line[tile + 1]) - line[tile]


def adjoint_steps(group, row_count, tangent):
    whole, fraction = shear_steps(group, row_count, tangent)
    place = lane_index() + (row_count // 2 - 1 - whole)
    return jnp.bitwise_and(place, LANES - 1), place < LANES, 1.0 - fraction


def sheared(base_ref, bend_ref, row, step, tiles):
    index, near, share = step
    before, out = None, []
    for tile in range(tiles + 1):
        cut = slice(tile * LANES, (tile + 1) * LANES)
        low = jnp.broadcast_to(base_ref[row : row + 1, cut], (SUBLANES, LANES))
        rise = jnp.broadcast_to(bend_ref[row : row + 1, cut], (SUBLANES, LANES))
        after = pick(low + share * rise, index)
        if tile:
            out.append(jnp.where(near, before, after))
        before = after
    return out


def subset_angles(angle_ref, lift_ref, subset_ref):
    members = subset_ref.shape[0]
    member = jnp.bitwise_and(sublane_index(), members - 1)
    cosine, _, flat = angle_facts(spread_scalars(lambda k: angle_ref[subset_ref[k]], members, member))
    lifts = spread_scalars(lambda k: lift_ref[subset_ref[k]], members, member).astype(F32)
    return cosine, flat, lifts


def member_tangents(angle_ref, subset_ref):
    indices = [angle_ref[subset_ref[k]] for k in range(subset_ref.shape[0])]
    return [angle_facts(jnp.full((SUBLANES, LANES), i, jnp.int32))[1] for i in indices]


def project_kernel(
    slab_count,
    angle_ref,
    lift_ref,
    subset_ref,
    volume_ref,
    measured_ref,
    block_ref,
    near_ref,
    low_ref,
    high_ref,
    cover_ref,
    rise_ref,
    first_ref,
    part_ref,
    end_ref,
    cell_ref,
    slope_ref,
):
    slab_depth, row_count, cell_count = volume_ref.shape
    row_share, view_count, column_count = measured_ref.shape
    subset_count = subset_ref.shape[0]
    half = row_count // 2
    tiles = cell_count // LANES
    groups = row_count // SUBLANES
    lane, sub = lane_index(), sublane_index()
    zero = jnp.zeros((SUBLANES, LANES), F32)
    width = column_count // 2

    assert (slab_depth, row_share) == (2, 3)
    slab = lax.axis_index("slab")
    odd = lax.rem(slab, 2)
    grows = odd == 1
    far_row = jnp.where(grows, 2, 0)
    for member in range(subset_count):
        view = pl.ds(subset_ref[member], 1)
        for side in range(2):
            at, cut = side * subset_count + member, slice(side * width, (side + 1) * width)
            rows = [measured_ref[row, view, cut] for row in range(row_share)]
            for row in range(row_share):
                block_ref[2 * slab_depth + row, at : at + 1, :] = rows[row]
            near_ref[2 * slab_depth, at : at + 1, :] = rows[1]
            near_ref[2 * slab_depth + 1, at : at + 1, :] = measured_ref[far_row, view, cut]
            low_ref[2 * slab_depth, at : at + 1, :] = rows[2]
            for more in range(2):
                high_ref[2 * slab_depth + more, at : at + 1, :] = rows[2]

    cosine, _, flat = angle_facts(spread_scalars(lambda v: angle_ref[v], view_count, sub))
    lifts = spread_scalars(lambda v: lift_ref[v], view_count, sub).astype(F32)
    ends = [
        cone_sample((slab * row_share + row).astype(F32), lifts, flat, row_share * slab_count, slab_depth * slab_count)
        - (slab * slab_depth).astype(F32)
        for row in (0, row_share - 1)
    ]
    picked = sub == subset_ref[0]
    for member in range(1, subset_count):
        picked = picked | (sub == subset_ref[member])
    picked = jnp.where(picked, 1, 0)
    as_int = lambda mask: jnp.where(mask, 1, 0)
    near_up, near_down = picked * as_int(ends[1] > 0.75), picked * as_int(ends[0] < 0.25)
    far_up, far_down = picked * as_int(ends[1] > 2.5), picked * as_int(ends[0] < -1.5)
    near_places = [(near_up * odd) == 1, (near_down * (1 - odd)) == 1]
    high_places = (far_up * odd + far_down * (1 - odd)) == 1
    low_places = (far_up * (1 - odd) + far_down * odd) == 1

    for depth in range(slab_depth):
        for group in range(groups):
            band = slice(group * SUBLANES, (group + 1) * SUBLANES)
            cells = [tile_of(volume_ref, (depth, band), tile) for tile in range(tiles)] + [zero]
            for tile in range(tiles):
                rise_ref[depth, band, tile * LANES : (tile + 1) * LANES] = (
                    next_lane(cells[tile], cells[tile + 1]) - cells[tile]
                )
            first_ref[depth, band, :] = column_of(cells[0], 0)

    def one_view(view, carry):
        _, tangent, _ = angle_facts(jnp.full((SUBLANES, LANES), angle_ref[view], jnp.int32))
        low_end, high_end = zero, zero
        sums = [[zero] * (tiles + 1) for _ in range(slab_depth)]
        for group in range(groups):
            band = slice(group * SUBLANES, (group + 1) * SUBLANES)
            whole, fraction = shear_steps(group, row_count, tangent)
            place = lane + (whole + half)
            index = jnp.bitwise_and(place, LANES - 1)
            near, last = place < LANES, index == LANES - 1
            enter = jnp.where(last, fraction, 0.0)
            low_end = low_end + jnp.where(near, enter, 1.0)
            high_end = high_end + jnp.where(near, 1.0 - enter, 0.0)
            for depth in range(slab_depth):
                before = enter * first_ref[depth, band, :]
                for tile in range(tiles + 1):
                    after = zero
                    if tile < tiles:
                        at = (depth, band)
                        after = pick(tile_of(volume_ref, at, tile) + fraction * tile_of(rise_ref, at, tile), index)
                    sums[depth][tile] = sums[depth][tile] + jnp.where(near, before, after)
                    before = after
        end_ref[0, view, :, :] = low_end
        end_ref[1, view, :, :] = high_end
        for depth in range(slab_depth):
            for tile in range(tiles + 1):
                part_ref[depth, view, :, tile * LANES : (tile + 1) * LANES] = sums[depth][tile]
        return carry

    lax.fori_loop(0, view_count, one_view, 0, unroll=8)

    shift = LANES - half
    inside = [None] * (tiles + 1)
    inside[0], inside[tiles] = lane >= shift, lane < shift

    def store(at, line):
        line = [jnp.where(mask, cells, 0.0) if mask is not None else cells for cells, mask in zip(line, inside)] + [zero]
        for tile in range(tiles + 1):
            cut = slice(tile * LANES, (tile + 1) * LANES)
            cell_ref[at, :, cut] = line[tile]
            slope_ref[at, :, cut] = next_lane(line[tile], line[tile + 1]) - line[tile]

    views = range(view_count)
    for depth in range(slab_depth):
        store(depth, [rows_summed([tile_of(part_ref, (depth, v), t) for v in views]) for t in range(tiles + 1)])
    level = zero + float(row_count)
    ends = [rows_summed([end_ref[e, v, :, :] for v in views]) for e in range(2)]
    store(slab_depth, [ends[0]] + [level] * (tiles - 1) + [ends[1]])

    factor = 1.0 / (row_count * cosine)
    least = angle_table()[0].min()
    for tile in range(column_count // LANES):
        column = (lane + tile * LANES).astype(F32)
        center = column_center(column, cosine, column_count, cell_count)
        whole = jnp.floor(center)
        fraction = center - whole
        place = jnp.clip(whole.astype(jnp.int32) + shift, shift - 2, shift + cell_count)
        block, index = jnp.right_shift(place, 7), jnp.bitwise_and(place, LANES - 1)
        ends = [column_center(tile * LANES + e, c, column_count, cell_count) for e in (0, LANES - 1) for c in (1.0, least)]
        low = min(max(math.floor(min(ends) - 1e-2) + shift, shift - 2), shift + cell_count) // LANES
        high = min(max(math.floor(max(ends) + 1e-2) + shift, shift - 2), shift + cell_count) // LANES
        cells, slopes = [zero] * slab_depth + [level], [zero] * (slab_depth + 1)
        for source in range(low, high + 1):
            here = block == source
            for at in range(slab_depth + 1):
                if at == slab_depth and source not in (0, tiles):
                    continue
                cells[at] = jnp.where(here, pick(tile_of(cell_ref, (at,), source), index), cells[at])
                slopes[at] = jnp.where(here, pick(tile_of(slope_ref, (at,), source), index), slopes[at])
        profiles = [(c + fraction * s) * factor for c, s in zip(cells, slopes)]
        side, inner = divmod(tile * LANES, width)
        for depth in range(slab_depth):
            to = (depth * 2 + side, slice(None), slice(inner, inner + LANES))
            measured = tile_of(measured_ref, (depth,), tile)
            last = tile_of(measured_ref, (depth * (row_share - 1),), tile)
            block_ref[to] = profiles[depth]
            near_ref[to] = jnp.where(near_places[depth], last, profiles[depth])
            low_ref[to] = jnp.where(low_places, measured, profiles[depth])
            high_ref[to] = jnp.where(high_places, measured, profiles[depth])
        cover_ref[:, tile * LANES : (tile + 1) * LANES] = profiles[slab_depth]


def divisor_kernel(
    slab_count,
    order,
    kinds,
    angle_ref,
    lift_ref,
    subset_ref,
    cover_ref,
    bound_ref,
    own_ref,
    rows_ref,
    own_cone_ref,
    cone_ref,
    place_ref,
    tap_ref,
    tangent_ref,
    view_ref,
    edge_ref,
    bend_ref,
    sub_ref,
):
    slab_depth, row_count, cell_count = bound_ref.shape
    row_share, view_count, column_count = own_ref.shape
    subset_count = subset_ref.shape[0]
    total_rows, total_slices = row_share * slab_count, slab_depth * slab_count
    tiles, columns = cell_count // LANES, column_count // LANES
    width = column_count // 2
    sub = sublane_index()
    zero = jnp.zeros((SUBLANES, LANES), F32)
    slab = lax.axis_index("slab")

    _, _, flat = angle_facts(spread_scalars(lambda v: angle_ref[v], view_count, sub))
    lifts = spread_scalars(lambda v: lift_ref[v], view_count, sub).astype(F32)
    lane = lane_index()
    origin = slabs_of(slab, order)
    source = sum(jnp.where(lane >= slab_depth * b, 1, 0) for b in range(1, len(order)))
    slices = spread_scalars(lambda b: origin[b], len(order), source) * slab_depth + (lane - source * slab_depth)
    held = (slices >= 0) & (slices < total_slices)
    slices = slices.astype(F32)
    for row in range(row_share):
        sample = cone_sample((slab * row_share + row).astype(F32), lifts, flat, total_rows, total_slices)
        weights = jnp.where(held, jnp.maximum(0.0, 1.0 - jnp.abs(sample - slices)), 0.0)
        for place in range(slab_depth * len(order)):
            own_cone_ref[place, row, :, :] = column_of(weights, place)
        total = cone_total(sample, total_slices)
        for tile in range(columns):
            cut = slice(tile * LANES, (tile + 1) * LANES)
            own_ref[row, :, cut] = 1.0 / jnp.maximum(total * cover_ref[:, cut], LEN_FLOOR)

    cosine, flat, lifts = subset_angles(angle_ref, lift_ref, subset_ref)
    tangents = member_tangents(angle_ref, subset_ref)
    for member in range(subset_count):
        tangent_ref[member, :, :] = tangents[member]
    view_ref[...] = spread_scalars(lambda k: subset_ref[k], subset_count, jnp.bitwise_and(sub, subset_count - 1))
    for member in range(subset_count):
        view = pl.ds(subset_ref[member], 1)
        for side in range(2):
            at = slice(side * subset_count + member, side * subset_count + member + 1)
            sub_ref[at, :] = cover_ref[view, side * width : (side + 1) * width]
    sample, weights = subset_cone(slab, slab_count, order, kinds, slab_depth, row_share, flat, lifts)
    total = cone_total(sample, total_slices)
    for place in range(row_share * len(order)):
        for z, w in enumerate(weights):
            cone_ref[place, z, :, :] = column_of(w, place)
        length = column_of(total, place)
        for tile in range(width // LANES):
            cut = slice(tile * LANES, (tile + 1) * LANES)
            rows_ref[place, :, cut] = 1.0 / jnp.maximum(length * sub_ref[:, cut], LEN_FLOOR)

    factor = 1.0 / (row_count * cosine)
    line = []
    for tile in range(tiles + 1):
        taps = adjoint_taps(tile, cosine, column_count, cell_count, row_count // 2)
        for tap, (place, weight) in enumerate(taps):
            place_ref[tile, tap, :, :] = place
            tap_ref[tile, tap, :, :] = weight * factor
        line.append(sum(weight for _, weight in taps) * factor)
    store_line(line, edge_ref, bend_ref)
    slice_total = []
    for depth in range(slab_depth):
        t = jnp.sum(weights[1 + depth], axis=1, keepdims=True)
        slice_total.append([jnp.broadcast_to(t[k : k + 1], (SUBLANES, LANES)) for k in range(subset_count)])

    def one_group(group, carry):
        band = pl.ds(pl.multiple_of(group * SUBLANES, SUBLANES), SUBLANES)
        weight = [[zero] * tiles for _ in range(slab_depth)]
        for member in range(subset_count):
            line = sheared(edge_ref, bend_ref, member, adjoint_steps(group, row_count, tangents[member]), tiles)
            for depth in range(slab_depth):
                for tile in range(tiles):
                    weight[depth][tile] = weight[depth][tile] + slice_total[depth][member] * line[tile]
        for depth in range(slab_depth):
            for tile in range(tiles):
                bound_ref[depth, band, tile * LANES : (tile + 1) * LANES] = 1.0 / jnp.maximum(
                    weight[depth][tile], LEN_FLOOR * subset_count / row_count
                )
        return carry

    lax.fori_loop(0, row_count // SUBLANES, one_group, 0)


def update_kernel(
    order,
    kinds,
    volume_ref,
    measured_ref,
    bound_ref,
    own_ref,
    rows_ref,
    own_cone_ref,
    cone_ref,
    place_ref,
    tap_ref,
    tangent_ref,
    view_ref,
    *refs,
):
    blocks = refs[: len(order)]
    residual_ref, updated_ref, profile_ref, spread_ref, cell_ref, slope_ref, rest_ref, new_ref, row_ref, sent = refs[len(order) :]
    slab_depth, row_count, cell_count = volume_ref.shape
    row_share, view_count, column_count = measured_ref.shape
    subset_count = tangent_ref.shape[0]
    tiles, columns = cell_count // LANES, column_count // LANES
    width = column_count // 2
    zero = jnp.zeros((SUBLANES, LANES), F32)
    slab = lax.axis_index("slab")
    odd = lax.rem(slab, 2)
    turns = turned(slab, kinds)
    mate_block, other_block = (blocks[order.index(away)] for away in (1, -1))

    groups = row_count // SUBLANES
    for tile in range(columns):
        side, inner = divmod(tile * LANES, width)
        image = [zero] * row_share
        for place, block in enumerate(blocks):
            for depth in range(slab_depth):
                cells = block[depth * 2 + side, :, inner : inner + LANES]
                for row in range(row_share):
                    image[row] = image[row] + own_cone_ref[place * slab_depth + depth, row, :, :] * cells
        cut = slice(tile * LANES, (tile + 1) * LANES)
        for row in range(row_share):
            rest_ref[row, :, cut] = (measured_ref[row, :, cut] - image[row]) * own_ref[row, :, cut]
    copies = [pltpu.make_async_copy(rest_ref, residual_ref, sent.at[groups])]
    copies[0].start()

    chosen, first_side = view_ref[...], sublane_index() < subset_count

    def of_members(read, tile):
        return jnp.where(first_side, pick_rows(read(0, tile), chosen), pick_rows(read(1, tile), chosen))

    inner_tiles = width // LANES
    for tile in range(inner_tiles):
        cut = slice(tile * LANES, (tile + 1) * LANES)
        last, first = (slab_depth - 1) * 2, 0
        below = lambda side, t: jnp.where(
            odd == 0, tile_of(other_block, (last + side,), t), tile_of(mate_block, (last + side,), t)
        )
        above = lambda side, t: jnp.where(
            odd == 0, tile_of(mate_block, (first + side,), t), tile_of(other_block, (first + side,), t)
        )
        profile_ref[0, :, cut] = of_members(below, tile)
        for depth in range(slab_depth):
            profile_ref[1 + depth, :, cut] = of_members(
                lambda side, t: tile_of(blocks[0], (depth * 2 + side,), t), tile
            )
        profile_ref[1 + slab_depth, :, cut] = of_members(above, tile)

    moved = [(b, j) for b, kind in enumerate(kinds) for j in range({FULL: 0, FAR: 2}.get(kind, 1))]
    for at_row, (b, j) in enumerate(moved):
        depth = turns[b] if kinds[b] in (NEAR, NEAR_SHARED) else j
        for tile in range(inner_tiles):
            row_ref[at_row, :, tile * LANES : (tile + 1) * LANES] = of_members(
                lambda side, t: tile_of(blocks[b], (depth * 2 + side,), t), tile
            )

    spread = [[zero] * inner_tiles for _ in range(slab_depth)]
    for place in range(row_share * len(order)):
        weight = [cone_ref[place, z, :, :] for z in range(slab_depth + 2)]
        block, row = divmod(place, row_share)
        here = (block, row) in moved
        held = row_ref if here else blocks[block]
        at_row = moved.index((block, row)) if here else 2 * slab_depth + row - sum(b == block for b, _ in moved)
        for tile in range(inner_tiles):
            cut = slice(tile * LANES, (tile + 1) * LANES)
            image = weight[0] * profile_ref[0, :, cut]
            for z in range(1, slab_depth + 2):
                image = image + weight[z] * profile_ref[z, :, cut]
            rest = (held[at_row, :, cut] - image) * rows_ref[place, :, cut]
            for depth in range(slab_depth):
                spread[depth][tile] = spread[depth][tile] + weight[1 + depth] * rest
    for depth in range(slab_depth):
        for tile in range(inner_tiles):
            for side in range(2):
                spread_ref[
                    depth * subset_count : (depth + 1) * subset_count,
                    side * width + tile * LANES : side * width + (tile + 1) * LANES,
                ] = spread[depth][tile][side * subset_count : (side + 1) * subset_count]

    line = []
    for tile in range(tiles + 1):
        value = zero
        for tap in range(3):
            place = place_ref[tile, tap, :, :]
            block, index = jnp.right_shift(place, 7), jnp.bitwise_and(place, LANES - 1)
            found = zero
            for at in adjoint_tiles(tile, tap, column_count, cell_count, row_count // 2):
                found = jnp.where(block == at, pick(tile_of(spread_ref, (), at), index), found)
            value = value + tap_ref[tile, tap, :, :] * found
        line.append(value)
    store_line(line, cell_ref, slope_ref)

    tangents = [tangent_ref[member, :, :] for member in range(subset_count)]
    for group in range(groups):
        band = slice(group * SUBLANES, (group + 1) * SUBLANES)
        back = [[zero] * tiles for _ in range(slab_depth)]
        for member in range(subset_count):
            step = adjoint_steps(group, row_count, tangents[member])
            for depth in range(slab_depth):
                line = sheared(cell_ref, slope_ref, depth * subset_count + member, step, tiles)
                back[depth] = [b + a for b, a in zip(back[depth], line)]
        for depth in range(slab_depth):
            for tile in range(tiles):
                cut = slice(tile * LANES, (tile + 1) * LANES)
                new_ref[depth, band, cut] = (
                    volume_ref[depth, band, cut] + back[depth][tile] * bound_ref[depth, band, cut]
                )
        copies.append(pltpu.make_async_copy(new_ref.at[:, band, :], updated_ref.at[:, band, :], sent.at[group]))
        copies[-1].start()
    for copy in copies:
        copy.wait()


def swapped(block):
    return lax.ppermute(block, "slab", [(i, i ^ 1) for i in range(lax.axis_size("slab"))])


def from_chip(block, distance):
    slabs = range(lax.axis_size("slab"))
    steps = [(i + 2 * distance * (1 - 2 * (i % 2)), i) for i in slabs]
    pairs = [p for p in steps if p[0] in slabs]
    idle = [i for i in slabs if i not in [p[0] for p in pairs]]
    unmet = [i for i in slabs if i not in [p[1] for p in pairs]]
    near = [i for i in idle if i ^ 1 in unmet]
    pairs += [(i, i ^ 1) for i in near]
    pairs += zip([i for i in idle if i not in near], [i for i in unmet if i ^ 1 not in near])
    return lax.ppermute(block, "slab", pairs)


def fetches(reach):
    return [s * d for d in range(reach // 2 + 1, 0, -1) for s in (1, -1) if 2 * d - (s > 0) <= reach]


def window(reach):
    order, kinds = [0, 1], [FULL, FULL]
    for distance in fetches(reach):
        near = distance == 1
        for away, kind in ((2 * distance, NEAR if near else FAR), (1 - 2 * distance, NEAR_SHARED if near else FAR)):
            if abs(away) <= reach:
                order.append(away)
                kinds.append(kind)
    assert sorted(order) == list(range(-reach, reach + 1))
    return tuple(order), tuple(kinds)


def gathered(own, near, low, high, reach, meanwhile):
    sent = {distance: near if distance == 1 else high if distance > 0 else low for distance in fetches(reach)}
    received = {distance: from_chip(block, distance) for distance, block in sent.items()}
    done = meanwhile()
    own, done = lax.optimization_barrier((own, done))
    blocks = {0: own, 1: swapped(own)}
    arrived = list(received.values())
    for distance, block in zip(received, arrived):
        if 2 * abs(distance) <= reach:
            blocks[2 * distance] = block
        if abs(1 - 2 * distance) <= reach:
            blocks[1 - 2 * distance] = swapped(block)
    return [blocks[away] for away in window(reach)[0]], done


def per_device(volume, measured, view_angle, view_lift, subset):
    slab_count = lax.axis_size("slab")
    slab_depth, row_count, cell_count = volume.shape
    row_share, view_count, column_count = measured.shape
    subset_count = subset.shape[0]
    tiles = cell_count // LANES
    reach = slab_reach(slab_count, slab_depth, row_share)
    here = lambda x: pltpu.with_memory_space_constraint(x, pltpu.VMEM)
    there = lambda x: pltpu.with_memory_space_constraint(x, pltpu.HBM)
    small = pltpu.CompilerParams(vmem_limit_bytes=VMEM_LIMIT)
    smem, vmem = pl.BlockSpec(memory_space=pltpu.SMEM), pl.BlockSpec(memory_space=pltpu.VMEM)
    wide = (tiles + 1) * LANES
    block_of = lambda rows: pltpu.VMEM((2 * slab_depth + rows, SUBLANES, column_count // 2), F32)
    own, near, low, high, cover = pl.pallas_call(
        functools.partial(project_kernel, slab_count),
        out_shape=(
            block_of(row_share),
            block_of(2),
            block_of(1),
            block_of(2),
            pltpu.VMEM((view_count, column_count), F32),
        ),
        in_specs=[smem] * 3 + [vmem] * 2,
        out_specs=(vmem,) * 5,
        scratch_shapes=[
            pltpu.VMEM(volume.shape, F32),
            pltpu.VMEM((slab_depth, row_count, LANES), F32),
            pltpu.VMEM((slab_depth, view_count, SUBLANES, wide), F32),
            pltpu.VMEM((2, view_count, SUBLANES, LANES), F32),
        ]
        + [pltpu.VMEM((slab_depth + 1, SUBLANES, wide), F32)] * 2,
        compiler_params=small,
        name="project",
    )(*map(there, (view_angle, view_lift, subset, volume, measured)))
    cover = here(cover)
    order, kinds = window(reach)
    divide = pl.pallas_call(
        functools.partial(divisor_kernel, slab_count, order, kinds),
        out_shape=(
            pltpu.VMEM(volume.shape, F32),
            pltpu.VMEM(measured.shape, F32),
            pltpu.VMEM((row_share * len(order), SUBLANES, column_count // 2), F32),
            pltpu.VMEM((slab_depth * len(order), row_share, SUBLANES, LANES), F32),
            pltpu.VMEM((row_share * len(order), slab_depth + 2, SUBLANES, LANES), F32),
            pltpu.VMEM((tiles + 1, 3, SUBLANES, LANES), jnp.int32),
            pltpu.VMEM((tiles + 1, 3, SUBLANES, LANES), F32),
            pltpu.VMEM((subset_count, SUBLANES, LANES), F32),
            pltpu.VMEM((SUBLANES, LANES), jnp.int32),
        ),
        in_specs=[smem] * 3 + [vmem],
        out_specs=(vmem,) * 9,
        scratch_shapes=[pltpu.VMEM((SUBLANES, wide), F32)] * 2 + [pltpu.VMEM((SUBLANES, column_count // 2), F32)],
        cost_estimate=pl.CostEstimate(flops=4_000_000, bytes_accessed=8_000_000, transcendentals=0),
        compiler_params=small,
        name="divisors",
    )
    blocks, divisors = gathered(own, near, low, high, reach, lambda: divide(view_angle, view_lift, subset, cover))
    return pl.pallas_call(
        functools.partial(update_kernel, order, kinds),
        out_shape=(
            jax.ShapeDtypeStruct(measured.shape, F32),
            jax.ShapeDtypeStruct(volume.shape, F32),
        ),
        in_specs=[vmem] * (2 + len(divisors) + len(order)),
        out_specs=(pl.BlockSpec(memory_space=pl.ANY),) * 2,
        scratch_shapes=[
            pltpu.VMEM((slab_depth + 2, SUBLANES, column_count // 2), F32),
            pltpu.VMEM((SUBLANES, column_count), F32),
            pltpu.VMEM((SUBLANES, wide), F32),
            pltpu.VMEM((SUBLANES, wide), F32),
            pltpu.VMEM(measured.shape, F32),
            pltpu.VMEM(volume.shape, F32),
            pltpu.VMEM((2 * len(order), SUBLANES, column_count // 2), F32),
            pltpu.SemaphoreType.DMA((row_count // SUBLANES + 1,)),
        ],
        compiler_params=small,
        name="update",
    )(*map(here, (volume, measured, *divisors, *blocks)))


def solution(mesh):
    in_specs = (
        P(("scan", "slab"), None, None),
        P(("scan", "slab"), None, None),
        P("scan"),
        P("scan"),
        P("scan"),
    )
    out_specs = (P(("scan", "slab"), None, None), P(("scan", "slab"), None, None))
    return jax.shard_map(
        per_device, mesh=mesh, in_specs=in_specs, out_specs=out_specs, check_vma=False
    )
```
